32 devices in a mesh: dp: 2 (over x), ctx: 4 (over z), exp: 4 (over y, core).
Axes of the slice: x: 2, y: 2, z: 4, core: 2. Of those that a mesh axis runs over, the one named last changes fastest.
Arguments:
- tokens: bfloat16 [2, 2048, 2048], P('dp', 'ctx'), may hold values from -6 to 6
- routes: int32 [2, 2048, 6], P('dp', 'ctx'), may hold values from 0 to 15, all different within a row; in each aligned block of 128 rows (0 to 127, 128 to 255, ..., all dimensions but the last counted through in order) at most 64 rows name the same one
- norm_attn: bfloat16 [2048], P(('dp', 'ctx')), may hold values from 0.25 to 1.75
- w_query: bfloat16 [2048, 2048], P(('dp', 'ctx'), 'exp'), may hold values from -0.125 to 0.125
- w_key: bfloat16 [2048, 2048], P(('dp', 'ctx'), 'exp'), may hold values from -0.125 to 0.125
- w_value: bfloat16 [2048, 2048], P(('dp', 'ctx'), 'exp'), may hold values from -0.125 to 0.125
- w_out: bfloat16 [2048, 2048], P('exp', ('dp', 'ctx')), may hold values from -2 to 2
- norm_mix: bfloat16 [2048], P(('dp', 'ctx')), may hold values from 0.25 to 1.75
- w_router: bfloat16 [2048, 16], P(('dp', 'ctx')), may hold values from -0.0625 to 0.0625
- shared_gate: bfloat16 [2048, 2816], P(('dp', 'ctx'), 'exp'), may hold values from -0.125 to 0.125
- shared_up: bfloat16 [2048, 2816], P(('dp', 'ctx'), 'exp'), may hold values from -0.125 to 0.125
- shared_down: bfloat16 [2816, 2048], P('exp', ('dp', 'ctx')), may hold values from -0.109375 to 0.109375
- expert_gate: bfloat16 [16, 2048, 1408], P(('ctx', 'exp'), None, 'dp'), may hold values from -0.125 to 0.125
- expert_up: bfloat16 [16, 2048, 1408], P(('ctx', 'exp'), None, 'dp'), may hold values from -0.125 to 0.125
- expert_down: bfloat16 [16, 1408, 2048], P(('ctx', 'exp'), 'dp'), may hold values from -6 to 6
- out_grad: bfloat16 [2, 2048, 2048], P('dp', 'ctx'), may hold values from -6 to 6
Outputs:
- mixed: bfloat16 [2, 2048, 2048], P('dp', 'ctx')
- tokens_grad: bfloat16 [2, 2048, 2048], P('dp', 'ctx')
- norm_attn_grad: float32 [2048], P(('dp', 'ctx'))
- w_query_grad: float32 [2048, 2048], P(('dp', 'ctx'), 'exp')
- w_key_grad: float32 [2048, 2048], P(('dp', 'ctx'), 'exp')
- w_value_grad: float32 [2048, 2048], P(('dp', 'ctx'), 'exp')
- w_out_grad: float32 [2048, 2048], P('exp', ('dp', 'ctx'))
- norm_mix_grad: float32 [2048], P(('dp', 'ctx'))
- w_router_grad: float32 [2048, 16], P(('dp', 'ctx'))
- shared_gate_grad: float32 [2048, 2816], P(('dp', 'ctx'), 'exp')
- shared_up_grad: float32 [2048, 2816], P(('dp', 'ctx'), 'exp')
- shared_down_grad: float32 [2816, 2048], P('exp', ('dp', 'ctx'))
- expert_gate_grad: float32 [16, 2048, 1408], P(('ctx', 'exp'), None, 'dp')
- expert_up_grad: float32 [16, 2048, 1408], P(('ctx', 'exp'), None, 'dp')
- expert_down_grad: float32 [16, 1408, 2048], P(('ctx', 'exp'), 'dp')
The draws below stay inside these ranges and needn't reach their ends.
Inputs may be any that keep to these rules, and one draw needn't show every extreme that they name: `routes`: A token names 6 different experts. Within each aligned group of 128 tokens of a sequence no expert is named more than 64 times, and in every draw some expert is named exactly 64 times in some group.
All inputs are finite; a program needn't handle non-finite values.
Results may differ from the reference program's by a relative error of at most 0.025.
Values may be sent and summed in bfloat16 or wider, within the bound.
A program may use at most 320 MiB of HBM per device.

```python
import math
import jax
import jax.numpy as jnp
import numpy as np
from jax import lax

D = 2048
HEADS = 16
HDIM = 128
FE = 1408
TOPK = 6
SEQ = 2048
HD = 2048
FS = 2816
EXPERTS = 16
SEQS = 2
QUARTER = 128
CAP = 64
N_DP = 2


def block_scale(own_key, extent, shards, least, top_value):
    def one(axis_at, blocks):
        draws = jax.random.uniform(jax.random.fold_in(jax.random.fold_in(own_key, 6), axis_at), (blocks,), jnp.float32, least / len(shards), top_value / len(shards))
        return jnp.repeat(jnp.exp(draws), extent[axis_at] // blocks).reshape((-1,) + (1,) * (len(extent) - axis_at - 1))

    gain = one(*shards[0])
    for cut in shards[1:]:
        gain = gain * one(*cut)
    return gain


def deal_out(own_key, own, number, rows, number_of, top, reach, slope):
    order = jax.random.permutation(own_key, number_of)
    heavy_load, usual = shares(number_of, rows * top, reach, slope, True), shares(number_of, rows * top, reach, slope, False)
    places = jnp.arange(number_of)

    def named(sizes, offset_by):
        used = int((sizes > 0).sum())
        fixed = max(1, used // 4)
        passed = fixed + (places - fixed + offset_by * (used - fixed)) % max(1, number_of - fixed)
        return jnp.zeros((number_of,), jnp.int32).at[order[jnp.where(places < fixed, places, passed)]].set(jnp.asarray(sizes, jnp.int32))

    sizes = jnp.where(number % 4 == 0, named(heavy_load, number // 4), named(usual, number - number // 4 - 1))
    mixed = jax.random.permutation(jax.random.fold_in(own, 3), number_of)
    donor, sink = mixed[0:number_of // 2 * 2:2], mixed[1:number_of // 2 * 2:2]
    margin = jnp.minimum(sizes[donor] - 1, reach - sizes[sink]) // 2
    margin = jnp.where((donor == order[0]) | (sink == order[0]) | (sizes[sink] == 0), 0, jnp.maximum(margin, 0))
    passed = jax.random.randint(jax.random.fold_in(own, 4), (number_of // 2,), 0, 1 << 20) % (margin + 1)
    sizes = sizes.at[donor].add(-passed).at[sink].add(passed)
    items = jnp.searchsorted(jnp.cumsum(sizes), jnp.arange(rows * top), side="right").astype(jnp.int32)
    listing = items.reshape(top, rows).T
    listing = listing[jax.random.permutation(jax.random.fold_in(own, 1), rows)]
    offset_by = jax.random.randint(jax.random.fold_in(own, 2), (rows, 1), 0, top)
    return jnp.take_along_axis(listing, (jnp.arange(top)[None, :] + offset_by) % top, axis=1)


def shares(number_of, total, bound, lean, full):
    weights = [(1 << 20) // math.isqrt(grade ** lean) + 1 for grade in range(1, number_of + 1)]
    largest = bound if full else min(bound, max(-(-total // number_of), total * weights[0] // sum(weights)))
    least = 1 if total - largest >= number_of - 1 else 0
    counts, surplus = [largest] + [least] * (number_of - 1), total - largest - least * (number_of - 1)
    while surplus > 0:
        candidates = [i for i in range(1, number_of) if counts[i] < largest] or [i for i in range(1, number_of) if counts[i] < bound]
        mass, budget = sum([weights[i] for i in candidates]), surplus
        for i in candidates:
            extra = min(bound - counts[i], max(1, budget * weights[i] // mass), surplus)
            counts[i] = counts[i] + extra
            surplus = surplus - extra
    return np.array(counts)


def bell_draw(key, dims, deviation, bound, cuts=(), held_as=jnp.bfloat16):
    array = deviation * jax.random.normal(key, dims, jnp.float32)
    if cuts:
        array = array * block_scale(key, dims, cuts, -0.22, 0.18)
    return jnp.clip(array, -bound, bound).astype(held_as)


def setup_inputs(seed: int = 0) -> dict:
    key_of = jax.random.split(jax.random.key(seed), 17)
    tokens = bell_draw(key_of[0], (SEQS, SEQ, D), 1.0, 6.0, ((0, 2), (1, 4)))
    routes_keys = jax.random.split(jax.random.fold_in(key_of[1], 1), SEQS * SEQ // QUARTER)
    routes_turns = jax.random.permutation(jax.random.fold_in(key_of[1], 3), SEQS * SEQ // QUARTER)
    routes = jax.vmap(lambda own, number: deal_out(jax.random.fold_in(key_of[1], 2), own, number, QUARTER, EXPERTS, TOPK, CAP, 1))(routes_keys, routes_turns).reshape((SEQS, SEQ, TOPK))
    norm_attn = jnp.clip(1.0 + 0.15 * jax.random.normal(key_of[2], (D,), jnp.float32), 0.25, 1.75).astype(jnp.bfloat16)
    w_query = bell_draw(key_of[3], (D, HD), D ** -0.5, 0.125, ((0, 8), (1, 4)))
    w_key = bell_draw(key_of[4], (D, HD), D ** -0.5, 0.125, ((0, 8), (1, 4)))
    w_value = bell_draw(key_of[5], (D, HD), D ** -0.5, 0.125, ((0, 8), (1, 4)))
    w_out = bell_draw(key_of[6], (HD, D), (max(HD // 256, 1)) ** -0.5, 2.0, ((0, 4), (1, 8)))
    norm_mix = jnp.clip(1.0 + 0.15 * jax.random.normal(key_of[7], (D,), jnp.float32), 0.25, 1.75).astype(jnp.bfloat16)
    w_router = bell_draw(key_of[8], (D, EXPERTS), (4 * D) ** -0.5, 0.0625, ((0, 8),))
    shared_gate = bell_draw(key_of[9], (D, FS), D ** -0.5, 0.125, ((0, 8), (1, 4)))
    shared_up = bell_draw(key_of[10], (D, FS), D ** -0.5, 0.125, ((0, 8), (1, 4)))
    shared_down = bell_draw(key_of[11], (FS, D), FS ** -0.5, 0.109375, ((0, 4), (1, 8)))
    expert_gate = bell_draw(key_of[12], (EXPERTS, D, FE), D ** -0.5, 0.125, ((0, 16), (2, 2)))
    expert_up = bell_draw(key_of[13], (EXPERTS, D, FE), D ** -0.5, 0.125, ((0, 16), (2, 2)))
    expert_down = bell_draw(key_of[14], (EXPERTS, FE, D), (max(FE // 1024, 1)) ** -0.5, 6.0, ((0, 16), (1, 2)))
    out_grad = bell_draw(key_of[15], (SEQS, SEQ, D), 1.0, 6.0, ((0, 2), (1, 4)))
    return dict(tokens=tokens, routes=routes, norm_attn=norm_attn, w_query=w_query, w_key=w_key, w_value=w_value, w_out=w_out, norm_mix=norm_mix, w_router=w_router, shared_gate=shared_gate, shared_up=shared_up, shared_down=shared_down, expert_gate=expert_gate, expert_up=expert_up, expert_down=expert_down, out_grad=out_grad)


@jax.custom_vjp
def low(v):
    return lax.optimization_barrier(v.astype(jnp.bfloat16)).astype(jnp.float32)

@jax.custom_vjp
def low_back(v):
    return v

def low_keep(v):
    return (low(v), None)

def low_pass(kept, grad):
    return (grad,)

def back_keep(v):
    return (v, None)

def back_low(kept, grad):
    return (low(grad),)
low.defvjp(low_keep, low_pass)
low_back.defvjp(back_keep, back_low)
EPSILON = 1e-06
MASKED = -1e+30
HIGHEST = lax.Precision.HIGHEST

def product(left_side, right_side):
    return jnp.dot(left_side, right_side, precision=HIGHEST, preferred_element_type=jnp.float32)

def rms_scale(values, gain_row):
    return values * lax.rsqrt(lax.optimization_barrier(jnp.mean(values * values, axis=-1, keepdims=True)) + EPSILON) * gain_row

def rope_tables(positions, rope_width):
    inverse = 10000.0 ** (-jnp.arange(rope_width // 2).astype(jnp.float32) * 2.0 / rope_width)
    angles = positions.astype(jnp.float32)[:, None] * inverse[None, :]
    return (jnp.cos(angles), jnp.sin(angles))

def rotate(values, cosine, sine_table):
    half_size = values.shape[-1] // 2
    first_half = values[..., :half_size]
    second = values[..., half_size:]
    cosine = cosine[:, None, :]
    sine_table = sine_table[:, None, :]
    return jnp.concatenate([first_half * cosine - second * sine_table, second * cosine + first_half * sine_table], axis=-1)

def attend_sequence(normed, query_matrix, key_matrix, value_matrix, output_matrix):
    length = normed.shape[0]
    positions = jnp.arange(length, dtype=jnp.int32)
    cosine, sine_table = rope_tables(positions, HDIM)
    query_rows = low_back(product(normed, query_matrix)).reshape(length, HEADS, HDIM)
    key_rows = low_back(product(normed, key_matrix)).reshape(length, HEADS, HDIM)
    valued = low(low_back(product(normed, value_matrix))).reshape(length, HEADS, HDIM)
    query_rot = low(rotate(query_rows, cosine, sine_table))
    key_rot = low(rotate(key_rows, cosine, sine_table))
    scores = low_back(jnp.einsum('qhd,khd->hqk', query_rot, key_rot, precision=HIGHEST) * HDIM ** (-0.5))
    visible = positions[:, None] >= positions[None, :]
    scores = jnp.where(visible[None], scores, MASKED)
    weights = low(jax.nn.softmax(scores, axis=-1))
    heads_out = jnp.einsum('hqk,khd->qhd', weights, valued, precision=HIGHEST).reshape(length, HEADS * HDIM)
    heads_out = low_back(low(heads_out))
    return low_back(product(heads_out, output_matrix))

def reference(tokens, routes, norm_attn, w_query, w_key, w_value, w_out, norm_mix, w_router, shared_gate, shared_up, shared_down, expert_gate, expert_up, expert_down, out_grad):
    total_rows = SEQS * SEQ
    blocks = total_rows // QUARTER
    route_rows = routes.reshape(blocks, QUARTER * TOPK)
    expert_choice_index = jnp.arange(EXPERTS, dtype=jnp.int32)
    expert_hits = (route_rows[:, :, None] == expert_choice_index[None, None, :]).astype(jnp.int32)
    slot_index = lax.optimization_barrier(jnp.sum(jnp.cumsum(expert_hits, axis=1) * expert_hits, axis=2)) - 1
    block_ids = jnp.broadcast_to(jnp.arange(blocks, dtype=jnp.int32)[:, None], route_rows.shape)
    token_rows = block_ids * QUARTER + jnp.arange(QUARTER * TOPK, dtype=jnp.int32)[None, :] // TOPK
    expert_slot_lookup = jnp.full((EXPERTS, blocks, CAP), total_rows, jnp.int32)
    expert_slot_lookup = expert_slot_lookup.at[route_rows, block_ids, slot_index].set(token_rows).reshape(EXPERTS, blocks * CAP)
    half_width = FE // N_DP

    def forward_layer(layer_input, attention_gain, query_matrix, key_matrix, value_matrix, output_matrix, mixer_gain, router_matrix, shared_gate_matrix, shared_up_matrix, shared_down_matrix, expert_gate_matrix, expert_up_matrix, expert_down_matrix):
        normed = low(rms_scale(layer_input, attention_gain))
        attended = lax.map(jax.checkpoint(lambda sequence: attend_sequence(sequence, query_matrix, key_matrix, value_matrix, output_matrix)), normed)
        middle = layer_input + attended
        normed_mix = low(rms_scale(middle, mixer_gain)).reshape(total_rows, D)
        logits = low_back(product(normed_mix, router_matrix))
        probabilities = jax.nn.softmax(logits, axis=-1)
        shared_hidden = low(jax.nn.silu(low_back(product(normed_mix, shared_gate_matrix))) * low_back(product(normed_mix, shared_up_matrix)))
        shared_result = product(shared_hidden, shared_down_matrix)
        padded = jnp.concatenate([normed_mix, jnp.zeros((1, D), normed_mix.dtype)], axis=0)
        padded_probs = jnp.concatenate([probabilities, jnp.zeros((1, EXPERTS), probabilities.dtype)], axis=0)

        def expert_token_rows(pieces):
            rows_index, expert_index, gate_weight, up_weight, down_weight = pieces
            chosen = padded[rows_index]
            gate_values = padded_probs[rows_index, expert_index]
            gated_rows = low_back(product(chosen, gate_weight))
            upward = low_back(product(chosen, up_weight))
            hidden = low(jax.nn.silu(gated_rows) * upward)
            summed = jnp.zeros((chosen.shape[0], D), jnp.float32)
            for portion in range(N_DP):
                lower = portion * half_width
                summed = summed + low(product(hidden[:, lower:lower + half_width], down_weight[lower:lower + half_width]))
            return low_back(low(summed)) * gate_values[:, None]
        layer_output = lax.map(jax.checkpoint(expert_token_rows), (expert_slot_lookup, expert_choice_index, expert_gate_matrix, expert_up_matrix, expert_down_matrix))
        combined = jnp.zeros((total_rows + 1, D), jnp.float32).at[expert_slot_lookup.reshape(-1)].add(layer_output.reshape(-1, D))[:total_rows]
        result = middle.reshape(total_rows, D) + shared_result + combined
        return result.reshape(SEQS, SEQ, D)
    primals = tuple((initial.astype(jnp.float32) for initial in (tokens, norm_attn, w_query, w_key, w_value, w_out, norm_mix, w_router, shared_gate, shared_up, shared_down, expert_gate, expert_up, expert_down)))
    result, pullback = jax.vjp(forward_layer, *primals)
    gradients = pullback(out_grad.astype(jnp.float32))
    return (result.astype(jnp.bfloat16), gradients[0].astype(jnp.bfloat16), gradients[1], gradients[2], gradients[3], gradients[4], gradients[5], gradients[6], gradients[7], gradients[8], gradients[9], gradients[10], gradients[11], gradients[12], gradients[13])
```

```python
import functools

import jax
import jax.numpy as jnp
import numpy as np
from jax import lax
from jax.experimental import pallas as pl
from jax.experimental.pallas import tpu as pltpu
from jax.sharding import PartitionSpec as P

HDIM = 128
TOPK = 6


EPSILON = 1e-06
MASKED = -1e30
HIGHEST = lax.Precision.HIGHEST


def rms_scale(values, gain_row):
    return (
        values * lax.rsqrt(jnp.mean(values * values, axis=-1, keepdims=True) + EPSILON) * gain_row
    )


def rope_tables(positions, rope_width):
    inverse = 10000.0 ** (-jnp.arange(rope_width // 2).astype(jnp.float32) * 2.0 / rope_width)
    angles = positions.astype(jnp.float32)[:, None] * inverse[None, :]
    return (jnp.cos(angles), jnp.sin(angles))


def rotate(values, cosine, sine_table):
    half_size = values.shape[-1] // 2
    first_half = values[..., :half_size]
    second = values[..., half_size:]
    cosine = cosine[:, None, :]
    sine_table = sine_table[:, None, :]
    return jnp.concatenate(
        [first_half * cosine - second * sine_table, second * cosine + first_half * sine_table],
        axis=-1,
    )


def silu_mix(gate_rows, up_rows):
    return jax.nn.silu(gate_rows) * up_rows


def product(left_side, right_side):
    return jnp.dot(left_side, right_side, preferred_element_type=jnp.float32)


def transposed_left(left_side, right_side):
    return lax.dot_general(
        left_side, right_side, (((0,), (0,)), ((), ())), preferred_element_type=jnp.float32
    )


def transposed_right(left_side, right_side):
    return lax.dot_general(
        left_side, right_side, (((1,), (1,)), ((), ())), preferred_element_type=jnp.float32
    )


def place_rows(part, start_row, total_rows):
    blank = jnp.zeros((total_rows, part.shape[1]), jnp.float32)
    return lax.dynamic_update_slice_in_dim(blank, part, start_row, 0)


def to_owners(buffer):
    copies = lax.axis_size("dp")
    widened = jnp.broadcast_to(buffer[None], (copies,) + buffer.shape)
    widened = widened.reshape((copies * buffer.shape[0],) + buffer.shape[1:])
    return lax.all_to_all(widened, ("dp", "ctx", "exp"), split_axis=0, concat_axis=0, tiled=True)


def values_home(partial_value):
    returned = lax.all_to_all(
        partial_value, ("dp", "ctx", "exp"), split_axis=0, concat_axis=0, tiled=True
    )
    grouped = returned.reshape((lax.axis_size("dp"), -1) + returned.shape[1:])
    return jnp.sum(grouped.astype(jnp.float32), axis=0).astype(jnp.bfloat16)


def grads_home(partial_value):
    returned = lax.all_to_all(
        partial_value.astype(jnp.bfloat16),
        ("dp", "ctx", "exp"),
        split_axis=0,
        concat_axis=0,
        tiled=True,
    ).astype(partial_value.dtype)
    grouped = returned.reshape((lax.axis_size("dp"), -1) + returned.shape[1:])
    return jnp.sum(grouped, axis=0)


def body(
    tokens,
    routes,
    norm_attn,
    w_query,
    w_key,
    w_value,
    w_out,
    norm_mix,
    w_router,
    shared_gate,
    shared_up,
    shared_down,
    expert_gate,
    expert_up,
    expert_down,
    out_grad,
):
    gathered = (
        lax.all_gather(norm_attn, ("dp", "ctx"), axis=0, tiled=True),
        lax.all_gather(w_query, ("dp", "ctx"), axis=0, tiled=True),
        lax.all_gather(w_key, ("dp", "ctx"), axis=0, tiled=True),
        lax.all_gather(w_value, ("dp", "ctx"), axis=0, tiled=True),
        lax.all_gather(w_out, ("dp", "ctx"), axis=1, tiled=True),
        lax.all_gather(norm_mix, ("dp", "ctx"), axis=0, tiled=True),
        lax.all_gather(w_router, ("dp", "ctx"), axis=0, tiled=True),
        lax.all_gather(shared_gate, ("dp", "ctx"), axis=0, tiled=True),
        lax.all_gather(shared_up, ("dp", "ctx"), axis=0, tiled=True),
        lax.all_gather(shared_down, ("dp", "ctx"), axis=1, tiled=True),
    )
    (
        attention_gain,
        query_matrix,
        key_matrix,
        value_matrix,
        output_matrix,
        mixer_gain,
        router_matrix,
        shared_gate_matrix,
        shared_up_matrix,
        shared_down_matrix,
    ) = gathered
    rows_here = tokens.shape[1]
    model_width = tokens.shape[2]
    heads_here = query_matrix.shape[1] // HDIM
    quarter = rows_here // lax.axis_size("exp")
    start_row = lax.axis_index("exp") * quarter
    layer_input = tokens[0].astype(jnp.float32)
    grad_rows = out_grad[0]
    grad_float = grad_rows.astype(jnp.float32)
    seq_length = rows_here * lax.axis_size("ctx")
    positions = lax.axis_index("ctx") * rows_here + jnp.arange(rows_here, dtype=jnp.int32)
    cosine, sine_table = rope_tables(positions, HDIM)
    visible = positions[:, None] >= jnp.arange(seq_length, dtype=jnp.int32)[None, :]
    scale = HDIM ** (-0.5)
    head_shape = (rows_here, heads_here, HDIM)
    normed = rms_scale(layer_input, attention_gain).astype(jnp.bfloat16)
    query_rot = rotate(
        product(normed, query_matrix).reshape(head_shape), cosine, sine_table
    ).astype(jnp.bfloat16)
    key_rot = (
        rotate(product(normed, key_matrix).reshape(head_shape), cosine, sine_table)
        .astype(jnp.bfloat16)
        .reshape(rows_here, -1)
    )
    value_low = product(normed, value_matrix).astype(jnp.bfloat16)
    key_all, value_all = (
        lax.all_gather(key_rot, "ctx", axis=0, tiled=True),
        lax.all_gather(value_low, "ctx", axis=0, tiled=True),
    )
    key_heads = key_all.reshape(seq_length, heads_here, HDIM)
    value_heads = value_all.reshape(seq_length, heads_here, HDIM)

    def attention_scores():
        scores = (
            jnp.einsum("qhd,khd->hqk", query_rot, key_heads, preferred_element_type=jnp.float32)
            * scale
        )
        return jnp.where(visible[None], scores, MASKED)

    scores = attention_scores()
    largest = jnp.max(scores, axis=-1, keepdims=True)
    log_total = largest + jnp.log(jnp.sum(jnp.exp(scores - largest), axis=-1, keepdims=True))
    weights_low = jnp.exp(scores - log_total).astype(jnp.bfloat16)
    heads_out = (
        jnp.einsum("hqk,khd->qhd", weights_low, value_heads, preferred_element_type=jnp.float32)
        .reshape(rows_here, -1)
        .astype(jnp.bfloat16)
    )
    attn_total = lax.psum(product(heads_out, output_matrix), "exp")
    middle = layer_input + attn_total
    normed_mix = rms_scale(middle, mixer_gain).astype(jnp.bfloat16)
    normed_quarter = lax.dynamic_slice_in_dim(normed_mix, start_row, quarter, 0)
    route_quarter = lax.dynamic_slice_in_dim(routes[0], start_row, quarter, 0)
    grad_quarter = lax.dynamic_slice_in_dim(grad_rows, start_row, quarter, 0)
    logits = product(normed_quarter, router_matrix)
    probabilities = jax.nn.softmax(logits, axis=-1)
    owners = lax.axis_size(("ctx", "exp"))
    local_experts = expert_gate.shape[0]
    experts = local_experts * owners
    capacity = max(quarter * TOPK * 4 // (3 * experts), 2)
    expert_choice_index = jnp.arange(experts, dtype=jnp.int32)
    chosen = (route_quarter[:, :, None] == expert_choice_index[None, None, :]).astype(jnp.float32)
    gates = jnp.sum(chosen * probabilities[:, None, :], axis=-1)
    route_flat = route_quarter.reshape(-1)
    expert_hits = (route_flat[:, None] == expert_choice_index[None, :]).astype(jnp.int32)
    slot_index = jnp.sum(jnp.cumsum(expert_hits, axis=0) * expert_hits, axis=1) - 1
    slot_place = route_flat * capacity + slot_index
    matches = (
        jnp.arange(experts * capacity, dtype=jnp.int32)[:, None] == slot_place[None, :]
    ).astype(jnp.float32)
    dispatch = jnp.sum(matches.reshape(experts * capacity, quarter, TOPK), axis=2).astype(
        jnp.bfloat16
    )
    slot_gates = jnp.dot(matches, gates.reshape(-1), precision=HIGHEST)
    buffer_shape = (owners, local_experts, capacity, model_width)
    outgoing = product(dispatch, normed_quarter).astype(jnp.bfloat16).reshape(buffer_shape)
    arrived = to_owners(outgoing)
    gate_hidden = jnp.einsum(
        "sicd,idf->sicf", arrived, expert_gate, preferred_element_type=jnp.float32
    )
    up_hidden = jnp.einsum("sicd,idf->sicf", arrived, expert_up, preferred_element_type=jnp.float32)
    expert_act = silu_mix(gate_hidden, up_hidden).astype(jnp.bfloat16)
    partial_value = jnp.einsum(
        "sicf,ifd->sicd", expert_act, expert_down, preferred_element_type=jnp.float32
    ).astype(jnp.bfloat16)
    expert_values = values_home(partial_value).reshape(experts * capacity, model_width)
    route_values = expert_values[slot_place].astype(jnp.float32).reshape(quarter, TOPK, model_width)
    combined = jnp.sum(route_values * gates[:, :, None], axis=1)
    shared_gate_rows = product(normed_mix, shared_gate_matrix)
    shared_up_rows = product(normed_mix, shared_up_matrix)
    shared_act = silu_mix(shared_gate_rows, shared_up_rows).astype(jnp.bfloat16)
    branch_part = product(shared_act, shared_down_matrix) + place_rows(
        combined, start_row, rows_here
    )
    result = middle + lax.psum(branch_part.astype(jnp.bfloat16), "exp").astype(jnp.float32)
    grad_slots = (
        (product(dispatch, grad_quarter) * slot_gates[:, None])
        .astype(jnp.bfloat16)
        .reshape(buffer_shape)
    )
    grad_arrived = to_owners(grad_slots)
    act_grad = jnp.einsum(
        "sicd,ifd->sicf", grad_arrived, expert_down, preferred_element_type=jnp.float32
    )
    down_grad = jnp.einsum(
        "sicf,sicd->ifd", expert_act, grad_arrived, preferred_element_type=jnp.float32
    )
    _, mix_back = jax.vjp(silu_mix, gate_hidden, up_hidden)
    gate_back, up_back = mix_back(act_grad)
    gate_back = gate_back.astype(jnp.bfloat16)
    up_back = up_back.astype(jnp.bfloat16)
    gate_grad = jnp.einsum("sicd,sicf->idf", arrived, gate_back, preferred_element_type=jnp.float32)
    up_grad = jnp.einsum("sicd,sicf->idf", arrived, up_back, preferred_element_type=jnp.float32)
    input_back = jnp.einsum(
        "sicf,idf->sicd", gate_back, expert_gate, preferred_element_type=jnp.float32
    ) + jnp.einsum("sicf,idf->sicd", up_back, expert_up, preferred_element_type=jnp.float32)
    rows_back = grads_home(input_back).reshape(experts * capacity, model_width)
    moe_back = jnp.sum(rows_back[slot_place].reshape(quarter, TOPK, model_width), axis=1)
    gate_route_back = jnp.sum(route_values * grad_quarter.astype(jnp.float32)[:, None, :], axis=-1)
    prob_back = jnp.sum(chosen * gate_route_back[:, :, None], axis=1)
    _, soft_back = jax.vjp(lambda values: jax.nn.softmax(values, axis=-1), logits)
    logit_back = soft_back(prob_back)[0].astype(jnp.bfloat16)
    router_term = transposed_left(normed_quarter, logit_back)
    shared_back = transposed_right(grad_rows, shared_down_matrix)
    _, shared_mix_back = jax.vjp(silu_mix, shared_gate_rows, shared_up_rows)
    sgate_back, sup_back = shared_mix_back(shared_back)
    sgate_back = sgate_back.astype(jnp.bfloat16)
    sup_back = sup_back.astype(jnp.bfloat16)
    quarter_back = transposed_right(logit_back, router_matrix) + moe_back
    mix_part = (
        transposed_right(sgate_back, shared_gate_matrix)
        + transposed_right(sup_back, shared_up_matrix)
        + place_rows(quarter_back, start_row, rows_here)
    )
    mix_total, router_grad = (
        lax.psum(mix_part.astype(jnp.bfloat16), "exp").astype(jnp.float32),
        lax.psum(router_term.astype(jnp.bfloat16), "exp").astype(jnp.float32),
    )
    _, norm_mix_back = jax.vjp(rms_scale, middle, mixer_gain.astype(jnp.float32))
    middle_norm_back, gain_mix_grad = norm_mix_back(mix_total)
    middle_grad = grad_float + middle_norm_back
    sdown_grad = transposed_left(shared_act, grad_rows)
    sgate_grad = transposed_left(normed_mix, sgate_back)
    sup_grad = transposed_left(normed_mix, sup_back)
    attn_back = middle_grad.astype(jnp.bfloat16)
    heads_back = transposed_right(attn_back, output_matrix).astype(jnp.bfloat16).reshape(head_shape)
    weights_full = jnp.exp(attention_scores() - log_total)
    weights_again = weights_full.astype(jnp.bfloat16)
    weight_back = jnp.einsum(
        "qhd,khd->hqk", heads_back, value_heads, preferred_element_type=jnp.float32
    )
    value_term = jnp.einsum(
        "hqk,qhd->khd", weights_again, heads_back, preferred_element_type=jnp.float32
    ).reshape(seq_length, -1)
    score_back = (
        weights_full * (weight_back - jnp.sum(weights_full * weight_back, axis=-1, keepdims=True))
    ).astype(jnp.bfloat16)
    query_rot_back = (
        jnp.einsum("hqk,khd->qhd", score_back, key_heads, preferred_element_type=jnp.float32)
        * scale
    )
    key_term = (
        jnp.einsum("hqk,qhd->khd", score_back, query_rot, preferred_element_type=jnp.float32)
        * scale
    ).reshape(seq_length, -1)
    key_sum, value_sum = (
        lax.psum_scatter(
            key_term.astype(jnp.bfloat16), "ctx", scatter_dimension=0, tiled=True
        ).astype(jnp.float32),
        lax.psum_scatter(
            value_term.astype(jnp.bfloat16), "ctx", scatter_dimension=0, tiled=True
        ).astype(jnp.float32),
    )
    _, rotate_back = jax.vjp(
        lambda values: rotate(values, cosine, sine_table), jnp.zeros(head_shape, jnp.float32)
    )
    query_low = rotate_back(query_rot_back)[0].reshape(rows_here, -1).astype(jnp.bfloat16)
    key_low = (
        rotate_back(key_sum.reshape(head_shape))[0].reshape(rows_here, -1).astype(jnp.bfloat16)
    )
    value_back_low = value_sum.astype(jnp.bfloat16)
    normed_part = (
        transposed_right(query_low, query_matrix)
        + transposed_right(key_low, key_matrix)
        + transposed_right(value_back_low, value_matrix)
    )
    normed_back = lax.psum(normed_part.astype(jnp.bfloat16), "exp").astype(jnp.float32)
    _, norm_attn_back = jax.vjp(rms_scale, layer_input, attention_gain.astype(jnp.float32))
    input_norm_back, gain_attn_grad = norm_attn_back(normed_back)
    tokens_back = (middle_grad + input_norm_back).astype(jnp.bfloat16)
    out_weight_grad = transposed_left(heads_out, attn_back)
    query_grad = transposed_left(normed, query_low)
    key_grad = transposed_left(normed, key_low)
    value_grad = transposed_left(normed, value_back_low)
    all_sums = (
        lax.psum_scatter(
            gain_attn_grad.astype(jnp.bfloat16), ("dp", "ctx"), scatter_dimension=0, tiled=True
        ).astype(jnp.float32),
        lax.psum_scatter(
            query_grad.astype(jnp.bfloat16), ("dp", "ctx"), scatter_dimension=0, tiled=True
        ).astype(jnp.float32),
        lax.psum_scatter(
            key_grad.astype(jnp.bfloat16), ("dp", "ctx"), scatter_dimension=0, tiled=True
        ).astype(jnp.float32),
        lax.psum_scatter(
            value_grad.astype(jnp.bfloat16), ("dp", "ctx"), scatter_dimension=0, tiled=True
        ).astype(jnp.float32),
        lax.psum_scatter(
            out_weight_grad.astype(jnp.bfloat16), ("dp", "ctx"), scatter_dimension=1, tiled=True
        ).astype(jnp.float32),
        lax.psum_scatter(
            gain_mix_grad.astype(jnp.bfloat16), ("dp", "ctx"), scatter_dimension=0, tiled=True
        ).astype(jnp.float32),
        lax.psum_scatter(
            router_grad.astype(jnp.bfloat16), ("dp", "ctx"), scatter_dimension=0, tiled=True
        ).astype(jnp.float32),
        lax.psum_scatter(
            sgate_grad.astype(jnp.bfloat16), ("dp", "ctx"), scatter_dimension=0, tiled=True
        ).astype(jnp.float32),
        lax.psum_scatter(
            sup_grad.astype(jnp.bfloat16), ("dp", "ctx"), scatter_dimension=0, tiled=True
        ).astype(jnp.float32),
        lax.psum_scatter(
            sdown_grad.astype(jnp.bfloat16), ("dp", "ctx"), scatter_dimension=1, tiled=True
        ).astype(jnp.float32),
    )
    (
        gain_attn_sum,
        query_sum,
        key_sum_out,
        value_sum_out,
        out_sum,
        gain_mix_sum,
        router_sum,
        sgate_sum,
        sup_sum,
        sdown_sum,
    ) = all_sums
    return (
        result.astype(jnp.bfloat16)[None],
        tokens_back[None],
        gain_attn_sum,
        query_sum,
        key_sum_out,
        value_sum_out,
        out_sum,
        gain_mix_sum,
        router_sum,
        sgate_sum,
        sup_sum,
        sdown_sum,
        gate_grad,
        up_grad,
        down_grad,
    )


MESH = pl.DeviceIdType.MESH
BF = jnp.bfloat16
F32 = jnp.float32


class Place:
    def __init__(self, wide):
        self.wide = wide
        self.x = lax.axis_index("dp")
        self.z = lax.axis_index("ctx")
        self.e = lax.axis_index("exp")
        self.y = lax.div(self.e, 2)
        self.c = lax.rem(self.e, 2)
        z = self.z
        high = lax.div(z, 2)
        self.zs = [z, z + 1 - 2 * lax.rem(z, 2), 2 - high, 3 - 3 * high]
        self.inner = 3 - z
        self.inside = lax.div(z * (3 - z), 2)
        self.middle = self.inside == 1
        self.dx = 1 - 2 * self.x
        self.dy = 2 - 4 * self.y
        self.dc = 1 - 2 * self.c

    def far(self, f, g):
        if not self.wide:
            return 0, f * self.dy
        a, b = (1 - self.c), self.c
        return (f * a + g * b) * self.dx, (f * b + g * a) * self.dy

    def far_twin(self, f, g):
        if not self.wide:
            return 0, f * self.dy
        a, b = self.c, (1 - self.c)
        return (f * a + g * b) * self.dx, (f * b + g * a) * self.dy

    def device(self, ox=0, oe=0, zi=0):
        return (self.x + ox, self.zs[zi], self.e + oe)

    def inward(self):
        return (self.x, self.inner, self.e)

    def shard(self, ox, oe, zi):
        rank = self.zs[zi] * 4 + self.e + oe
        if self.wide:
            rank = rank + (self.x + ox) * 16
        return rank


def greet(at):
    barrier = pltpu.get_barrier_semaphore()
    peers = [at.device(zi=1), at.device(*at.far(1, 0)), at.device(oe=at.dc)]
    if at.wide:
        peers.append(at.device(*at.far(0, 1)))
    for peer in peers:
        pl.semaphore_signal(barrier, inc=1, device_id=peer, device_id_type=MESH)

    @pl.when(at.middle)
    def _():
        pl.semaphore_signal(barrier, inc=1, device_id=at.inward(), device_id_type=MESH)

    pl.semaphore_wait(barrier, len(peers) + at.inside)


def gather_kernel(wide, rows, parts, x_ref, out_ref, own_sem, send_sem, recv_sem):
    at = Place(wide)
    greet(at)
    piece = rows // parts
    kinds = 4 if wide else 2
    slot_z, slot_f, slot_g, slot_s = 0, 3, 7, 15
    started, inside = [], []

    def where(f, g, zi, p):
        ox, oe = at.far(f, g)
        return pl.ds(pl.multiple_of(at.shard(ox, oe, zi) * rows + p * piece, piece), piece)

    def push(src, dst, slot, p, device, sends=None, record=None):
        k = slot * parts + p
        j = k if sends is None else sends * parts + p
        copy = pltpu.make_async_remote_copy(
            src_ref=src,
            dst_ref=out_ref.at[dst],
            send_sem=send_sem.at[j],
            recv_sem=recv_sem.at[k],
            device_id=device,
            device_id_type=MESH,
        )
        copy.start()
        (started if record is None else record).append(j)

    def gone(j):
        pltpu.make_async_remote_copy(
            src_ref=x_ref.at[pl.ds(0, piece)],
            dst_ref=out_ref.at[pl.ds(0, piece)],
            send_sem=send_sem.at[j],
            recv_sem=recv_sem.at[0],
            device_id=s_dev,
            device_id_type=MESH,
        ).wait_send()

    def arrive(slot, p):
        k = slot * parts + p
        pltpu.make_async_remote_copy(
            src_ref=x_ref.at[pl.ds(0, piece)],
            dst_ref=out_ref.at[pl.ds(0, piece)],
            send_sem=send_sem.at[k],
            recv_sem=recv_sem.at[k],
            device_id=at.device(oe=at.dc),
            device_id_type=MESH,
        ).wait_recv()

    f_dev, s_dev, z_dev = at.device(*at.far(1, 0)), at.device(oe=at.dc), at.device(zi=1)
    g_dev = at.device(*at.far(0, 1)) if wide else None
    own = pltpu.make_async_copy(
        x_ref, out_ref.at[pl.ds(pl.multiple_of(at.shard(0, 0, 0) * rows, rows), rows)], own_sem
    )
    own.start()

    def source(f, g, zi, p):
        if (f, g, zi) == (0, 0, 0):
            return x_ref.at[pl.ds(p * piece, piece)]
        return out_ref.at[where(f, g, zi, p)]

    def along(zi, p):
        src, dst = source(0, 0, zi, p), where(0, 0, zi, p)
        if zi == 0:
            push(src, dst, slot_z, p, z_dev)
        if zi < 2:
            pl.when(at.middle)(
                lambda: push(src, dst, slot_z + 1 + zi, p, at.inward(), 31 + zi, inside)
            )
        else:
            pl.when(at.middle)(lambda: push(src, dst, slot_z + zi - 1, p, z_dev, 31 + zi, inside))

    def forward(f, g, zi, p):
        src, dst = source(f, g, zi, p), where(f, g, zi, p)
        if f == 0 and g == 0:
            along(zi, p)
            push(src, dst, slot_f + zi, p, f_dev)
        if wide and g == 0:
            push(src, dst, slot_g + f * 4 + zi, p, g_dev)
        push(src, dst, slot_s + (g * 2 + f) * 4 + zi, p, s_dev)

    for zi in range(4):
        for p in range(parts):
            if zi > 0:
                arrive(slot_z + zi - 1, p)
            forward(0, 0, zi, p)
        for p in range(parts):
            arrive(slot_f + zi, p)
            forward(1, 0, zi, p)
    if wide:
        for f in range(2):
            for zi in range(4):
                for p in range(parts):
                    arrive(slot_g + f * 4 + zi, p)
                    forward(f, 1, zi, p)
    for k in range(4 * kinds):
        for p in range(parts):
            arrive(slot_s + k, p)
    own.wait()
    for j in started:
        gone(j)

    @pl.when(at.middle)
    def _():
        for j in inside:
            gone(j)


def all_rows(x, wide, cid, parts=1):
    rows, width = x.shape
    n = 32 if wide else 16
    return pl.pallas_call(
        functools.partial(gather_kernel, wide, rows, parts),
        out_shape=jax.ShapeDtypeStruct((n * rows, width), x.dtype),
        in_specs=[pl.BlockSpec(memory_space=pl.ANY)],
        out_specs=pl.BlockSpec(memory_space=pl.ANY),
        scratch_shapes=[
            pltpu.SemaphoreType.DMA,
            pltpu.SemaphoreType.DMA((35 * parts,)),
            pltpu.SemaphoreType.DMA((31 * parts,)),
        ],
        compiler_params=pltpu.CompilerParams(collective_id=cid, has_side_effects=True),
    )(x)


def scatter_kernel(wide, rows, in_ref, out_ref, acc, got_s, got_g, got_f, got_z, load_sem, send_sem, recv_sem):
    at = Place(wide)
    greet(at)
    slot_z, slot_f, slot_g, slot_s = 0, 5, 9, 17
    f_dev, s_dev, z_dev = at.device(*at.far(1, 0)), at.device(oe=at.dc), at.device(zi=1)
    g_dev = at.device(*at.far(0, 1)) if wide else None
    started, in_middle, at_end = [], [], []

    def rows_of(rank):
        return in_ref.at[pl.ds(pl.multiple_of(rank * rows, rows), rows)]

    def push(src, dst, slot, device, sends=None, record=started):
        copy = pltpu.make_async_remote_copy(
            src_ref=src,
            dst_ref=dst,
            send_sem=send_sem.at[slot if sends is None else sends],
            recv_sem=recv_sem.at[slot],
            device_id=device,
            device_id_type=MESH,
        )
        copy.start()
        record.append(slot if sends is None else sends)

    def gone(j):
        pltpu.make_async_remote_copy(
            src_ref=acc.at[0],
            dst_ref=acc.at[0],
            send_sem=send_sem.at[j],
            recv_sem=recv_sem.at[0],
            device_id=s_dev,
            device_id_type=MESH,
        ).wait_send()

    def arrive(dst, slot):
        pltpu.make_async_remote_copy(
            src_ref=acc.at[0],
            dst_ref=dst,
            send_sem=send_sem.at[slot],
            recv_sem=recv_sem.at[slot],
            device_id=s_dev,
            device_id_type=MESH,
        ).wait_recv()

    gs = (1, 0) if wide else (0,)
    order = [(f, g, zi) for g in gs for f in (1, 0) for zi in (3, 2, 1, 0)]
    loads = {}
    for f, g, zi in order:
        k = (g * 2 + f) * 4 + zi
        ox, oe = at.far_twin(f, g)
        push(rows_of(at.shard(ox, oe + at.dc, zi)), got_s.at[k], slot_s + k, s_dev)
        ox, oe = at.far(f, g)
        loads[k] = pltpu.make_async_copy(rows_of(at.shard(ox, oe, zi)), acc.at[k], load_sem.at[k])
        loads[k].start()

    def add(k, *others, into=None):
        @pl.loop(0, rows // 16)
        def _(i):
            span = pl.ds(pl.multiple_of(i * 16, 16), 16)
            total = acc[k, span, :].astype(F32)
            for ref, j in others:
                total = total + ref[j, span, :].astype(F32)
            if into is None:
                acc[k, span, :] = total.astype(BF)
            else:
                into[span, :] = total

    for f, g, zi in order:
        k = (g * 2 + f) * 4 + zi
        arrive(got_s.at[k], slot_s + k)
        loads[k].wait()
        others = [(got_s, k)]
        if g == 1:
            add(k, *others)
            push(acc.at[k], got_g.at[f * 4 + zi], slot_g + f * 4 + zi, g_dev)
            continue
        if wide:
            arrive(got_g.at[f * 4 + zi], slot_g + f * 4 + zi)
            others.append((got_g, f * 4 + zi))
        if f == 1:
            add(k, *others)
            push(acc.at[k], got_f.at[zi], slot_f + zi, f_dev)
            continue
        arrive(got_f.at[zi], slot_f + zi)
        others.append((got_f, zi))
        if zi >= 2:

            @pl.when(at.middle)
            def _():
                arrive(got_z.at[3 - zi], slot_z + 3 - zi)
                add(k, *others, (got_z, 3 - zi))
                push(acc.at[k], got_z.at[4 if zi == 2 else 3], slot_z + (4 if zi == 2 else 3), at.inward(), slot_z + zi, in_middle)

            @pl.when(jnp.logical_not(at.middle))
            def _():
                add(k, *others)
                push(acc.at[k], got_z.at[3 - zi], slot_z + 3 - zi, z_dev, slot_z + zi, at_end)
        elif zi == 1:

            @pl.when(at.middle)
            def _():
                arrive(got_z.at[3], slot_z + 3)
                add(k, *others, (got_z, 3))
                push(acc.at[k], got_z.at[4], slot_z + 4, z_dev, slot_z + 1, in_middle)

            @pl.when(jnp.logical_not(at.middle))
            def _():
                add(k, *others)
                push(acc.at[k], got_z.at[2], slot_z + 2, z_dev, slot_z + 1, at_end)
        else:

            @pl.when(at.middle)
            def _():
                arrive(got_z.at[2], slot_z + 2)
                arrive(got_z.at[4], slot_z + 4)
                add(k, *others, (got_z, 2), (got_z, 4), into=out_ref)

            @pl.when(jnp.logical_not(at.middle))
            def _():
                arrive(got_z.at[4], slot_z + 4)
                add(k, *others, (got_z, 4), into=out_ref)

    for j in started:
        gone(j)

    @pl.when(at.middle)
    def _():
        for j in in_middle:
            gone(j)

    @pl.when(jnp.logical_not(at.middle))
    def _():
        for j in at_end:
            gone(j)


def own_rows(x, wide, cid):
    n = 32 if wide else 16
    rows, width = x.shape[0] // n, x.shape[1]
    half = n // 2
    return pl.pallas_call(
        functools.partial(scatter_kernel, wide, rows),
        out_shape=jax.ShapeDtypeStruct((rows, width), F32),
        in_specs=[pl.BlockSpec(memory_space=pl.ANY)],
        out_specs=pl.BlockSpec(memory_space=pltpu.VMEM),
        scratch_shapes=[
            pltpu.VMEM((half, rows, width), BF),
            pltpu.VMEM((half, rows, width), BF),
            pltpu.VMEM((8, rows, width) if wide else (1, 16, 128), BF),
            pltpu.VMEM((4, rows, width), BF),
            pltpu.VMEM((5, rows, width), BF),
            pltpu.SemaphoreType.DMA((half,)),
            pltpu.SemaphoreType.DMA((33,)),
            pltpu.SemaphoreType.DMA((33,)),
        ],
        compiler_params=pltpu.CompilerParams(
            collective_id=cid, has_side_effects=True, vmem_limit_bytes=56 * 1024 * 1024
        ),
    )(x)


ALL = ("dp", "ctx", "exp")
DENSE = ("dp", "ctx")


def swap(blocks):
    return lax.all_to_all(blocks, DENSE, split_axis=0, concat_axis=0, tiled=True)


def for_heads(matrix):
    rows = matrix.shape[0]
    cut = matrix.reshape(rows, 4, HDIM).transpose(1, 0, 2)
    return jnp.concatenate([cut, cut], axis=0)


def attend_kernel(scale, block, q_ref, k_ref, v_ref, out_ref, lse_ref):
    length = q_ref.shape[0]
    for i in range(length // block):
        seen = (i + 1) * block
        rows = pl.ds(i * block, block)
        scores = transposed_right(q_ref[rows, :], k_ref[0:seen, :]) * scale
        row_at = lax.broadcasted_iota(jnp.int32, scores.shape, 0) + i * block
        col_at = lax.broadcasted_iota(jnp.int32, scores.shape, 1)
        scores = jnp.where(row_at >= col_at, scores, MASKED)
        top = jnp.max(scores, axis=-1, keepdims=True)
        lse = top + jnp.log(jnp.sum(jnp.exp(scores - top), axis=-1, keepdims=True))
        probs = jnp.exp(scores - lse).astype(BF)
        out_ref[rows, :] = product(probs, v_ref[0:seen, :]).astype(BF)
        lse_ref[rows, :] = jnp.broadcast_to(lse, (block, HDIM))


def attend(q, k, v):
    length = q.shape[0]
    return pl.pallas_call(
        functools.partial(attend_kernel, HDIM ** (-0.5), 256),
        out_shape=(
            jax.ShapeDtypeStruct((length, HDIM), BF),
            jax.ShapeDtypeStruct((length, HDIM), F32),
        ),
        in_specs=[pl.BlockSpec(memory_space=pltpu.VMEM)] * 3,
        out_specs=(pl.BlockSpec(memory_space=pltpu.VMEM),) * 2,
        compiler_params=pltpu.CompilerParams(vmem_limit_bytes=56 * 1024 * 1024),
    )(q, k, v)


def attend_back_kernel(scale, block, q_ref, k_ref, v_ref, do_ref, lse_ref, dq_ref, dk_ref, dv_ref):
    length = q_ref.shape[0]
    dk_ref[...] = jnp.zeros_like(dk_ref)
    dv_ref[...] = jnp.zeros_like(dv_ref)
    for i in range(length // block):
        seen = (i + 1) * block
        rows = pl.ds(i * block, block)
        q = q_ref[rows, :]
        do = do_ref[rows, :]
        scores = transposed_right(q, k_ref[0:seen, :]) * scale
        row_at = lax.broadcasted_iota(jnp.int32, scores.shape, 0) + i * block
        col_at = lax.broadcasted_iota(jnp.int32, scores.shape, 1)
        scores = jnp.where(row_at >= col_at, scores, MASKED)
        probs = jnp.exp(scores - lse_ref[rows, 0:1])
        weight_back = transposed_right(do, v_ref[0:seen, :])
        inner = jnp.sum(probs * weight_back, axis=-1, keepdims=True)
        score_back = (probs * (weight_back - inner)).astype(BF)
        dv_ref[0:seen, :] += transposed_left(probs.astype(BF), do)
        dk_ref[0:seen, :] += transposed_left(score_back, q) * scale
        dq_ref[rows, :] = product(score_back, k_ref[0:seen, :]) * scale


def attend_back(q, k, v, do, lse):
    length = q.shape[0]
    return pl.pallas_call(
        functools.partial(attend_back_kernel, HDIM ** (-0.5), 256),
        out_shape=(jax.ShapeDtypeStruct((length, HDIM), F32),) * 3,
        in_specs=[pl.BlockSpec(memory_space=pltpu.VMEM)] * 5,
        out_specs=(pl.BlockSpec(memory_space=pltpu.VMEM),) * 3,
        compiler_params=pltpu.CompilerParams(vmem_limit_bytes=56 * 1024 * 1024),
    )(q, k, v, do, lse)


def turn_tables(length):
    inverse = 10000.0 ** (-np.arange(HDIM // 2).astype(np.float64) * 2.0 / HDIM)
    angles = np.arange(length).astype(np.float64)[:, None] * inverse[None, :]
    return np.cos(angles).astype(np.float32), np.sin(angles).astype(np.float32)


def turn(rows, cosine, sine):
    a, b = rows[:, : HDIM // 2], rows[:, HDIM // 2 :]
    return jnp.concatenate([a * cosine - b * sine, b * cosine + a * sine], axis=1)


def turn_back(rows, cosine, sine):
    a, b = rows[:, : HDIM // 2], rows[:, HDIM // 2 :]
    return jnp.concatenate([a * cosine + b * sine, b * cosine - a * sine], axis=1)


def silu_parts(gate, up):
    s = jax.nn.sigmoid(gate)
    act = gate * s
    return act * up, s * (1.0 + gate * (1.0 - s)) * up, act


def fast_body(
    tokens,
    routes,
    norm_attn,
    w_query,
    w_key,
    w_value,
    w_out,
    norm_mix,
    w_router,
    shared_gate,
    shared_up,
    shared_down,
    expert_gate,
    expert_up,
    expert_down,
    out_grad,
):
    dp, ctx, exp = lax.axis_index("dp"), lax.axis_index("ctx"), lax.axis_index("exp")
    rows_here, width = tokens.shape[1], tokens.shape[2]
    quarter = rows_here // 4
    group = 8
    length = rows_here * 4
    total = length * 2
    experts = w_router.shape[1]
    capacity = quarter * TOPK * 4 // (3 * experts)
    groups = total // quarter
    dense = w_query.shape[0]
    hidden = expert_gate.shape[2]
    cut = shared_gate.shape[1] // group
    wide = 128
    start = exp * quarter
    tokens_own = lax.dynamic_slice_in_dim(tokens[0], start, quarter, 0)
    dy_own = lax.dynamic_slice_in_dim(out_grad[0], start, quarter, 0)

    named = jnp.any(
        routes[0][:, :, None] == (jnp.arange(4, dtype=jnp.int32) * 4 + exp)[None, None, :], axis=1
    )
    named = named.astype(BF).reshape(dense, 2, 4).transpose(2, 0, 1)
    named = jnp.concatenate([named, named], axis=0)
    little = jnp.concatenate([w_router, norm_attn[:, None], norm_mix[:, None]], axis=1)
    little = jnp.broadcast_to(little[None], (group,) + little.shape)
    little = jnp.concatenate([little, named], axis=2)
    little = jnp.pad(little, ((0, 0), (0, 0), (0, wide - little.shape[2])))
    early = swap(
        jnp.concatenate([for_heads(w_query), for_heads(w_key), for_heads(w_value), little], axis=2)
    ).reshape(width, 4 * HDIM)
    w_qkv = early[:, : 3 * HDIM]
    little = early[:, 3 * HDIM :]
    router_matrix = little[:, :experts]
    attention_gain = little[:, experts].astype(F32)
    mixer_gain = little[:, experts + 1].astype(F32)
    hits = little[:, experts + 2 : experts + 4].astype(F32)
    hits = hits.reshape(group, dense, 2).reshape(groups, quarter)

    def units(matrix):
        return jnp.pad(
            matrix.reshape(dense, group, cut).transpose(1, 0, 2), ((0, 0), (0, 0), (0, wide - cut))
        )

    out_cut = w_out.reshape(4, HDIM, dense)
    down_cut = jnp.pad(shared_down.reshape(group, cut, dense), ((0, 0), (0, wide - cut), (0, 0)))
    late = swap(
        jnp.concatenate(
            [
                units(shared_gate),
                units(shared_up),
                jnp.concatenate([jnp.concatenate([out_cut, out_cut], axis=0), down_cut], axis=1),
            ],
            axis=2,
        )
    )
    shared_in = late[:, :, : 2 * wide].reshape(width, 2 * wide)
    w_out_head = late[:, :HDIM, 2 * wide :].transpose(1, 0, 2).reshape(HDIM, width)
    shared_out = late[:, HDIM:, 2 * wide :].transpose(1, 0, 2).reshape(wide, width)

    cosine, sine = turn_tables(length)
    tokens_all = all_rows(tokens_own, False, 1)
    normed = rms_scale(tokens_all.astype(F32), attention_gain).astype(BF)
    qkv = product(normed, w_qkv)
    query = turn(qkv[:, :HDIM], cosine, sine).astype(BF)
    key = turn(qkv[:, HDIM : 2 * HDIM], cosine, sine).astype(BF)
    value = qkv[:, 2 * HDIM :].astype(BF)
    heads_out, lse = attend(query, key, value)
    attn = own_rows(product(heads_out, w_out_head).astype(BF), False, 2)
    middle = tokens_own.astype(F32) + attn
    normed_own = rms_scale(middle, mixer_gain).astype(BF)

    dy_all = all_rows(dy_own, True, 3)
    mix_all = all_rows(normed_own, True, 3)
    logits = product(mix_all, router_matrix)
    router = jax.nn.softmax(logits, axis=-1)
    mine = ctx * 4 + exp
    router_mine = jnp.sum(
        jnp.where(jnp.arange(experts, dtype=jnp.int32)[None, :] == mine, router, 0.0), axis=1
    ).reshape(groups, quarter)
    place = jnp.cumsum(hits, axis=1) - 1.0
    matches = jnp.where(
        (jnp.arange(capacity).astype(F32)[None, :, None] == place[:, None, :])
        & (hits[:, None, :] > 0.5),
        1.0,
        0.0,
    )
    dispatch = matches.astype(BF)
    slot_gate = jnp.sum(matches * router_mine[:, None, :], axis=2).reshape(-1, 1)

    def pick(rows):
        return jnp.einsum(
            "gst,gtd->gsd",
            dispatch,
            rows.reshape(groups, quarter, width),
            preferred_element_type=F32,
        ).astype(BF).reshape(groups * capacity, width)

    def spread(rows):
        return jnp.einsum(
            "gst,gsd->gtd",
            dispatch,
            rows.reshape(groups, capacity, width),
            preferred_element_type=F32,
        ).reshape(total, width)

    picked = pick(mix_all)
    picked_dy = pick(dy_all)
    gate_hidden = product(picked, expert_gate[0])
    up_hidden = product(picked, expert_up[0])
    act, by_gate, by_up = silu_parts(gate_hidden, up_hidden)
    dy_down = transposed_right(picked_dy, expert_down[0])
    act_back = slot_gate * dy_down
    g_back = (act_back * by_gate).astype(BF)
    u_back = (act_back * by_up).astype(BF)
    act_low = act.astype(BF)
    gate_back = jnp.sum(act_low.astype(F32) * dy_down, axis=1)
    input_back = transposed_right(g_back, expert_gate[0]) + transposed_right(u_back, expert_up[0])

    shared_hidden = product(mix_all, shared_in)
    shared_act, shared_by_gate, shared_by_up = silu_parts(
        shared_hidden[:, :wide], shared_hidden[:, wide:]
    )
    shared_act = shared_act.astype(BF)
    shared_back = transposed_right(dy_all, shared_out)
    shared_gu_back = jnp.concatenate(
        [(shared_back * shared_by_gate).astype(BF), (shared_back * shared_by_up).astype(BF)], axis=1
    )
    mix_part = (
        transposed_right(shared_gu_back, shared_in) + spread(input_back.astype(BF))
    ).astype(BF)
    mix_back = own_rows(mix_part, True, 4)

    gate_back_tokens = jnp.sum(
        dispatch.astype(F32) * gate_back.reshape(groups, capacity, 1), axis=1
    ).reshape(1, total)
    gate_back_all = lax.all_gather(gate_back_tokens, ALL, axis=0, tiled=True)
    gate_back_all = jnp.sum(gate_back_all.reshape(2, experts, total), axis=0).T
    logit_back = (
        router * (gate_back_all - jnp.sum(router * gate_back_all, axis=-1, keepdims=True))
    ).astype(BF)
    rank = (dp * 4 + ctx) * 4 + exp
    logit_back_own = lax.dynamic_slice_in_dim(logit_back, rank * quarter, quarter, 0)
    mix_columns = lax.dynamic_slice_in_dim(mix_all, (dp * 4 + ctx) * dense, dense, 1)
    router_grad = transposed_left(mix_columns, logit_back)

    half_out = product(act_low, expert_down[0])
    mixed_part = (
        product(shared_act, shared_out) + spread((half_out * slot_gate).astype(BF))
    ).astype(BF)
    mixed_own = (middle + own_rows(mixed_part, True, 4)).astype(BF)

    gate_grad = transposed_left(picked, g_back)[None]
    up_grad = transposed_left(picked, u_back)[None]
    down_grad = transposed_left((act * slot_gate).astype(BF), picked_dy)[None]
    shared_gu_grad = transposed_left(mix_all, shared_gu_back).astype(BF)
    shared_down_part = transposed_left(shared_act, dy_all).astype(BF)

    mix_back = mix_back + transposed_right(logit_back_own, router_matrix)
    _, norm_mix_back = jax.vjp(rms_scale, middle, mixer_gain)
    middle_norm_back, gain_mix_part = norm_mix_back(mix_back)
    middle_back = dy_own.astype(F32) + middle_norm_back
    attn_back = middle_back.astype(BF)
    attn_back_all = all_rows(attn_back, False, 1)
    heads_back = transposed_right(attn_back_all, w_out_head).astype(BF)
    out_part = transposed_left(heads_out, attn_back_all).astype(BF)
    dq, dk, dv = attend_back(query, key, value, heads_back, lse)
    qkv_back = jnp.concatenate(
        [
            turn_back(dq, cosine, sine).astype(BF),
            turn_back(dk, cosine, sine).astype(BF),
            dv.astype(BF),
        ],
        axis=1,
    )
    normed_back = own_rows(transposed_right(qkv_back, w_qkv).astype(BF), False, 2)
    qkv_part = transposed_left(normed, qkv_back).astype(BF)
    _, norm_attn_back = jax.vjp(rms_scale, tokens_own.astype(F32), attention_gain)
    input_norm_back, gain_attn_part = norm_attn_back(normed_back)
    tokens_back_own = (middle_back + input_norm_back).astype(BF)

    tokens_back = lax.all_gather(tokens_back_own, "exp", axis=0, tiled=True)
    mixed = lax.all_gather(mixed_own, "exp", axis=0, tiled=True)
    gains = jnp.stack([gain_attn_part, gain_mix_part], axis=0)
    gains = gains.reshape(2, group, 1, dense).transpose(1, 2, 0, 3)
    gains = jnp.broadcast_to(gains, (group, 4, 2, dense)).reshape(32, 2 * dense)
    gains = lax.all_to_all(gains, ALL, split_axis=0, concat_axis=0, tiled=True)
    gains = jnp.sum(gains, axis=0)
    dense_parts = swap(
        jnp.concatenate(
            [
                qkv_part.reshape(group, dense, 3 * HDIM),
                shared_gu_grad.reshape(group, dense, 2 * wide),
                jnp.concatenate(
                    [
                        out_part.reshape(HDIM, group, dense).transpose(1, 0, 2),
                        shared_down_part.reshape(wide, group, dense).transpose(1, 0, 2),
                    ],
                    axis=1,
                ),
            ],
            axis=2,
        )
    ).astype(F32)

    def head_columns(parts):
        summed = parts[:4] + parts[4:]
        return summed.transpose(1, 0, 2).reshape(dense, 4 * HDIM)

    def unit_columns(parts):
        return parts[:, :, :cut].transpose(1, 0, 2).reshape(dense, group * cut)

    query_grad = head_columns(dense_parts[:, :, :HDIM])
    key_grad = head_columns(dense_parts[:, :, HDIM : 2 * HDIM])
    value_grad = head_columns(dense_parts[:, :, 2 * HDIM : 3 * HDIM])
    base = 3 * HDIM
    sgate_grad = unit_columns(dense_parts[:, :, base : base + wide])
    sup_grad = unit_columns(dense_parts[:, :, base + wide : base + 2 * wide])
    base = base + 2 * wide
    out_blocks = dense_parts[:, :HDIM, base:]
    out_grad_weights = (out_blocks[:4] + out_blocks[4:]).reshape(4 * HDIM, dense)
    sdown_grad = dense_parts[:, HDIM : HDIM + cut, base:].reshape(group * cut, dense)
    return (
        mixed[None],
        tokens_back[None],
        gains[:dense],
        query_grad,
        key_grad,
        value_grad,
        out_grad_weights,
        gains[dense:],
        router_grad,
        sgate_grad,
        sup_grad,
        sdown_grad,
        gate_grad,
        up_grad,
        down_grad,
    )


def solution(mesh):
    sizes = dict(mesh.shape)

    def chosen(*args):
        heads = args[3].shape[1] * sizes["exp"] // HDIM
        one_head_each = heads == sizes["ctx"] * sizes["exp"]
        built_for = (sizes["dp"], sizes["ctx"], sizes["exp"]) == (2, 4, 4)
        return fast_body(*args) if one_head_each and built_for else body(*args)

    in_specs = (
        P("dp", "ctx", None),
        P("dp", "ctx", None),
        P(("dp", "ctx")),
        P(("dp", "ctx"), "exp"),
        P(("dp", "ctx"), "exp"),
        P(("dp", "ctx"), "exp"),
        P("exp", ("dp", "ctx")),
        P(("dp", "ctx")),
        P(("dp", "ctx"), None),
        P(("dp", "ctx"), "exp"),
        P(("dp", "ctx"), "exp"),
        P("exp", ("dp", "ctx")),
        P(("ctx", "exp"), None, "dp"),
        P(("ctx", "exp"), None, "dp"),
        P(("ctx", "exp"), "dp", None),
        P("dp", "ctx", None),
    )
    out_specs = (
        P("dp", "ctx", None),
        P("dp", "ctx", None),
        P(("dp", "ctx")),
        P(("dp", "ctx"), "exp"),
        P(("dp", "ctx"), "exp"),
        P(("dp", "ctx"), "exp"),
        P("exp", ("dp", "ctx")),
        P(("dp", "ctx")),
        P(("dp", "ctx"), None),
        P(("dp", "ctx"), "exp"),
        P(("dp", "ctx"), "exp"),
        P("exp", ("dp", "ctx")),
        P(("ctx", "exp"), None, "dp"),
        P(("ctx", "exp"), None, "dp"),
        P(("ctx", "exp"), "dp", None),
    )
    return jax.shard_map(chosen, mesh=mesh, in_specs=in_specs, out_specs=out_specs, check_vma=False)
```

```python
import functools

import jax
import jax.numpy as jnp
import numpy as np
from jax import lax
from jax.experimental import pallas as pl
from jax.experimental.pallas import tpu as pltpu
from jax.sharding import PartitionSpec as P

HDIM = 128
TOPK = 6


EPSILON = 1e-06
MASKED = -1e30
HIGHEST = lax.Precision.HIGHEST


def rms_scale(values, gain_row):
    return (
        values * lax.rsqrt(jnp.mean(values * values, axis=-1, keepdims=True) + EPSILON) * gain_row
    )


def rope_tables(positions, rope_width):
    inverse = 10000.0 ** (-jnp.arange(rope_width // 2).astype(jnp.float32) * 2.0 / rope_width)
    angles = positions.astype(jnp.float32)[:, None] * inverse[None, :]
    return (jnp.cos(angles), jnp.sin(angles))


def rotate(values, cosine, sine_table):
    half_size = values.shape[-1] // 2
    first_half = values[..., :half_size]
    second = values[..., half_size:]
    cosine = cosine[:, None, :]
    sine_table = sine_table[:, None, :]
    return jnp.concatenate(
        [first_half * cosine - second * sine_table, second * cosine + first_half * sine_table],
        axis=-1,
    )


def silu_mix(gate_rows, up_rows):
    return jax.nn.silu(gate_rows) * up_rows


def product(left_side, right_side):
    return jnp.dot(left_side, right_side, preferred_element_type=jnp.float32)


def transposed_left(left_side, right_side):
    return lax.dot_general(
        left_side, right_side, (((0,), (0,)), ((), ())), preferred_element_type=jnp.float32
    )


def transposed_right(left_side, right_side):
    return lax.dot_general(
        left_side, right_side, (((1,), (1,)), ((), ())), preferred_element_type=jnp.float32
    )


def place_rows(part, start_row, total_rows):
    blank = jnp.zeros((total_rows, part.shape[1]), jnp.float32)
    return lax.dynamic_update_slice_in_dim(blank, part, start_row, 0)


def to_owners(buffer):
    copies = lax.axis_size("dp")
    widened = jnp.broadcast_to(buffer[None], (copies,) + buffer.shape)
    widened = widened.reshape((copies * buffer.shape[0],) + buffer.shape[1:])
    return lax.all_to_all(widened, ("dp", "ctx", "exp"), split_axis=0, concat_axis=0, tiled=True)


def values_home(partial_value):
    returned = lax.all_to_all(
        partial_value, ("dp", "ctx", "exp"), split_axis=0, concat_axis=0, tiled=True
    )
    grouped = returned.reshape((lax.axis_size("dp"), -1) + returned.shape[1:])
    return jnp.sum(grouped.astype(jnp.float32), axis=0).astype(jnp.bfloat16)


def grads_home(partial_value):
    returned = lax.all_to_all(
        partial_value.astype(jnp.bfloat16),
        ("dp", "ctx", "exp"),
        split_axis=0,
        concat_axis=0,
        tiled=True,
    ).astype(partial_value.dtype)
    grouped = returned.reshape((lax.axis_size("dp"), -1) + returned.shape[1:])
    return jnp.sum(grouped, axis=0)


def body(
    tokens,
    routes,
    norm_attn,
    w_query,
    w_key,
    w_value,
    w_out,
    norm_mix,
    w_router,
    shared_gate,
    shared_up,
    shared_down,
    expert_gate,
    expert_up,
    expert_down,
    out_grad,
):
    gathered = (
        lax.all_gather(norm_attn, ("dp", "ctx"), axis=0, tiled=True),
        lax.all_gather(w_query, ("dp", "ctx"), axis=0, tiled=True),
        lax.all_gather(w_key, ("dp", "ctx"), axis=0, tiled=True),
        lax.all_gather(w_value, ("dp", "ctx"), axis=0, tiled=True),
        lax.all_gather(w_out, ("dp", "ctx"), axis=1, tiled=True),
        lax.all_gather(norm_mix, ("dp", "ctx"), axis=0, tiled=True),
        lax.all_gather(w_router, ("dp", "ctx"), axis=0, tiled=True),
        lax.all_gather(shared_gate, ("dp", "ctx"), axis=0, tiled=True),
        lax.all_gather(shared_up, ("dp", "ctx"), axis=0, tiled=True),
        lax.all_gather(shared_down, ("dp", "ctx"), axis=1, tiled=True),
    )
    (
        attention_gain,
        query_matrix,
        key_matrix,
        value_matrix,
        output_matrix,
        mixer_gain,
        router_matrix,
        shared_gate_matrix,
        shared_up_matrix,
        shared_down_matrix,
    ) = gathered
    rows_here = tokens.shape[1]
    model_width = tokens.shape[2]
    heads_here = query_matrix.shape[1] // HDIM
    quarter = rows_here // lax.axis_size("exp")
    start_row = lax.axis_index("exp") * quarter
    layer_input = tokens[0].astype(jnp.float32)
    grad_rows = out_grad[0]
    grad_float = grad_rows.astype(jnp.float32)
    seq_length = rows_here * lax.axis_size("ctx")
    positions = lax.axis_index("ctx") * rows_here + jnp.arange(rows_here, dtype=jnp.int32)
    cosine, sine_table = rope_tables(positions, HDIM)
    visible = positions[:, None] >= jnp.arange(seq_length, dtype=jnp.int32)[None, :]
    scale = HDIM ** (-0.5)
    head_shape = (rows_here, heads_here, HDIM)
    normed = rms_scale(layer_input, attention_gain).astype(jnp.bfloat16)
    query_rot = rotate(
        product(normed, query_matrix).reshape(head_shape), cosine, sine_table
    ).astype(jnp.bfloat16)
    key_rot = (
        rotate(product(normed, key_matrix).reshape(head_shape), cosine, sine_table)
        .astype(jnp.bfloat16)
        .reshape(rows_here, -1)
    )
    value_low = product(normed, value_matrix).astype(jnp.bfloat16)
    key_all, value_all = (
        lax.all_gather(key_rot, "ctx", axis=0, tiled=True),
        lax.all_gather(value_low, "ctx", axis=0, tiled=True),
    )
    key_heads = key_all.reshape(seq_length, heads_here, HDIM)
    value_heads = value_all.reshape(seq_length, heads_here, HDIM)

    def attention_scores():
        scores = (
            jnp.einsum("qhd,khd->hqk", query_rot, key_heads, preferred_element_type=jnp.float32)
            * scale
        )
        return jnp.where(visible[None], scores, MASKED)

    scores = attention_scores()
    largest = jnp.max(scores, axis=-1, keepdims=True)
    log_total = largest + jnp.log(jnp.sum(jnp.exp(scores - largest), axis=-1, keepdims=True))
    weights_low = jnp.exp(scores - log_total).astype(jnp.bfloat16)
    heads_out = (
        jnp.einsum("hqk,khd->qhd", weights_low, value_heads, preferred_element_type=jnp.float32)
        .reshape(rows_here, -1)
        .astype(jnp.bfloat16)
    )
    attn_total = lax.psum(product(heads_out, output_matrix), "exp")
    middle = layer_input + attn_total
    normed_mix = rms_scale(middle, mixer_gain).astype(jnp.bfloat16)
    normed_quarter = lax.dynamic_slice_in_dim(normed_mix, start_row, quarter, 0)
    route_quarter = lax.dynamic_slice_in_dim(routes[0], start_row, quarter, 0)
    grad_quarter = lax.dynamic_slice_in_dim(grad_rows, start_row, quarter, 0)
    logits = product(normed_quarter, router_matrix)
    probabilities = jax.nn.softmax(logits, axis=-1)
    owners = lax.axis_size(("ctx", "exp"))
    local_experts = expert_gate.shape[0]
    experts = local_experts * owners
    capacity = max(quarter * TOPK * 4 // (3 * experts), 2)
    expert_choice_index = jnp.arange(experts, dtype=jnp.int32)
    chosen = (route_quarter[:, :, None] == expert_choice_index[None, None, :]).astype(jnp.float32)
    gates = jnp.sum(chosen * probabilities[:, None, :], axis=-1)
    route_flat = route_quarter.reshape(-1)
    expert_hits = (route_flat[:, None] == expert_choice_index[None, :]).astype(jnp.int32)
    slot_index = jnp.sum(jnp.cumsum(expert_hits, axis=0) * expert_hits, axis=1) - 1
    slot_place = route_flat * capacity + slot_index
    matches = (
        jnp.arange(experts * capacity, dtype=jnp.int32)[:, None] == slot_place[None, :]
    ).astype(jnp.float32)
    dispatch = jnp.sum(matches.reshape(experts * capacity, quarter, TOPK), axis=2).astype(
        jnp.bfloat16
    )
    slot_gates = jnp.dot(matches, gates.reshape(-1), precision=HIGHEST)
    buffer_shape = (owners, local_experts, capacity, model_width)
    outgoing = product(dispatch, normed_quarter).astype(jnp.bfloat16).reshape(buffer_shape)
    arrived = to_owners(outgoing)
    gate_hidden = jnp.einsum(
        "sicd,idf->sicf", arrived, expert_gate, preferred_element_type=jnp.float32
    )
    up_hidden = jnp.einsum("sicd,idf->sicf", arrived, expert_up, preferred_element_type=jnp.float32)
    expert_act = silu_mix(gate_hidden, up_hidden).astype(jnp.bfloat16)
    partial_value = jnp.einsum(
        "sicf,ifd->sicd", expert_act, expert_down, preferred_element_type=jnp.float32
    ).astype(jnp.bfloat16)
    expert_values = values_home(partial_value).reshape(experts * capacity, model_width)
    route_values = expert_values[slot_place].astype(jnp.float32).reshape(quarter, TOPK, model_width)
    combined = jnp.sum(route_values * gates[:, :, None], axis=1)
    shared_gate_rows = product(normed_mix, shared_gate_matrix)
    shared_up_rows = product(normed_mix, shared_up_matrix)
    shared_act = silu_mix(shared_gate_rows, shared_up_rows).astype(jnp.bfloat16)
    branch_part = product(shared_act, shared_down_matrix) + place_rows(
        combined, start_row, rows_here
    )
    result = middle + lax.psum(branch_part.astype(jnp.bfloat16), "exp").astype(jnp.float32)
    grad_slots = (
        (product(dispatch, grad_quarter) * slot_gates[:, None])
        .astype(jnp.bfloat16)
        .reshape(buffer_shape)
    )
    grad_arrived = to_owners(grad_slots)
    act_grad = jnp.einsum(
        "sicd,ifd->sicf", grad_arrived, expert_down, preferred_element_type=jnp.float32
    )
    down_grad = jnp.einsum(
        "sicf,sicd->ifd", expert_act, grad_arrived, preferred_element_type=jnp.float32
    )
    _, mix_back = jax.vjp(silu_mix, gate_hidden, up_hidden)
    gate_back, up_back = mix_back(act_grad)
    gate_back = gate_back.astype(jnp.bfloat16)
    up_back = up_back.astype(jnp.bfloat16)
    gate_grad = jnp.einsum("sicd,sicf->idf", arrived, gate_back, preferred_element_type=jnp.float32)
    up_grad = jnp.einsum("sicd,sicf->idf", arrived, up_back, preferred_element_type=jnp.float32)
    input_back = jnp.einsum(
        "sicf,idf->sicd", gate_back, expert_gate, preferred_element_type=jnp.float32
    ) + jnp.einsum("sicf,idf->sicd", up_back, expert_up, preferred_element_type=jnp.float32)
    rows_back = grads_home(input_back).reshape(experts * capacity, model_width)
    moe_back = jnp.sum(rows_back[slot_place].reshape(quarter, TOPK, model_width), axis=1)
    gate_route_back = jnp.sum(route_values * grad_quarter.astype(jnp.float32)[:, None, :], axis=-1)
    prob_back = jnp.sum(chosen * gate_route_back[:, :, None], axis=1)
    _, soft_back = jax.vjp(lambda values: jax.nn.softmax(values, axis=-1), logits)
    logit_back = soft_back(prob_back)[0].astype(jnp.bfloat16)
    router_term = transposed_left(normed_quarter, logit_back)
    shared_back = transposed_right(grad_rows, shared_down_matrix)
    _, shared_mix_back = jax.vjp(silu_mix, shared_gate_rows, shared_up_rows)
    sgate_back, sup_back = shared_mix_back(shared_back)
    sgate_back = sgate_back.astype(jnp.bfloat16)
    sup_back = sup_back.astype(jnp.bfloat16)
    quarter_back = transposed_right(logit_back, router_matrix) + moe_back
    mix_part = (
        transposed_right(sgate_back, shared_gate_matrix)
        + transposed_right(sup_back, shared_up_matrix)
        + place_rows(quarter_back, start_row, rows_here)
    )
    mix_total, router_grad = (
        lax.psum(mix_part.astype(jnp.bfloat16), "exp").astype(jnp.float32),
        lax.psum(router_term.astype(jnp.bfloat16), "exp").astype(jnp.float32),
    )
    _, norm_mix_back = jax.vjp(rms_scale, middle, mixer_gain.astype(jnp.float32))
    middle_norm_back, gain_mix_grad = norm_mix_back(mix_total)
    middle_grad = grad_float + middle_norm_back
    sdown_grad = transposed_left(shared_act, grad_rows)
    sgate_grad = transposed_left(normed_mix, sgate_back)
    sup_grad = transposed_left(normed_mix, sup_back)
    attn_back = middle_grad.astype(jnp.bfloat16)
    heads_back = transposed_right(attn_back, output_matrix).astype(jnp.bfloat16).reshape(head_shape)
    weights_full = jnp.exp(attention_scores() - log_total)
    weights_again = weights_full.astype(jnp.bfloat16)
    weight_back = jnp.einsum(
        "qhd,khd->hqk", heads_back, value_heads, preferred_element_type=jnp.float32
    )
    value_term = jnp.einsum(
        "hqk,qhd->khd", weights_again, heads_back, preferred_element_type=jnp.float32
    ).reshape(seq_length, -1)
    score_back = (
        weights_full * (weight_back - jnp.sum(weights_full * weight_back, axis=-1, keepdims=True))
    ).astype(jnp.bfloat16)
    query_rot_back = (
        jnp.einsum("hqk,khd->qhd", score_back, key_heads, preferred_element_type=jnp.float32)
        * scale
    )
    key_term = (
        jnp.einsum("hqk,qhd->khd", score_back, query_rot, preferred_element_type=jnp.float32)
        * scale
    ).reshape(seq_length, -1)
    key_sum, value_sum = (
        lax.psum_scatter(
            key_term.astype(jnp.bfloat16), "ctx", scatter_dimension=0, tiled=True
        ).astype(jnp.float32),
        lax.psum_scatter(
            value_term.astype(jnp.bfloat16), "ctx", scatter_dimension=0, tiled=True
        ).astype(jnp.float32),
    )
    _, rotate_back = jax.vjp(
        lambda values: rotate(values, cosine, sine_table), jnp.zeros(head_shape, jnp.float32)
    )
    query_low = rotate_back(query_rot_back)[0].reshape(rows_here, -1).astype(jnp.bfloat16)
    key_low = (
        rotate_back(key_sum.reshape(head_shape))[0].reshape(rows_here, -1).astype(jnp.bfloat16)
    )
    value_back_low = value_sum.astype(jnp.bfloat16)
    normed_part = (
        transposed_right(query_low, query_matrix)
        + transposed_right(key_low, key_matrix)
        + transposed_right(value_back_low, value_matrix)
    )
    normed_back = lax.psum(normed_part.astype(jnp.bfloat16), "exp").astype(jnp.float32)
    _, norm_attn_back = jax.vjp(rms_scale, layer_input, attention_gain.astype(jnp.float32))
    input_norm_back, gain_attn_grad = norm_attn_back(normed_back)
    tokens_back = (middle_grad + input_norm_back).astype(jnp.bfloat16)
    out_weight_grad = transposed_left(heads_out, attn_back)
    query_grad = transposed_left(normed, query_low)
    key_grad = transposed_left(normed, key_low)
    value_grad = transposed_left(normed, value_back_low)
    all_sums = (
        lax.psum_scatter(
            gain_attn_grad.astype(jnp.bfloat16), ("dp", "ctx"), scatter_dimension=0, tiled=True
        ).astype(jnp.float32),
        lax.psum_scatter(
            query_grad.astype(jnp.bfloat16), ("dp", "ctx"), scatter_dimension=0, tiled=True
        ).astype(jnp.float32),
        lax.psum_scatter(
            key_grad.astype(jnp.bfloat16), ("dp", "ctx"), scatter_dimension=0, tiled=True
        ).astype(jnp.float32),
        lax.psum_scatter(
            value_grad.astype(jnp.bfloat16), ("dp", "ctx"), scatter_dimension=0, tiled=True
        ).astype(jnp.float32),
        lax.psum_scatter(
            out_weight_grad.astype(jnp.bfloat16), ("dp", "ctx"), scatter_dimension=1, tiled=True
        ).astype(jnp.float32),
        lax.psum_scatter(
            gain_mix_grad.astype(jnp.bfloat16), ("dp", "ctx"), scatter_dimension=0, tiled=True
        ).astype(jnp.float32),
        lax.psum_scatter(
            router_grad.astype(jnp.bfloat16), ("dp", "ctx"), scatter_dimension=0, tiled=True
        ).astype(jnp.float32),
        lax.psum_scatter(
            sgate_grad.astype(jnp.bfloat16), ("dp", "ctx"), scatter_dimension=0, tiled=True
        ).astype(jnp.float32),
        lax.psum_scatter(
            sup_grad.astype(jnp.bfloat16), ("dp", "ctx"), scatter_dimension=0, tiled=True
        ).astype(jnp.float32),
        lax.psum_scatter(
            sdown_grad.astype(jnp.bfloat16), ("dp", "ctx"), scatter_dimension=1, tiled=True
        ).astype(jnp.float32),
    )
    (
        gain_attn_sum,
        query_sum,
        key_sum_out,
        value_sum_out,
        out_sum,
        gain_mix_sum,
        router_sum,
        sgate_sum,
        sup_sum,
        sdown_sum,
    ) = all_sums
    return (
        result.astype(jnp.bfloat16)[None],
        tokens_back[None],
        gain_attn_sum,
        query_sum,
        key_sum_out,
        value_sum_out,
        out_sum,
        gain_mix_sum,
        router_sum,
        sgate_sum,
        sup_sum,
        sdown_sum,
        gate_grad,
        up_grad,
        down_grad,
    )


MESH = pl.DeviceIdType.MESH
BF = jnp.bfloat16
F32 = jnp.float32


class Place:
    def __init__(self):
        self.x = lax.axis_index("dp")
        self.z = lax.axis_index("ctx")
        self.e = lax.axis_index("exp")
        z = self.z
        high = lax.div(z, 2)
        self.zs = [z, z + 1 - 2 * lax.rem(z, 2), 2 - high, 3 - 3 * high]
        self.inner = 3 - z
        self.inside = lax.div(z * (3 - z), 2)
        self.middle = self.inside == 1
        self.dx = 1 - 2 * self.x
        self.dy = 2 - 4 * lax.div(self.e, 2)
        self.dc = 1 - 2 * lax.rem(self.e, 2)

    def device(self, ox=0, oe=0, zi=0):
        return (self.x + ox, self.zs[zi], self.e + oe)

    def inward(self):
        return (self.x, self.inner, self.e)

    def shard(self, oe, zi):
        return self.zs[zi] * 4 + self.e + oe


def greet(at, everyone, pair=False):
    barrier = pltpu.get_barrier_semaphore()
    peers = [at.device(zi=1), at.device(oe=at.dy), at.device(oe=at.dc)]
    if everyone or pair:
        peers.append(at.device(ox=at.dx))
    if everyone:
        peers += [at.device(zi=2), at.device(zi=3)]
    for peer in peers:
        pl.semaphore_signal(barrier, inc=1, device_id=peer, device_id_type=MESH)
    if everyone:
        pl.semaphore_wait(barrier, len(peers))
        return

    @pl.when(at.middle)
    def _():
        pl.semaphore_signal(barrier, inc=1, device_id=at.inward(), device_id_type=MESH)

    pl.semaphore_wait(barrier, len(peers) + at.inside)


def remote(src, dst, send, recv, device):
    return pltpu.make_async_remote_copy(
        src_ref=src, dst_ref=dst, send_sem=send, recv_sem=recv, device_id=device, device_id_type=MESH
    )


def cross(at, sent, got, send_sem, recv_sem):
    return [
        remote(a, b, send_sem.at[m], recv_sem.at[m], at.device(ox=at.dx))
        for m, (a, b) in enumerate(zip(sent, got))
    ]


class Exchange:
    def __init__(self, at, sent, got, local_sem, send_sem, recv_sem):
        self.at, self.sent, self.got = at, sent, got
        self.local_sem, self.send_sem, self.recv_sem = local_sem, send_sem, recv_sem
        self.waits = []

    def push(self, src, m, z_from, slot, device):
        at = self.at
        spot = self.got[m].at[at.x * 4 + z_from]
        copy = remote(
            src, spot, self.send_sem.at[m * 7 + slot], self.recv_sem.at[m * 8 + (0 if slot < 3 else 4) + z_from], device
        )
        copy.start()
        self.waits.append(copy)

    def start(self):
        at = self.at
        for m, sent in enumerate(self.sent):
            for zi in (1, 2, 3):
                self.push(sent.at[at.zs[zi]], m, at.z, zi - 1, at.device(zi=zi))
            self.push(sent.at[at.z], m, at.z, 3, at.device(ox=at.dx))
            pltpu.make_async_copy(
                sent.at[at.z], self.got[m].at[at.x * 4 + at.z], self.local_sem.at[m]
            ).start()

    def arrive(self, m, slot):
        src = self.sent[m].at[0]
        remote(
            src, self.got[m].at[0], self.send_sem.at[0], self.recv_sem.at[slot], self.at.device(ox=self.at.dx)
        ).wait_recv()

    def forward(self, zi):
        at = self.at
        for m in range(len(self.sent)):
            self.arrive(m, m * 8 + at.zs[zi])
            self.push(self.got[m].at[at.x * 4 + at.zs[zi]], m, at.zs[zi], 3 + zi, at.device(ox=at.dx))

    def finish(self):
        at = self.at
        for m, sent in enumerate(self.sent):
            for z in range(4):
                self.arrive(m, m * 8 + 4 + z)
            pltpu.make_async_copy(
                sent.at[at.z], self.got[m].at[at.x * 4 + at.z], self.local_sem.at[m]
            ).wait()
        for copy in self.waits:
            copy.wait_send()


def gather_kernel(block, rows, parts, extras, swaps, *refs):
    refs = list(refs)

    def take(count):
        taken = refs[:count]
        del refs[:count]
        return taken

    (x_ref,), sent, given = take(1), take(extras), take(swaps)
    (out_ref,), got, taken = take(1), take(extras), take(swaps)
    own_sem, send_sem, recv_sem = take(3)
    extra_sems = take(3 if extras else 0)
    at = Place()
    greet(at, extras > 0, swaps > 0)
    crossing = cross(at, given, taken, *refs) if swaps else []
    piece = rows // parts
    slot_z, slot_f, slot_s = 0, 3, 7
    started, inside = [], []
    firsts = 1 if block else 0
    shift = at.e * rows if block else 0

    def where(f, zi, p):
        return pl.ds(
            pl.multiple_of(at.shard(f * at.dy, zi) * rows + p * piece, piece), piece
        )

    def push(src, dst, slot, p, device, sends=None, record=None):
        k = slot * parts + p
        j = k if sends is None else sends * parts + p
        remote(src, out_ref.at[dst], send_sem.at[j], recv_sem.at[k], device).start()
        (started if record is None else record).append(j)

    f_dev, s_dev, z_dev = at.device(oe=at.dy), at.device(oe=at.dc), at.device(zi=1)

    def gone(j):
        remote(
            x_ref.at[pl.ds(0, piece)], out_ref.at[pl.ds(0, piece)], send_sem.at[j], recv_sem.at[0], s_dev
        ).wait_send()

    def arrive(slot, p):
        k = slot * parts + p
        remote(
            x_ref.at[pl.ds(0, piece)], out_ref.at[pl.ds(0, piece)], send_sem.at[k], recv_sem.at[k], s_dev
        ).wait_recv()

    if block:
        spot = pl.ds(pl.multiple_of(at.z * 4 * rows, 4 * rows), 4 * rows)
    else:
        spot = pl.ds(pl.multiple_of(at.shard(0, 0) * rows, rows), rows)
    own = pltpu.make_async_copy(x_ref, out_ref.at[spot], own_sem)

    def source(f, zi, p):
        if f == 0 and zi == 0:
            return x_ref.at[pl.ds(pl.multiple_of(shift + p * piece, piece), piece)]
        return out_ref.at[where(f, zi, p)]

    def along(zi, p):
        src, dst = source(0, zi, p), where(0, zi, p)
        if zi == 0:
            push(src, dst, slot_z, p, z_dev)
        if zi < 2:
            pl.when(at.middle)(
                lambda: push(src, dst, slot_z + 1 + zi, p, at.inward(), 15 + zi, inside)
            )
        else:
            pl.when(at.middle)(lambda: push(src, dst, slot_z + zi - 1, p, z_dev, 15 + zi, inside))

    def forward(f, zi, p):
        src, dst = source(f, zi, p), where(f, zi, p)
        if f == 0:
            along(zi, p)
        if zi >= firsts:
            if f == 0:
                push(src, dst, slot_f + zi, p, f_dev)
            push(src, dst, slot_s + f * 4 + zi, p, s_dev)

    for p in range(parts):
        forward(0, 0, p)
    own.start()
    for copy in crossing:
        copy.start()
    if extras:
        swap_in = Exchange(at, sent, got, *extra_sems)
        swap_in.start()
    for zi in range(4):
        if zi > 0:
            for p in range(parts):
                arrive(slot_z + zi - 1, p)
                forward(0, zi, p)
        if zi >= firsts:
            for p in range(parts):
                arrive(slot_f + zi, p)
                forward(1, zi, p)
        if extras and zi > 0:
            swap_in.forward(zi)
    for f in range(2):
        for zi in range(firsts, 4):
            for p in range(parts):
                arrive(slot_s + f * 4 + zi, p)
    own.wait()
    if extras:
        swap_in.finish()
    for copy in crossing:
        copy.wait()
    for j in started:
        gone(j)

    @pl.when(at.middle)
    def _():
        for j in inside:
            gone(j)


def all_rows(x, block, cid, sent=(), given=(), parts=2):
    rows, width = x.shape
    total = rows * (4 if block else 16)
    rows = rows // 4 if block else rows
    extras, swaps = len(sent), len(given)
    hbm = pl.BlockSpec(memory_space=pl.ANY)
    outs = [jax.ShapeDtypeStruct((total, width), x.dtype)]
    outs += [jax.ShapeDtypeStruct((8,) + a.shape[1:], a.dtype) for a in sent]
    outs += [jax.ShapeDtypeStruct(a.shape, a.dtype) for a in given]
    scratch = [
        pltpu.SemaphoreType.DMA,
        pltpu.SemaphoreType.DMA((19 * parts,)),
        pltpu.SemaphoreType.DMA((15 * parts,)),
    ]
    if extras:
        scratch += [
            pltpu.SemaphoreType.DMA((extras,)),
            pltpu.SemaphoreType.DMA((7 * extras,)),
            pltpu.SemaphoreType.DMA((8 * extras,)),
        ]
    if swaps:
        scratch += [pltpu.SemaphoreType.DMA((swaps,)), pltpu.SemaphoreType.DMA((swaps,))]
    got = pl.pallas_call(
        functools.partial(gather_kernel, block, rows, parts, extras, swaps),
        out_shape=outs,
        in_specs=[hbm] * len(outs),
        out_specs=[hbm] * len(outs),
        scratch_shapes=scratch,
        compiler_params=pltpu.CompilerParams(collective_id=cid, has_side_effects=True),
    )(x, *sent, *given)
    return got if extras or swaps else got[0]


def scatter_kernel(rows, swaps, in_ref, *refs):
    given, out_ref, taken = refs[:swaps], refs[swaps], refs[swaps + 1 : 2 * swaps + 1]
    acc, got_s, got_f, got_z, load_sem, send_sem, recv_sem = refs[2 * swaps + 1 : 2 * swaps + 8]
    at = Place()
    greet(at, False, swaps > 0)
    crossing = cross(at, given, taken, *refs[2 * swaps + 8 :]) if swaps else []
    for copy in crossing:
        copy.start()
    slot_z, slot_f, slot_s = 0, 5, 9
    f_dev, s_dev, z_dev = at.device(oe=at.dy), at.device(oe=at.dc), at.device(zi=1)
    started, in_middle, at_end = [], [], []

    def rows_of(rank):
        return in_ref.at[pl.ds(pl.multiple_of(rank * rows, rows), rows)]

    def push(src, dst, slot, device, sends=None, record=started):
        j = slot if sends is None else sends
        remote(src, dst, send_sem.at[j], recv_sem.at[slot], device).start()
        record.append(j)

    def gone(j):
        remote(acc.at[0], acc.at[0], send_sem.at[j], recv_sem.at[0], s_dev).wait_send()

    def arrive(dst, slot):
        remote(acc.at[0], dst, send_sem.at[slot], recv_sem.at[slot], s_dev).wait_recv()

    order = [(f, zi) for f in (1, 0) for zi in (3, 2, 1, 0)]
    loads = {}
    for f, zi in order:
        k = f * 4 + zi
        push(rows_of(at.shard(f * at.dy + at.dc, zi)), got_s.at[k], slot_s + k, s_dev)
        loads[k] = pltpu.make_async_copy(
            rows_of(at.shard(f * at.dy, zi)), acc.at[k], load_sem.at[k]
        )
        loads[k].start()

    def add(k, *others, into=None):
        @pl.loop(0, rows // 16)
        def _(i):
            span = pl.ds(pl.multiple_of(i * 16, 16), 16)
            total = acc[k, span, :].astype(F32)
            for ref, j in others:
                total = total + ref[j, span, :].astype(F32)
            if into is None:
                acc[k, span, :] = total.astype(BF)
            else:
                into[span, :] = total

    for f, zi in order:
        k = f * 4 + zi
        arrive(got_s.at[k], slot_s + k)
        loads[k].wait()
        others = [(got_s, k)]
        if f == 1:
            add(k, *others)
            push(acc.at[k], got_f.at[zi], slot_f + zi, f_dev)
            continue
        arrive(got_f.at[zi], slot_f + zi)
        others.append((got_f, zi))
        if zi >= 2:

            @pl.when(at.middle)
            def _():
                arrive(got_z.at[3 - zi], slot_z + 3 - zi)
                add(k, *others, (got_z, 3 - zi))
                there = 4 if zi == 2 else 3
                push(
                    acc.at[k], got_z.at[there], slot_z + there, at.inward(), slot_z + zi, in_middle
                )

            @pl.when(jnp.logical_not(at.middle))
            def _():
                add(k, *others)
                push(acc.at[k], got_z.at[3 - zi], slot_z + 3 - zi, z_dev, slot_z + zi, at_end)
        elif zi == 1:

            @pl.when(at.middle)
            def _():
                arrive(got_z.at[3], slot_z + 3)
                add(k, *others, (got_z, 3))
                push(acc.at[k], got_z.at[4], slot_z + 4, z_dev, slot_z + 1, in_middle)

            @pl.when(jnp.logical_not(at.middle))
            def _():
                add(k, *others)
                push(acc.at[k], got_z.at[2], slot_z + 2, z_dev, slot_z + 1, at_end)
        else:

            @pl.when(at.middle)
            def _():
                arrive(got_z.at[2], slot_z + 2)
                arrive(got_z.at[4], slot_z + 4)
                add(k, *others, (got_z, 2), (got_z, 4), into=out_ref)

            @pl.when(jnp.logical_not(at.middle))
            def _():
                arrive(got_z.at[4], slot_z + 4)
                add(k, *others, (got_z, 4), into=out_ref)

    for copy in crossing:
        copy.wait()
    for j in started:
        gone(j)

    @pl.when(at.middle)
    def _():
        for j in in_middle:
            gone(j)

    @pl.when(jnp.logical_not(at.middle))
    def _():
        for j in at_end:
            gone(j)


def own_rows(x, cid, given=()):
    rows, width = x.shape[0] // 16, x.shape[1]
    swaps = len(given)
    hbm = pl.BlockSpec(memory_space=pl.ANY)
    crossing = [pltpu.SemaphoreType.DMA((swaps,))] * 2 if swaps else []
    got = pl.pallas_call(
        functools.partial(scatter_kernel, rows, swaps),
        out_shape=[jax.ShapeDtypeStruct((rows, width), F32)]
        + [jax.ShapeDtypeStruct(a.shape, a.dtype) for a in given],
        in_specs=[hbm] * (1 + swaps),
        out_specs=[pl.BlockSpec(memory_space=pltpu.VMEM)] + [hbm] * swaps,
        scratch_shapes=[
            pltpu.VMEM((8, rows, width), BF),
            pltpu.VMEM((8, rows, width), BF),
            pltpu.VMEM((4, rows, width), BF),
            pltpu.VMEM((5, rows, width), BF),
            pltpu.SemaphoreType.DMA((8,)),
            pltpu.SemaphoreType.DMA((17,)),
            pltpu.SemaphoreType.DMA((17,)),
            *crossing,
        ],
        compiler_params=pltpu.CompilerParams(
            collective_id=cid, has_side_effects=True, vmem_limit_bytes=40 * 1024 * 1024
        ),
    )(x, *given)
    return got if swaps else got[0]


def share_kernel(rows, count, *refs):
    ins, outs = refs[:count], refs[count : 2 * count]
    own_sem, send_sem, recv_sem = refs[2 * count :]
    at = Place()
    barrier = pltpu.get_barrier_semaphore()
    f_dev, s_dev = at.device(oe=at.dy), at.device(oe=at.dc)
    for peer in (f_dev, s_dev):
        pl.semaphore_signal(barrier, inc=1, device_id=peer, device_id_type=MESH)
    pl.semaphore_wait(barrier, 2)

    def spot(oe):
        return pl.ds(pl.multiple_of((at.e + oe) * rows, rows), rows)

    copies = []
    for m in range(count):
        for j, device in enumerate((f_dev, s_dev)):
            copy = remote(
                ins[m], outs[m].at[spot(0)], send_sem.at[m * 3 + j], recv_sem.at[m * 3 + j], device
            )
            copy.start()
            copies.append(copy)
        local = pltpu.make_async_copy(ins[m], outs[m].at[spot(0)], own_sem.at[m])
        local.start()
        copies.append(local)
    for m in range(count):
        copies[m * 3].wait_recv()
        src = outs[m].at[spot(at.dy)]
        copy = remote(src, src, send_sem.at[m * 3 + 2], recv_sem.at[m * 3 + 2], s_dev)
        copy.start()
        copies.append(copy)
    for m in range(count):
        copies[m * 3].wait_send()
        copies[m * 3 + 1].wait()
        copies[m * 3 + 2].wait()
        copies[count * 3 + m].wait()


def share(arrays, cid):
    count = len(arrays)
    rows, width = arrays[0].shape
    hbm = pl.BlockSpec(memory_space=pl.ANY)
    return pl.pallas_call(
        functools.partial(share_kernel, rows, count),
        out_shape=[jax.ShapeDtypeStruct((4 * rows, width), a.dtype) for a in arrays],
        in_specs=[hbm] * count,
        out_specs=[hbm] * count,
        scratch_shapes=[
            pltpu.SemaphoreType.DMA((count,)),
            pltpu.SemaphoreType.DMA((3 * count,)),
            pltpu.SemaphoreType.DMA((3 * count,)),
        ],
        compiler_params=pltpu.CompilerParams(collective_id=cid, has_side_effects=True),
    )(*arrays)


ALL = ("dp", "ctx", "exp")
DENSE = ("dp", "ctx")


def swap(blocks):
    return lax.all_to_all(blocks, DENSE, split_axis=0, concat_axis=0, tiled=True)


def by_four(matrix):
    rows, columns = matrix.shape
    return matrix.reshape(rows, 4, columns // 4).transpose(1, 0, 2)


def across(values):
    return lax.ppermute(values, "dp", [(0, 1), (1, 0)])


def attend_kernel(scale, block, q_ref, k_ref, v_ref, out_ref, lse_ref):
    length = q_ref.shape[0]
    for i in range(length // block):
        seen = (i + 1) * block
        rows = pl.ds(i * block, block)
        scores = transposed_right(q_ref[rows, :], k_ref[0:seen, :]) * scale
        row_at = lax.broadcasted_iota(jnp.int32, scores.shape, 0) + i * block
        col_at = lax.broadcasted_iota(jnp.int32, scores.shape, 1)
        scores = jnp.where(row_at >= col_at, scores, MASKED)
        top = jnp.max(scores, axis=-1, keepdims=True)
        lse = top + jnp.log(jnp.sum(jnp.exp(scores - top), axis=-1, keepdims=True))
        probs = jnp.exp(scores - lse).astype(BF)
        out_ref[rows, :] = product(probs, v_ref[0:seen, :]).astype(BF)
        lse_ref[rows, :] = jnp.broadcast_to(lse, (block, HDIM))


def attend(q, k, v):
    length = q.shape[0]
    return pl.pallas_call(
        functools.partial(attend_kernel, HDIM ** (-0.5), 256),
        out_shape=(
            jax.ShapeDtypeStruct((length, HDIM), BF),
            jax.ShapeDtypeStruct((length, HDIM), F32),
        ),
        in_specs=[pl.BlockSpec(memory_space=pltpu.VMEM)] * 3,
        out_specs=(pl.BlockSpec(memory_space=pltpu.VMEM),) * 2,
        compiler_params=pltpu.CompilerParams(vmem_limit_bytes=56 * 1024 * 1024),
    )(q, k, v)


def attend_back_kernel(scale, block, q_ref, k_ref, v_ref, do_ref, lse_ref, dq_ref, dk_ref, dv_ref):
    length = q_ref.shape[0]
    dk_ref[...] = jnp.zeros_like(dk_ref)
    dv_ref[...] = jnp.zeros_like(dv_ref)
    for i in range(length // block):
        seen = (i + 1) * block
        rows = pl.ds(i * block, block)
        q = q_ref[rows, :]
        do = do_ref[rows, :]
        scores = transposed_right(q, k_ref[0:seen, :]) * scale
        row_at = lax.broadcasted_iota(jnp.int32, scores.shape, 0) + i * block
        col_at = lax.broadcasted_iota(jnp.int32, scores.shape, 1)
        scores = jnp.where(row_at >= col_at, scores, MASKED)
        probs = jnp.exp(scores - lse_ref[rows, 0:1])
        weight_back = transposed_right(do, v_ref[0:seen, :])
        inner = jnp.sum(probs * weight_back, axis=-1, keepdims=True)
        score_back = (probs * (weight_back - inner)).astype(BF)
        dv_ref[0:seen, :] += transposed_left(probs.astype(BF), do)
        dk_ref[0:seen, :] += transposed_left(score_back, q) * scale
        dq_ref[rows, :] = product(score_back, k_ref[0:seen, :]) * scale


def attend_back(q, k, v, do, lse):
    length = q.shape[0]
    return pl.pallas_call(
        functools.partial(attend_back_kernel, HDIM ** (-0.5), 256),
        out_shape=(jax.ShapeDtypeStruct((length, HDIM), F32),) * 3,
        in_specs=[pl.BlockSpec(memory_space=pltpu.VMEM)] * 5,
        out_specs=(pl.BlockSpec(memory_space=pltpu.VMEM),) * 3,
        compiler_params=pltpu.CompilerParams(vmem_limit_bytes=56 * 1024 * 1024),
    )(q, k, v, do, lse)


def turn_tables(length):
    inverse = 10000.0 ** (-np.arange(HDIM // 2).astype(np.float64) * 2.0 / HDIM)
    angles = np.arange(length).astype(np.float64)[:, None] * inverse[None, :]
    return np.cos(angles).astype(np.float32), np.sin(angles).astype(np.float32)


def turn(rows, cosine, sine):
    a, b = rows[:, : HDIM // 2], rows[:, HDIM // 2 :]
    return jnp.concatenate([a * cosine - b * sine, b * cosine + a * sine], axis=1)


def turn_back(rows, cosine, sine):
    a, b = rows[:, : HDIM // 2], rows[:, HDIM // 2 :]
    return jnp.concatenate([a * cosine + b * sine, b * cosine - a * sine], axis=1)


def silu_parts(gate, up):
    s = jax.nn.sigmoid(gate)
    act = gate * s
    return act * up, s * (1.0 + gate * (1.0 - s)) * up, act


def fast_body(
    tokens,
    routes,
    norm_attn,
    w_query,
    w_key,
    w_value,
    w_out,
    norm_mix,
    w_router,
    shared_gate,
    shared_up,
    shared_down,
    expert_gate,
    expert_up,
    expert_down,
    out_grad,
):
    dp, ctx, exp = lax.axis_index("dp"), lax.axis_index("ctx"), lax.axis_index("exp")
    rows_here, width = tokens.shape[1], tokens.shape[2]
    quarter = rows_here // 4
    length = rows_here * 4
    experts = w_router.shape[1]
    capacity = quarter * TOPK * 4 // (3 * experts)
    groups = length // quarter
    dense = w_query.shape[0]
    cut = shared_gate.shape[1] // 4
    wide = 256
    start = exp * quarter
    tokens_own = lax.dynamic_slice_in_dim(tokens[0], start, quarter, 0)
    dy_own = lax.dynamic_slice_in_dim(out_grad[0], start, quarter, 0)

    named = jnp.any(
        routes[0][:, :, None] == (jnp.arange(4, dtype=jnp.int32) * 4 + exp)[None, None, :], axis=1
    )
    named = named.astype(BF).reshape(dense, 2, 4).transpose(2, 0, 1)
    little = jnp.concatenate([w_router, norm_attn[:, None], norm_mix[:, None]], axis=1)
    little = jnp.broadcast_to(little[None], (4,) + little.shape)
    little = jnp.concatenate([little, named], axis=2)
    little = jnp.pad(little, ((0, 0), (0, 0), (0, HDIM - little.shape[2])))
    sent_head = jnp.concatenate([by_four(w_query), by_four(w_key), by_four(w_value), little], axis=2)
    sent_out = w_out.reshape(4, HDIM, dense)
    sent_units = jnp.concatenate([by_four(shared_gate), by_four(shared_up)], axis=2)
    sent_units = jnp.pad(sent_units, ((0, 0), (0, 0), (0, 3 * HDIM - 2 * cut)))
    sent_down = shared_down.reshape(4, cut, dense)
    tokens_all, early, early_out, late, late_down = all_rows(
        tokens[0], True, 1, (sent_head, sent_out, sent_units, sent_down)
    )

    tokens_all, sent_gate, sent_up, sent_down = lax.optimization_barrier(
        (tokens_all, expert_gate[0], expert_up[0], expert_down[0])
    )
    other_gate, other_up, other_down = across(sent_gate), across(sent_up), across(sent_down)
    early = early.reshape(width, 4 * HDIM)
    w_qkv = early[:, : 3 * HDIM]
    little = early[:, 3 * HDIM :]
    router_matrix = little[:, :experts]
    attention_gain = little[:, experts].astype(F32)
    mixer_gain = little[:, experts + 1].astype(F32)
    hits = little[:, experts + 2 : experts + 4].reshape(2, length)
    hits = lax.dynamic_index_in_dim(hits, dp, 0, False).astype(F32).reshape(groups, quarter)
    w_out_head = early_out.transpose(1, 0, 2).reshape(HDIM, width)

    dy_all = all_rows(out_grad[0], True, 2)
    late = late.reshape(width, 3 * HDIM)
    pads = ((0, 0), (0, wide - cut))
    shared_in = jnp.concatenate(
        [jnp.pad(late[:, :cut], pads), jnp.pad(late[:, cut : 2 * cut], pads)], axis=1
    )
    shared_out = jnp.pad(
        late_down.transpose(1, 0, 2).reshape(cut, width), ((0, wide - cut), (0, 0))
    )

    cosine, sine = turn_tables(length)
    normed = rms_scale(tokens_all.astype(F32), attention_gain).astype(BF)
    qkv = product(normed, w_qkv)
    query = turn(qkv[:, :HDIM], cosine, sine).astype(BF)
    key = turn(qkv[:, HDIM : 2 * HDIM], cosine, sine).astype(BF)
    value = qkv[:, 2 * HDIM :].astype(BF)
    heads_out, lse = attend(query, key, value)
    attn = own_rows(product(heads_out, w_out_head).astype(BF), 3)
    middle = tokens_own.astype(F32) + attn
    normed_own = rms_scale(middle, mixer_gain).astype(BF)

    mix_all = all_rows(normed_own, False, 4)
    logits = product(mix_all, router_matrix)
    router = jax.nn.softmax(logits, axis=-1)
    mine = ctx * 4 + exp
    columns = jnp.arange(experts, dtype=jnp.int32)[None, :] == mine
    router_mine = jnp.sum(jnp.where(columns, router, 0.0), axis=1).reshape(groups, quarter)
    place = jnp.cumsum(hits, axis=1) - 1.0
    matches = jnp.where(
        (jnp.arange(capacity).astype(F32)[None, :, None] == place[:, None, :])
        & (hits[:, None, :] > 0.5),
        1.0,
        0.0,
    )
    dispatch = matches.astype(BF)
    slot_gate = jnp.sum(matches * router_mine[:, None, :], axis=2).reshape(-1, 1)

    def pick(rows):
        return jnp.einsum(
            "gst,gtd->gsd",
            dispatch,
            rows.reshape(groups, quarter, width),
            preferred_element_type=F32,
        ).astype(BF).reshape(groups * capacity, width)

    def spread(rows):
        return jnp.einsum(
            "gst,gsd->gtd",
            dispatch,
            rows.reshape(groups, capacity, width),
            preferred_element_type=F32,
        ).reshape(length, width)

    picked = pick(mix_all)
    picked_dy = pick(dy_all)

    def half(gate_matrix, up_matrix, down_matrix):
        gate_hidden = product(picked, gate_matrix)
        up_hidden = product(picked, up_matrix)
        act, by_gate, by_up = silu_parts(gate_hidden, up_hidden)
        dy_down = transposed_right(picked_dy, down_matrix)
        act_back = slot_gate * dy_down
        g_back = (act_back * by_gate).astype(BF)
        u_back = (act_back * by_up).astype(BF)
        act_low = act.astype(BF)
        gate_back = jnp.sum(act_low.astype(F32) * dy_down, axis=1)
        return act_low, (act * slot_gate).astype(BF), g_back, u_back, gate_back

    act_a, scaled_a, g_a, u_a, gb_a = half(expert_gate[0], expert_up[0], expert_down[0])
    act_b, scaled_b, g_b, u_b, gb_b = half(other_gate, other_up, other_down)
    input_back = (
        transposed_right(g_a, expert_gate[0])
        + transposed_right(u_a, expert_up[0])
        + transposed_right(g_b, other_gate)
        + transposed_right(u_b, other_up)
    )
    gate_back = gb_a + gb_b

    shared_hidden = product(mix_all, shared_in)
    shared_act, shared_by_gate, shared_by_up = silu_parts(
        shared_hidden[:, :wide], shared_hidden[:, wide:]
    )
    shared_act = shared_act.astype(BF)
    shared_back = transposed_right(dy_all, shared_out)
    shared_gu_back = jnp.concatenate(
        [(shared_back * shared_by_gate).astype(BF), (shared_back * shared_by_up).astype(BF)], axis=1
    )
    mix_part = (
        transposed_right(shared_gu_back, shared_in) + spread(input_back.astype(BF))
    ).astype(BF)
    gate_back_tokens = jnp.sum(
        matches * gate_back.reshape(groups, capacity, 1), axis=1
    ).reshape(length, 1)
    gate_columns = jnp.where(
        jnp.arange(HDIM, dtype=jnp.int32)[None, :] == mine, gate_back_tokens, 0.0
    ).astype(BF)
    mix_sum = jnp.concatenate([mix_part, gate_columns], axis=1)
    gate_grad_b, up_grad_b, down_grad_b, mix_sum = lax.optimization_barrier(
        (
            transposed_left(picked, g_b).astype(BF),
            transposed_left(picked, u_b).astype(BF),
            transposed_left(scaled_b, picked_dy).astype(BF),
            mix_sum,
        )
    )
    mix_back, gate_grad_b = own_rows(mix_sum, 5, (gate_grad_b,))
    gate_back_own = mix_back[:, width : width + experts]
    mix_back = mix_back[:, :width]

    router_own = jax.nn.softmax(product(normed_own, router_matrix), axis=-1)
    logit_back = (
        router_own * (gate_back_own - jnp.sum(router_own * gate_back_own, axis=-1, keepdims=True))
    ).astype(BF)
    router_part = transposed_left(normed_own, logit_back)

    mix_back = mix_back + transposed_right(logit_back, router_matrix)
    _, norm_mix_back = jax.vjp(rms_scale, middle, mixer_gain)
    middle_norm_back, gain_mix_part = norm_mix_back(mix_back)
    middle_back = dy_own.astype(F32) + middle_norm_back
    attn_back = middle_back.astype(BF)
    attn_back_all, up_grad_b = all_rows(attn_back, False, 7, (), (up_grad_b,))
    heads_back = transposed_right(attn_back_all, w_out_head).astype(BF)
    out_part = transposed_left(heads_out, attn_back_all).astype(BF)
    dq, dk, dv = attend_back(query, key, value, heads_back, lse)
    qkv_back = jnp.concatenate(
        [
            turn_back(dq, cosine, sine).astype(BF),
            turn_back(dk, cosine, sine).astype(BF),
            dv.astype(BF),
        ],
        axis=1,
    )
    normed_back, down_grad_b = own_rows(transposed_right(qkv_back, w_qkv).astype(BF), 8, (down_grad_b,))
    qkv_part = transposed_left(normed, qkv_back).astype(BF)
    _, norm_attn_back = jax.vjp(rms_scale, tokens_own.astype(F32), attention_gain)
    input_norm_back, gain_attn_part = norm_attn_back(normed_back)
    tokens_back_own = (middle_back + input_norm_back).astype(BF)

    half_a = product(act_a, expert_down[0]).astype(BF).astype(F32)
    half_b = product(act_b, other_down).astype(BF).astype(F32)
    mixed_part = (
        product(shared_act, shared_out) + spread(((half_a + half_b) * slot_gate).astype(BF))
    ).astype(BF)
    mixed_own = (middle + own_rows(mixed_part, 3)).astype(BF)

    mixed, tokens_back = share([mixed_own, tokens_back_own], 6)
    small = jnp.concatenate(
        [gain_attn_part[:, None], gain_mix_part[:, None], router_part], axis=1
    ).reshape(8, 1, dense * (experts + 2))
    small = jnp.broadcast_to(small, (8, 4, dense * (experts + 2))).reshape(32, -1)
    small = lax.all_to_all(small, ALL, split_axis=0, concat_axis=0, tiled=True)
    small = jnp.sum(small, axis=0).reshape(dense, experts + 2)
    shared_gu_grad = transposed_left(mix_all, shared_gu_back).astype(BF)
    shared_gu_grad = jnp.concatenate(
        [shared_gu_grad[:, :cut], shared_gu_grad[:, wide : wide + cut]], axis=1
    )
    shared_gu_grad = jnp.pad(shared_gu_grad, ((0, 0), (0, 3 * HDIM - 2 * cut)))
    shared_down_part = transposed_left(shared_act, dy_all).astype(BF)[:cut]
    home_rows = swap(
        jnp.concatenate([qkv_part, shared_gu_grad], axis=1).reshape(8, dense, 6 * HDIM)
    ).astype(F32)
    home_columns = swap(
        jnp.concatenate([out_part, shared_down_part], axis=0)
        .reshape(HDIM + cut, 8, dense)
        .transpose(1, 0, 2)
    ).astype(F32)
    home_rows = home_rows[:4] + home_rows[4:]
    home_columns = home_columns[:4] + home_columns[4:]

    def columns_of(parts):
        return parts.transpose(1, 0, 2).reshape(dense, -1)

    units = 3 * HDIM
    gate_grad = transposed_left(picked, g_a) + gate_grad_b.astype(F32)
    up_grad = transposed_left(picked, u_a) + up_grad_b.astype(F32)
    down_grad = transposed_left(scaled_a, picked_dy) + down_grad_b.astype(F32)
    return (
        mixed[None],
        tokens_back[None],
        small[:, 0],
        columns_of(home_rows[:, :, :HDIM]),
        columns_of(home_rows[:, :, HDIM : 2 * HDIM]),
        columns_of(home_rows[:, :, 2 * HDIM : 3 * HDIM]),
        home_columns[:, :HDIM].reshape(4 * HDIM, dense),
        small[:, 1],
        small[:, 2:],
        columns_of(home_rows[:, :, units : units + cut]),
        columns_of(home_rows[:, :, units + cut : units + 2 * cut]),
        home_columns[:, HDIM:].reshape(4 * cut, dense),
        gate_grad[None],
        up_grad[None],
        down_grad[None],
    )


def solution(mesh):
    sizes = dict(mesh.shape)

    def chosen(*args):
        heads = args[3].shape[1] * sizes["exp"] // HDIM
        one_head_each = heads == sizes["ctx"] * sizes["exp"]
        built_for = (sizes["dp"], sizes["ctx"], sizes["exp"]) == (2, 4, 4)
        return fast_body(*args) if one_head_each and built_for else body(*args)

    in_specs = (
        P("dp", "ctx", None),
        P("dp", "ctx", None),
        P(("dp", "ctx")),
        P(("dp", "ctx"), "exp"),
        P(("dp", "ctx"), "exp"),
        P(("dp", "ctx"), "exp"),
        P("exp", ("dp", "ctx")),
        P(("dp", "ctx")),
        P(("dp", "ctx"), None),
        P(("dp", "ctx"), "exp"),
        P(("dp", "ctx"), "exp"),
        P("exp", ("dp", "ctx")),
        P(("ctx", "exp"), None, "dp"),
        P(("ctx", "exp"), None, "dp"),
        P(("ctx", "exp"), "dp", None),
        P("dp", "ctx", None),
    )
    out_specs = (
        P("dp", "ctx", None),
        P("dp", "ctx", None),
        P(("dp", "ctx")),
        P(("dp", "ctx"), "exp"),
        P(("dp", "ctx"), "exp"),
        P(("dp", "ctx"), "exp"),
        P("exp", ("dp", "ctx")),
        P(("dp", "ctx")),
        P(("dp", "ctx"), None),
        P(("dp", "ctx"), "exp"),
        P(("dp", "ctx"), "exp"),
        P("exp", ("dp", "ctx")),
        P(("ctx", "exp"), None, "dp"),
        P(("ctx", "exp"), None, "dp"),
        P(("ctx", "exp"), "dp", None),
    )
    return jax.shard_map(chosen, mesh=mesh, in_specs=in_specs, out_specs=out_specs, check_vma=False)
```

```python
import functools

import jax
import jax.numpy as jnp
import numpy as np
from jax import lax
from jax.experimental import pallas as pl
from jax.experimental.pallas import tpu as pltpu
from jax.sharding import PartitionSpec as P

HDIM = 128
TOPK = 6


EPSILON = 1e-06
MASKED = -1e30
HIGHEST = lax.Precision.HIGHEST


def rms_scale(values, gain_row):
    return (
        values * lax.rsqrt(jnp.mean(values * values, axis=-1, keepdims=True) + EPSILON) * gain_row
    )


def rope_tables(positions, rope_width):
    inverse = 10000.0 ** (-jnp.arange(rope_width // 2).astype(jnp.float32) * 2.0 / rope_width)
    angles = positions.astype(jnp.float32)[:, None] * inverse[None, :]
    return (jnp.cos(angles), jnp.sin(angles))


def rotate(values, cosine, sine_table):
    half_size = values.shape[-1] // 2
    first_half = values[..., :half_size]
    second = values[..., half_size:]
    cosine = cosine[:, None, :]
    sine_table = sine_table[:, None, :]
    return jnp.concatenate(
        [first_half * cosine - second * sine_table, second * cosine + first_half * sine_table],
        axis=-1,
    )


def silu_mix(gate_rows, up_rows):
    return jax.nn.silu(gate_rows) * up_rows


def product(left_side, right_side):
    return jnp.dot(left_side, right_side, preferred_element_type=jnp.float32)


def transposed_left(left_side, right_side):
    return lax.dot_general(
        left_side, right_side, (((0,), (0,)), ((), ())), preferred_element_type=jnp.float32
    )


def transposed_right(left_side, right_side):
    return lax.dot_general(
        left_side, right_side, (((1,), (1,)), ((), ())), preferred_element_type=jnp.float32
    )


def place_rows(part, start_row, total_rows):
    blank = jnp.zeros((total_rows, part.shape[1]), jnp.float32)
    return lax.dynamic_update_slice_in_dim(blank, part, start_row, 0)


def to_owners(buffer):
    copies = lax.axis_size("dp")
    widened = jnp.broadcast_to(buffer[None], (copies,) + buffer.shape)
    widened = widened.reshape((copies * buffer.shape[0],) + buffer.shape[1:])
    return lax.all_to_all(widened, ("dp", "ctx", "exp"), split_axis=0, concat_axis=0, tiled=True)


def values_home(partial_value):
    returned = lax.all_to_all(
        partial_value, ("dp", "ctx", "exp"), split_axis=0, concat_axis=0, tiled=True
    )
    grouped = returned.reshape((lax.axis_size("dp"), -1) + returned.shape[1:])
    return jnp.sum(grouped.astype(jnp.float32), axis=0).astype(jnp.bfloat16)


def grads_home(partial_value):
    returned = lax.all_to_all(
        partial_value.astype(jnp.bfloat16),
        ("dp", "ctx", "exp"),
        split_axis=0,
        concat_axis=0,
        tiled=True,
    ).astype(partial_value.dtype)
    grouped = returned.reshape((lax.axis_size("dp"), -1) + returned.shape[1:])
    return jnp.sum(grouped, axis=0)


def body(
    tokens,
    routes,
    norm_attn,
    w_query,
    w_key,
    w_value,
    w_out,
    norm_mix,
    w_router,
    shared_gate,
    shared_up,
    shared_down,
    expert_gate,
    expert_up,
    expert_down,
    out_grad,
):
    gathered = (
        lax.all_gather(norm_attn, ("dp", "ctx"), axis=0, tiled=True),
        lax.all_gather(w_query, ("dp", "ctx"), axis=0, tiled=True),
        lax.all_gather(w_key, ("dp", "ctx"), axis=0, tiled=True),
        lax.all_gather(w_value, ("dp", "ctx"), axis=0, tiled=True),
        lax.all_gather(w_out, ("dp", "ctx"), axis=1, tiled=True),
        lax.all_gather(norm_mix, ("dp", "ctx"), axis=0, tiled=True),
        lax.all_gather(w_router, ("dp", "ctx"), axis=0, tiled=True),
        lax.all_gather(shared_gate, ("dp", "ctx"), axis=0, tiled=True),
        lax.all_gather(shared_up, ("dp", "ctx"), axis=0, tiled=True),
        lax.all_gather(shared_down, ("dp", "ctx"), axis=1, tiled=True),
    )
    (
        attention_gain,
        query_matrix,
        key_matrix,
        value_matrix,
        output_matrix,
        mixer_gain,
        router_matrix,
        shared_gate_matrix,
        shared_up_matrix,
        shared_down_matrix,
    ) = gathered
    rows_here = tokens.shape[1]
    model_width = tokens.shape[2]
    heads_here = query_matrix.shape[1] // HDIM
    quarter = rows_here // lax.axis_size("exp")
    start_row = lax.axis_index("exp") * quarter
    layer_input = tokens[0].astype(jnp.float32)
    grad_rows = out_grad[0]
    grad_float = grad_rows.astype(jnp.float32)
    seq_length = rows_here * lax.axis_size("ctx")
    positions = lax.axis_index("ctx") * rows_here + jnp.arange(rows_here, dtype=jnp.int32)
    cosine, sine_table = rope_tables(positions, HDIM)
    visible = positions[:, None] >= jnp.arange(seq_length, dtype=jnp.int32)[None, :]
    scale = HDIM ** (-0.5)
    head_shape = (rows_here, heads_here, HDIM)
    normed = rms_scale(layer_input, attention_gain).astype(jnp.bfloat16)
    query_rot = rotate(
        product(normed, query_matrix).reshape(head_shape), cosine, sine_table
    ).astype(jnp.bfloat16)
    key_rot = (
        rotate(product(normed, key_matrix).reshape(head_shape), cosine, sine_table)
        .astype(jnp.bfloat16)
        .reshape(rows_here, -1)
    )
    value_low = product(normed, value_matrix).astype(jnp.bfloat16)
    key_all, value_all = (
        lax.all_gather(key_rot, "ctx", axis=0, tiled=True),
        lax.all_gather(value_low, "ctx", axis=0, tiled=True),
    )
    key_heads = key_all.reshape(seq_length, heads_here, HDIM)
    value_heads = value_all.reshape(seq_length, heads_here, HDIM)

    def attention_scores():
        scores = (
            jnp.einsum("qhd,khd->hqk", query_rot, key_heads, preferred_element_type=jnp.float32)
            * scale
        )
        return jnp.where(visible[None], scores, MASKED)

    scores = attention_scores()
    largest = jnp.max(scores, axis=-1, keepdims=True)
    log_total = largest + jnp.log(jnp.sum(jnp.exp(scores - largest), axis=-1, keepdims=True))
    weights_low = jnp.exp(scores - log_total).astype(jnp.bfloat16)
    heads_out = (
        jnp.einsum("hqk,khd->qhd", weights_low, value_heads, preferred_element_type=jnp.float32)
        .reshape(rows_here, -1)
        .astype(jnp.bfloat16)
    )
    attn_total = lax.psum(product(heads_out, output_matrix), "exp")
    middle = layer_input + attn_total
    normed_mix = rms_scale(middle, mixer_gain).astype(jnp.bfloat16)
    normed_quarter = lax.dynamic_slice_in_dim(normed_mix, start_row, quarter, 0)
    route_quarter = lax.dynamic_slice_in_dim(routes[0], start_row, quarter, 0)
    grad_quarter = lax.dynamic_slice_in_dim(grad_rows, start_row, quarter, 0)
    logits = product(normed_quarter, router_matrix)
    probabilities = jax.nn.softmax(logits, axis=-1)
    owners = lax.axis_size(("ctx", "exp"))
    local_experts = expert_gate.shape[0]
    experts = local_experts * owners
    capacity = max(quarter * TOPK * 4 // (3 * experts), 2)
    expert_choice_index = jnp.arange(experts, dtype=jnp.int32)
    chosen = (route_quarter[:, :, None] == expert_choice_index[None, None, :]).astype(jnp.float32)
    gates = jnp.sum(chosen * probabilities[:, None, :], axis=-1)
    route_flat = route_quarter.reshape(-1)
    expert_hits = (route_flat[:, None] == expert_choice_index[None, :]).astype(jnp.int32)
    slot_index = jnp.sum(jnp.cumsum(expert_hits, axis=0) * expert_hits, axis=1) - 1
    slot_place = route_flat * capacity + slot_index
    matches = (
        jnp.arange(experts * capacity, dtype=jnp.int32)[:, None] == slot_place[None, :]
    ).astype(jnp.float32)
    dispatch = jnp.sum(matches.reshape(experts * capacity, quarter, TOPK), axis=2).astype(
        jnp.bfloat16
    )
    slot_gates = jnp.dot(matches, gates.reshape(-1), precision=HIGHEST)
    buffer_shape = (owners, local_experts, capacity, model_width)
    outgoing = product(dispatch, normed_quarter).astype(jnp.bfloat16).reshape(buffer_shape)
    arrived = to_owners(outgoing)
    gate_hidden = jnp.einsum(
        "sicd,idf->sicf", arrived, expert_gate, preferred_element_type=jnp.float32
    )
    up_hidden = jnp.einsum("sicd,idf->sicf", arrived, expert_up, preferred_element_type=jnp.float32)
    expert_act = silu_mix(gate_hidden, up_hidden).astype(jnp.bfloat16)
    partial_value = jnp.einsum(
        "sicf,ifd->sicd", expert_act, expert_down, preferred_element_type=jnp.float32
    ).astype(jnp.bfloat16)
    expert_values = values_home(partial_value).reshape(experts * capacity, model_width)
    route_values = expert_values[slot_place].astype(jnp.float32).reshape(quarter, TOPK, model_width)
    combined = jnp.sum(route_values * gates[:, :, None], axis=1)
    shared_gate_rows = product(normed_mix, shared_gate_matrix)
    shared_up_rows = product(normed_mix, shared_up_matrix)
    shared_act = silu_mix(shared_gate_rows, shared_up_rows).astype(jnp.bfloat16)
    branch_part = product(shared_act, shared_down_matrix) + place_rows(
        combined, start_row, rows_here
    )
    result = middle + lax.psum(branch_part.astype(jnp.bfloat16), "exp").astype(jnp.float32)
    grad_slots = (
        (product(dispatch, grad_quarter) * slot_gates[:, None])
        .astype(jnp.bfloat16)
        .reshape(buffer_shape)
    )
    grad_arrived = to_owners(grad_slots)
    act_grad = jnp.einsum(
        "sicd,ifd->sicf", grad_arrived, expert_down, preferred_element_type=jnp.float32
    )
    down_grad = jnp.einsum(
        "sicf,sicd->ifd", expert_act, grad_arrived, preferred_element_type=jnp.float32
    )
    _, mix_back = jax.vjp(silu_mix, gate_hidden, up_hidden)
    gate_back, up_back = mix_back(act_grad)
    gate_back = gate_back.astype(jnp.bfloat16)
    up_back = up_back.astype(jnp.bfloat16)
    gate_grad = jnp.einsum("sicd,sicf->idf", arrived, gate_back, preferred_element_type=jnp.float32)
    up_grad = jnp.einsum("sicd,sicf->idf", arrived, up_back, preferred_element_type=jnp.float32)
    input_back = jnp.einsum(
        "sicf,idf->sicd", gate_back, expert_gate, preferred_element_type=jnp.float32
    ) + jnp.einsum("sicf,idf->sicd", up_back, expert_up, preferred_element_type=jnp.float32)
    rows_back = grads_home(input_back).reshape(experts * capacity, model_width)
    moe_back = jnp.sum(rows_back[slot_place].reshape(quarter, TOPK, model_width), axis=1)
    gate_route_back = jnp.sum(route_values * grad_quarter.astype(jnp.float32)[:, None, :], axis=-1)
    prob_back = jnp.sum(chosen * gate_route_back[:, :, None], axis=1)
    _, soft_back = jax.vjp(lambda values: jax.nn.softmax(values, axis=-1), logits)
    logit_back = soft_back(prob_back)[0].astype(jnp.bfloat16)
    router_term = transposed_left(normed_quarter, logit_back)
    shared_back = transposed_right(grad_rows, shared_down_matrix)
    _, shared_mix_back = jax.vjp(silu_mix, shared_gate_rows, shared_up_rows)
    sgate_back, sup_back = shared_mix_back(shared_back)
    sgate_back = sgate_back.astype(jnp.bfloat16)
    sup_back = sup_back.astype(jnp.bfloat16)
    quarter_back = transposed_right(logit_back, router_matrix) + moe_back
    mix_part = (
        transposed_right(sgate_back, shared_gate_matrix)
        + transposed_right(sup_back, shared_up_matrix)
        + place_rows(quarter_back, start_row, rows_here)
    )
    mix_total, router_grad = (
        lax.psum(mix_part.astype(jnp.bfloat16), "exp").astype(jnp.float32),
        lax.psum(router_term.astype(jnp.bfloat16), "exp").astype(jnp.float32),
    )
    _, norm_mix_back = jax.vjp(rms_scale, middle, mixer_gain.astype(jnp.float32))
    middle_norm_back, gain_mix_grad = norm_mix_back(mix_total)
    middle_grad = grad_float + middle_norm_back
    sdown_grad = transposed_left(shared_act, grad_rows)
    sgate_grad = transposed_left(normed_mix, sgate_back)
    sup_grad = transposed_left(normed_mix, sup_back)
    attn_back = middle_grad.astype(jnp.bfloat16)
    heads_back = transposed_right(attn_back, output_matrix).astype(jnp.bfloat16).reshape(head_shape)
    weights_full = jnp.exp(attention_scores() - log_total)
    weights_again = weights_full.astype(jnp.bfloat16)
    weight_back = jnp.einsum(
        "qhd,khd->hqk", heads_back, value_heads, preferred_element_type=jnp.float32
    )
    value_term = jnp.einsum(
        "hqk,qhd->khd", weights_again, heads_back, preferred_element_type=jnp.float32
    ).reshape(seq_length, -1)
    score_back = (
        weights_full * (weight_back - jnp.sum(weights_full * weight_back, axis=-1, keepdims=True))
    ).astype(jnp.bfloat16)
    query_rot_back = (
        jnp.einsum("hqk,khd->qhd", score_back, key_heads, preferred_element_type=jnp.float32)
        * scale
    )
    key_term = (
        jnp.einsum("hqk,qhd->khd", score_back, query_rot, preferred_element_type=jnp.float32)
        * scale
    ).reshape(seq_length, -1)
    key_sum, value_sum = (
        lax.psum_scatter(
            key_term.astype(jnp.bfloat16), "ctx", scatter_dimension=0, tiled=True
        ).astype(jnp.float32),
        lax.psum_scatter(
            value_term.astype(jnp.bfloat16), "ctx", scatter_dimension=0, tiled=True
        ).astype(jnp.float32),
    )
    _, rotate_back = jax.vjp(
        lambda values: rotate(values, cosine, sine_table), jnp.zeros(head_shape, jnp.float32)
    )
    query_low = rotate_back(query_rot_back)[0].reshape(rows_here, -1).astype(jnp.bfloat16)
    key_low = (
        rotate_back(key_sum.reshape(head_shape))[0].reshape(rows_here, -1).astype(jnp.bfloat16)
    )
    value_back_low = value_sum.astype(jnp.bfloat16)
    normed_part = (
        transposed_right(query_low, query_matrix)
        + transposed_right(key_low, key_matrix)
        + transposed_right(value_back_low, value_matrix)
    )
    normed_back = lax.psum(normed_part.astype(jnp.bfloat16), "exp").astype(jnp.float32)
    _, norm_attn_back = jax.vjp(rms_scale, layer_input, attention_gain.astype(jnp.float32))
    input_norm_back, gain_attn_grad = norm_attn_back(normed_back)
    tokens_back = (middle_grad + input_norm_back).astype(jnp.bfloat16)
    out_weight_grad = transposed_left(heads_out, attn_back)
    query_grad = transposed_left(normed, query_low)
    key_grad = transposed_left(normed, key_low)
    value_grad = transposed_left(normed, value_back_low)
    all_sums = (
        lax.psum_scatter(
            gain_attn_grad.astype(jnp.bfloat16), ("dp", "ctx"), scatter_dimension=0, tiled=True
        ).astype(jnp.float32),
        lax.psum_scatter(
            query_grad.astype(jnp.bfloat16), ("dp", "ctx"), scatter_dimension=0, tiled=True
        ).astype(jnp.float32),
        lax.psum_scatter(
            key_grad.astype(jnp.bfloat16), ("dp", "ctx"), scatter_dimension=0, tiled=True
        ).astype(jnp.float32),
        lax.psum_scatter(
            value_grad.astype(jnp.bfloat16), ("dp", "ctx"), scatter_dimension=0, tiled=True
        ).astype(jnp.float32),
        lax.psum_scatter(
            out_weight_grad.astype(jnp.bfloat16), ("dp", "ctx"), scatter_dimension=1, tiled=True
        ).astype(jnp.float32),
        lax.psum_scatter(
            gain_mix_grad.astype(jnp.bfloat16), ("dp", "ctx"), scatter_dimension=0, tiled=True
        ).astype(jnp.float32),
        lax.psum_scatter(
            router_grad.astype(jnp.bfloat16), ("dp", "ctx"), scatter_dimension=0, tiled=True
        ).astype(jnp.float32),
        lax.psum_scatter(
            sgate_grad.astype(jnp.bfloat16), ("dp", "ctx"), scatter_dimension=0, tiled=True
        ).astype(jnp.float32),
        lax.psum_scatter(
            sup_grad.astype(jnp.bfloat16), ("dp", "ctx"), scatter_dimension=0, tiled=True
        ).astype(jnp.float32),
        lax.psum_scatter(
            sdown_grad.astype(jnp.bfloat16), ("dp", "ctx"), scatter_dimension=1, tiled=True
        ).astype(jnp.float32),
    )
    (
        gain_attn_sum,
        query_sum,
        key_sum_out,
        value_sum_out,
        out_sum,
        gain_mix_sum,
        router_sum,
        sgate_sum,
        sup_sum,
        sdown_sum,
    ) = all_sums
    return (
        result.astype(jnp.bfloat16)[None],
        tokens_back[None],
        gain_attn_sum,
        query_sum,
        key_sum_out,
        value_sum_out,
        out_sum,
        gain_mix_sum,
        router_sum,
        sgate_sum,
        sup_sum,
        sdown_sum,
        gate_grad,
        up_grad,
        down_grad,
    )


MESH = pl.DeviceIdType.MESH
BF = jnp.bfloat16
F32 = jnp.float32


class Place:
    def __init__(self):
        self.x = lax.axis_index("dp")
        self.z = lax.axis_index("ctx")
        self.e = lax.axis_index("exp")
        z = self.z
        high = lax.div(z, 2)
        self.zs = [z, z + 1 - 2 * lax.rem(z, 2), 2 - high, 3 - 3 * high]
        self.inner = 3 - z
        self.inside = lax.div(z * (3 - z), 2)
        self.middle = self.inside == 1
        self.dx = 1 - 2 * self.x
        self.dy = 2 - 4 * lax.div(self.e, 2)
        self.dc = 1 - 2 * lax.rem(self.e, 2)

    def device(self, ox=0, oe=0, zi=0):
        return (self.x + ox, self.zs[zi], self.e + oe)

    def inward(self):
        return (self.x, self.inner, self.e)

    def shard(self, oe, zi):
        return self.zs[zi] * 4 + self.e + oe


def greet(at, everyone, pair=False):
    barrier = pltpu.get_barrier_semaphore()
    peers = [at.device(zi=1), at.device(oe=at.dy), at.device(oe=at.dc)]
    if everyone or pair:
        peers.append(at.device(ox=at.dx))
    if everyone:
        peers += [at.device(zi=2), at.device(zi=3)]
    for peer in peers:
        pl.semaphore_signal(barrier, inc=1, device_id=peer, device_id_type=MESH)
    if everyone:
        pl.semaphore_wait(barrier, len(peers))
        return

    @pl.when(at.middle)
    def _():
        pl.semaphore_signal(barrier, inc=1, device_id=at.inward(), device_id_type=MESH)

    pl.semaphore_wait(barrier, len(peers) + at.inside)


def remote(src, dst, send, recv, device):
    return pltpu.make_async_remote_copy(
        src_ref=src, dst_ref=dst, send_sem=send, recv_sem=recv, device_id=device, device_id_type=MESH
    )


def cross(at, sent, got, send_sem, recv_sem):
    return [
        remote(a, b, send_sem.at[m], recv_sem.at[m], at.device(ox=at.dx))
        for m, (a, b) in enumerate(zip(sent, got))
    ]


class Exchange:
    def __init__(self, at, sent, got, local_sem, send_sem, recv_sem):
        self.at, self.sent, self.got = at, sent, got
        self.local_sem, self.send_sem, self.recv_sem = local_sem, send_sem, recv_sem
        self.waits = []

    def push(self, src, m, z_from, slot, device):
        at = self.at
        spot = self.got[m].at[at.x * 4 + z_from]
        copy = remote(
            src, spot, self.send_sem.at[m * 7 + slot], self.recv_sem.at[m * 8 + (0 if slot < 3 else 4) + z_from], device
        )
        copy.start()
        self.waits.append(copy)

    def start(self):
        at = self.at
        for m, sent in enumerate(self.sent):
            for zi in (1, 2, 3):
                self.push(sent.at[at.zs[zi]], m, at.z, zi - 1, at.device(zi=zi))
            self.push(sent.at[at.z], m, at.z, 3, at.device(ox=at.dx))
            pltpu.make_async_copy(
                sent.at[at.z], self.got[m].at[at.x * 4 + at.z], self.local_sem.at[m]
            ).start()

    def arrive(self, m, slot):
        src = self.sent[m].at[0]
        remote(
            src, self.got[m].at[0], self.send_sem.at[0], self.recv_sem.at[slot], self.at.device(ox=self.at.dx)
        ).wait_recv()

    def forward(self, zi):
        at = self.at
        for m in range(len(self.sent)):
            self.arrive(m, m * 8 + at.zs[zi])
            self.push(self.got[m].at[at.x * 4 + at.zs[zi]], m, at.zs[zi], 3 + zi, at.device(ox=at.dx))

    def finish(self):
        at = self.at
        for m, sent in enumerate(self.sent):
            for z in range(4):
                self.arrive(m, m * 8 + 4 + z)
            pltpu.make_async_copy(
                sent.at[at.z], self.got[m].at[at.x * 4 + at.z], self.local_sem.at[m]
            ).wait()
        for copy in self.waits:
            copy.wait_send()


def gather_kernel(block, rows, parts, extras, swaps, *refs):
    refs = list(refs)

    def take(count):
        taken = refs[:count]
        del refs[:count]
        return taken

    (x_ref,), sent, given = take(1), take(extras), take(swaps)
    (out_ref,), got, taken = take(1), take(extras), take(swaps)
    own_sem, send_sem, recv_sem = take(3)
    extra_sems = take(3 if extras else 0)
    at = Place()
    greet(at, extras > 0, swaps > 0)
    crossing = cross(at, given, taken, *refs) if swaps else []
    piece = rows // parts
    slot_z, slot_f, slot_s = 0, 3, 7
    started, inside = [], []
    firsts = 1 if block else 0
    shift = at.e * rows if block else 0

    def where(f, zi, p):
        return pl.ds(
            pl.multiple_of(at.shard(f * at.dy, zi) * rows + p * piece, piece), piece
        )

    def push(src, dst, slot, p, device, sends=None, record=None):
        k = slot * parts + p
        j = k if sends is None else sends * parts + p
        remote(src, out_ref.at[dst], send_sem.at[j], recv_sem.at[k], device).start()
        (started if record is None else record).append(j)

    f_dev, s_dev, z_dev = at.device(oe=at.dy), at.device(oe=at.dc), at.device(zi=1)

    def gone(j):
        remote(
            x_ref.at[pl.ds(0, piece)], out_ref.at[pl.ds(0, piece)], send_sem.at[j], recv_sem.at[0], s_dev
        ).wait_send()

    def arrive(slot, p):
        k = slot * parts + p
        remote(
            x_ref.at[pl.ds(0, piece)], out_ref.at[pl.ds(0, piece)], send_sem.at[k], recv_sem.at[k], s_dev
        ).wait_recv()

    if block:
        spot = pl.ds(pl.multiple_of(at.z * 4 * rows, 4 * rows), 4 * rows)
    else:
        spot = pl.ds(pl.multiple_of(at.shard(0, 0) * rows, rows), rows)
    own = pltpu.make_async_copy(x_ref, out_ref.at[spot], own_sem)

    def source(f, zi, p):
        if f == 0 and zi == 0:
            return x_ref.at[pl.ds(pl.multiple_of(shift + p * piece, piece), piece)]
        return out_ref.at[where(f, zi, p)]

    def along(zi, p):
        src, dst = source(0, zi, p), where(0, zi, p)
        if zi == 0:
            push(src, dst, slot_z, p, z_dev)
        if zi < 2:
            pl.when(at.middle)(
                lambda: push(src, dst, slot_z + 1 + zi, p, at.inward(), 15 + zi, inside)
            )
        else:
            pl.when(at.middle)(lambda: push(src, dst, slot_z + zi - 1, p, z_dev, 15 + zi, inside))

    def forward(f, zi, p):
        src, dst = source(f, zi, p), where(f, zi, p)
        if f == 0:
            along(zi, p)
        if zi >= firsts:
            if f == 0:
                push(src, dst, slot_f + zi, p, f_dev)
            push(src, dst, slot_s + f * 4 + zi, p, s_dev)

    for p in range(parts):
        forward(0, 0, p)
    own.start()
    for copy in crossing:
        copy.start()
    if extras:
        swap_in = Exchange(at, sent, got, *extra_sems)
        swap_in.start()
    for zi in range(4):
        if zi > 0:
            for p in range(parts):
                arrive(slot_z + zi - 1, p)
                forward(0, zi, p)
        if zi >= firsts:
            for p in range(parts):
                arrive(slot_f + zi, p)
                forward(1, zi, p)
        if extras and zi > 0:
            swap_in.forward(zi)
    for f in range(2):
        for zi in range(firsts, 4):
            for p in range(parts):
                arrive(slot_s + f * 4 + zi, p)
    own.wait()
    if extras:
        swap_in.finish()
    for copy in crossing:
        copy.wait()
    for j in started:
        gone(j)

    @pl.when(at.middle)
    def _():
        for j in inside:
            gone(j)


def all_rows(x, block, cid, sent=(), given=(), parts=2):
    rows, width = x.shape
    total = rows * (4 if block else 16)
    rows = rows // 4 if block else rows
    extras, swaps = len(sent), len(given)
    hbm = pl.BlockSpec(memory_space=pl.ANY)
    outs = [jax.ShapeDtypeStruct((total, width), x.dtype)]
    outs += [jax.ShapeDtypeStruct((8,) + a.shape[1:], a.dtype) for a in sent]
    outs += [jax.ShapeDtypeStruct(a.shape, a.dtype) for a in given]
    scratch = [
        pltpu.SemaphoreType.DMA,
        pltpu.SemaphoreType.DMA((19 * parts,)),
        pltpu.SemaphoreType.DMA((15 * parts,)),
    ]
    if extras:
        scratch += [
            pltpu.SemaphoreType.DMA((extras,)),
            pltpu.SemaphoreType.DMA((7 * extras,)),
            pltpu.SemaphoreType.DMA((8 * extras,)),
        ]
    if swaps:
        scratch += [pltpu.SemaphoreType.DMA((swaps,)), pltpu.SemaphoreType.DMA((swaps,))]
    got = pl.pallas_call(
        functools.partial(gather_kernel, block, rows, parts, extras, swaps),
        out_shape=outs,
        in_specs=[hbm] * len(outs),
        out_specs=[hbm] * len(outs),
        scratch_shapes=scratch,
        compiler_params=pltpu.CompilerParams(collective_id=cid, has_side_effects=True),
    )(x, *sent, *given)
    return got if extras or swaps else got[0]


def scatter_kernel(rows, swaps, in_ref, *refs):
    given, out_ref, taken = refs[:swaps], refs[swaps], refs[swaps + 1 : 2 * swaps + 1]
    acc, got_s, got_f, got_z, load_sem, send_sem, recv_sem = refs[2 * swaps + 1 : 2 * swaps + 8]
    at = Place()
    greet(at, False, swaps > 0)
    crossing = cross(at, given, taken, *refs[2 * swaps + 8 :]) if swaps else []
    for copy in crossing:
        copy.start()
    slot_z, slot_f, slot_s = 0, 5, 9
    f_dev, s_dev, z_dev = at.device(oe=at.dy), at.device(oe=at.dc), at.device(zi=1)
    started, in_middle, at_end = [], [], []

    def rows_of(rank):
        return in_ref.at[pl.ds(pl.multiple_of(rank * rows, rows), rows)]

    def push(src, dst, slot, device, sends=None, record=started):
        j = slot if sends is None else sends
        remote(src, dst, send_sem.at[j], recv_sem.at[slot], device).start()
        record.append(j)

    def gone(j):
        remote(acc.at[0], acc.at[0], send_sem.at[j], recv_sem.at[0], s_dev).wait_send()

    def arrive(dst, slot):
        remote(acc.at[0], dst, send_sem.at[slot], recv_sem.at[slot], s_dev).wait_recv()

    order = [(f, zi) for f in (1, 0) for zi in (3, 2, 1, 0)]
    loads = {}
    for f, zi in order:
        k = f * 4 + zi
        push(rows_of(at.shard(f * at.dy + at.dc, zi)), got_s.at[k], slot_s + k, s_dev)
        loads[k] = pltpu.make_async_copy(
            rows_of(at.shard(f * at.dy, zi)), acc.at[k], load_sem.at[k]
        )
        loads[k].start()

    def add(k, *others, into=None):
        @pl.loop(0, rows // 16)
        def _(i):
            span = pl.ds(pl.multiple_of(i * 16, 16), 16)
            total = acc[k, span, :].astype(F32)
            for ref, j in others:
                total = total + ref[j, span, :].astype(F32)
            if into is None:
                acc[k, span, :] = total.astype(BF)
            else:
                into[span, :] = total

    for f, zi in order:
        k = f * 4 + zi
        arrive(got_s.at[k], slot_s + k)
        loads[k].wait()
        others = [(got_s, k)]
        if f == 1:
            add(k, *others)
            push(acc.at[k], got_f.at[zi], slot_f + zi, f_dev)
            continue
        arrive(got_f.at[zi], slot_f + zi)
        others.append((got_f, zi))
        if zi >= 2:

            @pl.when(at.middle)
            def _():
                arrive(got_z.at[3 - zi], slot_z + 3 - zi)
                add(k, *others, (got_z, 3 - zi))
                there = 4 if zi == 2 else 3
                push(
                    acc.at[k], got_z.at[there], slot_z + there, at.inward(), slot_z + zi, in_middle
                )

            @pl.when(jnp.logical_not(at.middle))
            def _():
                add(k, *others)
                push(acc.at[k], got_z.at[3 - zi], slot_z + 3 - zi, z_dev, slot_z + zi, at_end)
        elif zi == 1:

            @pl.when(at.middle)
            def _():
                arrive(got_z.at[3], slot_z + 3)
                add(k, *others, (got_z, 3))
                push(acc.at[k], got_z.at[4], slot_z + 4, z_dev, slot_z + 1, in_middle)

            @pl.when(jnp.logical_not(at.middle))
            def _():
                add(k, *others)
                push(acc.at[k], got_z.at[2], slot_z + 2, z_dev, slot_z + 1, at_end)
        else:

            @pl.when(at.middle)
            def _():
                arrive(got_z.at[2], slot_z + 2)
                arrive(got_z.at[4], slot_z + 4)
                add(k, *others, (got_z, 2), (got_z, 4), into=out_ref)

            @pl.when(jnp.logical_not(at.middle))
            def _():
                arrive(got_z.at[4], slot_z + 4)
                add(k, *others, (got_z, 4), into=out_ref)

    for copy in crossing:
        copy.wait()
    for j in started:
        gone(j)

    @pl.when(at.middle)
    def _():
        for j in in_middle:
            gone(j)

    @pl.when(jnp.logical_not(at.middle))
    def _():
        for j in at_end:
            gone(j)


def own_rows(x, cid, given=()):
    rows, width = x.shape[0] // 16, x.shape[1]
    swaps = len(given)
    hbm = pl.BlockSpec(memory_space=pl.ANY)
    crossing = [pltpu.SemaphoreType.DMA((swaps,))] * 2 if swaps else []
    got = pl.pallas_call(
        functools.partial(scatter_kernel, rows, swaps),
        out_shape=[jax.ShapeDtypeStruct((rows, width), F32)]
        + [jax.ShapeDtypeStruct(a.shape, a.dtype) for a in given],
        in_specs=[hbm] * (1 + swaps),
        out_specs=[pl.BlockSpec(memory_space=pltpu.VMEM)] + [hbm] * swaps,
        scratch_shapes=[
            pltpu.VMEM((8, rows, width), BF),
            pltpu.VMEM((8, rows, width), BF),
            pltpu.VMEM((4, rows, width), BF),
            pltpu.VMEM((5, rows, width), BF),
            pltpu.SemaphoreType.DMA((8,)),
            pltpu.SemaphoreType.DMA((17,)),
            pltpu.SemaphoreType.DMA((17,)),
            *crossing,
        ],
        compiler_params=pltpu.CompilerParams(
            collective_id=cid, has_side_effects=True, vmem_limit_bytes=40 * 1024 * 1024
        ),
    )(x, *given)
    return got if swaps else got[0]


def share_kernel(rows, count, *refs):
    ins, outs = refs[:count], refs[count : 2 * count]
    own_sem, send_sem, recv_sem = refs[2 * count :]
    at = Place()
    barrier = pltpu.get_barrier_semaphore()
    f_dev, s_dev = at.device(oe=at.dy), at.device(oe=at.dc)
    for peer in (f_dev, s_dev):
        pl.semaphore_signal(barrier, inc=1, device_id=peer, device_id_type=MESH)
    pl.semaphore_wait(barrier, 2)

    def spot(oe):
        return pl.ds(pl.multiple_of((at.e + oe) * rows, rows), rows)

    copies = []
    for m in range(count):
        for j, device in enumerate((f_dev, s_dev)):
            copy = remote(
                ins[m], outs[m].at[spot(0)], send_sem.at[m * 3 + j], recv_sem.at[m * 3 + j], device
            )
            copy.start()
            copies.append(copy)
        local = pltpu.make_async_copy(ins[m], outs[m].at[spot(0)], own_sem.at[m])
        local.start()
        copies.append(local)
    for m in range(count):
        copies[m * 3].wait_recv()
        src = outs[m].at[spot(at.dy)]
        copy = remote(src, src, send_sem.at[m * 3 + 2], recv_sem.at[m * 3 + 2], s_dev)
        copy.start()
        copies.append(copy)
    for m in range(count):
        copies[m * 3].wait_send()
        copies[m * 3 + 1].wait()
        copies[m * 3 + 2].wait()
        copies[count * 3 + m].wait()


def share(arrays, cid):
    count = len(arrays)
    rows, width = arrays[0].shape
    hbm = pl.BlockSpec(memory_space=pl.ANY)
    return pl.pallas_call(
        functools.partial(share_kernel, rows, count),
        out_shape=[jax.ShapeDtypeStruct((4 * rows, width), a.dtype) for a in arrays],
        in_specs=[hbm] * count,
        out_specs=[hbm] * count,
        scratch_shapes=[
            pltpu.SemaphoreType.DMA((count,)),
            pltpu.SemaphoreType.DMA((3 * count,)),
            pltpu.SemaphoreType.DMA((3 * count,)),
        ],
        compiler_params=pltpu.CompilerParams(collective_id=cid, has_side_effects=True),
    )(*arrays)


def expert_gather_kernel(experts, *refs):
    refs = list(refs)

    def take(count):
        taken = refs[:count]
        del refs[:count]
        return taken

    x_ref, dy_ref, disp, w_router, shared_in, shared_out = take(6)
    weights = take(6)
    out_ref, picked, picked_dy, scaled_out, g_out, u_out, gb_out, sa_out, sg_out = take(9)
    wg, wu, wd, xb, dyb, pk, pdy, sc, gg, uu, gb, sa, sg = take(13)
    own_sem, send_sem, recv_sem, load_sem, block_sem, store_sem = take(6)
    at = Place()
    greet(at, False)
    rows = x_ref.shape[0]
    block = 4 * rows
    slots = pk.shape[1]
    groups = 4
    slot_z, slot_f, slot_s = 0, 3, 7
    started, inside = [], []
    mine = at.z * 4 + at.e

    def where(f, zi):
        return pl.ds(pl.multiple_of(at.shard(f * at.dy, zi) * rows, rows), rows)

    def push(src, dst, slot, device, sends=None, record=None):
        j = slot if sends is None else sends
        remote(src, out_ref.at[dst], send_sem.at[j], recv_sem.at[slot], device).start()
        (started if record is None else record).append(j)

    f_dev, s_dev, z_dev = at.device(oe=at.dy), at.device(oe=at.dc), at.device(zi=1)

    def gone(j):
        remote(x_ref, out_ref.at[pl.ds(0, rows)], send_sem.at[j], recv_sem.at[0], s_dev).wait_send()

    def arrive(slot):
        remote(
            x_ref, out_ref.at[pl.ds(0, rows)], send_sem.at[slot], recv_sem.at[slot], s_dev
        ).wait_recv()

    own = pltpu.make_async_copy(x_ref, out_ref.at[where(0, 0)], own_sem)

    def source(f, zi):
        return x_ref if f == 0 and zi == 0 else out_ref.at[where(f, zi)]

    def along(zi):
        src, dst = source(0, zi), where(0, zi)
        if zi == 0:
            push(src, dst, slot_z, z_dev)
        if zi < 2:
            pl.when(at.middle)(lambda: push(src, dst, slot_z + 1 + zi, at.inward(), 15 + zi, inside))
        else:
            pl.when(at.middle)(lambda: push(src, dst, slot_z + zi - 1, z_dev, 15 + zi, inside))

    def forward(f, zi):
        src, dst = source(f, zi), where(f, zi)
        if f == 0:
            along(zi)
            push(src, dst, slot_f + zi, f_dev)
        push(src, dst, slot_s + f * 4 + zi, s_dev)

    def span(zi, size):
        return pl.ds(pl.multiple_of(at.zs[zi] * size, size), size)

    def dy_load(zi):
        return pltpu.make_async_copy(
            dy_ref.at[span(zi, block)], dyb.at[zi % 2], block_sem.at[2 + zi % 2]
        )

    def x_load(zi):
        return pltpu.make_async_copy(
            out_ref.at[span(zi, block)], xb.at[zi % 2], block_sem.at[zi % 2]
        )

    def stores(zi):
        b = zi % 2
        pairs = [
            (pk.at[b], picked.at[span(zi, slots)]),
            (pdy.at[b], picked_dy.at[span(zi, slots)]),
            (gb.at[b], gb_out.at[span(zi, slots)]),
            (sa.at[b], sa_out.at[span(zi, block)]),
            (sg.at[b], sg_out.at[span(zi, block)]),
        ]
        for h in range(2):
            pairs += [
                (sc.at[b, h], scaled_out.at[h, span(zi, slots)]),
                (gg.at[b, h], g_out.at[h, span(zi, slots)]),
                (uu.at[b, h], u_out.at[h, span(zi, slots)]),
            ]
        return [
            pltpu.make_async_copy(src, dst, store_sem.at[b, j]) for j, (src, dst) in enumerate(pairs)
        ]

    def parts_of(gate, up):
        s = 1.0 / (1.0 + jnp.exp(-gate))
        act = gate * s
        return act * up, s * (1.0 + gate * (1.0 - s)) * up, act

    def work(zi):
        b = zi % 2
        dy_load(zi).wait()
        x_load(zi).wait()
        if zi >= 2:
            for copy in stores(zi - 2):
                copy.wait()

        @pl.loop(0, groups)
        def _(i):
            hot = disp[at.zs[zi] * groups + i]
            source_rows = pl.ds(pl.multiple_of(i * rows, rows), rows)
            into = pl.ds(pl.multiple_of(i * (slots // groups), slots // groups), slots // groups)
            pk[b, into, :] = product(hot, xb[b, source_rows, :]).astype(BF)
            pdy[b, into, :] = product(hot, dyb[b, source_rows, :]).astype(BF)

        logits = transposed_right(pk[b], w_router[...])
        lane = lax.broadcasted_iota(jnp.int32, logits.shape, 1)
        logits = jnp.where(lane < experts, logits, MASKED)
        powers = jnp.exp(logits - jnp.max(logits, axis=1, keepdims=True))
        own_power = jnp.sum(jnp.where(lane == mine, powers, 0.0), axis=1, keepdims=True)
        gate_of = own_power / jnp.sum(powers, axis=1, keepdims=True)
        gb[b] = jnp.zeros(gb.shape[1:], F32)

        @pl.loop(0, 2)
        def _(h):
            hidden, by_gate, by_up = parts_of(
                transposed_right(pk[b], wg[h]), transposed_right(pk[b], wu[h])
            )
            dy_down = transposed_right(pdy[b], wd[h])
            act_back = gate_of * dy_down
            gg[b, h] = (act_back * by_gate).astype(BF)
            uu[b, h] = (act_back * by_up).astype(BF)
            sc[b, h] = (hidden * gate_of).astype(BF)
            gb[b] += jnp.broadcast_to(
                jnp.sum(hidden * dy_down, axis=1, keepdims=True), gb.shape[1:]
            )

        @pl.loop(0, groups)
        def _(i):
            token_rows = pl.ds(pl.multiple_of(i * rows, rows), rows)
            both = transposed_right(xb[b, token_rows, :], shared_in[...])
            wide = both.shape[1] // 2
            hidden, by_gate, by_up = parts_of(both[:, :wide], both[:, wide:])
            back = transposed_right(dyb[b, token_rows, :], shared_out[...])
            sa[b, token_rows, :] = hidden.astype(BF)
            sg[b, token_rows, :wide] = (back * by_gate).astype(BF)
            sg[b, token_rows, wide:] = (back * by_up).astype(BF)

        for copy in stores(zi):
            copy.start()

    forward(0, 0)
    own.start()
    loads = []
    for m, (ref, half) in enumerate([(wg, 0), (wu, 0), (wd, 0), (wg, 1), (wu, 1), (wd, 1)]):
        loads.append(pltpu.make_async_copy(weights[m], ref.at[half], load_sem.at[m]))
        loads[-1].start()
    dy_load(0).start()
    for zi in range(4):
        arrive(slot_f + zi)
        forward(1, zi)
        if zi < 3:
            arrive(slot_z + zi)
            forward(0, zi + 1)
            dy_load(zi + 1).start()
        for f in range(2):
            arrive(slot_s + f * 4 + zi)
        if zi == 0:
            own.wait()
            for copy in loads:
                copy.wait()
        x_load(zi).start()
        work(zi)
    for zi in (2, 3):
        for copy in stores(zi):
            copy.wait()
    for j in started:
        gone(j)

    @pl.when(at.middle)
    def _():
        for j in inside:
            gone(j)


def expert_rows(x, dy_all, dispatch, w_router, experts, shared_in, shared_out, weights, cid):
    rows, width = x.shape
    total, block = 16 * rows, 4 * rows
    slots = 4 * dispatch.shape[1]
    hidden = weights[0].shape[0]
    wide = shared_out.shape[0]
    hbm, vmem = pl.BlockSpec(memory_space=pl.ANY), pl.BlockSpec(memory_space=pltpu.VMEM)
    shape = jax.ShapeDtypeStruct
    return pl.pallas_call(
        functools.partial(expert_gather_kernel, experts),
        out_shape=[
            shape((total, width), BF),
            shape((4 * slots, width), BF),
            shape((4 * slots, width), BF),
            shape((2, 4 * slots, hidden), BF),
            shape((2, 4 * slots, hidden), BF),
            shape((2, 4 * slots, hidden), BF),
            shape((4 * slots, 128), F32),
            shape((total, wide), BF),
            shape((total, 2 * wide), BF),
        ],
        in_specs=[hbm, hbm, vmem, vmem, vmem, vmem] + [hbm] * 6,
        out_specs=[hbm] * 9,
        scratch_shapes=[
            pltpu.VMEM((2, hidden, width), BF),
            pltpu.VMEM((2, hidden, width), BF),
            pltpu.VMEM((2, hidden, width), BF),
            pltpu.VMEM((2, block, width), BF),
            pltpu.VMEM((2, block, width), BF),
            pltpu.VMEM((2, slots, width), BF),
            pltpu.VMEM((2, slots, width), BF),
            pltpu.VMEM((2, 2, slots, hidden), BF),
            pltpu.VMEM((2, 2, slots, hidden), BF),
            pltpu.VMEM((2, 2, slots, hidden), BF),
            pltpu.VMEM((2, slots, 128), F32),
            pltpu.VMEM((2, block, wide), BF),
            pltpu.VMEM((2, block, 2 * wide), BF),
            pltpu.SemaphoreType.DMA,
            pltpu.SemaphoreType.DMA((19,)),
            pltpu.SemaphoreType.DMA((15,)),
            pltpu.SemaphoreType.DMA((6,)),
            pltpu.SemaphoreType.DMA((4,)),
            pltpu.SemaphoreType.DMA((2, 11)),
        ],
        compiler_params=pltpu.CompilerParams(
            collective_id=cid, has_side_effects=True, vmem_limit_bytes=60 * 1024 * 1024
        ),
    )(x, dy_all, dispatch, w_router, shared_in, shared_out, *weights)


def expert_scatter_kernel(*refs):
    refs = list(refs)

    def take(count):
        taken = refs[:count]
        del refs[:count]
        return taken

    disp, gate_back, shared_in, g_ref, u_ref, sg_ref, picked_ref, dy_ref, scaled_ref = take(9)
    weights = take(4)
    out_ref, grad_gate, grad_up, grad_down = take(4)
    wg, wu, gs, us, sg, picked, picked_dy, scaled, ib, grad, turned = take(11)
    acc, got_s, got_f, got_z, out_s = take(5)
    load_sem, store_sem, send_sem, recv_sem = take(4)
    at = Place()
    greet(at, False)
    rows, full = acc.shape[1:]
    width = shared_in.shape[1]
    slots = ib.shape[0]
    capacity = slots // 4
    mine = at.z * 4 + at.e
    slot_z, slot_f, slot_s = 0, 5, 9
    f_dev, s_dev, z_dev = at.device(oe=at.dy), at.device(oe=at.dc), at.device(zi=1)
    started, in_middle, at_end = [], [], []

    def push(src, dst, slot, device, sends=None, record=started):
        j = slot if sends is None else sends
        remote(src, dst, send_sem.at[j], recv_sem.at[slot], device).start()
        record.append(j)

    def gone(j):
        remote(acc.at[0], acc.at[0], send_sem.at[j], recv_sem.at[0], s_dev).wait_send()

    def arrive(dst, slot):
        remote(acc.at[0], dst, send_sem.at[slot], recv_sem.at[slot], s_dev).wait_recv()

    pairs = [
        (weights[0], wg.at[0]),
        (weights[1], wu.at[0]),
        (weights[2], wg.at[1]),
        (weights[3], wu.at[1]),
        (g_ref, gs),
        (u_ref, us),
        (sg_ref, sg),
        (picked_ref, picked),
        (dy_ref, picked_dy),
        (scaled_ref.at[1], scaled),
    ]
    loads = [pltpu.make_async_copy(a, b, load_sem.at[j]) for j, (a, b) in enumerate(pairs)]
    for copy in loads:
        copy.start()

    def work(zi):
        place = at.zs[zi]
        some = pl.ds(pl.multiple_of(place * slots, slots), slots)

        @pl.loop(0, 4)
        def _(n):
            columns = pl.ds(pl.multiple_of(n * (width // 4), width // 4), width // 4)
            total = product(gs[0, some, :], wg[0, :, columns])
            total += product(us[0, some, :], wu[0, :, columns])
            total += product(gs[1, some, :], wg[1, :, columns])
            total += product(us[1, some, :], wu[1, :, columns])
            ib[:, columns] = total.astype(BF)

        for twin in range(2):
            for f in range(2):
                e = at.e + f * at.dy + twin * at.dc
                hot = disp[place * 4 + e]
                mine_slots = pl.ds(pl.multiple_of(e * capacity, capacity), capacity)
                tokens = pl.ds(pl.multiple_of((place * 4 + e) * rows, rows), rows)
                into, k = (out_s, f * 2 + zi % 2) if twin else (acc, f * 4 + zi)

                @pl.loop(0, 2)
                def _(n):
                    columns = pl.ds(pl.multiple_of(n * (width // 2), width // 2), width // 2)
                    total = transposed_left(hot, ib[mine_slots, columns])
                    total += product(sg[tokens, :], shared_in[:, columns])
                    into[k, :, columns] = total.astype(BF)

                from_gates = gate_back[
                    pl.ds(pl.multiple_of(place * slots + e * capacity, capacity), capacity), :
                ]
                lane = lax.broadcasted_iota(jnp.int32, from_gates.shape, 1)
                from_gates = jnp.where(lane == mine, from_gates, 0.0).astype(BF)
                into[k, :, width:] = transposed_left(hot, from_gates).astype(BF)

    def to_twin(zi):
        for f in range(2):
            push(
                out_s.at[f * 2 + zi % 2],
                got_s.at[f * 4 + zi],
                slot_s + f * 4 + zi,
                s_dev,
                None,
                twins[zi],
            )

    twins = [[], [], [], []]

    def add(k, *others, into=None):
        @pl.loop(0, rows // 16)
        def _(i):
            span = pl.ds(pl.multiple_of(i * 16, 16), 16)
            total = acc[k, span, :].astype(F32)
            for ref, j in others:
                total = total + ref[j, span, :].astype(F32)
            if into is None:
                acc[k, span, :] = total.astype(BF)
            else:
                into[span, :] = total

    def first(zi):
        arrive(got_s.at[4 + zi], slot_s + 4 + zi)
        add(4 + zi, (got_s, 4 + zi))
        push(acc.at[4 + zi], got_f.at[zi], slot_f + zi, f_dev)

    def second(zi):
        arrive(got_s.at[zi], slot_s + zi)
        arrive(got_f.at[zi], slot_f + zi)
        others = [(got_s, zi), (got_f, zi)]
        if zi >= 2:

            @pl.when(at.middle)
            def _():
                arrive(got_z.at[3 - zi], slot_z + 3 - zi)
                add(zi, *others, (got_z, 3 - zi))
                there = 4 if zi == 2 else 3
                push(
                    acc.at[zi], got_z.at[there], slot_z + there, at.inward(), slot_z + zi, in_middle
                )

            @pl.when(jnp.logical_not(at.middle))
            def _():
                add(zi, *others)
                push(acc.at[zi], got_z.at[3 - zi], slot_z + 3 - zi, z_dev, slot_z + zi, at_end)
        elif zi == 1:

            @pl.when(at.middle)
            def _():
                arrive(got_z.at[3], slot_z + 3)
                add(zi, *others, (got_z, 3))
                push(acc.at[zi], got_z.at[4], slot_z + 4, z_dev, slot_z + 1, in_middle)

            @pl.when(jnp.logical_not(at.middle))
            def _():
                add(zi, *others)
                push(acc.at[zi], got_z.at[2], slot_z + 2, z_dev, slot_z + 1, at_end)
        else:

            @pl.when(at.middle)
            def _():
                arrive(got_z.at[2], slot_z + 2)
                arrive(got_z.at[4], slot_z + 4)
                add(zi, *others, (got_z, 2), (got_z, 4), into=out_ref)

            @pl.when(jnp.logical_not(at.middle))
            def _():
                arrive(got_z.at[4], slot_z + 4)
                add(zi, *others, (got_z, 4), into=out_ref)

    def gradient(m):
        step = 256
        right = picked_dy if m == 2 else picked
        turned[...] = (scaled[...] if m == 2 else gs[1] if m == 0 else us[1]).T

        @pl.loop(0, width // step)
        def _(n):
            columns = pl.ds(pl.multiple_of(n * step, step), step)
            grad[m, :, columns] = product(turned[...], right[:, columns]).astype(BF)

    stores = [
        pltpu.make_async_copy(grad.at[m], ref, store_sem.at[m])
        for m, ref in enumerate((grad_gate, grad_up, grad_down))
    ]
    for copy in loads[:7]:
        copy.wait()
    for zi in (3, 2, 1, 0):
        if zi < 2:
            for j in twins[zi + 2]:
                gone(j)
        work(zi)
        to_twin(zi)
        first(zi)
        if zi == 1:
            second(3)
    for copy in loads[7:]:
        copy.wait()
    for m, zi in ((0, 2), (1, 1), (2, 0)):
        gradient(m)
        stores[m].start()
        second(zi)
    for copy in stores:
        copy.wait()
    for j in started + twins[1] + twins[0]:
        gone(j)

    @pl.when(at.middle)
    def _():
        for j in in_middle:
            gone(j)

    @pl.when(jnp.logical_not(at.middle))
    def _():
        for j in at_end:
            gone(j)


def expert_back(dispatch, gate_back, shared_in, g, u, sg, picked, picked_dy, scaled, weights, cid):
    total, wide = sg.shape
    width = shared_in.shape[1]
    rows, full = total // 16, width + 128
    slots = picked.shape[0]
    hidden = g.shape[2]
    hbm, vmem = pl.BlockSpec(memory_space=pl.ANY), pl.BlockSpec(memory_space=pltpu.VMEM)
    shape = jax.ShapeDtypeStruct
    return pl.pallas_call(
        expert_scatter_kernel,
        out_shape=[
            shape((rows, full), F32),
            shape((hidden, width), BF),
            shape((hidden, width), BF),
            shape((hidden, width), BF),
        ],
        in_specs=[vmem] * 3 + [hbm] * 10,
        out_specs=[vmem] + [hbm] * 3,
        scratch_shapes=[
            pltpu.VMEM((2, hidden, width), BF),
            pltpu.VMEM((2, hidden, width), BF),
            pltpu.VMEM((2, slots, hidden), BF),
            pltpu.VMEM((2, slots, hidden), BF),
            pltpu.VMEM((total, wide), BF),
            pltpu.VMEM((slots, width), BF),
            pltpu.VMEM((slots, width), BF),
            pltpu.VMEM((slots, hidden), BF),
            pltpu.VMEM((slots // 4, width), BF),
            pltpu.VMEM((3, hidden, width), BF),
            pltpu.VMEM((hidden, slots), BF),
            pltpu.VMEM((8, rows, full), BF),
            pltpu.VMEM((8, rows, full), BF),
            pltpu.VMEM((4, rows, full), BF),
            pltpu.VMEM((5, rows, full), BF),
            pltpu.VMEM((4, rows, full), BF),
            pltpu.SemaphoreType.DMA((10,)),
            pltpu.SemaphoreType.DMA((3,)),
            pltpu.SemaphoreType.DMA((17,)),
            pltpu.SemaphoreType.DMA((17,)),
        ],
        compiler_params=pltpu.CompilerParams(
            collective_id=cid, has_side_effects=True, vmem_limit_bytes=63 * 1024 * 1024
        ),
    )(dispatch, gate_back, shared_in, g, u, sg, picked, picked_dy, scaled, *weights)


ALL = ("dp", "ctx", "exp")
DENSE = ("dp", "ctx")


def swap(blocks):
    return lax.all_to_all(blocks, DENSE, split_axis=0, concat_axis=0, tiled=True)


def by_four(matrix):
    rows, columns = matrix.shape
    return matrix.reshape(rows, 4, columns // 4).transpose(1, 0, 2)


def across(values):
    return lax.ppermute(values, "dp", [(0, 1), (1, 0)])


def attend_kernel(scale, block, q_ref, k_ref, v_ref, out_ref, lse_ref):
    length = q_ref.shape[0]
    for i in range(length // block):
        seen = (i + 1) * block
        rows = pl.ds(i * block, block)
        scores = transposed_right(q_ref[rows, :], k_ref[0:seen, :]) * scale
        row_at = lax.broadcasted_iota(jnp.int32, scores.shape, 0) + i * block
        col_at = lax.broadcasted_iota(jnp.int32, scores.shape, 1)
        scores = jnp.where(row_at >= col_at, scores, MASKED)
        top = jnp.max(scores, axis=-1, keepdims=True)
        lse = top + jnp.log(jnp.sum(jnp.exp(scores - top), axis=-1, keepdims=True))
        probs = jnp.exp(scores - lse).astype(BF)
        out_ref[rows, :] = product(probs, v_ref[0:seen, :]).astype(BF)
        lse_ref[rows, :] = jnp.broadcast_to(lse, (block, HDIM))


def attend(q, k, v):
    length = q.shape[0]
    return pl.pallas_call(
        functools.partial(attend_kernel, HDIM ** (-0.5), 256),
        out_shape=(
            jax.ShapeDtypeStruct((length, HDIM), BF),
            jax.ShapeDtypeStruct((length, HDIM), F32),
        ),
        in_specs=[pl.BlockSpec(memory_space=pltpu.VMEM)] * 3,
        out_specs=(pl.BlockSpec(memory_space=pltpu.VMEM),) * 2,
        compiler_params=pltpu.CompilerParams(vmem_limit_bytes=56 * 1024 * 1024),
    )(q, k, v)


def attend_back_kernel(scale, block, q_ref, k_ref, v_ref, do_ref, lse_ref, dq_ref, dk_ref, dv_ref):
    length = q_ref.shape[0]
    dk_ref[...] = jnp.zeros_like(dk_ref)
    dv_ref[...] = jnp.zeros_like(dv_ref)
    for i in range(length // block):
        seen = (i + 1) * block
        rows = pl.ds(i * block, block)
        q = q_ref[rows, :]
        do = do_ref[rows, :]
        scores = transposed_right(q, k_ref[0:seen, :]) * scale
        row_at = lax.broadcasted_iota(jnp.int32, scores.shape, 0) + i * block
        col_at = lax.broadcasted_iota(jnp.int32, scores.shape, 1)
        scores = jnp.where(row_at >= col_at, scores, MASKED)
        probs = jnp.exp(scores - lse_ref[rows, 0:1])
        weight_back = transposed_right(do, v_ref[0:seen, :])
        inner = jnp.sum(probs * weight_back, axis=-1, keepdims=True)
        score_back = (probs * (weight_back - inner)).astype(BF)
        dv_ref[0:seen, :] += transposed_left(probs.astype(BF), do)
        dk_ref[0:seen, :] += transposed_left(score_back, q) * scale
        dq_ref[rows, :] = product(score_back, k_ref[0:seen, :]) * scale


def attend_back(q, k, v, do, lse):
    length = q.shape[0]
    return pl.pallas_call(
        functools.partial(attend_back_kernel, HDIM ** (-0.5), 256),
        out_shape=(jax.ShapeDtypeStruct((length, HDIM), F32),) * 3,
        in_specs=[pl.BlockSpec(memory_space=pltpu.VMEM)] * 5,
        out_specs=(pl.BlockSpec(memory_space=pltpu.VMEM),) * 3,
        compiler_params=pltpu.CompilerParams(vmem_limit_bytes=56 * 1024 * 1024),
    )(q, k, v, do, lse)


def turn_tables(length):
    inverse = 10000.0 ** (-np.arange(HDIM // 2).astype(np.float64) * 2.0 / HDIM)
    angles = np.arange(length).astype(np.float64)[:, None] * inverse[None, :]
    return np.cos(angles).astype(np.float32), np.sin(angles).astype(np.float32)


def turn(rows, cosine, sine):
    a, b = rows[:, : HDIM // 2], rows[:, HDIM // 2 :]
    return jnp.concatenate([a * cosine - b * sine, b * cosine + a * sine], axis=1)


def turn_back(rows, cosine, sine):
    a, b = rows[:, : HDIM // 2], rows[:, HDIM // 2 :]
    return jnp.concatenate([a * cosine + b * sine, b * cosine - a * sine], axis=1)


def silu_parts(gate, up):
    s = jax.nn.sigmoid(gate)
    act = gate * s
    return act * up, s * (1.0 + gate * (1.0 - s)) * up, act


def fast_body(
    tokens,
    routes,
    norm_attn,
    w_query,
    w_key,
    w_value,
    w_out,
    norm_mix,
    w_router,
    shared_gate,
    shared_up,
    shared_down,
    expert_gate,
    expert_up,
    expert_down,
    out_grad,
):
    dp, ctx, exp = lax.axis_index("dp"), lax.axis_index("ctx"), lax.axis_index("exp")
    rows_here, width = tokens.shape[1], tokens.shape[2]
    quarter = rows_here // 4
    length = rows_here * 4
    experts = w_router.shape[1]
    capacity = quarter * TOPK * 4 // (3 * experts)
    groups = length // quarter
    dense = w_query.shape[0]
    cut = shared_gate.shape[1] // 4
    wide = 256
    start = exp * quarter
    tokens_own = lax.dynamic_slice_in_dim(tokens[0], start, quarter, 0)
    dy_own = lax.dynamic_slice_in_dim(out_grad[0], start, quarter, 0)

    route_rows = routes[0].T
    theirs = jnp.arange(4, dtype=jnp.int32)[:, None, None] * 4 + exp
    named = jnp.any(route_rows[None] == theirs, axis=1).astype(BF).reshape(4, 2, dense)
    little = jnp.concatenate([w_router.T, norm_attn[None], norm_mix[None]], axis=0)
    little = jnp.concatenate([jnp.broadcast_to(little[None], (4,) + little.shape), named], axis=1)
    few = -(-little.shape[1] // 16) * 16
    little = jnp.pad(little, ((0, 0), (0, few - little.shape[1]), (0, 0)))
    sent_head = jnp.concatenate([by_four(w_query), by_four(w_key), by_four(w_value)], axis=2)
    sent_out = w_out.reshape(4, HDIM, dense)
    sent_units = jnp.stack([shared_gate.T, shared_up.T, shared_down], axis=0)
    sent_units = sent_units.reshape(3, 4, cut, dense).transpose(1, 0, 2, 3).reshape(4, 3 * cut, dense)
    tokens_all, early, early_out, late, early_little = all_rows(
        tokens[0], True, 1, (sent_head, sent_out, sent_units, little)
    )

    own_gate, own_up, own_down = expert_gate[0].T, expert_up[0].T, expert_down[0]
    tokens_all, sent_gate, sent_up, sent_down = lax.optimization_barrier(
        (tokens_all, own_gate, own_up, own_down)
    )
    other_gate, other_up, other_down = across(sent_gate), across(sent_up), across(sent_down)
    w_qkv = early.reshape(width, 3 * HDIM)
    early_little = early_little.transpose(1, 0, 2)
    router_rows = early_little[:experts].reshape(experts, width)
    attention_gain = early_little[experts].reshape(width).astype(F32)
    mixer_gain = early_little[experts + 1].reshape(width).astype(F32)
    hits = early_little[experts + 2 : experts + 4].transpose(1, 0, 2).reshape(2, length)
    hits = lax.dynamic_index_in_dim(hits, dp, 0, False).astype(F32).reshape(groups, quarter)
    w_out_head = early_out.transpose(1, 0, 2).reshape(HDIM, width)

    dy_all = all_rows(out_grad[0], True, 2)
    late = late.transpose(1, 0, 2).reshape(3, cut, width)
    late = jnp.pad(late, ((0, 0), (0, wide - cut), (0, 0)))
    shared_in = late[:2].reshape(2 * wide, width)
    shared_out = late[2]

    cosine, sine = turn_tables(length)
    normed = rms_scale(tokens_all.astype(F32), attention_gain).astype(BF)
    qkv = product(normed, w_qkv)
    query = turn(qkv[:, :HDIM], cosine, sine).astype(BF)
    key = turn(qkv[:, HDIM : 2 * HDIM], cosine, sine).astype(BF)
    value = qkv[:, 2 * HDIM :].astype(BF)
    heads_out, lse = attend(query, key, value)
    attn = own_rows(product(heads_out, w_out_head).astype(BF), 3)
    middle = tokens_own.astype(F32) + attn
    normed_own = rms_scale(middle, mixer_gain).astype(BF)

    mine = ctx * 4 + exp
    place = jnp.cumsum(hits, axis=1) - 1.0
    dispatch = jnp.where(
        (jnp.arange(capacity).astype(F32)[None, :, None] == place[:, None, :])
        & (hits[:, None, :] > 0.5),
        1.0,
        0.0,
    ).astype(BF)
    router_wide = jnp.pad(router_rows, ((0, HDIM - experts), (0, 0)))
    mix_all, picked, picked_dy, scaled, g_back, u_back, gate_back, shared_act, shared_gu_back = (
        expert_rows(
            normed_own,
            dy_all,
            dispatch,
            router_wide,
            experts,
            shared_in,
            shared_out,
            (own_gate, own_up, own_down, other_gate, other_up, other_down),
            4,
        )
    )

    def spread(rows):
        return jnp.einsum(
            "gst,gsd->gtd",
            dispatch,
            rows.reshape(groups, capacity, width),
            preferred_element_type=F32,
        ).reshape(length, width)

    mix_back, gate_grad_b, up_grad_b, down_grad_b = expert_back(
        dispatch,
        gate_back,
        shared_in,
        g_back,
        u_back,
        shared_gu_back,
        picked,
        picked_dy,
        scaled,
        (own_gate, own_up, other_gate, other_up),
        5,
    )
    gate_back_own = mix_back[:, width : width + experts]
    mix_back = mix_back[:, :width]

    router_own = jax.nn.softmax(transposed_right(normed_own, router_rows), axis=-1)
    logit_back = (
        router_own * (gate_back_own - jnp.sum(router_own * gate_back_own, axis=-1, keepdims=True))
    ).astype(BF)
    router_part = transposed_left(logit_back, normed_own)

    mix_back = mix_back + product(logit_back, router_rows)
    _, norm_mix_back = jax.vjp(rms_scale, middle, mixer_gain)
    middle_norm_back, gain_mix_part = norm_mix_back(mix_back)
    middle_back = dy_own.astype(F32) + middle_norm_back
    attn_back = middle_back.astype(BF)
    attn_back_all, gate_grad_b = all_rows(attn_back, False, 7, (), (gate_grad_b,))
    heads_back = transposed_right(attn_back_all, w_out_head).astype(BF)
    out_part = transposed_left(heads_out, attn_back_all).astype(BF)
    dq, dk, dv = attend_back(query, key, value, heads_back, lse)
    qkv_back = jnp.concatenate(
        [
            turn_back(dq, cosine, sine).astype(BF),
            turn_back(dk, cosine, sine).astype(BF),
            dv.astype(BF),
        ],
        axis=1,
    )
    normed_back, down_grad_b = own_rows(transposed_right(qkv_back, w_qkv).astype(BF), 8, (down_grad_b,))
    qkv_part = transposed_left(normed, qkv_back).astype(BF)
    _, norm_attn_back = jax.vjp(rms_scale, tokens_own.astype(F32), attention_gain)
    input_norm_back, gain_attn_part = norm_attn_back(normed_back)
    tokens_back_own = (middle_back + input_norm_back).astype(BF)

    expert_out = product(scaled[0], expert_down[0]) + product(scaled[1], other_down)
    mixed_part = (product(shared_act, shared_out) + spread(expert_out.astype(BF))).astype(BF)
    mixed_sum, up_grad_b = own_rows(mixed_part, 9, (up_grad_b,))
    mixed_own = (middle + mixed_sum).astype(BF)

    mixed, tokens_back = share([mixed_own, tokens_back_own], 6)
    small = jnp.concatenate([gain_attn_part[None], gain_mix_part[None], router_part], axis=0)
    small = small.reshape(experts + 2, 8, 1, dense).transpose(1, 2, 0, 3)
    small = jnp.broadcast_to(small, (8, 4, experts + 2, dense)).reshape(32, experts + 2, dense)
    small = lax.all_to_all(small, ALL, split_axis=0, concat_axis=0, tiled=True)
    small = jnp.sum(small, axis=0)
    shared_gu_grad = transposed_left(shared_gu_back, mix_all).astype(BF).reshape(2, wide, width)
    shared_down_part = transposed_left(shared_act, dy_all).astype(BF)
    home_rows = swap(qkv_part.reshape(8, dense, 3 * HDIM)).astype(F32)
    home_columns = swap(
        jnp.concatenate(
            [out_part, shared_gu_grad[0, :cut], shared_gu_grad[1, :cut], shared_down_part[:cut]],
            axis=0,
        )
        .reshape(HDIM + 3 * cut, 8, dense)
        .transpose(1, 0, 2)
    ).astype(F32)
    home_rows = home_rows[:4] + home_rows[4:]
    home_columns = home_columns[:4] + home_columns[4:]

    def columns_of(parts):
        return parts.transpose(1, 0, 2).reshape(dense, -1)

    def rows_of(parts):
        return parts.reshape(-1, dense)

    gate_grad = transposed_left(g_back[0], picked) + gate_grad_b.astype(F32)
    up_grad = transposed_left(u_back[0], picked) + up_grad_b.astype(F32)
    down_grad = transposed_left(scaled[0], picked_dy) + down_grad_b.astype(F32)
    return (
        mixed[None],
        tokens_back[None],
        small[0],
        columns_of(home_rows[:, :, :HDIM]),
        columns_of(home_rows[:, :, HDIM : 2 * HDIM]),
        columns_of(home_rows[:, :, 2 * HDIM : 3 * HDIM]),
        rows_of(home_columns[:, :HDIM]),
        small[1],
        small[2:].T,
        rows_of(home_columns[:, HDIM : HDIM + cut]).T,
        rows_of(home_columns[:, HDIM + cut : HDIM + 2 * cut]).T,
        rows_of(home_columns[:, HDIM + 2 * cut :]),
        gate_grad.T[None],
        up_grad.T[None],
        down_grad[None],
    )


def solution(mesh):
    sizes = dict(mesh.shape)

    def chosen(*args):
        heads = args[3].shape[1] * sizes["exp"] // HDIM
        one_head_each = heads == sizes["ctx"] * sizes["exp"]
        built_for = (sizes["dp"], sizes["ctx"], sizes["exp"]) == (2, 4, 4)
        return fast_body(*args) if one_head_each and built_for else body(*args)

    in_specs = (
        P("dp", "ctx", None),
        P("dp", "ctx", None),
        P(("dp", "ctx")),
        P(("dp", "ctx"), "exp"),
        P(("dp", "ctx"), "exp"),
        P(("dp", "ctx"), "exp"),
        P("exp", ("dp", "ctx")),
        P(("dp", "ctx")),
        P(("dp", "ctx"), None),
        P(("dp", "ctx"), "exp"),
        P(("dp", "ctx"), "exp"),
        P("exp", ("dp", "ctx")),
        P(("ctx", "exp"), None, "dp"),
        P(("ctx", "exp"), None, "dp"),
        P(("ctx", "exp"), "dp", None),
        P("dp", "ctx", None),
    )
    out_specs = (
        P("dp", "ctx", None),
        P("dp", "ctx", None),
        P(("dp", "ctx")),
        P(("dp", "ctx"), "exp"),
        P(("dp", "ctx"), "exp"),
        P(("dp", "ctx"), "exp"),
        P("exp", ("dp", "ctx")),
        P(("dp", "ctx")),
        P(("dp", "ctx"), None),
        P(("dp", "ctx"), "exp"),
        P(("dp", "ctx"), "exp"),
        P("exp", ("dp", "ctx")),
        P(("ctx", "exp"), None, "dp"),
        P(("ctx", "exp"), None, "dp"),
        P(("ctx", "exp"), "dp", None),
    )
    return jax.shard_map(chosen, mesh=mesh, in_specs=in_specs, out_specs=out_specs, check_vma=False)
```

```python
import functools

import jax
import jax.numpy as jnp
import numpy as np
from jax import lax
from jax.experimental import pallas as pl
from jax.experimental.pallas import tpu as pltpu
from jax.sharding import PartitionSpec as P

HDIM = 128
TOPK = 6


EPSILON = 1e-06
MASKED = -1e30
HIGHEST = lax.Precision.HIGHEST


def rms_scale(values, gain_row):
    return (
        values * lax.rsqrt(jnp.mean(values * values, axis=-1, keepdims=True) + EPSILON) * gain_row
    )


def rope_tables(positions, rope_width):
    inverse = 10000.0 ** (-jnp.arange(rope_width // 2).astype(jnp.float32) * 2.0 / rope_width)
    angles = positions.astype(jnp.float32)[:, None] * inverse[None, :]
    return (jnp.cos(angles), jnp.sin(angles))


def rotate(values, cosine, sine_table):
    half_size = values.shape[-1] // 2
    first_half = values[..., :half_size]
    second = values[..., half_size:]
    cosine = cosine[:, None, :]
    sine_table = sine_table[:, None, :]
    return jnp.concatenate(
        [first_half * cosine - second * sine_table, second * cosine + first_half * sine_table],
        axis=-1,
    )


def silu_mix(gate_rows, up_rows):
    return jax.nn.silu(gate_rows) * up_rows


def product(left_side, right_side):
    return jnp.dot(left_side, right_side, preferred_element_type=jnp.float32)


def transposed_left(left_side, right_side):
    return lax.dot_general(
        left_side, right_side, (((0,), (0,)), ((), ())), preferred_element_type=jnp.float32
    )


def transposed_right(left_side, right_side):
    return lax.dot_general(
        left_side, right_side, (((1,), (1,)), ((), ())), preferred_element_type=jnp.float32
    )


def place_rows(part, start_row, total_rows):
    blank = jnp.zeros((total_rows, part.shape[1]), jnp.float32)
    return lax.dynamic_update_slice_in_dim(blank, part, start_row, 0)


def to_owners(buffer):
    copies = lax.axis_size("dp")
    widened = jnp.broadcast_to(buffer[None], (copies,) + buffer.shape)
    widened = widened.reshape((copies * buffer.shape[0],) + buffer.shape[1:])
    return lax.all_to_all(widened, ("dp", "ctx", "exp"), split_axis=0, concat_axis=0, tiled=True)


def values_home(partial_value):
    returned = lax.all_to_all(
        partial_value, ("dp", "ctx", "exp"), split_axis=0, concat_axis=0, tiled=True
    )
    grouped = returned.reshape((lax.axis_size("dp"), -1) + returned.shape[1:])
    return jnp.sum(grouped.astype(jnp.float32), axis=0).astype(jnp.bfloat16)


def grads_home(partial_value):
    returned = lax.all_to_all(
        partial_value.astype(jnp.bfloat16),
        ("dp", "ctx", "exp"),
        split_axis=0,
        concat_axis=0,
        tiled=True,
    ).astype(partial_value.dtype)
    grouped = returned.reshape((lax.axis_size("dp"), -1) + returned.shape[1:])
    return jnp.sum(grouped, axis=0)


def body(
    tokens,
    routes,
    norm_attn,
    w_query,
    w_key,
    w_value,
    w_out,
    norm_mix,
    w_router,
    shared_gate,
    shared_up,
    shared_down,
    expert_gate,
    expert_up,
    expert_down,
    out_grad,
):
    gathered = (
        lax.all_gather(norm_attn, ("dp", "ctx"), axis=0, tiled=True),
        lax.all_gather(w_query, ("dp", "ctx"), axis=0, tiled=True),
        lax.all_gather(w_key, ("dp", "ctx"), axis=0, tiled=True),
        lax.all_gather(w_value, ("dp", "ctx"), axis=0, tiled=True),
        lax.all_gather(w_out, ("dp", "ctx"), axis=1, tiled=True),
        lax.all_gather(norm_mix, ("dp", "ctx"), axis=0, tiled=True),
        lax.all_gather(w_router, ("dp", "ctx"), axis=0, tiled=True),
        lax.all_gather(shared_gate, ("dp", "ctx"), axis=0, tiled=True),
        lax.all_gather(shared_up, ("dp", "ctx"), axis=0, tiled=True),
        lax.all_gather(shared_down, ("dp", "ctx"), axis=1, tiled=True),
    )
    (
        attention_gain,
        query_matrix,
        key_matrix,
        value_matrix,
        output_matrix,
        mixer_gain,
        router_matrix,
        shared_gate_matrix,
        shared_up_matrix,
        shared_down_matrix,
    ) = gathered
    rows_here = tokens.shape[1]
    model_width = tokens.shape[2]
    heads_here = query_matrix.shape[1] // HDIM
    quarter = rows_here // lax.axis_size("exp")
    start_row = lax.axis_index("exp") * quarter
    layer_input = tokens[0].astype(jnp.float32)
    grad_rows = out_grad[0]
    grad_float = grad_rows.astype(jnp.float32)
    seq_length = rows_here * lax.axis_size("ctx")
    positions = lax.axis_index("ctx") * rows_here + jnp.arange(rows_here, dtype=jnp.int32)
    cosine, sine_table = rope_tables(positions, HDIM)
    visible = positions[:, None] >= jnp.arange(seq_length, dtype=jnp.int32)[None, :]
    scale = HDIM ** (-0.5)
    head_shape = (rows_here, heads_here, HDIM)
    normed = rms_scale(layer_input, attention_gain).astype(jnp.bfloat16)
    query_rot = rotate(
        product(normed, query_matrix).reshape(head_shape), cosine, sine_table
    ).astype(jnp.bfloat16)
    key_rot = (
        rotate(product(normed, key_matrix).reshape(head_shape), cosine, sine_table)
        .astype(jnp.bfloat16)
        .reshape(rows_here, -1)
    )
    value_low = product(normed, value_matrix).astype(jnp.bfloat16)
    key_all, value_all = (
        lax.all_gather(key_rot, "ctx", axis=0, tiled=True),
        lax.all_gather(value_low, "ctx", axis=0, tiled=True),
    )
    key_heads = key_all.reshape(seq_length, heads_here, HDIM)
    value_heads = value_all.reshape(seq_length, heads_here, HDIM)

    def attention_scores():
        scores = (
            jnp.einsum("qhd,khd->hqk", query_rot, key_heads, preferred_element_type=jnp.float32)
            * scale
        )
        return jnp.where(visible[None], scores, MASKED)

    scores = attention_scores()
    largest = jnp.max(scores, axis=-1, keepdims=True)
    log_total = largest + jnp.log(jnp.sum(jnp.exp(scores - largest), axis=-1, keepdims=True))
    weights_low = jnp.exp(scores - log_total).astype(jnp.bfloat16)
    heads_out = (
        jnp.einsum("hqk,khd->qhd", weights_low, value_heads, preferred_element_type=jnp.float32)
        .reshape(rows_here, -1)
        .astype(jnp.bfloat16)
    )
    attn_total = lax.psum(product(heads_out, output_matrix), "exp")
    middle = layer_input + attn_total
    normed_mix = rms_scale(middle, mixer_gain).astype(jnp.bfloat16)
    normed_quarter = lax.dynamic_slice_in_dim(normed_mix, start_row, quarter, 0)
    route_quarter = lax.dynamic_slice_in_dim(routes[0], start_row, quarter, 0)
    grad_quarter = lax.dynamic_slice_in_dim(grad_rows, start_row, quarter, 0)
    logits = product(normed_quarter, router_matrix)
    probabilities = jax.nn.softmax(logits, axis=-1)
    owners = lax.axis_size(("ctx", "exp"))
    local_experts = expert_gate.shape[0]
    experts = local_experts * owners
    capacity = max(quarter * TOPK * 4 // (3 * experts), 2)
    expert_choice_index = jnp.arange(experts, dtype=jnp.int32)
    chosen = (route_quarter[:, :, None] == expert_choice_index[None, None, :]).astype(jnp.float32)
    gates = jnp.sum(chosen * probabilities[:, None, :], axis=-1)
    route_flat = route_quarter.reshape(-1)
    expert_hits = (route_flat[:, None] == expert_choice_index[None, :]).astype(jnp.int32)
    slot_index = jnp.sum(jnp.cumsum(expert_hits, axis=0) * expert_hits, axis=1) - 1
    slot_place = route_flat * capacity + slot_index
    matches = (
        jnp.arange(experts * capacity, dtype=jnp.int32)[:, None] == slot_place[None, :]
    ).astype(jnp.float32)
    dispatch = jnp.sum(matches.reshape(experts * capacity, quarter, TOPK), axis=2).astype(
        jnp.bfloat16
    )
    slot_gates = jnp.dot(matches, gates.reshape(-1), precision=HIGHEST)
    buffer_shape = (owners, local_experts, capacity, model_width)
    outgoing = product(dispatch, normed_quarter).astype(jnp.bfloat16).reshape(buffer_shape)
    arrived = to_owners(outgoing)
    gate_hidden = jnp.einsum(
        "sicd,idf->sicf", arrived, expert_gate, preferred_element_type=jnp.float32
    )
    up_hidden = jnp.einsum("sicd,idf->sicf", arrived, expert_up, preferred_element_type=jnp.float32)
    expert_act = silu_mix(gate_hidden, up_hidden).astype(jnp.bfloat16)
    partial_value = jnp.einsum(
        "sicf,ifd->sicd", expert_act, expert_down, preferred_element_type=jnp.float32
    ).astype(jnp.bfloat16)
    expert_values = values_home(partial_value).reshape(experts * capacity, model_width)
    route_values = expert_values[slot_place].astype(jnp.float32).reshape(quarter, TOPK, model_width)
    combined = jnp.sum(route_values * gates[:, :, None], axis=1)
    shared_gate_rows = product(normed_mix, shared_gate_matrix)
    shared_up_rows = product(normed_mix, shared_up_matrix)
    shared_act = silu_mix(shared_gate_rows, shared_up_rows).astype(jnp.bfloat16)
    branch_part = product(shared_act, shared_down_matrix) + place_rows(
        combined, start_row, rows_here
    )
    result = middle + lax.psum(branch_part.astype(jnp.bfloat16), "exp").astype(jnp.float32)
    grad_slots = (
        (product(dispatch, grad_quarter) * slot_gates[:, None])
        .astype(jnp.bfloat16)
        .reshape(buffer_shape)
    )
    grad_arrived = to_owners(grad_slots)
    act_grad = jnp.einsum(
        "sicd,ifd->sicf", grad_arrived, expert_down, preferred_element_type=jnp.float32
    )
    down_grad = jnp.einsum(
        "sicf,sicd->ifd", expert_act, grad_arrived, preferred_element_type=jnp.float32
    )
    _, mix_back = jax.vjp(silu_mix, gate_hidden, up_hidden)
    gate_back, up_back = mix_back(act_grad)
    gate_back = gate_back.astype(jnp.bfloat16)
    up_back = up_back.astype(jnp.bfloat16)
    gate_grad = jnp.einsum("sicd,sicf->idf", arrived, gate_back, preferred_element_type=jnp.float32)
    up_grad = jnp.einsum("sicd,sicf->idf", arrived, up_back, preferred_element_type=jnp.float32)
    input_back = jnp.einsum(
        "sicf,idf->sicd", gate_back, expert_gate, preferred_element_type=jnp.float32
    ) + jnp.einsum("sicf,idf->sicd", up_back, expert_up, preferred_element_type=jnp.float32)
    rows_back = grads_home(input_back).reshape(experts * capacity, model_width)
    moe_back = jnp.sum(rows_back[slot_place].reshape(quarter, TOPK, model_width), axis=1)
    gate_route_back = jnp.sum(route_values * grad_quarter.astype(jnp.float32)[:, None, :], axis=-1)
    prob_back = jnp.sum(chosen * gate_route_back[:, :, None], axis=1)
    _, soft_back = jax.vjp(lambda values: jax.nn.softmax(values, axis=-1), logits)
    logit_back = soft_back(prob_back)[0].astype(jnp.bfloat16)
    router_term = transposed_left(normed_quarter, logit_back)
    shared_back = transposed_right(grad_rows, shared_down_matrix)
    _, shared_mix_back = jax.vjp(silu_mix, shared_gate_rows, shared_up_rows)
    sgate_back, sup_back = shared_mix_back(shared_back)
    sgate_back = sgate_back.astype(jnp.bfloat16)
    sup_back = sup_back.astype(jnp.bfloat16)
    quarter_back = transposed_right(logit_back, router_matrix) + moe_back
    mix_part = (
        transposed_right(sgate_back, shared_gate_matrix)
        + transposed_right(sup_back, shared_up_matrix)
        + place_rows(quarter_back, start_row, rows_here)
    )
    mix_total, router_grad = (
        lax.psum(mix_part.astype(jnp.bfloat16), "exp").astype(jnp.float32),
        lax.psum(router_term.astype(jnp.bfloat16), "exp").astype(jnp.float32),
    )
    _, norm_mix_back = jax.vjp(rms_scale, middle, mixer_gain.astype(jnp.float32))
    middle_norm_back, gain_mix_grad = norm_mix_back(mix_total)
    middle_grad = grad_float + middle_norm_back
    sdown_grad = transposed_left(shared_act, grad_rows)
    sgate_grad = transposed_left(normed_mix, sgate_back)
    sup_grad = transposed_left(normed_mix, sup_back)
    attn_back = middle_grad.astype(jnp.bfloat16)
    heads_back = transposed_right(attn_back, output_matrix).astype(jnp.bfloat16).reshape(head_shape)
    weights_full = jnp.exp(attention_scores() - log_total)
    weights_again = weights_full.astype(jnp.bfloat16)
    weight_back = jnp.einsum(
        "qhd,khd->hqk", heads_back, value_heads, preferred_element_type=jnp.float32
    )
    value_term = jnp.einsum(
        "hqk,qhd->khd", weights_again, heads_back, preferred_element_type=jnp.float32
    ).reshape(seq_length, -1)
    score_back = (
        weights_full * (weight_back - jnp.sum(weights_full * weight_back, axis=-1, keepdims=True))
    ).astype(jnp.bfloat16)
    query_rot_back = (
        jnp.einsum("hqk,khd->qhd", score_back, key_heads, preferred_element_type=jnp.float32)
        * scale
    )
    key_term = (
        jnp.einsum("hqk,qhd->khd", score_back, query_rot, preferred_element_type=jnp.float32)
        * scale
    ).reshape(seq_length, -1)
    key_sum, value_sum = (
        lax.psum_scatter(
            key_term.astype(jnp.bfloat16), "ctx", scatter_dimension=0, tiled=True
        ).astype(jnp.float32),
        lax.psum_scatter(
            value_term.astype(jnp.bfloat16), "ctx", scatter_dimension=0, tiled=True
        ).astype(jnp.float32),
    )
    _, rotate_back = jax.vjp(
        lambda values: rotate(values, cosine, sine_table), jnp.zeros(head_shape, jnp.float32)
    )
    query_low = rotate_back(query_rot_back)[0].reshape(rows_here, -1).astype(jnp.bfloat16)
    key_low = (
        rotate_back(key_sum.reshape(head_shape))[0].reshape(rows_here, -1).astype(jnp.bfloat16)
    )
    value_back_low = value_sum.astype(jnp.bfloat16)
    normed_part = (
        transposed_right(query_low, query_matrix)
        + transposed_right(key_low, key_matrix)
        + transposed_right(value_back_low, value_matrix)
    )
    normed_back = lax.psum(normed_part.astype(jnp.bfloat16), "exp").astype(jnp.float32)
    _, norm_attn_back = jax.vjp(rms_scale, layer_input, attention_gain.astype(jnp.float32))
    input_norm_back, gain_attn_grad = norm_attn_back(normed_back)
    tokens_back = (middle_grad + input_norm_back).astype(jnp.bfloat16)
    out_weight_grad = transposed_left(heads_out, attn_back)
    query_grad = transposed_left(normed, query_low)
    key_grad = transposed_left(normed, key_low)
    value_grad = transposed_left(normed, value_back_low)
    all_sums = (
        lax.psum_scatter(
            gain_attn_grad.astype(jnp.bfloat16), ("dp", "ctx"), scatter_dimension=0, tiled=True
        ).astype(jnp.float32),
        lax.psum_scatter(
            query_grad.astype(jnp.bfloat16), ("dp", "ctx"), scatter_dimension=0, tiled=True
        ).astype(jnp.float32),
        lax.psum_scatter(
            key_grad.astype(jnp.bfloat16), ("dp", "ctx"), scatter_dimension=0, tiled=True
        ).astype(jnp.float32),
        lax.psum_scatter(
            value_grad.astype(jnp.bfloat16), ("dp", "ctx"), scatter_dimension=0, tiled=True
        ).astype(jnp.float32),
        lax.psum_scatter(
            out_weight_grad.astype(jnp.bfloat16), ("dp", "ctx"), scatter_dimension=1, tiled=True
        ).astype(jnp.float32),
        lax.psum_scatter(
            gain_mix_grad.astype(jnp.bfloat16), ("dp", "ctx"), scatter_dimension=0, tiled=True
        ).astype(jnp.float32),
        lax.psum_scatter(
            router_grad.astype(jnp.bfloat16), ("dp", "ctx"), scatter_dimension=0, tiled=True
        ).astype(jnp.float32),
        lax.psum_scatter(
            sgate_grad.astype(jnp.bfloat16), ("dp", "ctx"), scatter_dimension=0, tiled=True
        ).astype(jnp.float32),
        lax.psum_scatter(
            sup_grad.astype(jnp.bfloat16), ("dp", "ctx"), scatter_dimension=0, tiled=True
        ).astype(jnp.float32),
        lax.psum_scatter(
            sdown_grad.astype(jnp.bfloat16), ("dp", "ctx"), scatter_dimension=1, tiled=True
        ).astype(jnp.float32),
    )
    (
        gain_attn_sum,
        query_sum,
        key_sum_out,
        value_sum_out,
        out_sum,
        gain_mix_sum,
        router_sum,
        sgate_sum,
        sup_sum,
        sdown_sum,
    ) = all_sums
    return (
        result.astype(jnp.bfloat16)[None],
        tokens_back[None],
        gain_attn_sum,
        query_sum,
        key_sum_out,
        value_sum_out,
        out_sum,
        gain_mix_sum,
        router_sum,
        sgate_sum,
        sup_sum,
        sdown_sum,
        gate_grad,
        up_grad,
        down_grad,
    )


MESH = pl.DeviceIdType.MESH
BF = jnp.bfloat16
F32 = jnp.float32


class Place:
    def __init__(self):
        self.x = lax.axis_index("dp")
        self.z = lax.axis_index("ctx")
        self.e = lax.axis_index("exp")
        z = self.z
        high = lax.div(z, 2)
        self.zs = [z, z + 1 - 2 * lax.rem(z, 2), 2 - high, 3 - 3 * high]
        self.inner = 3 - z
        self.inside = lax.div(z * (3 - z), 2)
        self.middle = self.inside == 1
        self.dx = 1 - 2 * self.x
        self.dy = 2 - 4 * lax.div(self.e, 2)
        self.dc = 1 - 2 * lax.rem(self.e, 2)

    def device(self, ox=0, oe=0, zi=0):
        return (self.x + ox, self.zs[zi], self.e + oe)

    def inward(self):
        return (self.x, self.inner, self.e)

    def shard(self, oe, zi):
        return self.zs[zi] * 4 + self.e + oe


def greet(at, everyone, pair=False):
    barrier = pltpu.get_barrier_semaphore()
    peers = [at.device(zi=1), at.device(oe=at.dy), at.device(oe=at.dc)]
    if everyone or pair:
        peers.append(at.device(ox=at.dx))
    if everyone:
        peers += [at.device(zi=2), at.device(zi=3)]
    for peer in peers:
        pl.semaphore_signal(barrier, inc=1, device_id=peer, device_id_type=MESH)
    if everyone:
        pl.semaphore_wait(barrier, len(peers))
        return

    @pl.when(at.middle)
    def _():
        pl.semaphore_signal(barrier, inc=1, device_id=at.inward(), device_id_type=MESH)

    pl.semaphore_wait(barrier, len(peers) + at.inside)


def remote(src, dst, send, recv, device):
    return pltpu.make_async_remote_copy(
        src_ref=src, dst_ref=dst, send_sem=send, recv_sem=recv, device_id=device, device_id_type=MESH
    )


def cross(at, sent, got, send_sem, recv_sem):
    return [
        remote(a, b, send_sem.at[m], recv_sem.at[m], at.device(ox=at.dx))
        for m, (a, b) in enumerate(zip(sent, got))
    ]


class Exchange:
    def __init__(self, at, sent, got, local_sem, send_sem, recv_sem):
        self.at, self.sent, self.got = at, sent, got
        self.local_sem, self.send_sem, self.recv_sem = local_sem, send_sem, recv_sem
        self.waits = []

    def push(self, src, m, z_from, slot, device):
        at = self.at
        spot = self.got[m].at[at.x * 4 + z_from]
        copy = remote(
            src, spot, self.send_sem.at[m * 7 + slot], self.recv_sem.at[m * 8 + (0 if slot < 3 else 4) + z_from], device
        )
        copy.start()
        self.waits.append(copy)

    def start(self):
        at = self.at
        for m, sent in enumerate(self.sent):
            for zi in (1, 2, 3):
                self.push(sent.at[at.zs[zi]], m, at.z, zi - 1, at.device(zi=zi))
            self.push(sent.at[at.z], m, at.z, 3, at.device(ox=at.dx))
            pltpu.make_async_copy(
                sent.at[at.z], self.got[m].at[at.x * 4 + at.z], self.local_sem.at[m]
            ).start()

    def arrive(self, m, slot):
        src = self.sent[m].at[0]
        remote(
            src, self.got[m].at[0], self.send_sem.at[0], self.recv_sem.at[slot], self.at.device(ox=self.at.dx)
        ).wait_recv()

    def forward(self, zi):
        at = self.at
        for m in range(len(self.sent)):
            self.arrive(m, m * 8 + at.zs[zi])
            self.push(self.got[m].at[at.x * 4 + at.zs[zi]], m, at.zs[zi], 3 + zi, at.device(ox=at.dx))

    def finish(self):
        at = self.at
        for m, sent in enumerate(self.sent):
            for z in range(4):
                self.arrive(m, m * 8 + 4 + z)
            pltpu.make_async_copy(
                sent.at[at.z], self.got[m].at[at.x * 4 + at.z], self.local_sem.at[m]
            ).wait()
        for copy in self.waits:
            copy.wait_send()


def gather_kernel(block, rows, parts, extras, swaps, *refs):
    refs = list(refs)

    def take(count):
        taken = refs[:count]
        del refs[:count]
        return taken

    (x_ref,), sent, given = take(1), take(extras), take(swaps)
    (out_ref,), got, taken = take(1), take(extras), take(swaps)
    own_sem, send_sem, recv_sem = take(3)
    extra_sems = take(3 if extras else 0)
    at = Place()
    greet(at, extras > 0, swaps > 0)
    crossing = cross(at, given, taken, *refs) if swaps else []
    piece = rows // parts
    slot_z, slot_f, slot_s = 0, 3, 7
    started, inside = [], []
    firsts = 1 if block else 0
    shift = at.e * rows if block else 0

    def where(f, zi, p):
        return pl.ds(
            pl.multiple_of(at.shard(f * at.dy, zi) * rows + p * piece, piece), piece
        )

    def push(src, dst, slot, p, device, sends=None, record=None):
        k = slot * parts + p
        j = k if sends is None else sends * parts + p
        remote(src, out_ref.at[dst], send_sem.at[j], recv_sem.at[k], device).start()
        (started if record is None else record).append(j)

    f_dev, s_dev, z_dev = at.device(oe=at.dy), at.device(oe=at.dc), at.device(zi=1)

    def gone(j):
        remote(
            x_ref.at[pl.ds(0, piece)], out_ref.at[pl.ds(0, piece)], send_sem.at[j], recv_sem.at[0], s_dev
        ).wait_send()

    def arrive(slot, p):
        k = slot * parts + p
        remote(
            x_ref.at[pl.ds(0, piece)], out_ref.at[pl.ds(0, piece)], send_sem.at[k], recv_sem.at[k], s_dev
        ).wait_recv()

    if block:
        spot = pl.ds(pl.multiple_of(at.z * 4 * rows, 4 * rows), 4 * rows)
    else:
        spot = pl.ds(pl.multiple_of(at.shard(0, 0) * rows, rows), rows)
    own = pltpu.make_async_copy(x_ref, out_ref.at[spot], own_sem)

    def source(f, zi, p):
        if f == 0 and zi == 0:
            return x_ref.at[pl.ds(pl.multiple_of(shift + p * piece, piece), piece)]
        return out_ref.at[where(f, zi, p)]

    def along(zi, p):
        src, dst = source(0, zi, p), where(0, zi, p)
        if zi == 0:
            push(src, dst, slot_z, p, z_dev)
        if zi < 2:
            pl.when(at.middle)(
                lambda: push(src, dst, slot_z + 1 + zi, p, at.inward(), 15 + zi, inside)
            )
        else:
            pl.when(at.middle)(lambda: push(src, dst, slot_z + zi - 1, p, z_dev, 15 + zi, inside))

    def forward(f, zi, p):
        src, dst = source(f, zi, p), where(f, zi, p)
        if f == 0:
            along(zi, p)
        if zi >= firsts:
            if f == 0:
                push(src, dst, slot_f + zi, p, f_dev)
            push(src, dst, slot_s + f * 4 + zi, p, s_dev)

    for p in range(parts):
        forward(0, 0, p)
    own.start()
    for copy in crossing:
        copy.start()
    if extras:
        swap_in = Exchange(at, sent, got, *extra_sems)
        swap_in.start()
    for zi in range(4):
        if zi > 0:
            for p in range(parts):
                arrive(slot_z + zi - 1, p)
                forward(0, zi, p)
        if zi >= firsts:
            for p in range(parts):
                arrive(slot_f + zi, p)
                forward(1, zi, p)
        if extras and zi > 0:
            swap_in.forward(zi)
    for f in range(2):
        for zi in range(firsts, 4):
            for p in range(parts):
                arrive(slot_s + f * 4 + zi, p)
    own.wait()
    if extras:
        swap_in.finish()
    for copy in crossing:
        copy.wait()
    for j in started:
        gone(j)

    @pl.when(at.middle)
    def _():
        for j in inside:
            gone(j)


def all_rows(x, block, cid, sent=(), given=(), parts=2):
    rows, width = x.shape
    total = rows * (4 if block else 16)
    rows = rows // 4 if block else rows
    extras, swaps = len(sent), len(given)
    hbm = pl.BlockSpec(memory_space=pl.ANY)
    outs = [jax.ShapeDtypeStruct((total, width), x.dtype)]
    outs += [jax.ShapeDtypeStruct((8,) + a.shape[1:], a.dtype) for a in sent]
    outs += [jax.ShapeDtypeStruct(a.shape, a.dtype) for a in given]
    scratch = [
        pltpu.SemaphoreType.DMA,
        pltpu.SemaphoreType.DMA((19 * parts,)),
        pltpu.SemaphoreType.DMA((15 * parts,)),
    ]
    if extras:
        scratch += [
            pltpu.SemaphoreType.DMA((extras,)),
            pltpu.SemaphoreType.DMA((7 * extras,)),
            pltpu.SemaphoreType.DMA((8 * extras,)),
        ]
    if swaps:
        scratch += [pltpu.SemaphoreType.DMA((swaps,)), pltpu.SemaphoreType.DMA((swaps,))]
    got = pl.pallas_call(
        functools.partial(gather_kernel, block, rows, parts, extras, swaps),
        out_shape=outs,
        in_specs=[hbm] * len(outs),
        out_specs=[hbm] * len(outs),
        scratch_shapes=scratch,
        compiler_params=pltpu.CompilerParams(collective_id=cid, has_side_effects=True),
    )(x, *sent, *given)
    return got if extras or swaps else got[0]


class Scatter:
    def __init__(self, at, acc, got_s, got_f, got_z, send_sem, recv_sem, out_ref):
        self.at, self.acc, self.got_s, self.got_f, self.got_z = at, acc, got_s, got_f, got_z
        self.send_sem, self.recv_sem, self.out_ref = send_sem, recv_sem, out_ref
        self.rows = acc.shape[1]
        self.f_dev, self.s_dev, self.z_dev = (
            at.device(oe=at.dy),
            at.device(oe=at.dc),
            at.device(zi=1),
        )
        self.twins = [[], [], [], []]
        self.started, self.in_middle, self.at_end = [], [], []

    def push(self, src, dst, slot, device, sends=None, record=None):
        j = slot if sends is None else sends
        remote(src, dst, self.send_sem.at[j], self.recv_sem.at[slot], device).start()
        (self.started if record is None else record).append(j)

    def gone(self, j):
        spot = self.acc.at[0]
        remote(spot, spot, self.send_sem.at[j], self.recv_sem.at[0], self.s_dev).wait_send()

    def arrive(self, dst, slot):
        remote(
            self.acc.at[0], dst, self.send_sem.at[slot], self.recv_sem.at[slot], self.s_dev
        ).wait_recv()

    def to_twin(self, src, f, zi):
        k = f * 4 + zi
        self.push(src, self.got_s.at[k], 9 + k, self.s_dev, None, self.twins[zi])

    def twin_gone(self, zi):
        for j in self.twins[zi]:
            self.gone(j)
        self.twins[zi] = []

    def add(self, k, *others, into=None):
        acc = self.acc

        @pl.loop(0, self.rows // 16)
        def _(i):
            span = pl.ds(pl.multiple_of(i * 16, 16), 16)
            total = acc[k, span, :].astype(F32)
            for ref, j in others:
                total = total + ref[j, span, :].astype(F32)
            if into is None:
                acc[k, span, :] = total.astype(BF)
            else:
                into[span, :] = total

    def first(self, zi):
        k = 4 + zi
        self.arrive(self.got_s.at[k], 9 + k)
        self.add(k, (self.got_s, k))
        self.push(self.acc.at[k], self.got_f.at[zi], 5 + zi, self.f_dev)

    def second(self, zi):
        at, acc, got_z = self.at, self.acc, self.got_z
        self.arrive(self.got_s.at[zi], 9 + zi)
        self.arrive(self.got_f.at[zi], 5 + zi)
        others = [(self.got_s, zi), (self.got_f, zi)]
        if zi >= 2:

            @pl.when(at.middle)
            def _():
                self.arrive(got_z.at[3 - zi], 3 - zi)
                self.add(zi, *others, (got_z, 3 - zi))
                there = 4 if zi == 2 else 3
                self.push(acc.at[zi], got_z.at[there], there, at.inward(), zi, self.in_middle)

            @pl.when(jnp.logical_not(at.middle))
            def _():
                self.add(zi, *others)
                self.push(acc.at[zi], got_z.at[3 - zi], 3 - zi, self.z_dev, zi, self.at_end)
        elif zi == 1:

            @pl.when(at.middle)
            def _():
                self.arrive(got_z.at[3], 3)
                self.add(zi, *others, (got_z, 3))
                self.push(acc.at[zi], got_z.at[4], 4, self.z_dev, 1, self.in_middle)

            @pl.when(jnp.logical_not(at.middle))
            def _():
                self.add(zi, *others)
                self.push(acc.at[zi], got_z.at[2], 2, self.z_dev, 1, self.at_end)
        else:

            @pl.when(at.middle)
            def _():
                self.arrive(got_z.at[2], 2)
                self.arrive(got_z.at[4], 4)
                self.add(zi, *others, (got_z, 2), (got_z, 4), into=self.out_ref)

            @pl.when(jnp.logical_not(at.middle))
            def _():
                self.arrive(got_z.at[4], 4)
                self.add(zi, *others, (got_z, 4), into=self.out_ref)

    def finish(self):
        for zi in range(4):
            self.twin_gone(zi)
        for j in self.started:
            self.gone(j)

        @pl.when(self.at.middle)
        def _():
            for j in self.in_middle:
                self.gone(j)

        @pl.when(jnp.logical_not(self.at.middle))
        def _():
            for j in self.at_end:
                self.gone(j)


def scatter_buffers(rows, width):
    return [
        pltpu.VMEM((8, rows, width), BF),
        pltpu.VMEM((8, rows, width), BF),
        pltpu.VMEM((4, rows, width), BF),
        pltpu.VMEM((5, rows, width), BF),
        pltpu.SemaphoreType.DMA((17,)),
        pltpu.SemaphoreType.DMA((17,)),
    ]


def scatter_kernel(rows, swaps, in_ref, *refs):
    given, out_ref, taken = refs[:swaps], refs[swaps], refs[swaps + 1 : 2 * swaps + 1]
    buffers, load_sem = refs[2 * swaps + 1 : 2 * swaps + 7], refs[2 * swaps + 7]
    acc = buffers[0]
    at = Place()
    greet(at, False, swaps > 0)
    crossing = cross(at, given, taken, *refs[2 * swaps + 8 :]) if swaps else []
    total = Scatter(at, *buffers, out_ref)

    def rows_of(rank):
        return in_ref.at[pl.ds(pl.multiple_of(rank * rows, rows), rows)]

    order = [(f, zi) for f in (1, 0) for zi in (3, 2, 1, 0)]
    loads = {}
    for f, zi in order:
        k = f * 4 + zi
        total.to_twin(rows_of(at.shard(f * at.dy + at.dc, zi)), f, zi)
        loads[k] = pltpu.make_async_copy(
            rows_of(at.shard(f * at.dy, zi)), acc.at[k], load_sem.at[k]
        )
        loads[k].start()
    for copy in crossing:
        copy.start()
    for f, zi in order:
        loads[f * 4 + zi].wait()
        (total.first if f else total.second)(zi)
    for copy in crossing:
        copy.wait()
    total.finish()


def own_rows(x, cid, given=()):
    rows, width = x.shape[0] // 16, x.shape[1]
    swaps = len(given)
    hbm = pl.BlockSpec(memory_space=pl.ANY)
    crossing = [pltpu.SemaphoreType.DMA((swaps,))] * 2 if swaps else []
    got = pl.pallas_call(
        functools.partial(scatter_kernel, rows, swaps),
        out_shape=[jax.ShapeDtypeStruct((rows, width), F32)]
        + [jax.ShapeDtypeStruct(a.shape, a.dtype) for a in given],
        in_specs=[hbm] * (1 + swaps),
        out_specs=[pl.BlockSpec(memory_space=pltpu.VMEM)] + [hbm] * swaps,
        scratch_shapes=[
            *scatter_buffers(rows, width),
            pltpu.SemaphoreType.DMA((8,)),
            *crossing,
        ],
        compiler_params=pltpu.CompilerParams(
            collective_id=cid, has_side_effects=True, vmem_limit_bytes=40 * 1024 * 1024
        ),
    )(x, *given)
    return got if swaps else got[0]


def expert_gather_kernel(experts, *refs):
    refs = list(refs)

    def take(count):
        taken = refs[:count]
        del refs[:count]
        return taken

    x_ref, dy_ref, disp, w_router, shared_in, shared_out = take(6)
    weights = take(6)
    out_ref, picked, picked_dy, scaled_out, g_out, u_out, gb_out, sa_out, sg_out = take(9)
    wg, wu, wd, xb, dyb, pk, pdy, sc, gg, uu, gb, sa, sg = take(13)
    own_sem, send_sem, recv_sem, load_sem, block_sem, store_sem = take(6)
    at = Place()
    greet(at, False)
    rows = x_ref.shape[0]
    block = 4 * rows
    slots = pk.shape[1]
    groups = 4
    slot_z, slot_f, slot_s = 0, 3, 7
    started, inside = [], []
    mine = at.z * 4 + at.e

    def where(f, zi):
        return pl.ds(pl.multiple_of(at.shard(f * at.dy, zi) * rows, rows), rows)

    def push(src, dst, slot, device, sends=None, record=None):
        j = slot if sends is None else sends
        remote(src, out_ref.at[dst], send_sem.at[j], recv_sem.at[slot], device).start()
        (started if record is None else record).append(j)

    f_dev, s_dev, z_dev = at.device(oe=at.dy), at.device(oe=at.dc), at.device(zi=1)

    def gone(j):
        remote(x_ref, out_ref.at[pl.ds(0, rows)], send_sem.at[j], recv_sem.at[0], s_dev).wait_send()

    def arrive(slot):
        remote(
            x_ref, out_ref.at[pl.ds(0, rows)], send_sem.at[slot], recv_sem.at[slot], s_dev
        ).wait_recv()

    own = pltpu.make_async_copy(x_ref, out_ref.at[where(0, 0)], own_sem)

    def source(f, zi):
        return x_ref if f == 0 and zi == 0 else out_ref.at[where(f, zi)]

    def along(zi):
        src, dst = source(0, zi), where(0, zi)
        if zi == 0:
            push(src, dst, slot_z, z_dev)
        if zi < 2:
            pl.when(at.middle)(lambda: push(src, dst, slot_z + 1 + zi, at.inward(), 15 + zi, inside))
        else:
            pl.when(at.middle)(lambda: push(src, dst, slot_z + zi - 1, z_dev, 15 + zi, inside))

    def forward(f, zi):
        src, dst = source(f, zi), where(f, zi)
        if f == 0:
            along(zi)
            push(src, dst, slot_f + zi, f_dev)
        push(src, dst, slot_s + f * 4 + zi, s_dev)

    def span(zi, size):
        return pl.ds(pl.multiple_of(at.zs[zi] * size, size), size)

    def dy_load(zi):
        return pltpu.make_async_copy(
            dy_ref.at[span(zi, block)], dyb.at[zi % 2], block_sem.at[2 + zi % 2]
        )

    def x_load(zi):
        return pltpu.make_async_copy(
            out_ref.at[span(zi, block)], xb.at[zi % 2], block_sem.at[zi % 2]
        )

    def stores(zi):
        b = zi % 2
        pairs = [
            (pk.at[b], picked.at[span(zi, slots)]),
            (pdy.at[b], picked_dy.at[span(zi, slots)]),
            (gb.at[b], gb_out.at[span(zi, slots)]),
            (sa.at[b], sa_out.at[span(zi, block)]),
            (sg.at[b], sg_out.at[span(zi, block)]),
        ]
        for h in range(2):
            pairs += [
                (sc.at[b, h], scaled_out.at[h, span(zi, slots)]),
                (gg.at[b, h], g_out.at[h, span(zi, slots)]),
                (uu.at[b, h], u_out.at[h, span(zi, slots)]),
            ]
        return [
            pltpu.make_async_copy(src, dst, store_sem.at[b, j]) for j, (src, dst) in enumerate(pairs)
        ]

    def parts_of(gate, up):
        s = 1.0 / (1.0 + jnp.exp(-gate))
        act = gate * s
        return act * up, s * (1.0 + gate * (1.0 - s)) * up, act

    def work(zi):
        b = zi % 2
        dy_load(zi).wait()
        x_load(zi).wait()
        if zi >= 2:
            for copy in stores(zi - 2):
                copy.wait()

        @pl.loop(0, groups)
        def _(i):
            hot = disp[at.zs[zi] * groups + i]
            source_rows = pl.ds(pl.multiple_of(i * rows, rows), rows)
            into = pl.ds(pl.multiple_of(i * (slots // groups), slots // groups), slots // groups)
            pk[b, into, :] = product(hot, xb[b, source_rows, :]).astype(BF)
            pdy[b, into, :] = product(hot, dyb[b, source_rows, :]).astype(BF)

        logits = transposed_right(pk[b], w_router[...])
        lane = lax.broadcasted_iota(jnp.int32, logits.shape, 1)
        logits = jnp.where(lane < experts, logits, MASKED)
        powers = jnp.exp(logits - jnp.max(logits, axis=1, keepdims=True))
        own_power = jnp.sum(jnp.where(lane == mine, powers, 0.0), axis=1, keepdims=True)
        gate_of = own_power / jnp.sum(powers, axis=1, keepdims=True)
        gb[b] = jnp.zeros(gb.shape[1:], F32)

        @pl.loop(0, 2)
        def _(h):
            hidden, by_gate, by_up = parts_of(
                transposed_right(pk[b], wg[h]), transposed_right(pk[b], wu[h])
            )
            dy_down = transposed_right(pdy[b], wd[h])
            act_back = gate_of * dy_down
            gg[b, h] = (act_back * by_gate).astype(BF)
            uu[b, h] = (act_back * by_up).astype(BF)
            sc[b, h] = (hidden * gate_of).astype(BF)
            gb[b] += jnp.broadcast_to(
                jnp.sum(hidden * dy_down, axis=1, keepdims=True), gb.shape[1:]
            )

        @pl.loop(0, groups)
        def _(i):
            token_rows = pl.ds(pl.multiple_of(i * rows, rows), rows)
            both = transposed_right(xb[b, token_rows, :], shared_in[...])
            wide = both.shape[1] // 2
            hidden, by_gate, by_up = parts_of(both[:, :wide], both[:, wide:])
            back = transposed_right(dyb[b, token_rows, :], shared_out[...])
            sa[b, token_rows, :] = hidden.astype(BF)
            sg[b, token_rows, :wide] = (back * by_gate).astype(BF)
            sg[b, token_rows, wide:] = (back * by_up).astype(BF)

        for copy in stores(zi):
            copy.start()

    forward(0, 0)
    own.start()
    loads = []
    for m, (ref, half) in enumerate([(wg, 0), (wu, 0), (wd, 0), (wg, 1), (wu, 1), (wd, 1)]):
        loads.append(pltpu.make_async_copy(weights[m], ref.at[half], load_sem.at[m]))
        loads[-1].start()
    dy_load(0).start()
    for zi in range(4):
        arrive(slot_f + zi)
        forward(1, zi)
        if zi < 3:
            arrive(slot_z + zi)
            forward(0, zi + 1)
            dy_load(zi + 1).start()
        for f in range(2):
            arrive(slot_s + f * 4 + zi)
        if zi == 0:
            own.wait()
            for copy in loads:
                copy.wait()
        x_load(zi).start()
        work(zi)
    for zi in (2, 3):
        for copy in stores(zi):
            copy.wait()
    for j in started:
        gone(j)

    @pl.when(at.middle)
    def _():
        for j in inside:
            gone(j)


def expert_rows(x, dy_all, dispatch, w_router, experts, shared_in, shared_out, weights, cid):
    rows, width = x.shape
    total, block = 16 * rows, 4 * rows
    slots = 4 * dispatch.shape[1]
    hidden = weights[0].shape[0]
    wide = shared_out.shape[0]
    hbm, vmem = pl.BlockSpec(memory_space=pl.ANY), pl.BlockSpec(memory_space=pltpu.VMEM)
    shape = jax.ShapeDtypeStruct
    return pl.pallas_call(
        functools.partial(expert_gather_kernel, experts),
        out_shape=[
            shape((total, width), BF),
            shape((4 * slots, width), BF),
            shape((4 * slots, width), BF),
            shape((2, 4 * slots, hidden), BF),
            shape((2, 4 * slots, hidden), BF),
            shape((2, 4 * slots, hidden), BF),
            shape((4 * slots, 128), F32),
            shape((total, wide), BF),
            shape((total, 2 * wide), BF),
        ],
        in_specs=[hbm, hbm, vmem, vmem, vmem, vmem] + [hbm] * 6,
        out_specs=[hbm] * 9,
        scratch_shapes=[
            pltpu.VMEM((2, hidden, width), BF),
            pltpu.VMEM((2, hidden, width), BF),
            pltpu.VMEM((2, hidden, width), BF),
            pltpu.VMEM((2, block, width), BF),
            pltpu.VMEM((2, block, width), BF),
            pltpu.VMEM((2, slots, width), BF),
            pltpu.VMEM((2, slots, width), BF),
            pltpu.VMEM((2, 2, slots, hidden), BF),
            pltpu.VMEM((2, 2, slots, hidden), BF),
            pltpu.VMEM((2, 2, slots, hidden), BF),
            pltpu.VMEM((2, slots, 128), F32),
            pltpu.VMEM((2, block, wide), BF),
            pltpu.VMEM((2, block, 2 * wide), BF),
            pltpu.SemaphoreType.DMA,
            pltpu.SemaphoreType.DMA((19,)),
            pltpu.SemaphoreType.DMA((15,)),
            pltpu.SemaphoreType.DMA((6,)),
            pltpu.SemaphoreType.DMA((4,)),
            pltpu.SemaphoreType.DMA((2, 11)),
        ],
        compiler_params=pltpu.CompilerParams(
            collective_id=cid, has_side_effects=True, vmem_limit_bytes=60 * 1024 * 1024
        ),
    )(x, dy_all, dispatch, w_router, shared_in, shared_out, *weights)


def expert_scatter_kernel(*refs):
    refs = list(refs)

    def take(count):
        taken = refs[:count]
        del refs[:count]
        return taken

    disp, gate_back, shared_in, g_ref, u_ref, sg_ref, picked_ref, dy_ref, scaled_ref = take(9)
    weights = take(4)
    out_ref, taken, *grads = take(7)
    wg, wu, gs, us, sg, picked, picked_dy, scaled, ib, grad, turned = take(11)
    acc, got_s, got_f, got_z, send_sem, recv_sem = take(6)
    out_s, load_sem, store_sem, cross_send, cross_recv = take(5)
    at = Place()
    greet(at, False, True)
    rows, full = acc.shape[1:]
    width = shared_in.shape[1]
    slots = ib.shape[0]
    capacity = slots // 4
    mine = at.z * 4 + at.e
    total = Scatter(at, acc, got_s, got_f, got_z, send_sem, recv_sem, out_ref)

    pairs = [
        (weights[0], wg.at[0]),
        (weights[1], wu.at[0]),
        (weights[2], wg.at[1]),
        (weights[3], wu.at[1]),
        (g_ref, gs),
        (u_ref, us),
        (sg_ref, sg),
        (picked_ref, picked),
        (dy_ref, picked_dy),
        (scaled_ref.at[1], scaled),
    ]
    loads = [pltpu.make_async_copy(a, b, load_sem.at[j]) for j, (a, b) in enumerate(pairs)]
    for copy in loads:
        copy.start()

    def work(zi):
        place = at.zs[zi]
        some = pl.ds(pl.multiple_of(place * slots, slots), slots)

        @pl.loop(0, 4)
        def _(n):
            columns = pl.ds(pl.multiple_of(n * (width // 4), width // 4), width // 4)
            terms = product(gs[0, some, :], wg[0, :, columns])
            terms += product(us[0, some, :], wu[0, :, columns])
            terms += product(gs[1, some, :], wg[1, :, columns])
            terms += product(us[1, some, :], wu[1, :, columns])
            ib[:, columns] = terms.astype(BF)

        for twin in range(2):
            for f in range(2):
                e = at.e + f * at.dy + twin * at.dc
                hot = disp[place * 4 + e]
                mine_slots = pl.ds(pl.multiple_of(e * capacity, capacity), capacity)
                tokens = pl.ds(pl.multiple_of((place * 4 + e) * rows, rows), rows)
                into, k = (out_s, f * 2 + zi % 2) if twin else (acc, f * 4 + zi)

                @pl.loop(0, 2)
                def _(n):
                    columns = pl.ds(pl.multiple_of(n * (width // 2), width // 2), width // 2)
                    terms = transposed_left(hot, ib[mine_slots, columns])
                    terms += product(sg[tokens, :], shared_in[:, columns])
                    into[k, :, columns] = terms.astype(BF)

                from_gates = gate_back[
                    pl.ds(pl.multiple_of(place * slots + e * capacity, capacity), capacity), :
                ]
                lane = lax.broadcasted_iota(jnp.int32, from_gates.shape, 1)
                from_gates = jnp.where(lane == mine, from_gates, 0.0).astype(BF)
                into[k, :, width:] = transposed_left(hot, from_gates).astype(BF)

    def gradient(m):
        step = 256
        right = picked_dy if m == 2 else picked
        turned[...] = (scaled[...] if m == 2 else gs[1] if m == 0 else us[1]).T

        @pl.loop(0, width // step)
        def _(n):
            columns = pl.ds(pl.multiple_of(n * step, step), step)
            grad[m, :, columns] = product(turned[...], right[:, columns]).astype(BF)

    part = grad.shape[1] // 2
    crossing = cross(at, [grad.at[0, pl.ds(0, part)]], [taken], cross_send, cross_recv)[0]
    stores = [
        pltpu.make_async_copy(grad.at[j // 2, pl.ds(j % 2 * part, part)], grads[j - 1], store_sem.at[j])
        for j in range(1, 6)
    ]
    for copy in loads[:7]:
        copy.wait()
    for zi in (3, 2, 1, 0):
        if zi < 2:
            total.twin_gone(zi + 2)
        work(zi)
        for f in range(2):
            total.to_twin(out_s.at[f * 2 + zi % 2], f, zi)
        total.first(zi)
        if zi == 1:
            total.second(3)
    for copy in loads[7:]:
        copy.wait()
    for m, zi in ((0, 2), (1, 1), (2, 0)):
        gradient(m)
        if m == 0:
            crossing.start()
        for j in (2 * m, 2 * m + 1):
            if j > 0:
                stores[j - 1].start()
        total.second(zi)
    for copy in stores:
        copy.wait()
    crossing.wait()
    total.finish()


def expert_back(dispatch, gate_back, shared_in, g, u, sg, picked, picked_dy, scaled, weights, cid):
    total, wide = sg.shape
    width = shared_in.shape[1]
    rows, full = total // 16, width + 128
    slots = picked.shape[0]
    hidden = g.shape[2]
    hbm, vmem = pl.BlockSpec(memory_space=pl.ANY), pl.BlockSpec(memory_space=pltpu.VMEM)
    shape = jax.ShapeDtypeStruct
    return pl.pallas_call(
        expert_scatter_kernel,
        out_shape=[
            shape((rows, full), F32),
            *[shape((hidden // 2, width), BF)] * 6,
        ],
        in_specs=[vmem] * 3 + [hbm] * 10,
        out_specs=[vmem] + [hbm] * 6,
        scratch_shapes=[
            pltpu.VMEM((2, hidden, width), BF),
            pltpu.VMEM((2, hidden, width), BF),
            pltpu.VMEM((2, slots, hidden), BF),
            pltpu.VMEM((2, slots, hidden), BF),
            pltpu.VMEM((total, wide), BF),
            pltpu.VMEM((slots, width), BF),
            pltpu.VMEM((slots, width), BF),
            pltpu.VMEM((slots, hidden), BF),
            pltpu.VMEM((slots // 4, width), BF),
            pltpu.VMEM((3, hidden, width), BF),
            pltpu.VMEM((hidden, slots), BF),
            *scatter_buffers(rows, full),
            pltpu.VMEM((4, rows, full), BF),
            pltpu.SemaphoreType.DMA((10,)),
            pltpu.SemaphoreType.DMA((6,)),
            pltpu.SemaphoreType.DMA((1,)),
            pltpu.SemaphoreType.DMA((1,)),
        ],
        compiler_params=pltpu.CompilerParams(
            collective_id=cid, has_side_effects=True, vmem_limit_bytes=63 * 1024 * 1024
        ),
    )(dispatch, gate_back, shared_in, g, u, sg, picked, picked_dy, scaled, *weights)


def mixed_kernel(*refs):
    refs = list(refs)

    def take(count):
        taken = refs[:count]
        del refs[:count]
        return taken

    w_out, w_qkv, tables, q_ref, k_ref, v_ref, lse_ref, heads_out = take(8)
    in_ref, back_ref, normed_ref, *given = take(5)
    out_ref, normed_back, qkv_grad, out_grad, *taken = take(6)
    rows_in, do, dk, dv, qkv, out_sum, qkv_sum, staged = take(8)
    buffers = take(6)
    first_sem, in_sem, store_sem, cross_send, cross_recv = take(5)
    at = Place()
    greet(at, False, True)
    total = Scatter(at, *buffers, out_ref)
    acc = buffers[0]
    rows, width = acc.shape[1:]
    length = q_ref.shape[0]
    block = length // 4
    crossing = cross(at, given, taken, cross_send, cross_recv)

    def rows_of(rank):
        return in_ref.at[pl.ds(pl.multiple_of(rank * rows, rows), rows)]

    order = [(f, zi) for f in (1, 0) for zi in (3, 2, 1, 0)]
    firsts = {}
    for f, zi in order:
        m = f * 4 + zi
        total.to_twin(rows_of(at.shard(f * at.dy + at.dc, zi)), f, zi)
        firsts[m] = pltpu.make_async_copy(
            rows_of(at.shard(f * at.dy, zi)), acc.at[m], first_sem.at[m]
        )
        firsts[m].start()
    for copy in crossing:
        copy.start()

    def rows_load(j):
        ref = back_ref if j < 4 else normed_ref
        return pltpu.make_async_copy(
            ref.at[pl.ds(j % 4 * block, block)], rows_in.at[j % 2], in_sem.at[j % 2]
        )

    rows_load(0).start()
    rows_load(1).start()

    def heads_back(j):
        rows_load(j).wait()
        here = pl.ds(j * block, block)
        do[here, :] = transposed_right(rows_in[j % 2], w_out[...]).astype(BF)
        turned = heads_out[here, :].T

        @pl.loop(0, 4)
        def _(n):
            columns = pl.ds(pl.multiple_of(n * (width // 4), width // 4), width // 4)
            terms = product(turned, rows_in[j % 2, :, columns])
            out_sum[:, columns] = terms if j == 0 else out_sum[:, columns] + terms

        rows_load(j + 2).start()

    scale = HDIM ** (-0.5)
    step = 256

    def attend_rows(i):
        seen = (i + 1) * step
        here = pl.ds(i * step, step)
        q, go = q_ref[here, :], do[here, :]
        scores = transposed_right(q, k_ref[0:seen, :]) * scale
        row_at = lax.broadcasted_iota(jnp.int32, scores.shape, 0) + i * step
        col_at = lax.broadcasted_iota(jnp.int32, scores.shape, 1)
        scores = jnp.where(row_at >= col_at, scores, MASKED)
        probs = jnp.exp(scores - lse_ref[here, 0:1])
        weight_back = transposed_right(go, v_ref[0:seen, :])
        inner = jnp.sum(probs * weight_back, axis=-1, keepdims=True)
        score_back = (probs * (weight_back - inner)).astype(BF)
        dv[0:seen, :] += transposed_left(probs.astype(BF), go)
        dk[0:seen, :] += transposed_left(score_back, q) * scale
        qkv[here, 0:HDIM] = turn_rows(product(score_back, k_ref[0:seen, :]) * scale, here)

    def turn_rows(values, here):
        other = pltpu.roll(values, HDIM // 2, 1)
        return (values * tables[0, here, :] + other * tables[1, here, :]).astype(BF)

    def finish_heads():
        for j in range(8):
            here = pl.ds(j * step, step)
            qkv[here, HDIM : 2 * HDIM] = turn_rows(dk[here, :], here)
            qkv[here, 2 * HDIM :] = dv[here, :].astype(BF)

    def normed_store(j):
        return pltpu.make_async_copy(
            staged.at[j % 2], normed_back.at[pl.ds(j * step, step)], store_sem.at[j % 2]
        )

    def normed_rows(j):
        if j >= 2:
            normed_store(j - 2).wait()

        @pl.loop(0, 4)
        def _(n):
            columns = pl.ds(pl.multiple_of(n * (width // 4), width // 4), width // 4)
            staged[j % 2, :, columns] = product(
                qkv[pl.ds(j * step, step), :], w_qkv[:, columns]
            ).astype(BF)

        normed_store(j).start()

    def qkv_rows(j):
        rows_load(4 + j).wait()
        turned = qkv[pl.ds(j * block, block), :].T

        @pl.loop(0, 4)
        def _(n):
            columns = pl.ds(pl.multiple_of(n * (width // 4), width // 4), width // 4)
            terms = product(turned, rows_in[j % 2, :, columns])
            qkv_sum[:, columns] = terms if j == 0 else qkv_sum[:, columns] + terms

        if j < 2:
            rows_load(6 + j).start()

    for zi in (3, 2, 1, 0):
        firsts[4 + zi].wait()
        total.first(zi)
    for j in range(4):
        heads_back(j)
    firsts[3].wait()
    total.second(3)
    dk[...] = jnp.zeros_like(dk)
    dv[...] = jnp.zeros_like(dv)
    for i in range(3):
        attend_rows(i)
    firsts[2].wait()
    total.second(2)
    for i in range(3, 6):
        attend_rows(i)
    firsts[1].wait()
    total.second(1)
    for i in range(6, 8):
        attend_rows(i)
    finish_heads()
    for j in range(8):
        normed_rows(j)
    for j in range(4):
        qkv_rows(j)
    qkv_grad[...] = qkv_sum[...].astype(BF)
    out_grad[...] = out_sum[...].astype(BF)
    firsts[0].wait()
    total.second(0)
    for j in (6, 7):
        normed_store(j).wait()
    for copy in crossing:
        copy.wait()
    total.finish()


def mixed_rows(
    w_out, w_qkv, tables, q, k, v, lse, heads_out, mixed_part, attn_back, normed, given, cid
):
    length, width = attn_back.shape
    rows = length // 16
    hbm, vmem = pl.BlockSpec(memory_space=pl.ANY), pl.BlockSpec(memory_space=pltpu.VMEM)
    shape = jax.ShapeDtypeStruct
    return pl.pallas_call(
        mixed_kernel,
        out_shape=[
            shape((rows, width), F32),
            shape((length, width), BF),
            shape((3 * HDIM, width), BF),
            shape((HDIM, width), BF),
            *[shape(a.shape, BF) for a in given],
        ],
        in_specs=[vmem] * 8 + [hbm] * 5,
        out_specs=[vmem, hbm, vmem, vmem, hbm, hbm],
        scratch_shapes=[
            pltpu.VMEM((2, length // 4, width), BF),
            pltpu.VMEM((length, HDIM), BF),
            pltpu.VMEM((length, HDIM), F32),
            pltpu.VMEM((length, HDIM), F32),
            pltpu.VMEM((length, 3 * HDIM), BF),
            pltpu.VMEM((HDIM, width), F32),
            pltpu.VMEM((3 * HDIM, width), F32),
            pltpu.VMEM((2, 256, width), BF),
            *scatter_buffers(rows, width),
            pltpu.SemaphoreType.DMA((8,)),
            pltpu.SemaphoreType.DMA((2,)),
            pltpu.SemaphoreType.DMA((2,)),
            pltpu.SemaphoreType.DMA((2,)),
            pltpu.SemaphoreType.DMA((2,)),
        ],
        compiler_params=pltpu.CompilerParams(
            collective_id=cid, has_side_effects=True, vmem_limit_bytes=63 * 1024 * 1024
        ),
    )(w_out, w_qkv, tables, q, k, v, lse, heads_out, mixed_part, attn_back, normed, *given)


class Gather:
    def __init__(self, at, x_ref, out_ref, own_sem, send_sem, recv_sem):
        self.at, self.x_ref, self.out_ref = at, x_ref, out_ref
        self.send_sem, self.recv_sem = send_sem, recv_sem
        self.rows = x_ref.shape[0]
        self.f_dev, self.s_dev, self.z_dev = (
            at.device(oe=at.dy),
            at.device(oe=at.dc),
            at.device(zi=1),
        )
        self.started, self.inside = [], []
        self.own = pltpu.make_async_copy(x_ref, out_ref.at[self.where(0, 0)], own_sem)

    def where(self, f, zi):
        rows = self.rows
        return pl.ds(pl.multiple_of(self.at.shard(f * self.at.dy, zi) * rows, rows), rows)

    def push(self, f, zi, slot, device, sends=None, record=None):
        src = self.x_ref if f == 0 and zi == 0 else self.out_ref.at[self.where(f, zi)]
        dst = self.out_ref.at[self.where(f, zi)]
        j = slot if sends is None else sends
        remote(src, dst, self.send_sem.at[j], self.recv_sem.at[slot], device).start()
        (self.started if record is None else record).append(j)

    def spot(self):
        return self.x_ref, self.out_ref.at[pl.ds(0, self.rows)]

    def arrive(self, slot):
        remote(*self.spot(), self.send_sem.at[slot], self.recv_sem.at[slot], self.s_dev).wait_recv()

    def forward(self, f, zi):
        if f == 0:
            if zi == 0:
                self.push(0, 0, 0, self.z_dev)
            if zi < 2:
                pl.when(self.at.middle)(
                    lambda: self.push(0, zi, 1 + zi, self.at.inward(), 15 + zi, self.inside)
                )
            else:
                pl.when(self.at.middle)(
                    lambda: self.push(0, zi, zi - 1, self.z_dev, 15 + zi, self.inside)
                )
            self.push(0, zi, 3 + zi, self.f_dev)
        self.push(f, zi, 7 + f * 4 + zi, self.s_dev)

    def begin(self):
        self.forward(0, 0)
        self.own.start()

    def line(self, zi):
        self.arrive(zi - 1)
        self.forward(0, zi)

    def other(self, zi):
        self.arrive(3 + zi)
        self.forward(1, zi)

    def finish(self):
        for k in range(8):
            self.arrive(7 + k)
        self.own.wait()
        for j in self.started:
            remote(*self.spot(), self.send_sem.at[j], self.recv_sem.at[0], self.s_dev).wait_send()

        @pl.when(self.at.middle)
        def _():
            for j in self.inside:
                remote(
                    *self.spot(), self.send_sem.at[j], self.recv_sem.at[0], self.s_dev
                ).wait_send()


def columns_loop(width, parts):
    size = width // parts

    def over(run):
        @pl.loop(0, parts)
        def _(n):
            run(pl.ds(pl.multiple_of(n * size, size), size))

    return over


def gather_back_kernel(*refs):
    refs = list(refs)

    def take(count):
        taken = refs[:count]
        del refs[:count]
        return taken

    x_ref, disp, shared_out = take(3)
    scaled_ref, act_ref, sg_ref, wd_a, wd_b, mix_ref, dy_ref, *given = take(9)
    out_ref, mixed_part, units_grad, *taken = take(5)
    scaled, acts, sg, wd, eb, rows_in, staged, unit_sum = take(8)
    own_sem, send_sem, recv_sem, cross_send, cross_recv, load_sem, in_sem, store_sem = take(8)
    at = Place()
    greet(at, False, True)
    gather = Gather(at, x_ref, out_ref, own_sem, send_sem, recv_sem)
    crossing = cross(at, given, taken, cross_send, cross_recv)
    rows, width = x_ref.shape
    slots = eb.shape[0]
    capacity = slots // 4
    block = 4 * rows
    units = acts.shape[1]
    over = columns_loop(width, 4)

    gather.begin()
    for copy in crossing:
        copy.start()
    pairs = [
        (scaled_ref, scaled),
        (act_ref, acts),
        (wd_a, wd.at[0]),
        (wd_b, wd.at[1]),
        (sg_ref, sg),
    ]
    loads = [pltpu.make_async_copy(a, b, load_sem.at[j]) for j, (a, b) in enumerate(pairs)]
    for copy in loads:
        copy.start()

    def rows_load(j):
        ref = mix_ref if j < 4 else dy_ref
        return pltpu.make_async_copy(
            ref.at[pl.ds(j % 4 * block, block)], rows_in.at[j % 2], in_sem.at[j % 2]
        )

    def mixed_store(j):
        return pltpu.make_async_copy(
            staged.at[j % 2], mixed_part.at[pl.ds(j * block, block)], store_sem.at[j % 2]
        )

    def mixed_rows_of(j):
        some = pl.ds(j * slots, slots)

        @over
        def _(columns):
            terms = product(scaled[0, some, :], wd[0, :, columns])
            terms += product(scaled[1, some, :], wd[1, :, columns])
            eb[:, columns] = terms.astype(BF)

        if j >= 2:
            mixed_store(j - 2).wait()
        for i in range(4):
            hot = disp[j * 4 + i]

            @over
            def _(columns):
                terms = transposed_left(hot, eb[pl.ds(i * capacity, capacity), columns])
                terms += product(acts[pl.ds((j * 4 + i) * rows, rows), :], shared_out[:, columns])
                staged[j % 2, pl.ds(i * rows, rows), columns] = terms.astype(BF)

        mixed_store(j).start()

    def units_of(j):
        rows_load(j).wait()
        here = pl.ds(j % 4 * block, block)
        turned = (sg[here, :] if j < 4 else acts[here, :]).T
        into = pl.ds(0, 2 * units) if j < 4 else pl.ds(2 * units, units)

        @over
        def _(columns):
            terms = product(turned, rows_in[j % 2, :, columns])
            unit_sum[into, columns] = terms if j % 4 == 0 else unit_sum[into, columns] + terms

        if j < 6:
            rows_load(j + 2).start()

    rows_load(0).start()
    rows_load(1).start()
    for copy in loads:
        copy.wait()
    for zi in range(4):
        if zi > 0:
            gather.line(zi)
        mixed_rows_of(zi)
        gather.other(zi)
        units_of(2 * zi)
        units_of(2 * zi + 1)
    units_grad[...] = unit_sum[...].astype(BF)
    for j in (2, 3):
        mixed_store(j).wait()
    for copy in crossing:
        copy.wait()
    gather.finish()


def gather_back(x, given, dispatch, shared_out, scaled, acts, sg, wd_a, wd_b, mix_all, dy_all, cid):
    rows, width = x.shape
    length, units = acts.shape
    slots, hidden = scaled.shape[1:]
    hbm, vmem = pl.BlockSpec(memory_space=pl.ANY), pl.BlockSpec(memory_space=pltpu.VMEM)
    shape = jax.ShapeDtypeStruct
    return pl.pallas_call(
        gather_back_kernel,
        out_shape=[
            shape((length, width), BF),
            shape((length, width), BF),
            shape((3 * units, width), BF),
            *[shape(a.shape, BF) for a in given],
        ],
        in_specs=[hbm, vmem, vmem] + [hbm] * 9,
        out_specs=[hbm, hbm, vmem, hbm, hbm],
        scratch_shapes=[
            pltpu.VMEM((2, slots, hidden), BF),
            pltpu.VMEM(acts.shape, BF),
            pltpu.VMEM(sg.shape, BF),
            pltpu.VMEM((2, hidden, width), BF),
            pltpu.VMEM((slots // 4, width), BF),
            pltpu.VMEM((2, 4 * rows, width), BF),
            pltpu.VMEM((2, 4 * rows, width), BF),
            pltpu.VMEM((3 * units, width), F32),
            pltpu.SemaphoreType.DMA,
            pltpu.SemaphoreType.DMA((19,)),
            pltpu.SemaphoreType.DMA((15,)),
            pltpu.SemaphoreType.DMA((2,)),
            pltpu.SemaphoreType.DMA((2,)),
            pltpu.SemaphoreType.DMA((5,)),
            pltpu.SemaphoreType.DMA((2,)),
            pltpu.SemaphoreType.DMA((2,)),
        ],
        compiler_params=pltpu.CompilerParams(
            collective_id=cid, has_side_effects=True, vmem_limit_bytes=60 * 1024 * 1024
        ),
    )(x, dispatch, shared_out, scaled, acts, sg, wd_a, wd_b, mix_all, dy_all, *given)


class Home:
    def __init__(self, at, home, home_out, mine, got, load_sem, x_send, x_recv, z_send, z_recv):
        self.at, self.home, self.home_out, self.mine, self.got = at, home, home_out, mine, got
        self.z_send, self.z_recv = z_send, z_recv
        there = (1 - at.x) * 4
        self.loads, self.crossing = [], []
        for k in range(4):
            spot = at.zs[k]
            self.loads.append(
                pltpu.make_async_copy(home.at[at.x * 4 + spot], mine.at[spot], load_sem.at[k])
            )
            self.crossing.append(
                remote(
                    home.at[there + spot], got.at[spot], x_send.at[k], x_recv.at[k], at.device(ox=at.dx)
                )
            )
        self.keep = pltpu.make_async_copy(mine.at[at.z], home_out.at[at.z], load_sem.at[4])

    def start(self):
        for k in (3, 2, 1, 0):
            self.loads[k].start()
            self.crossing[k].start()

    def line(self, k):
        at = self.at
        spot = at.zs[k]
        self.loads[k].wait()
        self.crossing[k].wait_recv()
        mine, got = self.mine, self.got

        @pl.loop(0, mine.shape[1] // 16)
        def _(i):
            span = pl.ds(pl.multiple_of(i * 16, 16), 16)
            both = mine[spot, span, :].astype(F32) + got[spot, span, :].astype(F32)
            mine[spot, span, :] = both.astype(BF)

        if k == 0:
            self.keep.start()
        else:
            self.copy(k).start()

    def copy(self, k):
        at = self.at
        return remote(
            self.mine.at[at.zs[k]],
            self.home_out.at[at.z],
            self.z_send.at[k - 1],
            self.z_recv.at[at.z],
            at.device(zi=k),
        )

    def finish(self):
        at = self.at
        for k in (1, 2, 3):
            remote(
                self.mine.at[at.z],
                self.home_out.at[at.zs[k]],
                self.z_send.at[k - 1],
                self.z_recv.at[at.zs[k]],
                at.device(zi=k),
            ).wait_recv()
            self.copy(k).wait_send()
        self.keep.wait()
        for copy in self.crossing:
            copy.wait_send()


class Share:
    def __init__(self, at, ref, out, own_sem, send_sem, recv_sem):
        self.at, rows = at, ref.shape[0]
        spot = lambda oe: out.at[pl.ds(pl.multiple_of((at.e + oe) * rows, rows), rows)]
        f_dev, s_dev = at.device(oe=at.dy), at.device(oe=at.dc)
        self.local = pltpu.make_async_copy(ref, spot(0), own_sem)
        self.far = remote(ref, spot(0), send_sem.at[0], recv_sem.at[0], f_dev)
        self.near = remote(ref, spot(0), send_sem.at[1], recv_sem.at[1], s_dev)
        self.over = remote(spot(at.dy), spot(at.dy), send_sem.at[2], recv_sem.at[2], s_dev)

    def start(self):
        for copy in (self.far, self.near, self.local):
            copy.start()

    def forward(self):
        self.far.wait_recv()
        self.over.start()

    def finish(self):
        self.far.wait_send()
        self.near.wait()
        self.over.wait()
        self.local.wait()


def last_scatter_kernel(*refs):
    refs = list(refs)

    def take(count):
        taken = refs[:count]
        del refs[:count]
        return taken

    in_ref, g_ref, u_ref, scaled_ref, picked_ref, dy_ref, home_ref, mixed_ref, given = take(9)
    halves = take(5)
    out_ref, taken, grad_gate, grad_up, grad_down, home_out, mixed_out = take(7)
    right, left, other, grad, turned, mine, got = take(7)
    buffers = take(6)
    first_sem, cross_send, cross_recv, load_sem, store_sem = take(5)
    home_sems, share_sems = take(5), take(3)
    at = Place()
    greet(at, True)
    total = Scatter(at, *buffers, out_ref)
    acc = buffers[0]
    rows, width = acc.shape[1:]
    part = given.shape[0]
    crossing = cross(at, [given], [taken], cross_send, cross_recv)[0]
    home = Home(at, home_ref, home_out, mine, got, *home_sems)
    sharing = Share(at, mixed_ref, mixed_out, *share_sems)

    def rows_of(rank):
        return in_ref.at[pl.ds(pl.multiple_of(rank * rows, rows), rows)]

    order = [(f, zi) for f in (1, 0) for zi in (3, 2, 1, 0)]
    firsts = {}
    for f, zi in order:
        k = f * 4 + zi
        total.to_twin(rows_of(at.shard(f * at.dy + at.dc, zi)), f, zi)
        firsts[k] = pltpu.make_async_copy(
            rows_of(at.shard(f * at.dy, zi)), acc.at[k], first_sem.at[k]
        )
        firsts[k].start()
    home.start()
    crossing.start()
    pairs = [
        (picked_ref, right.at[0]),
        (dy_ref, right.at[1]),
        (g_ref.at[0], left.at[0]),
        (u_ref.at[0], left.at[1]),
        (scaled_ref.at[0], left.at[2]),
    ]
    pairs += [
        (ref, other.at[j // 2 % 2, pl.ds(j % 2 * part, part)])
        for j, ref in enumerate(halves + [taken])
    ]
    loads = [pltpu.make_async_copy(a, b, load_sem.at[j]) for j, (a, b) in enumerate(pairs)]
    for copy in loads[:9]:
        copy.start()

    def store(m):
        ref = (grad_gate, grad_up, grad_down)[m]
        return pltpu.make_async_copy(grad.at[m % 2], ref, store_sem.at[m])

    def gradient(m):
        turned[...] = left[m].T

        @columns_loop(width, 8)
        def _(columns):
            terms = product(turned[...], right[m // 2, :, columns])
            grad[m % 2, :, columns] = terms + other[m % 2, :, columns].astype(F32)

        store(m).start()

    for zi in (3, 2, 1, 0):
        firsts[4 + zi].wait()
        total.first(zi)
    sharing.start()
    for copy in loads[:9]:
        copy.wait()
    gradient(0)
    loads[9].start()
    home.line(3)
    firsts[3].wait()
    total.second(3)
    gradient(1)
    home.line(2)
    firsts[2].wait()
    total.second(2)
    home.line(1)
    firsts[1].wait()
    total.second(1)
    home.line(0)
    sharing.forward()
    crossing.wait_recv()
    loads[10].start()
    loads[9].wait()
    loads[10].wait()
    store(0).wait()
    gradient(2)
    firsts[0].wait()
    total.second(0)
    home.finish()
    sharing.finish()
    store(1).wait()
    store(2).wait()
    crossing.wait_send()
    total.finish()


def last_rows(x, g, u, scaled, picked, picked_dy, home, mixed_own, given, halves, cid):
    rows, width = x.shape[0] // 16, x.shape[1]
    slots, hidden = g.shape[1:]
    hbm, vmem = pl.BlockSpec(memory_space=pl.ANY), pl.BlockSpec(memory_space=pltpu.VMEM)
    shape, sems = jax.ShapeDtypeStruct, lambda n: pltpu.SemaphoreType.DMA((n,))
    return pl.pallas_call(
        last_scatter_kernel,
        out_shape=[
            shape((rows, width), F32),
            shape(given.shape, BF),
            *[shape((hidden, width), F32)] * 3,
            shape((4,) + home.shape[1:], BF),
            shape((4 * rows, width), BF),
        ],
        in_specs=[hbm] * 14,
        out_specs=[vmem] + [hbm] * 6,
        scratch_shapes=[
            pltpu.VMEM((2, slots, width), BF),
            pltpu.VMEM((3, slots, hidden), BF),
            pltpu.VMEM((2, hidden, width), BF),
            pltpu.VMEM((2, hidden, width), F32),
            pltpu.VMEM((hidden, slots), BF),
            pltpu.VMEM((4,) + home.shape[1:], BF),
            pltpu.VMEM((4,) + home.shape[1:], BF),
            *scatter_buffers(rows, width),
            sems(8),
            sems(1),
            sems(1),
            sems(11),
            sems(3),
            sems(5),
            sems(4),
            sems(4),
            sems(3),
            sems(4),
            pltpu.SemaphoreType.DMA,
            sems(3),
            sems(3),
        ],
        compiler_params=pltpu.CompilerParams(
            collective_id=cid, has_side_effects=True, vmem_limit_bytes=62 * 1024 * 1024
        ),
    )(x, g, u, scaled, picked, picked_dy, home, mixed_own, given, *halves)


def end_kernel(tokens_ref, gain_ref, small_ref, out_ref, gain_out, small_out, *scratch):
    gain_got, gain_sum, gain_all, small_all = scratch[:4]
    share_sems = scratch[4:7]
    gain_send, gain_recv, sum_send, sum_recv, small_send, small_recv = scratch[7:]
    at = Place()
    barrier = pltpu.get_barrier_semaphore()
    blocks = [(at.device(ox=ox, zi=k), m * 4 + k) for m, ox in enumerate((0, at.dx)) for k in range(4)]
    group = [at.device(oe=oe) for oe in (at.dy, at.dc, at.dy + at.dc)]
    for peer in [device for device, j in blocks[1:]] + group:
        pl.semaphore_signal(barrier, inc=1, device_id=peer, device_id_type=MESH)
    pl.semaphore_wait(barrier, 10)
    sharing = Share(at, tokens_ref, out_ref, *share_sems)
    own = at.x * 4 + at.z
    copies = []
    for device, j in blocks[1:]:
        copy = remote(
            gain_ref.at[device[0] * 4 + device[1]],
            gain_got.at[own],
            gain_send.at[j],
            gain_recv.at[own],
            device,
        )
        copy.start()
        copies.append(copy)
    for j, device in enumerate(group):
        copy = remote(small_ref, small_all.at[j], small_send.at[j], small_recv.at[j], device)
        copy.start()
        copies.append(copy)
    sharing.start()
    gain = gain_ref[own]
    for device, j in blocks[1:]:
        there = device[0] * 4 + device[1]
        remote(
            gain_ref.at[0], gain_got.at[there], gain_send.at[j], gain_recv.at[there], device
        ).wait_recv()
        gain = gain + gain_got[there]
    gain_sum[...] = gain
    for j, device in enumerate(group):
        copy = remote(gain_sum, gain_all.at[j], sum_send.at[j], sum_recv.at[j], device)
        copy.start()
        copies.append(copy)
    small = small_ref[...]
    for j in range(3):
        copies[7 + j].wait_recv()
        copies[10 + j].wait_recv()
        small = small + small_all[j]
        gain = gain + gain_all[j]
    gain_out[...] = gain
    small_out[...] = small
    sharing.forward()
    sharing.finish()
    for copy in copies:
        copy.wait_send()


def end(tokens_own, gain_part, small, cid):
    rows, width = tokens_own.shape
    vmem, hbm = pl.BlockSpec(memory_space=pltpu.VMEM), pl.BlockSpec(memory_space=pl.ANY)
    shape, sems = jax.ShapeDtypeStruct, lambda n: pltpu.SemaphoreType.DMA((n,))
    return pl.pallas_call(
        end_kernel,
        out_shape=[
            shape((4 * rows, width), tokens_own.dtype),
            shape(gain_part.shape[1:], F32),
            shape(small.shape, F32),
        ],
        in_specs=[hbm, vmem, vmem],
        out_specs=[hbm, vmem, vmem],
        scratch_shapes=[
            pltpu.VMEM(gain_part.shape, F32),
            pltpu.VMEM(gain_part.shape[1:], F32),
            pltpu.VMEM((3,) + gain_part.shape[1:], F32),
            pltpu.VMEM((3,) + small.shape, F32),
            pltpu.SemaphoreType.DMA,
            sems(3),
            sems(3),
            sems(8),
            sems(8),
            sems(3),
            sems(3),
            sems(3),
            sems(3),
        ],
        compiler_params=pltpu.CompilerParams(collective_id=cid, has_side_effects=True),
    )(tokens_own, gain_part, small)


ALL = ("dp", "ctx", "exp")
DENSE = ("dp", "ctx")


def swap(blocks):
    return lax.all_to_all(blocks, DENSE, split_axis=0, concat_axis=0, tiled=True)


def by_four(matrix):
    rows, columns = matrix.shape
    return matrix.reshape(rows, 4, columns // 4).transpose(1, 0, 2)


def across(values):
    return lax.ppermute(values, "dp", [(0, 1), (1, 0)])


def attend_kernel(scale, block, q_ref, k_ref, v_ref, out_ref, lse_ref):
    length = q_ref.shape[0]
    for i in range(length // block):
        seen = (i + 1) * block
        rows = pl.ds(i * block, block)
        scores = transposed_right(q_ref[rows, :], k_ref[0:seen, :]) * scale
        row_at = lax.broadcasted_iota(jnp.int32, scores.shape, 0) + i * block
        col_at = lax.broadcasted_iota(jnp.int32, scores.shape, 1)
        scores = jnp.where(row_at >= col_at, scores, MASKED)
        top = jnp.max(scores, axis=-1, keepdims=True)
        lse = top + jnp.log(jnp.sum(jnp.exp(scores - top), axis=-1, keepdims=True))
        probs = jnp.exp(scores - lse).astype(BF)
        out_ref[rows, :] = product(probs, v_ref[0:seen, :]).astype(BF)
        lse_ref[rows, :] = jnp.broadcast_to(lse, (block, HDIM))


def attend(q, k, v):
    length = q.shape[0]
    return pl.pallas_call(
        functools.partial(attend_kernel, HDIM ** (-0.5), 256),
        out_shape=(
            jax.ShapeDtypeStruct((length, HDIM), BF),
            jax.ShapeDtypeStruct((length, HDIM), F32),
        ),
        in_specs=[pl.BlockSpec(memory_space=pltpu.VMEM)] * 3,
        out_specs=(pl.BlockSpec(memory_space=pltpu.VMEM),) * 2,
        compiler_params=pltpu.CompilerParams(vmem_limit_bytes=56 * 1024 * 1024),
    )(q, k, v)


def turn_tables(length):
    inverse = 10000.0 ** (-np.arange(HDIM // 2).astype(np.float64) * 2.0 / HDIM)
    angles = np.arange(length).astype(np.float64)[:, None] * inverse[None, :]
    return np.cos(angles).astype(np.float32), np.sin(angles).astype(np.float32)


def turn(rows, cosine, sine):
    a, b = rows[:, : HDIM // 2], rows[:, HDIM // 2 :]
    return jnp.concatenate([a * cosine - b * sine, b * cosine + a * sine], axis=1)


def fast_body(
    tokens,
    routes,
    norm_attn,
    w_query,
    w_key,
    w_value,
    w_out,
    norm_mix,
    w_router,
    shared_gate,
    shared_up,
    shared_down,
    expert_gate,
    expert_up,
    expert_down,
    out_grad,
):
    dp, ctx, exp = lax.axis_index("dp"), lax.axis_index("ctx"), lax.axis_index("exp")
    rows_here, width = tokens.shape[1], tokens.shape[2]
    quarter = rows_here // 4
    length = rows_here * 4
    experts = w_router.shape[1]
    capacity = quarter * TOPK * 4 // (3 * experts)
    groups = length // quarter
    dense = w_query.shape[0]
    cut = shared_gate.shape[1] // 4
    wide = 256
    start = exp * quarter
    tokens_own = lax.dynamic_slice_in_dim(tokens[0], start, quarter, 0)
    dy_own = lax.dynamic_slice_in_dim(out_grad[0], start, quarter, 0)

    route_rows = routes[0].T
    theirs = jnp.arange(4, dtype=jnp.int32)[:, None, None] * 4 + exp
    named = jnp.any(route_rows[None] == theirs, axis=1).astype(BF).reshape(4, 2, dense)
    little = jnp.concatenate([w_router.T, norm_attn[None], norm_mix[None]], axis=0)
    little = jnp.concatenate([jnp.broadcast_to(little[None], (4,) + little.shape), named], axis=1)
    few = -(-little.shape[1] // 16) * 16
    little = jnp.pad(little, ((0, 0), (0, few - little.shape[1]), (0, 0)))
    sent_head = jnp.concatenate([by_four(w_query), by_four(w_key), by_four(w_value)], axis=2)
    sent_out = w_out.reshape(4, HDIM, dense)
    sent_units = jnp.stack([shared_gate.T, shared_up.T, shared_down], axis=0)
    sent_units = sent_units.reshape(3, 4, cut, dense).transpose(1, 0, 2, 3).reshape(4, 3 * cut, dense)
    tokens_all, early, early_out, late, early_little = all_rows(
        tokens[0], True, 1, (sent_head, sent_out, sent_units, little)
    )

    own_gate, own_up, own_down = expert_gate[0].T, expert_up[0].T, expert_down[0]
    tokens_all, sent_gate, sent_up, sent_down = lax.optimization_barrier(
        (tokens_all, own_gate, own_up, own_down)
    )
    other_gate, other_up, other_down = across(sent_gate), across(sent_up), across(sent_down)
    w_qkv = early.reshape(width, 3 * HDIM)
    early_little = early_little.transpose(1, 0, 2)
    router_rows = early_little[:experts].reshape(experts, width)
    attention_gain = early_little[experts].reshape(width).astype(F32)
    mixer_gain = early_little[experts + 1].reshape(width).astype(F32)
    hits = early_little[experts + 2 : experts + 4].transpose(1, 0, 2).reshape(2, length)
    hits = lax.dynamic_index_in_dim(hits, dp, 0, False).astype(F32).reshape(groups, quarter)
    w_out_head = early_out.transpose(1, 0, 2).reshape(HDIM, width)

    dy_all = all_rows(out_grad[0], True, 2)
    late = late.transpose(1, 0, 2).reshape(3, cut, width)
    late = jnp.pad(late, ((0, 0), (0, wide - cut), (0, 0)))
    shared_in = late[:2].reshape(2 * wide, width)
    shared_out = late[2]

    cosine, sine = turn_tables(length)
    normed = rms_scale(tokens_all.astype(F32), attention_gain).astype(BF)
    qkv = product(normed, w_qkv)
    query = turn(qkv[:, :HDIM], cosine, sine).astype(BF)
    key = turn(qkv[:, HDIM : 2 * HDIM], cosine, sine).astype(BF)
    value = qkv[:, 2 * HDIM :].astype(BF)
    heads_out, lse = attend(query, key, value)
    attn = own_rows(product(heads_out, w_out_head).astype(BF), 3)
    middle = tokens_own.astype(F32) + attn
    normed_own = rms_scale(middle, mixer_gain).astype(BF)

    mine = ctx * 4 + exp
    place = jnp.cumsum(hits, axis=1) - 1.0
    dispatch = jnp.where(
        (jnp.arange(capacity).astype(F32)[None, :, None] == place[:, None, :])
        & (hits[:, None, :] > 0.5),
        1.0,
        0.0,
    ).astype(BF)
    router_wide = jnp.pad(router_rows, ((0, HDIM - experts), (0, 0)))
    mix_all, picked, picked_dy, scaled, g_back, u_back, gate_back, shared_act, shared_gu_back = (
        expert_rows(
            normed_own,
            dy_all,
            dispatch,
            router_wide,
            experts,
            shared_in,
            shared_out,
            (own_gate, own_up, own_down, other_gate, other_up, other_down),
            4,
        )
    )

    mix_back, gate_0, gate_1, up_0, up_1, down_0, down_1 = expert_back(
        dispatch,
        gate_back,
        shared_in,
        g_back,
        u_back,
        shared_gu_back,
        picked,
        picked_dy,
        scaled,
        (own_gate, own_up, other_gate, other_up),
        5,
    )
    gate_back_own = mix_back[:, width : width + experts]
    mix_back = mix_back[:, :width]

    router_own = jax.nn.softmax(transposed_right(normed_own, router_rows), axis=-1)
    logit_back = (
        router_own * (gate_back_own - jnp.sum(router_own * gate_back_own, axis=-1, keepdims=True))
    ).astype(BF)
    router_part = transposed_left(logit_back, normed_own)

    mix_back = mix_back + product(logit_back, router_rows)
    _, norm_mix_back = jax.vjp(rms_scale, middle, mixer_gain)
    middle_norm_back, gain_mix_part = norm_mix_back(mix_back)
    middle_back = dy_own.astype(F32) + middle_norm_back
    attn_back = middle_back.astype(BF)
    attn_back_all, mixed_part, units_part, gate_1, up_0 = gather_back(
        attn_back,
        (gate_1, up_0),
        dispatch,
        shared_out,
        scaled,
        shared_act,
        shared_gu_back,
        own_down,
        other_down,
        mix_all,
        dy_all,
        7,
    )
    tables = jnp.stack(
        [jnp.concatenate([cosine, cosine], axis=1), jnp.concatenate([sine, -sine], axis=1)]
    )
    mixed_sum, normed_part, qkv_part, out_part, up_1, down_0 = mixed_rows(
        w_out_head,
        w_qkv.T,
        tables,
        query,
        key,
        value,
        lse,
        heads_out,
        mixed_part,
        attn_back_all,
        normed,
        (up_1, down_0),
        9,
    )
    mixed_own = (middle + mixed_sum).astype(BF)
    units_part = units_part.reshape(3, wide, width)[:, :cut].reshape(3 * cut, width)
    small_part = jnp.concatenate([gain_mix_part[None], router_part], axis=0).astype(BF)
    small_rows = -(-(experts + 1) // 16) * 16
    small_part = jnp.pad(small_part, ((0, small_rows - experts - 1), (0, 0)))
    home = jnp.concatenate([qkv_part, out_part, units_part, small_part], axis=0)
    home = home.reshape(-1, 8, dense).transpose(1, 0, 2)
    normed_back, _, gate_grad, up_grad, down_grad, home, mixed = last_rows(
        normed_part,
        g_back,
        u_back,
        scaled,
        picked,
        picked_dy,
        home,
        mixed_own,
        down_1,
        (gate_0, gate_1, up_0, up_1, down_0),
        8,
    )
    home = home.astype(F32)
    small_part = jnp.sum(home[:, -small_rows:], axis=0)
    _, norm_attn_back = jax.vjp(rms_scale, tokens_own.astype(F32), attention_gain)
    input_norm_back, gain_attn_part = norm_attn_back(normed_back)
    tokens_back_own = (middle_back + input_norm_back).astype(BF)

    gain_part = jnp.pad(gain_attn_part.reshape(8, 1, dense), ((0, 0), (0, 7), (0, 0)))
    tokens_back, gain_attn, small = end(tokens_back_own, gain_part, small_part, 6)

    def columns_of(parts):
        return parts.transpose(2, 0, 1).reshape(dense, -1)

    def rows_of(parts):
        return parts.reshape(-1, dense)

    units = 4 * HDIM
    return (
        mixed[None],
        tokens_back[None],
        gain_attn[0],
        columns_of(home[:, :HDIM]),
        columns_of(home[:, HDIM : 2 * HDIM]),
        columns_of(home[:, 2 * HDIM : 3 * HDIM]),
        rows_of(home[:, 3 * HDIM : units]),
        small[0],
        small[1 : experts + 1].T,
        rows_of(home[:, units : units + cut]).T,
        rows_of(home[:, units + cut : units + 2 * cut]).T,
        rows_of(home[:, units + 2 * cut : units + 3 * cut]),
        gate_grad.T[None],
        up_grad.T[None],
        down_grad[None],
    )


def solution(mesh):
    sizes = dict(mesh.shape)

    def chosen(*args):
        heads = args[3].shape[1] * sizes["exp"] // HDIM
        one_head_each = heads == sizes["ctx"] * sizes["exp"]
        built_for = (sizes["dp"], sizes["ctx"], sizes["exp"]) == (2, 4, 4)
        return fast_body(*args) if one_head_each and built_for else body(*args)

    in_specs = (
        P("dp", "ctx", None),
        P("dp", "ctx", None),
        P(("dp", "ctx")),
        P(("dp", "ctx"), "exp"),
        P(("dp", "ctx"), "exp"),
        P(("dp", "ctx"), "exp"),
        P("exp", ("dp", "ctx")),
        P(("dp", "ctx")),
        P(("dp", "ctx"), None),
        P(("dp", "ctx"), "exp"),
        P(("dp", "ctx"), "exp"),
        P("exp", ("dp", "ctx")),
        P(("ctx", "exp"), None, "dp"),
        P(("ctx", "exp"), None, "dp"),
        P(("ctx", "exp"), "dp", None),
        P("dp", "ctx", None),
    )
    out_specs = (
        P("dp", "ctx", None),
        P("dp", "ctx", None),
        P(("dp", "ctx")),
        P(("dp", "ctx"), "exp"),
        P(("dp", "ctx"), "exp"),
        P(("dp", "ctx"), "exp"),
        P("exp", ("dp", "ctx")),
        P(("dp", "ctx")),
        P(("dp", "ctx"), None),
        P(("dp", "ctx"), "exp"),
        P(("dp", "ctx"), "exp"),
        P("exp", ("dp", "ctx")),
        P(("ctx", "exp"), None, "dp"),
        P(("ctx", "exp"), None, "dp"),
        P(("ctx", "exp"), "dp", None),
    )
    return jax.shard_map(chosen, mesh=mesh, in_specs=in_specs, out_specs=out_specs, check_vma=False)
```

```python
import functools

import jax
import jax.numpy as jnp
import numpy as np
from jax import lax
from jax.experimental import pallas as pl
from jax.experimental.pallas import tpu as pltpu
from jax.sharding import PartitionSpec as P

HDIM = 128
TOPK = 6


EPSILON = 1e-06
MASKED = -1e30
HIGHEST = lax.Precision.HIGHEST


def rms_scale(values, gain_row):
    return (
        values * lax.rsqrt(jnp.mean(values * values, axis=-1, keepdims=True) + EPSILON) * gain_row
    )


def rope_tables(positions, rope_width):
    inverse = 10000.0 ** (-jnp.arange(rope_width // 2).astype(jnp.float32) * 2.0 / rope_width)
    angles = positions.astype(jnp.float32)[:, None] * inverse[None, :]
    return (jnp.cos(angles), jnp.sin(angles))


def rotate(values, cosine, sine_table):
    half_size = values.shape[-1] // 2
    first_half = values[..., :half_size]
    second = values[..., half_size:]
    cosine = cosine[:, None, :]
    sine_table = sine_table[:, None, :]
    return jnp.concatenate(
        [first_half * cosine - second * sine_table, second * cosine + first_half * sine_table],
        axis=-1,
    )


def silu_mix(gate_rows, up_rows):
    return jax.nn.silu(gate_rows) * up_rows


def product(left_side, right_side):
    return jnp.dot(left_side, right_side, preferred_element_type=jnp.float32)


def transposed_left(left_side, right_side):
    return lax.dot_general(
        left_side, right_side, (((0,), (0,)), ((), ())), preferred_element_type=jnp.float32
    )


def transposed_right(left_side, right_side):
    return lax.dot_general(
        left_side, right_side, (((1,), (1,)), ((), ())), preferred_element_type=jnp.float32
    )


def place_rows(part, start_row, total_rows):
    blank = jnp.zeros((total_rows, part.shape[1]), jnp.float32)
    return lax.dynamic_update_slice_in_dim(blank, part, start_row, 0)


def to_owners(buffer):
    copies = lax.axis_size("dp")
    widened = jnp.broadcast_to(buffer[None], (copies,) + buffer.shape)
    widened = widened.reshape((copies * buffer.shape[0],) + buffer.shape[1:])
    return lax.all_to_all(widened, ("dp", "ctx", "exp"), split_axis=0, concat_axis=0, tiled=True)


def values_home(partial_value):
    returned = lax.all_to_all(
        partial_value, ("dp", "ctx", "exp"), split_axis=0, concat_axis=0, tiled=True
    )
    grouped = returned.reshape((lax.axis_size("dp"), -1) + returned.shape[1:])
    return jnp.sum(grouped.astype(jnp.float32), axis=0).astype(jnp.bfloat16)


def grads_home(partial_value):
    returned = lax.all_to_all(
        partial_value.astype(jnp.bfloat16),
        ("dp", "ctx", "exp"),
        split_axis=0,
        concat_axis=0,
        tiled=True,
    ).astype(partial_value.dtype)
    grouped = returned.reshape((lax.axis_size("dp"), -1) + returned.shape[1:])
    return jnp.sum(grouped, axis=0)


def body(
    tokens,
    routes,
    norm_attn,
    w_query,
    w_key,
    w_value,
    w_out,
    norm_mix,
    w_router,
    shared_gate,
    shared_up,
    shared_down,
    expert_gate,
    expert_up,
    expert_down,
    out_grad,
):
    gathered = (
        lax.all_gather(norm_attn, ("dp", "ctx"), axis=0, tiled=True),
        lax.all_gather(w_query, ("dp", "ctx"), axis=0, tiled=True),
        lax.all_gather(w_key, ("dp", "ctx"), axis=0, tiled=True),
        lax.all_gather(w_value, ("dp", "ctx"), axis=0, tiled=True),
        lax.all_gather(w_out, ("dp", "ctx"), axis=1, tiled=True),
        lax.all_gather(norm_mix, ("dp", "ctx"), axis=0, tiled=True),
        lax.all_gather(w_router, ("dp", "ctx"), axis=0, tiled=True),
        lax.all_gather(shared_gate, ("dp", "ctx"), axis=0, tiled=True),
        lax.all_gather(shared_up, ("dp", "ctx"), axis=0, tiled=True),
        lax.all_gather(shared_down, ("dp", "ctx"), axis=1, tiled=True),
    )
    (
        attention_gain,
        query_matrix,
        key_matrix,
        value_matrix,
        output_matrix,
        mixer_gain,
        router_matrix,
        shared_gate_matrix,
        shared_up_matrix,
        shared_down_matrix,
    ) = gathered
    rows_here = tokens.shape[1]
    model_width = tokens.shape[2]
    heads_here = query_matrix.shape[1] // HDIM
    quarter = rows_here // lax.axis_size("exp")
    start_row = lax.axis_index("exp") * quarter
    layer_input = tokens[0].astype(jnp.float32)
    grad_rows = out_grad[0]
    grad_float = grad_rows.astype(jnp.float32)
    seq_length = rows_here * lax.axis_size("ctx")
    positions = lax.axis_index("ctx") * rows_here + jnp.arange(rows_here, dtype=jnp.int32)
    cosine, sine_table = rope_tables(positions, HDIM)
    visible = positions[:, None] >= jnp.arange(seq_length, dtype=jnp.int32)[None, :]
    scale = HDIM ** (-0.5)
    head_shape = (rows_here, heads_here, HDIM)
    normed = rms_scale(layer_input, attention_gain).astype(jnp.bfloat16)
    query_rot = rotate(
        product(normed, query_matrix).reshape(head_shape), cosine, sine_table
    ).astype(jnp.bfloat16)
    key_rot = (
        rotate(product(normed, key_matrix).reshape(head_shape), cosine, sine_table)
        .astype(jnp.bfloat16)
        .reshape(rows_here, -1)
    )
    value_low = product(normed, value_matrix).astype(jnp.bfloat16)
    key_all, value_all = (
        lax.all_gather(key_rot, "ctx", axis=0, tiled=True),
        lax.all_gather(value_low, "ctx", axis=0, tiled=True),
    )
    key_heads = key_all.reshape(seq_length, heads_here, HDIM)
    value_heads = value_all.reshape(seq_length, heads_here, HDIM)

    def attention_scores():
        scores = (
            jnp.einsum("qhd,khd->hqk", query_rot, key_heads, preferred_element_type=jnp.float32)
            * scale
        )
        return jnp.where(visible[None], scores, MASKED)

    scores = attention_scores()
    largest = jnp.max(scores, axis=-1, keepdims=True)
    log_total = largest + jnp.log(jnp.sum(jnp.exp(scores - largest), axis=-1, keepdims=True))
    weights_low = jnp.exp(scores - log_total).astype(jnp.bfloat16)
    heads_out = (
        jnp.einsum("hqk,khd->qhd", weights_low, value_heads, preferred_element_type=jnp.float32)
        .reshape(rows_here, -1)
        .astype(jnp.bfloat16)
    )
    attn_total = lax.psum(product(heads_out, output_matrix), "exp")
    middle = layer_input + attn_total
    normed_mix = rms_scale(middle, mixer_gain).astype(jnp.bfloat16)
    normed_quarter = lax.dynamic_slice_in_dim(normed_mix, start_row, quarter, 0)
    route_quarter = lax.dynamic_slice_in_dim(routes[0], start_row, quarter, 0)
    grad_quarter = lax.dynamic_slice_in_dim(grad_rows, start_row, quarter, 0)
    logits = product(normed_quarter, router_matrix)
    probabilities = jax.nn.softmax(logits, axis=-1)
    owners = lax.axis_size(("ctx", "exp"))
    local_experts = expert_gate.shape[0]
    experts = local_experts * owners
    capacity = max(quarter * TOPK * 4 // (3 * experts), 2)
    expert_choice_index = jnp.arange(experts, dtype=jnp.int32)
    chosen = (route_quarter[:, :, None] == expert_choice_index[None, None, :]).astype(jnp.float32)
    gates = jnp.sum(chosen * probabilities[:, None, :], axis=-1)
    route_flat = route_quarter.reshape(-1)
    expert_hits = (route_flat[:, None] == expert_choice_index[None, :]).astype(jnp.int32)
    slot_index = jnp.sum(jnp.cumsum(expert_hits, axis=0) * expert_hits, axis=1) - 1
    slot_place = route_flat * capacity + slot_index
    matches = (
        jnp.arange(experts * capacity, dtype=jnp.int32)[:, None] == slot_place[None, :]
    ).astype(jnp.float32)
    dispatch = jnp.sum(matches.reshape(experts * capacity, quarter, TOPK), axis=2).astype(
        jnp.bfloat16
    )
    slot_gates = jnp.dot(matches, gates.reshape(-1), precision=HIGHEST)
    buffer_shape = (owners, local_experts, capacity, model_width)
    outgoing = product(dispatch, normed_quarter).astype(jnp.bfloat16).reshape(buffer_shape)
    arrived = to_owners(outgoing)
    gate_hidden = jnp.einsum(
        "sicd,idf->sicf", arrived, expert_gate, preferred_element_type=jnp.float32
    )
    up_hidden = jnp.einsum("sicd,idf->sicf", arrived, expert_up, preferred_element_type=jnp.float32)
    expert_act = silu_mix(gate_hidden, up_hidden).astype(jnp.bfloat16)
    partial_value = jnp.einsum(
        "sicf,ifd->sicd", expert_act, expert_down, preferred_element_type=jnp.float32
    ).astype(jnp.bfloat16)
    expert_values = values_home(partial_value).reshape(experts * capacity, model_width)
    route_values = expert_values[slot_place].astype(jnp.float32).reshape(quarter, TOPK, model_width)
    combined = jnp.sum(route_values * gates[:, :, None], axis=1)
    shared_gate_rows = product(normed_mix, shared_gate_matrix)
    shared_up_rows = product(normed_mix, shared_up_matrix)
    shared_act = silu_mix(shared_gate_rows, shared_up_rows).astype(jnp.bfloat16)
    branch_part = product(shared_act, shared_down_matrix) + place_rows(
        combined, start_row, rows_here
    )
    result = middle + lax.psum(branch_part.astype(jnp.bfloat16), "exp").astype(jnp.float32)
    grad_slots = (
        (product(dispatch, grad_quarter) * slot_gates[:, None])
        .astype(jnp.bfloat16)
        .reshape(buffer_shape)
    )
    grad_arrived = to_owners(grad_slots)
    act_grad = jnp.einsum(
        "sicd,ifd->sicf", grad_arrived, expert_down, preferred_element_type=jnp.float32
    )
    down_grad = jnp.einsum(
        "sicf,sicd->ifd", expert_act, grad_arrived, preferred_element_type=jnp.float32
    )
    _, mix_back = jax.vjp(silu_mix, gate_hidden, up_hidden)
    gate_back, up_back = mix_back(act_grad)
    gate_back = gate_back.astype(jnp.bfloat16)
    up_back = up_back.astype(jnp.bfloat16)
    gate_grad = jnp.einsum("sicd,sicf->idf", arrived, gate_back, preferred_element_type=jnp.float32)
    up_grad = jnp.einsum("sicd,sicf->idf", arrived, up_back, preferred_element_type=jnp.float32)
    input_back = jnp.einsum(
        "sicf,idf->sicd", gate_back, expert_gate, preferred_element_type=jnp.float32
    ) + jnp.einsum("sicf,idf->sicd", up_back, expert_up, preferred_element_type=jnp.float32)
    rows_back = grads_home(input_back).reshape(experts * capacity, model_width)
    moe_back = jnp.sum(rows_back[slot_place].reshape(quarter, TOPK, model_width), axis=1)
    gate_route_back = jnp.sum(route_values * grad_quarter.astype(jnp.float32)[:, None, :], axis=-1)
    prob_back = jnp.sum(chosen * gate_route_back[:, :, None], axis=1)
    _, soft_back = jax.vjp(lambda values: jax.nn.softmax(values, axis=-1), logits)
    logit_back = soft_back(prob_back)[0].astype(jnp.bfloat16)
    router_term = transposed_left(normed_quarter, logit_back)
    shared_back = transposed_right(grad_rows, shared_down_matrix)
    _, shared_mix_back = jax.vjp(silu_mix, shared_gate_rows, shared_up_rows)
    sgate_back, sup_back = shared_mix_back(shared_back)
    sgate_back = sgate_back.astype(jnp.bfloat16)
    sup_back = sup_back.astype(jnp.bfloat16)
    quarter_back = transposed_right(logit_back, router_matrix) + moe_back
    mix_part = (
        transposed_right(sgate_back, shared_gate_matrix)
        + transposed_right(sup_back, shared_up_matrix)
        + place_rows(quarter_back, start_row, rows_here)
    )
    mix_total, router_grad = (
        lax.psum(mix_part.astype(jnp.bfloat16), "exp").astype(jnp.float32),
        lax.psum(router_term.astype(jnp.bfloat16), "exp").astype(jnp.float32),
    )
    _, norm_mix_back = jax.vjp(rms_scale, middle, mixer_gain.astype(jnp.float32))
    middle_norm_back, gain_mix_grad = norm_mix_back(mix_total)
    middle_grad = grad_float + middle_norm_back
    sdown_grad = transposed_left(shared_act, grad_rows)
    sgate_grad = transposed_left(normed_mix, sgate_back)
    sup_grad = transposed_left(normed_mix, sup_back)
    attn_back = middle_grad.astype(jnp.bfloat16)
    heads_back = transposed_right(attn_back, output_matrix).astype(jnp.bfloat16).reshape(head_shape)
    weights_full = jnp.exp(attention_scores() - log_total)
    weights_again = weights_full.astype(jnp.bfloat16)
    weight_back = jnp.einsum(
        "qhd,khd->hqk", heads_back, value_heads, preferred_element_type=jnp.float32
    )
    value_term = jnp.einsum(
        "hqk,qhd->khd", weights_again, heads_back, preferred_element_type=jnp.float32
    ).reshape(seq_length, -1)
    score_back = (
        weights_full * (weight_back - jnp.sum(weights_full * weight_back, axis=-1, keepdims=True))
    ).astype(jnp.bfloat16)
    query_rot_back = (
        jnp.einsum("hqk,khd->qhd", score_back, key_heads, preferred_element_type=jnp.float32)
        * scale
    )
    key_term = (
        jnp.einsum("hqk,qhd->khd", score_back, query_rot, preferred_element_type=jnp.float32)
        * scale
    ).reshape(seq_length, -1)
    key_sum, value_sum = (
        lax.psum_scatter(
            key_term.astype(jnp.bfloat16), "ctx", scatter_dimension=0, tiled=True
        ).astype(jnp.float32),
        lax.psum_scatter(
            value_term.astype(jnp.bfloat16), "ctx", scatter_dimension=0, tiled=True
        ).astype(jnp.float32),
    )
    _, rotate_back = jax.vjp(
        lambda values: rotate(values, cosine, sine_table), jnp.zeros(head_shape, jnp.float32)
    )
    query_low = rotate_back(query_rot_back)[0].reshape(rows_here, -1).astype(jnp.bfloat16)
    key_low = (
        rotate_back(key_sum.reshape(head_shape))[0].reshape(rows_here, -1).astype(jnp.bfloat16)
    )
    value_back_low = value_sum.astype(jnp.bfloat16)
    normed_part = (
        transposed_right(query_low, query_matrix)
        + transposed_right(key_low, key_matrix)
        + transposed_right(value_back_low, value_matrix)
    )
    normed_back = lax.psum(normed_part.astype(jnp.bfloat16), "exp").astype(jnp.float32)
    _, norm_attn_back = jax.vjp(rms_scale, layer_input, attention_gain.astype(jnp.float32))
    input_norm_back, gain_attn_grad = norm_attn_back(normed_back)
    tokens_back = (middle_grad + input_norm_back).astype(jnp.bfloat16)
    out_weight_grad = transposed_left(heads_out, attn_back)
    query_grad = transposed_left(normed, query_low)
    key_grad = transposed_left(normed, key_low)
    value_grad = transposed_left(normed, value_back_low)
    all_sums = (
        lax.psum_scatter(
            gain_attn_grad.astype(jnp.bfloat16), ("dp", "ctx"), scatter_dimension=0, tiled=True
        ).astype(jnp.float32),
        lax.psum_scatter(
            query_grad.astype(jnp.bfloat16), ("dp", "ctx"), scatter_dimension=0, tiled=True
        ).astype(jnp.float32),
        lax.psum_scatter(
            key_grad.astype(jnp.bfloat16), ("dp", "ctx"), scatter_dimension=0, tiled=True
        ).astype(jnp.float32),
        lax.psum_scatter(
            value_grad.astype(jnp.bfloat16), ("dp", "ctx"), scatter_dimension=0, tiled=True
        ).astype(jnp.float32),
        lax.psum_scatter(
            out_weight_grad.astype(jnp.bfloat16), ("dp", "ctx"), scatter_dimension=1, tiled=True
        ).astype(jnp.float32),
        lax.psum_scatter(
            gain_mix_grad.astype(jnp.bfloat16), ("dp", "ctx"), scatter_dimension=0, tiled=True
        ).astype(jnp.float32),
        lax.psum_scatter(
            router_grad.astype(jnp.bfloat16), ("dp", "ctx"), scatter_dimension=0, tiled=True
        ).astype(jnp.float32),
        lax.psum_scatter(
            sgate_grad.astype(jnp.bfloat16), ("dp", "ctx"), scatter_dimension=0, tiled=True
        ).astype(jnp.float32),
        lax.psum_scatter(
            sup_grad.astype(jnp.bfloat16), ("dp", "ctx"), scatter_dimension=0, tiled=True
        ).astype(jnp.float32),
        lax.psum_scatter(
            sdown_grad.astype(jnp.bfloat16), ("dp", "ctx"), scatter_dimension=1, tiled=True
        ).astype(jnp.float32),
    )
    (
        gain_attn_sum,
        query_sum,
        key_sum_out,
        value_sum_out,
        out_sum,
        gain_mix_sum,
        router_sum,
        sgate_sum,
        sup_sum,
        sdown_sum,
    ) = all_sums
    return (
        result.astype(jnp.bfloat16)[None],
        tokens_back[None],
        gain_attn_sum,
        query_sum,
        key_sum_out,
        value_sum_out,
        out_sum,
        gain_mix_sum,
        router_sum,
        sgate_sum,
        sup_sum,
        sdown_sum,
        gate_grad,
        up_grad,
        down_grad,
    )


MESH = pl.DeviceIdType.MESH
BF = jnp.bfloat16
F32 = jnp.float32


class Place:
    def __init__(self):
        self.x = lax.axis_index("dp")
        self.z = lax.axis_index("ctx")
        self.e = lax.axis_index("exp")
        z = self.z
        high = lax.div(z, 2)
        self.zs = [z, z + 1 - 2 * lax.rem(z, 2), 2 - high, 3 - 3 * high]
        self.inner = 3 - z
        self.inside = lax.div(z * (3 - z), 2)
        self.middle = self.inside == 1
        self.dx = 1 - 2 * self.x
        self.dy = 2 - 4 * lax.div(self.e, 2)
        self.dc = 1 - 2 * lax.rem(self.e, 2)

    def device(self, ox=0, oe=0, zi=0):
        return (self.x + ox, self.zs[zi], self.e + oe)

    def inward(self):
        return (self.x, self.inner, self.e)

    def shard(self, oe, zi):
        return self.zs[zi] * 4 + self.e + oe


def greet(at, everyone, pair=False):
    barrier = pltpu.get_barrier_semaphore()
    peers = [at.device(zi=1), at.device(oe=at.dy), at.device(oe=at.dc)]
    if everyone or pair:
        peers.append(at.device(ox=at.dx))
    if everyone:
        peers += [at.device(zi=2), at.device(zi=3)]
    for peer in peers:
        pl.semaphore_signal(barrier, inc=1, device_id=peer, device_id_type=MESH)
    if everyone:
        pl.semaphore_wait(barrier, len(peers))
        return

    @pl.when(at.middle)
    def _():
        pl.semaphore_signal(barrier, inc=1, device_id=at.inward(), device_id_type=MESH)

    pl.semaphore_wait(barrier, len(peers) + at.inside)


def remote(src, dst, send, recv, device):
    return pltpu.make_async_remote_copy(
        src_ref=src, dst_ref=dst, send_sem=send, recv_sem=recv, device_id=device, device_id_type=MESH
    )


def half_of(array):
    return jax.ShapeDtypeStruct((array.shape[0] // 2,) + array.shape[1:], array.dtype)


def cross(at, sent, got, send_sem, recv_sem, starts=None):
    starts = starts or (0,) * len(sent)
    return [
        remote(
            a.at[pl.ds(start, b.shape[0])],
            b,
            send_sem.at[m],
            recv_sem.at[m],
            at.device(ox=at.dx),
        )
        for m, (a, b, start) in enumerate(zip(sent, got, starts))
    ]


class Exchange:
    def __init__(self, at, sent, got, local_sem, send_sem, recv_sem):
        self.at, self.sent, self.got = at, sent, got
        self.local_sem, self.send_sem, self.recv_sem = local_sem, send_sem, recv_sem
        self.waits = []

    def push(self, src, m, z_from, slot, device):
        at = self.at
        spot = self.got[m].at[at.x * 4 + z_from]
        copy = remote(
            src, spot, self.send_sem.at[m * 7 + slot], self.recv_sem.at[m * 8 + (0 if slot < 3 else 4) + z_from], device
        )
        copy.start()
        self.waits.append(copy)

    def start(self):
        at = self.at
        for m, sent in enumerate(self.sent):
            for zi in (1, 2, 3):
                self.push(sent.at[at.zs[zi]], m, at.z, zi - 1, at.device(zi=zi))
            self.push(sent.at[at.z], m, at.z, 3, at.device(ox=at.dx))
            pltpu.make_async_copy(
                sent.at[at.z], self.got[m].at[at.x * 4 + at.z], self.local_sem.at[m]
            ).start()

    def arrive(self, m, slot):
        src = self.sent[m].at[0]
        remote(
            src, self.got[m].at[0], self.send_sem.at[0], self.recv_sem.at[slot], self.at.device(ox=self.at.dx)
        ).wait_recv()

    def forward(self, zi):
        at = self.at
        for m in range(len(self.sent)):
            self.arrive(m, m * 8 + at.zs[zi])
            self.push(self.got[m].at[at.x * 4 + at.zs[zi]], m, at.zs[zi], 3 + zi, at.device(ox=at.dx))

    def finish(self):
        at = self.at
        for m, sent in enumerate(self.sent):
            for z in range(4):
                self.arrive(m, m * 8 + 4 + z)
            pltpu.make_async_copy(
                sent.at[at.z], self.got[m].at[at.x * 4 + at.z], self.local_sem.at[m]
            ).wait()
        for copy in self.waits:
            copy.wait_send()


def gather_kernel(block, rows, parts, extras, starts, *refs):
    swaps = len(starts)
    refs = list(refs)

    def take(count):
        taken = refs[:count]
        del refs[:count]
        return taken

    (x_ref,), sent, given = take(1), take(extras), take(swaps)
    (out_ref,), got, taken = take(1), take(extras), take(swaps)
    own_sem, send_sem, recv_sem = take(3)
    extra_sems = take(3 if extras else 0)
    at = Place()
    greet(at, extras > 0, swaps > 0)
    crossing = cross(at, given, taken, *refs, starts) if swaps else []
    piece = rows // parts
    slot_z, slot_f, slot_s = 0, 3, 7
    started, inside = [], []
    firsts = 1 if block else 0
    shift = at.e * rows if block else 0

    def where(f, zi, p):
        return pl.ds(
            pl.multiple_of(at.shard(f * at.dy, zi) * rows + p * piece, piece), piece
        )

    def push(src, dst, slot, p, device, sends=None, record=None):
        k = slot * parts + p
        j = k if sends is None else sends * parts + p
        remote(src, out_ref.at[dst], send_sem.at[j], recv_sem.at[k], device).start()
        (started if record is None else record).append(j)

    f_dev, s_dev, z_dev = at.device(oe=at.dy), at.device(oe=at.dc), at.device(zi=1)

    def gone(j):
        remote(
            x_ref.at[pl.ds(0, piece)], out_ref.at[pl.ds(0, piece)], send_sem.at[j], recv_sem.at[0], s_dev
        ).wait_send()

    def arrive(slot, p):
        k = slot * parts + p
        remote(
            x_ref.at[pl.ds(0, piece)], out_ref.at[pl.ds(0, piece)], send_sem.at[k], recv_sem.at[k], s_dev
        ).wait_recv()

    if block:
        spot = pl.ds(pl.multiple_of(at.z * 4 * rows, 4 * rows), 4 * rows)
    else:
        spot = pl.ds(pl.multiple_of(at.shard(0, 0) * rows, rows), rows)
    own = pltpu.make_async_copy(x_ref, out_ref.at[spot], own_sem)

    def source(f, zi, p):
        if f == 0 and zi == 0:
            return x_ref.at[pl.ds(pl.multiple_of(shift + p * piece, piece), piece)]
        return out_ref.at[where(f, zi, p)]

    def along(zi, p):
        src, dst = source(0, zi, p), where(0, zi, p)
        if zi == 0:
            push(src, dst, slot_z, p, z_dev)
        if zi < 2:
            pl.when(at.middle)(
                lambda: push(src, dst, slot_z + 1 + zi, p, at.inward(), 15 + zi, inside)
            )
        else:
            pl.when(at.middle)(lambda: push(src, dst, slot_z + zi - 1, p, z_dev, 15 + zi, inside))

    def forward(f, zi, p):
        src, dst = source(f, zi, p), where(f, zi, p)
        if f == 0:
            along(zi, p)
        if zi >= firsts:
            if f == 0:
                push(src, dst, slot_f + zi, p, f_dev)
            push(src, dst, slot_s + f * 4 + zi, p, s_dev)

    for p in range(parts):
        forward(0, 0, p)
    own.start()
    for copy in crossing:
        copy.start()
    if extras:
        swap_in = Exchange(at, sent, got, *extra_sems)
        swap_in.start()
    for zi in range(4):
        if zi > 0:
            for p in range(parts):
                arrive(slot_z + zi - 1, p)
                forward(0, zi, p)
        if zi >= firsts:
            for p in range(parts):
                arrive(slot_f + zi, p)
                forward(1, zi, p)
        if extras and zi > 0:
            swap_in.forward(zi)
    for f in range(2):
        for zi in range(firsts, 4):
            for p in range(parts):
                arrive(slot_s + f * 4 + zi, p)
    own.wait()
    if extras:
        swap_in.finish()
    for copy in crossing:
        copy.wait()
    for j in started:
        gone(j)

    @pl.when(at.middle)
    def _():
        for j in inside:
            gone(j)


def all_rows(x, block, cid, sent=(), given=(), starts=(), parts=2):
    rows, width = x.shape
    total = rows * (4 if block else 16)
    rows = rows // 4 if block else rows
    extras, swaps = len(sent), len(given)
    hbm = pl.BlockSpec(memory_space=pl.ANY)
    outs = [jax.ShapeDtypeStruct((total, width), x.dtype)]
    outs += [jax.ShapeDtypeStruct((8,) + a.shape[1:], a.dtype) for a in sent]
    outs += [half_of(a) for a in given]
    scratch = [
        pltpu.SemaphoreType.DMA,
        pltpu.SemaphoreType.DMA((19 * parts,)),
        pltpu.SemaphoreType.DMA((15 * parts,)),
    ]
    if extras:
        scratch += [
            pltpu.SemaphoreType.DMA((extras,)),
            pltpu.SemaphoreType.DMA((7 * extras,)),
            pltpu.SemaphoreType.DMA((8 * extras,)),
        ]
    if swaps:
        scratch += [pltpu.SemaphoreType.DMA((swaps,)), pltpu.SemaphoreType.DMA((swaps,))]
    got = pl.pallas_call(
        functools.partial(gather_kernel, block, rows, parts, extras, starts),
        out_shape=outs,
        in_specs=[hbm] * len(outs),
        out_specs=[hbm] * len(outs),
        scratch_shapes=scratch,
        compiler_params=pltpu.CompilerParams(collective_id=cid, has_side_effects=True),
    )(x, *sent, *given)
    return got if extras or swaps else got[0]


class Scatter:
    def __init__(self, at, acc, got_s, got_f, got_z, send_sem, recv_sem, out_ref, by_block=False):
        self.by_block = by_block
        self.at, self.acc, self.got_s, self.got_f, self.got_z = at, acc, got_s, got_f, got_z
        self.send_sem, self.recv_sem, self.out_ref = send_sem, recv_sem, out_ref
        self.rows = acc.shape[1]
        self.f_dev, self.s_dev, self.z_dev = (
            at.device(oe=at.dy),
            at.device(oe=at.dc),
            at.device(zi=1),
        )
        self.twins = [[], [], [], []]
        self.started, self.in_middle, self.at_end = [], [], []

    def held(self, f, zi, twin=0):
        at = self.at
        return zi * 4 + at.e + f * at.dy + twin * at.dc if self.by_block else f * 4 + zi

    def push(self, src, dst, slot, device, sends=None, record=None):
        j = slot if sends is None else sends
        remote(src, dst, self.send_sem.at[j], self.recv_sem.at[slot], device).start()
        (self.started if record is None else record).append(j)

    def gone(self, j):
        spot = self.acc.at[0]
        remote(spot, spot, self.send_sem.at[j], self.recv_sem.at[0], self.s_dev).wait_send()

    def arrive(self, dst, slot):
        remote(
            self.acc.at[0], dst, self.send_sem.at[slot], self.recv_sem.at[slot], self.s_dev
        ).wait_recv()

    def to_twin(self, src, f, zi):
        k = f * 4 + zi
        self.push(src, self.got_s.at[k], 9 + k, self.s_dev, None, self.twins[zi])

    def twin_gone(self, zi):
        for j in self.twins[zi]:
            self.gone(j)
        self.twins[zi] = []

    def add(self, k, *others, into=None):
        acc = self.acc

        @pl.loop(0, self.rows // 16)
        def _(i):
            span = pl.ds(pl.multiple_of(i * 16, 16), 16)
            total = acc[k, span, :].astype(F32)
            for ref, j in others:
                total = total + ref[j, span, :].astype(F32)
            if into is None:
                acc[k, span, :] = total.astype(BF)
            else:
                into[span, :] = total

    def first(self, zi):
        k = self.held(1, zi)
        self.arrive(self.got_s.at[4 + zi], 13 + zi)
        self.add(k, (self.got_s, 4 + zi))
        self.push(self.acc.at[k], self.got_f.at[zi], 5 + zi, self.f_dev)

    def second(self, zi):
        at, acc, got_z = self.at, self.acc, self.got_z
        self.arrive(self.got_s.at[zi], 9 + zi)
        self.arrive(self.got_f.at[zi], 5 + zi)
        others = [(self.got_s, zi), (self.got_f, zi)]
        k = self.held(0, zi)
        if zi >= 2:

            @pl.when(at.middle)
            def _():
                self.arrive(got_z.at[3 - zi], 3 - zi)
                self.add(k, *others, (got_z, 3 - zi))
                there = 4 if zi == 2 else 3
                self.push(acc.at[k], got_z.at[there], there, at.inward(), zi, self.in_middle)

            @pl.when(jnp.logical_not(at.middle))
            def _():
                self.add(k, *others)
                self.push(acc.at[k], got_z.at[3 - zi], 3 - zi, self.z_dev, zi, self.at_end)
        elif zi == 1:

            @pl.when(at.middle)
            def _():
                self.arrive(got_z.at[3], 3)
                self.add(k, *others, (got_z, 3))
                self.push(acc.at[k], got_z.at[4], 4, self.z_dev, 1, self.in_middle)

            @pl.when(jnp.logical_not(at.middle))
            def _():
                self.add(k, *others)
                self.push(acc.at[k], got_z.at[2], 2, self.z_dev, 1, self.at_end)
        else:

            @pl.when(at.middle)
            def _():
                self.arrive(got_z.at[2], 2)
                self.arrive(got_z.at[4], 4)
                self.add(k, *others, (got_z, 2), (got_z, 4), into=self.out_ref)

            @pl.when(jnp.logical_not(at.middle))
            def _():
                self.arrive(got_z.at[4], 4)
                self.add(k, *others, (got_z, 4), into=self.out_ref)

    def finish(self):
        for zi in range(4):
            self.twin_gone(zi)
        for j in self.started:
            self.gone(j)

        @pl.when(self.at.middle)
        def _():
            for j in self.in_middle:
                self.gone(j)

        @pl.when(jnp.logical_not(self.at.middle))
        def _():
            for j in self.at_end:
                self.gone(j)


def scatter_buffers(rows, width, held=8):
    return [
        pltpu.VMEM((held, rows, width), BF),
        pltpu.VMEM((8, rows, width), BF),
        pltpu.VMEM((4, rows, width), BF),
        pltpu.VMEM((5, rows, width), BF),
        pltpu.SemaphoreType.DMA((17,)),
        pltpu.SemaphoreType.DMA((17,)),
    ]


def scatter_kernel(rows, starts, in_ref, *refs):
    swaps = len(starts)
    given, out_ref, taken = refs[:swaps], refs[swaps], refs[swaps + 1 : 2 * swaps + 1]
    buffers, load_sem = refs[2 * swaps + 1 : 2 * swaps + 7], refs[2 * swaps + 7]
    acc = buffers[0]
    at = Place()
    greet(at, False, swaps > 0)
    crossing = cross(at, given, taken, *refs[2 * swaps + 8 :], starts) if swaps else []
    total = Scatter(at, *buffers, out_ref)

    def rows_of(rank):
        return in_ref.at[pl.ds(pl.multiple_of(rank * rows, rows), rows)]

    order = [(f, zi) for f in (1, 0) for zi in (3, 2, 1, 0)]
    loads = {}
    for f, zi in order:
        k = f * 4 + zi
        total.to_twin(rows_of(at.shard(f * at.dy + at.dc, zi)), f, zi)
        loads[k] = pltpu.make_async_copy(
            rows_of(at.shard(f * at.dy, zi)), acc.at[k], load_sem.at[k]
        )
        loads[k].start()
    for copy in crossing:
        copy.start()
    for f, zi in order:
        loads[f * 4 + zi].wait()
        (total.first if f else total.second)(zi)
    for copy in crossing:
        copy.wait()
    total.finish()


def own_rows(x, cid, given=(), starts=()):
    rows, width = x.shape[0] // 16, x.shape[1]
    swaps = len(given)
    hbm = pl.BlockSpec(memory_space=pl.ANY)
    crossing = [pltpu.SemaphoreType.DMA((swaps,))] * 2 if swaps else []
    got = pl.pallas_call(
        functools.partial(scatter_kernel, rows, starts),
        out_shape=[jax.ShapeDtypeStruct((rows, width), F32)]
        + [half_of(a) for a in given],
        in_specs=[hbm] * (1 + swaps),
        out_specs=[pl.BlockSpec(memory_space=pltpu.VMEM)] + [hbm] * swaps,
        scratch_shapes=[
            *scatter_buffers(rows, width),
            pltpu.SemaphoreType.DMA((8,)),
            *crossing,
        ],
        compiler_params=pltpu.CompilerParams(
            collective_id=cid, has_side_effects=True, vmem_limit_bytes=40 * 1024 * 1024
        ),
    )(x, *given)
    return got if swaps else got[0]


class Gather:
    def __init__(self, at, x_ref, out_ref, own_sem, send_sem, recv_sem, block=False):
        self.at, self.x_ref, self.out_ref, self.block = at, x_ref, out_ref, block
        self.send_sem, self.recv_sem = send_sem, recv_sem
        self.rows = x_ref.shape[0] // (4 if block else 1)
        self.f_dev, self.s_dev, self.z_dev = (
            at.device(oe=at.dy),
            at.device(oe=at.dc),
            at.device(zi=1),
        )
        self.started, self.inside = [], []
        rows, self.source = self.rows, x_ref
        spot = self.where(0, 0)
        if block:
            self.source = x_ref.at[pl.ds(pl.multiple_of(at.e * rows, rows), rows)]
            spot = pl.ds(pl.multiple_of(at.z * 4 * rows, 4 * rows), 4 * rows)
        self.own = pltpu.make_async_copy(x_ref, out_ref.at[spot], own_sem)

    def where(self, f, zi):
        rows = self.rows
        return pl.ds(pl.multiple_of(self.at.shard(f * self.at.dy, zi) * rows, rows), rows)

    def push(self, f, zi, slot, device, sends=None, record=None):
        src = self.source if f == 0 and zi == 0 else self.out_ref.at[self.where(f, zi)]
        dst = self.out_ref.at[self.where(f, zi)]
        j = slot if sends is None else sends
        remote(src, dst, self.send_sem.at[j], self.recv_sem.at[slot], device).start()
        (self.started if record is None else record).append(j)

    def spot(self):
        return self.x_ref.at[pl.ds(0, self.rows)], self.out_ref.at[pl.ds(0, self.rows)]

    def arrive(self, slot):
        remote(*self.spot(), self.send_sem.at[slot], self.recv_sem.at[slot], self.s_dev).wait_recv()

    def forward(self, f, zi):
        if f == 0:
            if zi == 0:
                self.push(0, 0, 0, self.z_dev)
            if zi < 2:
                pl.when(self.at.middle)(
                    lambda: self.push(0, zi, 1 + zi, self.at.inward(), 15 + zi, self.inside)
                )
            else:
                pl.when(self.at.middle)(
                    lambda: self.push(0, zi, zi - 1, self.z_dev, 15 + zi, self.inside)
                )
        if self.block and zi == 0:
            return
        if f == 0:
            self.push(0, zi, 3 + zi, self.f_dev)
        self.push(f, zi, 7 + f * 4 + zi, self.s_dev)

    def begin(self):
        self.forward(0, 0)
        self.own.start()

    def line(self, zi):
        self.arrive(zi - 1)
        self.forward(0, zi)

    def other(self, zi):
        self.arrive(3 + zi)
        self.forward(1, zi)

    def twin(self, zi):
        self.arrive(7 + zi)
        self.arrive(11 + zi)

    def finish(self, arrived=False):
        for zi in range(4):
            if not arrived and not (self.block and zi == 0):
                self.twin(zi)
        if not arrived:
            self.own.wait()
        for j in self.started:
            remote(*self.spot(), self.send_sem.at[j], self.recv_sem.at[0], self.s_dev).wait_send()

        @pl.when(self.at.middle)
        def _():
            for j in self.inside:
                remote(
                    *self.spot(), self.send_sem.at[j], self.recv_sem.at[0], self.s_dev
                ).wait_send()


def columns_loop(width, parts):
    size = width // parts

    def over(run):
        @pl.loop(0, parts)
        def _(n):
            run(pl.ds(pl.multiple_of(n * size, size), size))

    return over


def expert_gather_kernel(experts, *refs):
    refs = list(refs)

    def take(count):
        taken = refs[:count]
        del refs[:count]
        return taken

    x_ref, dy_ref, disp, w_router, shared_in, shared_out = take(6)
    weights, given = take(7), take(2)
    out_ref, picked, picked_dy, scaled_out, g_out, u_out, gb_out, sa_out, sg_out = take(9)
    taken = take(2)
    wg, wu, wd, xb, dyd, sb, pk, pdy, sc, gg, uu, hid, gb, sa, sg = take(15)
    own_sem, send_sem, recv_sem, load_sem, block_sem, store_sem, cross_send, cross_recv = take(8)
    at = Place()
    greet(at, False, True)
    gather = Gather(at, x_ref, out_ref, own_sem, send_sem, recv_sem)
    crossing = cross(at, given, taken, cross_send, cross_recv, (0, taken[0].shape[0]))
    block = xb.shape[1]
    slots = pk.shape[0] // 4
    part = wd.shape[1] // 2
    mine = at.z * 4 + at.e

    def span(zi, size):
        return pl.ds(pl.multiple_of(at.zs[zi] * size, size), size)

    def dy_load(zi):
        return pltpu.make_async_copy(
            dy_ref.at[span(zi, block)], xb.at[zi % 2], block_sem.at[2 + zi % 2]
        )

    def x_load(zi):
        return pltpu.make_async_copy(
            out_ref.at[span(zi, block)], xb.at[zi % 2], block_sem.at[zi % 2]
        )

    def stores(zi):
        b = zi % 2
        pairs = [(sa.at[b], sa_out.at[span(zi, block)]), (sg.at[b], sg_out.at[span(zi, block)])]
        return [
            pltpu.make_async_copy(src, dst, store_sem.at[b * 2 + j])
            for j, (src, dst) in enumerate(pairs)
        ]

    def parts_of(gate, up):
        s = 1.0 / (1.0 + jnp.exp(-gate))
        act = gate * s
        return act * up, s * (1.0 + gate * (1.0 - s)) * up, act

    def ahead(zi):
        b = zi % 2
        some = span(zi, slots)
        dy_load(zi).wait()
        pdy[some, :] = product(disp[at.zs[zi]], xb[b]).astype(BF)
        sb[span(zi, block), :] = transposed_right(xb[b], shared_out[...])
        if zi < 2:
            dy_load(zi + 2).start()
        dyd[some, :] = transposed_right(pdy[some, :], wd[0])

    def work(zi):
        b = zi % 2
        some = span(zi, slots)
        x_load(zi).wait()
        if zi >= 2:
            for copy in stores(zi - 2):
                copy.wait()
        pk[some, :] = product(disp[at.zs[zi]], xb[b]).astype(BF)
        logits = transposed_right(pk[some, :], w_router[...])
        lane = lax.broadcasted_iota(jnp.int32, logits.shape, 1)
        logits = jnp.where(lane < experts, logits, MASKED)
        powers = jnp.exp(logits - jnp.max(logits, axis=1, keepdims=True))
        own_power = jnp.sum(jnp.where(lane == mine, powers, 0.0), axis=1, keepdims=True)
        gate_of = own_power / jnp.sum(powers, axis=1, keepdims=True)
        for h in range(2):
            hidden, by_gate, by_up = parts_of(
                transposed_right(pk[some, :], wg[h]), transposed_right(pk[some, :], wu[h])
            )
            sc[h, some, :] = (hidden * gate_of).astype(BF)
            if h == 0:
                dy_down = dyd[some, :]
                act_back = gate_of * dy_down
                gg[0, some, :] = (act_back * by_gate).astype(BF)
                uu[0, some, :] = (act_back * by_up).astype(BF)
                gb[some, :] = jnp.broadcast_to(
                    jnp.sum(hidden * dy_down, axis=1, keepdims=True), (slots, gb.shape[1])
                )
            else:
                hid[some, :] = hidden.astype(BF)
                gg[1, some, :] = (gate_of * by_gate).astype(BF)
                uu[1, some, :] = (gate_of * by_up).astype(BF)
        both = transposed_right(xb[b], shared_in[...])
        wide = both.shape[1] // 2
        hidden, by_gate, by_up = parts_of(both[:, :wide], both[:, wide:])
        back = sb[span(zi, block), :]
        sa[b] = hidden.astype(BF)
        sg[b, :, :wide] = (back * by_gate).astype(BF)
        sg[b, :, wide:] = (back * by_up).astype(BF)
        for copy in stores(zi):
            copy.start()

    def other_half(zi):
        some = span(zi, slots)
        dy_down = transposed_right(pdy[some, :], wd[1])
        gg[1, some, :] = (dy_down * gg[1, some, :].astype(F32)).astype(BF)
        uu[1, some, :] = (dy_down * uu[1, some, :].astype(F32)).astype(BF)
        gb[some, :] += jnp.broadcast_to(
            jnp.sum(hid[some, :].astype(F32) * dy_down, axis=1, keepdims=True), (slots, gb.shape[1])
        )

    gather.begin()
    places = [
        wg.at[0],
        wu.at[0],
        wd.at[0],
        wg.at[1, pl.ds(0, part)],
        wg.at[1, pl.ds(part, part)],
        wu.at[1, pl.ds(0, part)],
        wu.at[1, pl.ds(part, part)],
        wd.at[1, pl.ds(0, part)],
        wd.at[1, pl.ds(part, part)],
    ]
    loads = [
        pltpu.make_async_copy(a, b, load_sem.at[j]) for j, (a, b) in enumerate(zip(weights + taken, places))
    ]
    dy_load(0).start()
    dy_load(1).start()
    for j in (2, 0, 1, 3, 4, 5, 6):
        loads[j].start()
    for copy in crossing:
        copy.start()
    loads[2].wait()
    for zi in range(3):
        ahead(zi)
    for zi in range(4):
        gather.other(zi)
        if zi < 3:
            gather.line(zi + 1)
        if zi == 0:
            ahead(3)
        gather.twin(zi)
        if zi == 0:
            gather.own.wait()
        x_load(zi).start()
        if zi == 0:
            for j in (0, 1, 3, 4, 5, 6):
                loads[j].wait()
        work(zi)
    results = [(pk, picked), (pdy, picked_dy), (sc, scaled_out), (gg, g_out), (uu, u_out), (gb, gb_out)]
    results = [
        pltpu.make_async_copy(a, b, store_sem.at[4 + j]) for j, (a, b) in enumerate(results)
    ]
    for copy in results[:3]:
        copy.start()
    for m in range(2):
        crossing[m].wait_recv()
        loads[7 + m].start()
    for m in range(2):
        loads[7 + m].wait()
    for zi in range(4):
        other_half(zi)
    for copy in results[3:]:
        copy.start()
    for copy in results:
        copy.wait()
    for zi in (2, 3):
        for copy in stores(zi):
            copy.wait()
    for copy in crossing:
        copy.wait_send()
    gather.finish(True)


def expert_rows(x, dy_all, dispatch, w_router, experts, shared_in, shared_out, weights, given, cid):
    rows, width = x.shape
    total, block = 16 * rows, 4 * rows
    slots = 4 * dispatch.shape[1]
    hidden = weights[0].shape[0]
    wide = shared_out.shape[0]
    halves = [half_of(a) for a in given]
    hbm, vmem = pl.BlockSpec(memory_space=pl.ANY), pl.BlockSpec(memory_space=pltpu.VMEM)
    shape, sems = jax.ShapeDtypeStruct, lambda n: pltpu.SemaphoreType.DMA((n,))
    return pl.pallas_call(
        functools.partial(expert_gather_kernel, experts),
        out_shape=[
            shape((total, width), BF),
            shape((slots, width), BF),
            shape((slots, width), BF),
            shape((2, slots, hidden), BF),
            shape((2, slots, hidden), BF),
            shape((2, slots, hidden), BF),
            shape((slots, 128), F32),
            shape((total, wide), BF),
            shape((total, 2 * wide), BF),
            *halves,
        ],
        in_specs=[hbm, hbm, vmem, vmem, vmem, vmem] + [hbm] * 9,
        out_specs=[hbm] * 11,
        scratch_shapes=[
            pltpu.VMEM((2, hidden, width), BF),
            pltpu.VMEM((2, hidden, width), BF),
            pltpu.VMEM((2, hidden, width), BF),
            pltpu.VMEM((2, block, width), BF),
            pltpu.VMEM((slots, hidden), F32),
            pltpu.VMEM((total, wide), F32),
            pltpu.VMEM((slots, width), BF),
            pltpu.VMEM((slots, width), BF),
            pltpu.VMEM((2, slots, hidden), BF),
            pltpu.VMEM((2, slots, hidden), BF),
            pltpu.VMEM((2, slots, hidden), BF),
            pltpu.VMEM((slots, hidden), BF),
            pltpu.VMEM((slots, 128), F32),
            pltpu.VMEM((2, block, wide), BF),
            pltpu.VMEM((2, block, 2 * wide), BF),
            pltpu.SemaphoreType.DMA,
            sems(19),
            sems(15),
            sems(9),
            sems(4),
            sems(10),
            sems(2),
            sems(2),
        ],
        compiler_params=pltpu.CompilerParams(
            collective_id=cid, has_side_effects=True, vmem_limit_bytes=62 * 1024 * 1024
        ),
    )(x, dy_all, dispatch, w_router, shared_in, shared_out, *weights, *given)


def expert_scatter_kernel(*refs):
    refs = list(refs)

    def take(count):
        taken = refs[:count]
        del refs[:count]
        return taken

    disp, gate_back, shared_in, g_ref, u_ref, sg_ref, picked_ref, dy_ref, scaled_ref = take(9)
    weights = take(6)
    out_ref, taken, *grads = take(7)
    wg, wu, gs, us, sg, picked, picked_dy, scaled, ib, grad, turned = take(11)
    acc, got_s, got_f, got_z, send_sem, recv_sem = take(6)
    load_sem, store_sem, cross_send, cross_recv = take(4)
    at = Place()
    greet(at, False, True)
    rows, full = acc.shape[1:]
    width = shared_in.shape[1]
    slots = ib.shape[0]
    block = 4 * rows
    over = columns_loop(width, 4)
    mine = at.z * 4 + at.e
    total = Scatter(at, acc, got_s, got_f, got_z, send_sem, recv_sem, out_ref, True)

    part = wg.shape[1] // 2
    pairs = [
        (weights[0], wg.at[0]),
        (weights[1], wu.at[0]),
        (weights[2], wg.at[1, pl.ds(0, part)]),
        (weights[3], wg.at[1, pl.ds(part, part)]),
        (weights[4], wu.at[1, pl.ds(0, part)]),
        (weights[5], wu.at[1, pl.ds(part, part)]),
        (g_ref, gs),
        (u_ref, us),
        (sg_ref, sg),
        (picked_ref, picked),
        (dy_ref, picked_dy),
        (scaled_ref.at[1], scaled),
    ]
    loads = [pltpu.make_async_copy(a, b, load_sem.at[j]) for j, (a, b) in enumerate(pairs)]
    for copy in loads:
        copy.start()

    def work(zi):
        place = at.zs[zi]
        some = pl.ds(pl.multiple_of(place * slots, slots), slots)

        hot = disp[place]
        tokens = pl.ds(pl.multiple_of(place * block, block), block)

        @over
        def _(columns):
            terms = product(gs[0, some, :], wg[0, :, columns])
            terms += product(us[0, some, :], wu[0, :, columns])
            terms += product(gs[1, some, :], wg[1, :, columns])
            terms += product(us[1, some, :], wu[1, :, columns])
            ib[:, columns] = terms.astype(BF)

        @over
        def _(columns):
            terms = transposed_left(hot, ib[:, columns])
            terms += product(sg[tokens, :], shared_in[:, columns])
            for e in range(4):
                acc[zi * 4 + e, :, columns] = terms[e * rows : (e + 1) * rows].astype(BF)

        from_gates = gate_back[some, :]
        lane = lax.broadcasted_iota(jnp.int32, from_gates.shape, 1)
        terms = transposed_left(hot, jnp.where(lane == mine, from_gates, 0.0).astype(BF))
        for e in range(4):
            acc[zi * 4 + e, :, width:] = terms[e * rows : (e + 1) * rows].astype(BF)

    def gradient(m):
        step = 256
        right = picked_dy if m == 2 else picked
        turned[...] = (scaled[...] if m == 2 else gs[1] if m == 0 else us[1]).T

        @pl.loop(0, width // step)
        def _(n):
            columns = pl.ds(pl.multiple_of(n * step, step), step)
            grad[min(m, 1), :, columns] = product(turned[...], right[:, columns]).astype(BF)

    crossing = cross(at, [grad.at[0, pl.ds(0, part)]], [taken], cross_send, cross_recv)[0]
    stores = [
        pltpu.make_async_copy(
            grad.at[min(j // 2, 1), pl.ds(j % 2 * part, part)], grads[j - 1], store_sem.at[j]
        )
        for j in range(1, 6)
    ]
    for copy in loads[:9]:
        copy.wait()
    for zi in (3, 2, 1, 0):
        work(zi)
        for f in range(2):
            total.to_twin(acc.at[total.held(f, zi, 1)], f, zi)
        total.first(zi)
        if zi == 1:
            total.second(3)
    for copy in loads[9:]:
        copy.wait()
    for m, zi in ((0, 2), (1, 1), (2, 0)):
        if m == 2:
            stores[1].wait()
            stores[2].wait()
        gradient(m)
        if m == 0:
            crossing.start()
        for j in (2 * m, 2 * m + 1):
            if j > 0:
                stores[j - 1].start()
        total.second(zi)
    for j in (0, 3, 4):
        stores[j].wait()
    crossing.wait()
    total.finish()


def expert_back(dispatch, gate_back, shared_in, g, u, sg, picked, picked_dy, scaled, weights, cid):
    total, wide = sg.shape
    width = shared_in.shape[1]
    rows, full = total // 16, width + 128
    slots = picked.shape[0]
    hidden = g.shape[2]
    hbm, vmem = pl.BlockSpec(memory_space=pl.ANY), pl.BlockSpec(memory_space=pltpu.VMEM)
    shape = jax.ShapeDtypeStruct
    return pl.pallas_call(
        expert_scatter_kernel,
        out_shape=[
            shape((rows, full), F32),
            *[shape((hidden // 2, width), BF)] * 6,
        ],
        in_specs=[vmem] * 3 + [hbm] * 12,
        out_specs=[vmem] + [hbm] * 6,
        scratch_shapes=[
            pltpu.VMEM((2, hidden, width), BF),
            pltpu.VMEM((2, hidden, width), BF),
            pltpu.VMEM((2, slots, hidden), BF),
            pltpu.VMEM((2, slots, hidden), BF),
            pltpu.VMEM((total, wide), BF),
            pltpu.VMEM((slots, width), BF),
            pltpu.VMEM((slots, width), BF),
            pltpu.VMEM((slots, hidden), BF),
            pltpu.VMEM((slots // 4, width), BF),
            pltpu.VMEM((2, hidden, width), BF),
            pltpu.VMEM((hidden, slots), BF),
            *scatter_buffers(rows, full, 16),
            pltpu.SemaphoreType.DMA((12,)),
            pltpu.SemaphoreType.DMA((6,)),
            pltpu.SemaphoreType.DMA((1,)),
            pltpu.SemaphoreType.DMA((1,)),
        ],
        compiler_params=pltpu.CompilerParams(
            collective_id=cid, has_side_effects=True, vmem_limit_bytes=63 * 1024 * 1024
        ),
    )(dispatch, gate_back, shared_in, g, u, sg, picked, picked_dy, scaled, *weights)


def mixed_kernel(*refs):
    refs = list(refs)

    def take(count):
        taken = refs[:count]
        del refs[:count]
        return taken

    w_out, w_qkv, tables, q_ref, k_ref, v_ref, lse_ref, heads_out = take(8)
    in_ref, back_ref, normed_ref, *given = take(5)
    out_ref, normed_back, home_out, *taken = take(5)
    rows_in, do, dk, dv, qkv, out_sum, qkv_sum, staged = take(8)
    buffers = take(6)
    first_sem, in_sem, store_sem, cross_send, cross_recv = take(5)
    at = Place()
    greet(at, False, True)
    total = Scatter(at, *buffers, out_ref)
    acc = buffers[0]
    rows, width = acc.shape[1:]
    length = q_ref.shape[0]
    block = length // 4
    crossing = cross(at, given, taken, cross_send, cross_recv)

    def rows_of(rank):
        return in_ref.at[pl.ds(pl.multiple_of(rank * rows, rows), rows)]

    order = [(f, zi) for f in (1, 0) for zi in (3, 2, 1, 0)]
    firsts = {}
    for f, zi in order:
        m = f * 4 + zi
        total.to_twin(rows_of(at.shard(f * at.dy + at.dc, zi)), f, zi)
        firsts[m] = pltpu.make_async_copy(
            rows_of(at.shard(f * at.dy, zi)), acc.at[m], first_sem.at[m]
        )
        firsts[m].start()
    for copy in crossing:
        copy.start()

    def rows_load(j):
        ref = back_ref if j < 4 else normed_ref
        return pltpu.make_async_copy(
            ref.at[pl.ds(j % 4 * block, block)], rows_in.at[j % 2], in_sem.at[j % 2]
        )

    rows_load(0).start()
    rows_load(1).start()

    def heads_back(j):
        rows_load(j).wait()
        here = pl.ds(j * block, block)
        do[here, :] = transposed_right(rows_in[j % 2], w_out[...]).astype(BF)
        turned = heads_out[here, :].T

        @pl.loop(0, 4)
        def _(n):
            columns = pl.ds(pl.multiple_of(n * (width // 4), width // 4), width // 4)
            terms = product(turned, rows_in[j % 2, :, columns])
            out_sum[:, columns] = terms if j == 0 else out_sum[:, columns] + terms

        rows_load(j + 2).start()

    scale = HDIM ** (-0.5)
    step = 256

    def attend_rows(i):
        seen = (i + 1) * step
        here = pl.ds(i * step, step)
        q, go = q_ref[here, :], do[here, :]
        scores = transposed_right(q, k_ref[0:seen, :]) * scale
        row_at = lax.broadcasted_iota(jnp.int32, scores.shape, 0) + i * step
        col_at = lax.broadcasted_iota(jnp.int32, scores.shape, 1)
        scores = jnp.where(row_at >= col_at, scores, MASKED)
        probs = jnp.exp(scores - lse_ref[here, 0:1])
        weight_back = transposed_right(go, v_ref[0:seen, :])
        inner = jnp.sum(probs * weight_back, axis=-1, keepdims=True)
        score_back = (probs * (weight_back - inner)).astype(BF)
        dv[0:seen, :] += transposed_left(probs.astype(BF), go)
        dk[0:seen, :] += transposed_left(score_back, q) * scale
        qkv[here, 0:HDIM] = turn_rows(product(score_back, k_ref[0:seen, :]) * scale, here)

    def turn_rows(values, here):
        other = pltpu.roll(values, HDIM // 2, 1)
        return (values * tables[0, here, :] + other * tables[1, here, :]).astype(BF)

    def finish_heads():
        for j in range(8):
            here = pl.ds(j * step, step)
            qkv[here, HDIM : 2 * HDIM] = turn_rows(dk[here, :], here)
            qkv[here, 2 * HDIM :] = dv[here, :].astype(BF)

    def normed_store(j):
        return pltpu.make_async_copy(
            staged.at[j % 2], normed_back.at[pl.ds(j * step, step)], store_sem.at[j % 2]
        )

    def normed_rows(j):
        if j >= 2:
            normed_store(j - 2).wait()

        @pl.loop(0, 4)
        def _(n):
            columns = pl.ds(pl.multiple_of(n * (width // 4), width // 4), width // 4)
            staged[j % 2, :, columns] = product(
                qkv[pl.ds(j * step, step), :], w_qkv[:, columns]
            ).astype(BF)

        normed_store(j).start()

    def qkv_rows(j):
        rows_load(4 + j).wait()
        turned = qkv[pl.ds(j * block, block), :].T

        @pl.loop(0, 4)
        def _(n):
            columns = pl.ds(pl.multiple_of(n * (width // 4), width // 4), width // 4)
            terms = product(turned, rows_in[j % 2, :, columns])
            qkv_sum[:, columns] = terms if j == 0 else qkv_sum[:, columns] + terms

        if j < 2:
            rows_load(6 + j).start()

    for zi in (3, 2, 1, 0):
        firsts[4 + zi].wait()
        total.first(zi)
    for j in range(4):
        heads_back(j)
    firsts[3].wait()
    total.second(3)
    dk[...] = jnp.zeros_like(dk)
    dv[...] = jnp.zeros_like(dv)
    for i in range(3):
        attend_rows(i)
    firsts[2].wait()
    total.second(2)
    for i in range(3, 6):
        attend_rows(i)
    firsts[1].wait()
    total.second(1)
    for i in range(6, 8):
        attend_rows(i)
    finish_heads()
    for j in range(8):
        normed_rows(j)
    for j in range(4):
        qkv_rows(j)
    size = home_out.shape[2]
    for j in range(8):
        columns = slice(j * size, (j + 1) * size)
        home_out[j, : 3 * HDIM, :] = qkv_sum[:, columns].astype(BF)
        home_out[j, 3 * HDIM :, :] = out_sum[:, columns].astype(BF)
    firsts[0].wait()
    total.second(0)
    for j in (6, 7):
        normed_store(j).wait()
    for copy in crossing:
        copy.wait()
    total.finish()


def mixed_rows(
    w_out, w_qkv, tables, q, k, v, lse, heads_out, mixed_part, attn_back, normed, given, cid
):
    length, width = attn_back.shape
    rows = length // 16
    hbm, vmem = pl.BlockSpec(memory_space=pl.ANY), pl.BlockSpec(memory_space=pltpu.VMEM)
    shape = jax.ShapeDtypeStruct
    return pl.pallas_call(
        mixed_kernel,
        out_shape=[
            shape((rows, width), F32),
            shape((length, width), BF),
            shape((8, 4 * HDIM, width // 8), BF),
            *[shape(a.shape, BF) for a in given],
        ],
        in_specs=[vmem] * 8 + [hbm] * 5,
        out_specs=[vmem, hbm, vmem, hbm, hbm],
        scratch_shapes=[
            pltpu.VMEM((2, length // 4, width), BF),
            pltpu.VMEM((length, HDIM), BF),
            pltpu.VMEM((length, HDIM), F32),
            pltpu.VMEM((length, HDIM), F32),
            pltpu.VMEM((length, 3 * HDIM), BF),
            pltpu.VMEM((HDIM, width), F32),
            pltpu.VMEM((3 * HDIM, width), F32),
            pltpu.VMEM((2, 256, width), BF),
            *scatter_buffers(rows, width),
            pltpu.SemaphoreType.DMA((8,)),
            pltpu.SemaphoreType.DMA((2,)),
            pltpu.SemaphoreType.DMA((2,)),
            pltpu.SemaphoreType.DMA((2,)),
            pltpu.SemaphoreType.DMA((2,)),
        ],
        compiler_params=pltpu.CompilerParams(
            collective_id=cid, has_side_effects=True, vmem_limit_bytes=63 * 1024 * 1024
        ),
    )(w_out, w_qkv, tables, q, k, v, lse, heads_out, mixed_part, attn_back, normed, *given)


def gather_back_kernel(*refs):
    refs = list(refs)

    def take(count):
        taken = refs[:count]
        del refs[:count]
        return taken

    x_ref, disp, shared_out = take(3)
    scaled_ref, act_ref, sg_ref, wd_a, wd_0, wd_1, mix_ref, dy_ref, *given = take(10)
    out_ref, mixed_part, units_grad, *taken = take(5)
    scaled, acts, sg, wd, eb, mixes, dys, staged, turned, turned_acts = take(10)
    own_sem, send_sem, recv_sem, cross_send, cross_recv, load_sem, store_sem = take(7)
    at = Place()
    greet(at, False, True)
    gather = Gather(at, x_ref, out_ref, own_sem, send_sem, recv_sem)
    crossing = cross(at, given, taken, cross_send, cross_recv)
    rows, width = x_ref.shape
    slots = eb.shape[0]
    block = 4 * rows
    units = acts.shape[1]
    cut = units_grad.shape[1] // 3
    over = columns_loop(width, 4)

    gather.begin()
    for copy in crossing:
        copy.start()
    pairs = [
        (scaled_ref, scaled),
        (act_ref, acts),
        (wd_a, wd.at[0]),
        (wd_0, wd.at[1, pl.ds(0, wd_0.shape[0])]),
        (wd_1, wd.at[1, pl.ds(wd_0.shape[0], wd_0.shape[0])]),
        (sg_ref, sg),
        (mix_ref, mixes),
        (dy_ref, dys),
    ]
    loads = [pltpu.make_async_copy(a, b, load_sem.at[j]) for j, (a, b) in enumerate(pairs)]
    for copy in loads:
        copy.start()

    def mixed_store(j):
        return pltpu.make_async_copy(
            staged.at[j % 2], mixed_part.at[pl.ds(j * block, block)], store_sem.at[j % 2]
        )

    def mixed_rows_of(j):
        some = pl.ds(j * slots, slots)

        @over
        def _(columns):
            terms = product(scaled[0, some, :], wd[0, :, columns])
            terms += product(scaled[1, some, :], wd[1, :, columns])
            eb[:, columns] = terms.astype(BF)

        if j >= 2:
            mixed_store(j - 2).wait()
        tokens = pl.ds(j * block, block)

        @over
        def _(columns):
            terms = transposed_left(disp[j], eb[:, columns])
            terms += product(acts[tokens, :], shared_out[:, columns])
            staged[j % 2, :, columns] = terms.astype(BF)

        mixed_store(j).start()

    def units_of(first, count):
        size = units_grad.shape[2]

        @pl.loop(first, first + count)
        def _(n):
            columns = pl.ds(pl.multiple_of(n * size, size), size)
            terms = product(turned[...], mixes[:, columns]).astype(BF)
            units_grad[n, 0:cut, :] = terms[:cut]
            units_grad[n, cut : 2 * cut, :] = terms[units : units + cut]
            terms = product(turned_acts[...], dys[:, columns]).astype(BF)
            units_grad[n, 2 * cut :, :] = terms[:cut]

    for copy in loads[:5]:
        copy.wait()
    for zi in range(4):
        if zi > 0:
            gather.line(zi)
        mixed_rows_of(zi)
        if zi == 0:
            for copy in loads[5:]:
                copy.wait()
            turned[...] = sg[...].T
            turned_acts[...] = acts[...].T
        gather.other(zi)
        units_of(2 * zi, 2)
    for j in (2, 3):
        mixed_store(j).wait()
    for copy in crossing:
        copy.wait()
    gather.finish()


def gather_back(x, given, dispatch, shared_out, scaled, acts, sg, wd, mix_all, dy_all, cut, cid):
    rows, width = x.shape
    length, units = acts.shape
    slots, hidden = scaled.shape[1:]
    hbm, vmem = pl.BlockSpec(memory_space=pl.ANY), pl.BlockSpec(memory_space=pltpu.VMEM)
    shape = jax.ShapeDtypeStruct
    return pl.pallas_call(
        gather_back_kernel,
        out_shape=[
            shape((length, width), BF),
            shape((length, width), BF),
            shape((8, 3 * cut, width // 8), BF),
            *[shape(a.shape, BF) for a in given],
        ],
        in_specs=[hbm, vmem, vmem] + [hbm] * 10,
        out_specs=[hbm, hbm, vmem, hbm, hbm],
        scratch_shapes=[
            pltpu.VMEM((2, slots, hidden), BF),
            pltpu.VMEM(acts.shape, BF),
            pltpu.VMEM(sg.shape, BF),
            pltpu.VMEM((2, hidden, width), BF),
            pltpu.VMEM((slots // 4, width), BF),
            pltpu.VMEM((length, width), BF),
            pltpu.VMEM((length, width), BF),
            pltpu.VMEM((2, 4 * rows, width), BF),
            pltpu.VMEM((2 * units, length), BF),
            pltpu.VMEM((units, length), BF),
            pltpu.SemaphoreType.DMA,
            pltpu.SemaphoreType.DMA((19,)),
            pltpu.SemaphoreType.DMA((15,)),
            pltpu.SemaphoreType.DMA((2,)),
            pltpu.SemaphoreType.DMA((2,)),
            pltpu.SemaphoreType.DMA((8,)),
            pltpu.SemaphoreType.DMA((2,)),
        ],
        compiler_params=pltpu.CompilerParams(
            collective_id=cid, has_side_effects=True, vmem_limit_bytes=60 * 1024 * 1024
        ),
    )(x, dispatch, shared_out, scaled, acts, sg, *wd, mix_all, dy_all, *given)


class Home:
    def __init__(self, at, arrays, outs, mine, got, load_sem, x_send, x_recv, z_send, z_recv):
        self.at, self.outs, self.mine, self.got = at, outs, mine, got
        self.z_send, self.z_recv = z_send, z_recv
        there = (1 - at.x) * 4
        self.loads, self.crossing, self.keep = {}, {}, []
        self.count = len(arrays)
        for m, array in enumerate(arrays):
            for k in range(4):
                spot, j = at.zs[k], m * 4 + k
                self.loads[m, k] = pltpu.make_async_copy(
                    array.at[at.x * 4 + spot], mine[m].at[spot], load_sem.at[m * 5 + k]
                )
                self.crossing[m, k] = remote(
                    array.at[there + spot],
                    got[m].at[spot],
                    x_send.at[j],
                    x_recv.at[j],
                    at.device(ox=at.dx),
                )
            self.keep.append(
                pltpu.make_async_copy(mine[m].at[at.z], outs[m].at[at.z], load_sem.at[m * 5 + 4])
            )

    def start(self):
        for k in (3, 2, 1, 0):
            for m in range(self.count):
                self.loads[m, k].start()
                self.crossing[m, k].start()

    def line(self, k):
        spot = self.at.zs[k]
        for m in range(self.count):
            mine, got = self.mine[m], self.got[m]
            self.loads[m, k].wait()
            self.crossing[m, k].wait_recv()

            @pl.loop(0, mine.shape[1] // 16)
            def _(i):
                span = pl.ds(pl.multiple_of(i * 16, 16), 16)
                both = mine[spot, span, :].astype(F32) + got[spot, span, :].astype(F32)
                mine[spot, span, :] = both.astype(BF)

            (self.copy(m, k) if k else self.keep[m]).start()

    def copy(self, m, k):
        at = self.at
        return remote(
            self.mine[m].at[at.zs[k]],
            self.outs[m].at[at.z],
            self.z_send.at[m * 3 + k - 1],
            self.z_recv.at[m * 4 + at.z],
            at.device(zi=k),
        )

    def finish(self):
        at = self.at
        for m in range(self.count):
            for k in (1, 2, 3):
                remote(
                    self.mine[m].at[at.z],
                    self.outs[m].at[at.zs[k]],
                    self.z_send.at[m * 3 + k - 1],
                    self.z_recv.at[m * 4 + at.zs[k]],
                    at.device(zi=k),
                ).wait_recv()
                self.copy(m, k).wait_send()
            self.keep[m].wait()
        for copy in self.crossing.values():
            copy.wait_send()


class Share:
    def __init__(self, at, ref, out, own_sem, send_sem, recv_sem):
        self.at, rows = at, ref.shape[0]
        spot = lambda oe: out.at[pl.ds(pl.multiple_of((at.e + oe) * rows, rows), rows)]
        f_dev, s_dev = at.device(oe=at.dy), at.device(oe=at.dc)
        self.local = pltpu.make_async_copy(ref, spot(0), own_sem)
        self.far = remote(ref, spot(0), send_sem.at[0], recv_sem.at[0], f_dev)
        self.near = remote(ref, spot(0), send_sem.at[1], recv_sem.at[1], s_dev)
        self.over = remote(spot(at.dy), spot(at.dy), send_sem.at[2], recv_sem.at[2], s_dev)

    def start(self):
        for copy in (self.far, self.near, self.local):
            copy.start()

    def forward(self):
        self.far.wait_recv()
        self.over.start()

    def finish(self):
        self.far.wait_send()
        self.near.wait()
        self.over.wait()
        self.local.wait()


def last_scatter_kernel(*refs):
    refs = list(refs)

    def take(count):
        taken = refs[:count]
        del refs[:count]
        return taken

    in_ref, g_ref, u_ref, scaled_ref, picked_ref, dy_ref, mixed_ref, given = take(8)
    halves, home_refs = take(5), take(3)
    out_ref, taken, grad_gate, grad_up, grad_down, mixed_out = take(6)
    home_outs = take(3)
    right, left, other, grad, turned = take(5)
    mine, got = take(3), take(3)
    buffers = take(6)
    first_sem, cross_send, cross_recv, load_sem, store_sem = take(5)
    home_sems, share_sems = take(5), take(3)
    at = Place()
    greet(at, True)
    total = Scatter(at, *buffers, out_ref)
    acc = buffers[0]
    rows, width = acc.shape[1:]
    part = given.shape[0]
    crossing = cross(at, [given], [taken], cross_send, cross_recv)[0]
    home = Home(at, home_refs, home_outs, mine, got, *home_sems)
    sharing = Share(at, mixed_ref, mixed_out, *share_sems)

    def rows_of(rank):
        return in_ref.at[pl.ds(pl.multiple_of(rank * rows, rows), rows)]

    order = [(f, zi) for f in (1, 0) for zi in (3, 2, 1, 0)]
    firsts = {}
    for f, zi in order:
        k = f * 4 + zi
        total.to_twin(rows_of(at.shard(f * at.dy + at.dc, zi)), f, zi)
        firsts[k] = pltpu.make_async_copy(
            rows_of(at.shard(f * at.dy, zi)), acc.at[k], first_sem.at[k]
        )
        firsts[k].start()
    home.start()
    crossing.start()
    pairs = [
        (picked_ref, right.at[0]),
        (dy_ref, right.at[1]),
        (g_ref.at[0], left.at[0]),
        (u_ref.at[0], left.at[1]),
        (scaled_ref.at[0], left.at[2]),
    ]
    pairs += [
        (ref, other.at[j // 2 % 2, pl.ds(j % 2 * part, part)])
        for j, ref in enumerate(halves + [taken])
    ]
    loads = [pltpu.make_async_copy(a, b, load_sem.at[j]) for j, (a, b) in enumerate(pairs)]
    for copy in loads[:9]:
        copy.start()

    def store(m):
        ref = (grad_gate, grad_up, grad_down)[m]
        return pltpu.make_async_copy(grad.at[m % 2], ref, store_sem.at[m])

    def gradient(m):
        turned[...] = left[m].T

        @columns_loop(width, 8)
        def _(columns):
            terms = product(turned[...], right[m // 2, :, columns])
            grad[m % 2, :, columns] = terms + other[m % 2, :, columns].astype(F32)

        store(m).start()

    for zi in (3, 2, 1, 0):
        firsts[4 + zi].wait()
        total.first(zi)
    sharing.start()
    for copy in loads[:9]:
        copy.wait()
    gradient(0)
    loads[9].start()
    home.line(3)
    firsts[3].wait()
    total.second(3)
    gradient(1)
    home.line(2)
    firsts[2].wait()
    total.second(2)
    home.line(1)
    firsts[1].wait()
    total.second(1)
    home.line(0)
    sharing.forward()
    crossing.wait_recv()
    loads[10].start()
    loads[9].wait()
    loads[10].wait()
    store(0).wait()
    gradient(2)
    firsts[0].wait()
    total.second(0)
    home.finish()
    sharing.finish()
    store(1).wait()
    store(2).wait()
    crossing.wait_send()
    total.finish()


def last_rows(x, g, u, scaled, picked, picked_dy, home, mixed_own, given, halves, cid):
    rows, width = x.shape[0] // 16, x.shape[1]
    slots, hidden = g.shape[1:]
    hbm, vmem = pl.BlockSpec(memory_space=pl.ANY), pl.BlockSpec(memory_space=pltpu.VMEM)
    shape, sems = jax.ShapeDtypeStruct, lambda n: pltpu.SemaphoreType.DMA((n,))
    return pl.pallas_call(
        last_scatter_kernel,
        out_shape=[
            shape((rows, width), F32),
            shape(given.shape, BF),
            *[shape((hidden, width), F32)] * 3,
            shape((4 * rows, width), BF),
            *[shape((4,) + a.shape[1:], BF) for a in home],
        ],
        in_specs=[hbm] * 16,
        out_specs=[vmem] + [hbm] * 8,
        scratch_shapes=[
            pltpu.VMEM((2, slots, width), BF),
            pltpu.VMEM((3, slots, hidden), BF),
            pltpu.VMEM((2, hidden, width), BF),
            pltpu.VMEM((2, hidden, width), F32),
            pltpu.VMEM((hidden, slots), BF),
            *[pltpu.VMEM((4,) + a.shape[1:], BF) for a in home] * 2,
            *scatter_buffers(rows, width),
            sems(8),
            sems(1),
            sems(1),
            sems(11),
            sems(3),
            sems(15),
            sems(12),
            sems(12),
            sems(9),
            sems(12),
            pltpu.SemaphoreType.DMA,
            sems(3),
            sems(3),
        ],
        compiler_params=pltpu.CompilerParams(
            collective_id=cid, has_side_effects=True, vmem_limit_bytes=62 * 1024 * 1024
        ),
    )(x, g, u, scaled, picked, picked_dy, mixed_own, given, *halves, *home)


def end_kernel(tokens_ref, gain_ref, small_ref, out_ref, gain_out, small_out, *scratch):
    gain_got, gain_sum, gain_all, small_all = scratch[:4]
    share_sems = scratch[4:7]
    gain_send, gain_recv, sum_send, sum_recv, small_send, small_recv = scratch[7:]
    at = Place()
    barrier = pltpu.get_barrier_semaphore()
    blocks = [(at.device(ox=ox, zi=k), m * 4 + k) for m, ox in enumerate((0, at.dx)) for k in range(4)]
    group = [at.device(oe=oe) for oe in (at.dy, at.dc, at.dy + at.dc)]
    for peer in [device for device, j in blocks[1:]] + group:
        pl.semaphore_signal(barrier, inc=1, device_id=peer, device_id_type=MESH)
    pl.semaphore_wait(barrier, 10)
    sharing = Share(at, tokens_ref, out_ref, *share_sems)
    own = at.x * 4 + at.z
    copies = []
    for device, j in blocks[1:]:
        copy = remote(
            gain_ref.at[device[0] * 4 + device[1]],
            gain_got.at[own],
            gain_send.at[j],
            gain_recv.at[own],
            device,
        )
        copy.start()
        copies.append(copy)
    for j, device in enumerate(group):
        copy = remote(small_ref, small_all.at[j], small_send.at[j], small_recv.at[j], device)
        copy.start()
        copies.append(copy)
    sharing.start()
    gain = gain_ref[own]
    for device, j in blocks[1:]:
        there = device[0] * 4 + device[1]
        remote(
            gain_ref.at[0], gain_got.at[there], gain_send.at[j], gain_recv.at[there], device
        ).wait_recv()
        gain = gain + gain_got[there]
    gain_sum[...] = gain
    for j, device in enumerate(group):
        copy = remote(gain_sum, gain_all.at[j], sum_send.at[j], sum_recv.at[j], device)
        copy.start()
        copies.append(copy)
    small = small_ref[...]
    for j in range(3):
        copies[7 + j].wait_recv()
        copies[10 + j].wait_recv()
        small = small + small_all[j]
        gain = gain + gain_all[j]
    gain_out[...] = gain
    small_out[...] = small
    sharing.forward()
    sharing.finish()
    for copy in copies:
        copy.wait_send()


def end(tokens_own, gain_part, small, cid):
    rows, width = tokens_own.shape
    vmem, hbm = pl.BlockSpec(memory_space=pltpu.VMEM), pl.BlockSpec(memory_space=pl.ANY)
    shape, sems = jax.ShapeDtypeStruct, lambda n: pltpu.SemaphoreType.DMA((n,))
    return pl.pallas_call(
        end_kernel,
        out_shape=[
            shape((4 * rows, width), tokens_own.dtype),
            shape(gain_part.shape[1:], F32),
            shape(small.shape, F32),
        ],
        in_specs=[hbm, vmem, vmem],
        out_specs=[hbm, vmem, vmem],
        scratch_shapes=[
            pltpu.VMEM(gain_part.shape, F32),
            pltpu.VMEM(gain_part.shape[1:], F32),
            pltpu.VMEM((3,) + gain_part.shape[1:], F32),
            pltpu.VMEM((3,) + small.shape, F32),
            pltpu.SemaphoreType.DMA,
            sems(3),
            sems(3),
            sems(8),
            sems(8),
            sems(3),
            sems(3),
            sems(3),
            sems(3),
        ],
        compiler_params=pltpu.CompilerParams(collective_id=cid, has_side_effects=True),
    )(tokens_own, gain_part, small)


def front_kernel(scale, *refs):
    refs = list(refs)

    def take(count):
        taken = refs[:count]
        del refs[:count]
        return taken

    dy_ref, tokens_ref, units, given, gain, w_qkv, w_out, tables = take(8)
    dy_out, units_out, taken, normed_out, part_out, q_out, k_out, v_out, heads_out, lse_out = take(10)
    rows_in, normed, staged = take(3)
    own_sem, send_sem, recv_sem, local_sem, swap_send, swap_recv = take(6)
    cross_send, cross_recv, in_sem, normed_sem, part_sem = take(5)
    at = Place()
    greet(at, True)
    gather = Gather(at, dy_ref, dy_out, own_sem, send_sem, recv_sem, True)
    swap_in = Exchange(at, [units], [units_out], local_sem, swap_send, swap_recv)
    crossing = cross(at, [given], [taken], cross_send, cross_recv, (taken.shape[0],))[0]
    length, width = tokens_ref.shape
    block = length // 4
    step = 256
    over = columns_loop(width, 4)

    def rows_load(j):
        return pltpu.make_async_copy(
            tokens_ref.at[pl.ds(j * block, block)], rows_in.at[j % 2], in_sem.at[j % 2]
        )

    def normed_store(j):
        return pltpu.make_async_copy(
            normed.at[j % 2], normed_out.at[pl.ds(j * block, block)], normed_sem.at[j % 2]
        )

    def part_store(i):
        return pltpu.make_async_copy(
            staged.at[i % 2], part_out.at[pl.ds(i * step, step)], part_sem.at[i % 2]
        )

    def turn_rows(values, here):
        other = pltpu.roll(values, HDIM // 2, 1)
        return (values * tables[0, here, :] - other * tables[1, here, :]).astype(BF)

    def project(j):
        rows_load(j).wait()
        if j >= 2:
            normed_store(j - 2).wait()

        @pl.loop(0, block // 64)
        def _(n):
            span = pl.ds(pl.multiple_of(n * 64, 64), 64)
            values = rows_in[j % 2, span, :].astype(F32)
            size = jnp.mean(values * values, axis=-1, keepdims=True)
            normed[j % 2, span, :] = (values * lax.rsqrt(size + EPSILON) * gain[0:1, :]).astype(BF)

        normed_store(j).start()
        if j < 2:
            rows_load(j + 2).start()
        here = pl.ds(j * block, block)
        qkv = product(normed[j % 2], w_qkv[...])
        q_out[here, :] = turn_rows(qkv[:, :HDIM], here)
        k_out[here, :] = turn_rows(qkv[:, HDIM : 2 * HDIM], here)
        v_out[here, :] = qkv[:, 2 * HDIM :].astype(BF)

    def attend_rows(i):
        seen = (i + 1) * step
        here = pl.ds(i * step, step)
        scores = transposed_right(q_out[here, :], k_out[0:seen, :]) * scale
        row_at = lax.broadcasted_iota(jnp.int32, scores.shape, 0) + i * step
        col_at = lax.broadcasted_iota(jnp.int32, scores.shape, 1)
        scores = jnp.where(row_at >= col_at, scores, MASKED)
        top = jnp.max(scores, axis=-1, keepdims=True)
        powers = jnp.exp(scores - top)
        lse = top + jnp.log(jnp.sum(powers, axis=-1, keepdims=True))
        probs = jnp.exp(scores - lse).astype(BF)
        heads_out[here, :] = product(probs, v_out[0:seen, :]).astype(BF)
        lse_out[here, :] = jnp.broadcast_to(lse, (step, HDIM))
        if i >= 2:
            part_store(i - 2).wait()

        @over
        def _(columns):
            staged[i % 2, :, columns] = product(heads_out[here, :], w_out[:, columns]).astype(BF)

        part_store(i).start()

    gather.begin()
    swap_in.start()
    crossing.start()
    rows_load(0).start()
    rows_load(1).start()
    project(0)
    project(1)
    attend_rows(0)
    gather.line(1)
    swap_in.forward(1)
    project(2)
    attend_rows(1)
    attend_rows(2)
    gather.other(1)
    gather.line(2)
    swap_in.forward(2)
    project(3)
    attend_rows(3)
    attend_rows(4)
    gather.other(2)
    gather.line(3)
    swap_in.forward(3)
    attend_rows(5)
    attend_rows(6)
    attend_rows(7)
    gather.other(3)
    for j in (2, 3):
        normed_store(j).wait()
    for i in (6, 7):
        part_store(i).wait()
    swap_in.finish()
    crossing.wait()
    gather.finish()


def front(dy, tokens_all, units, given, gain, w_qkv, w_out, tables, cid):
    length, width = tokens_all.shape
    hbm, vmem = pl.BlockSpec(memory_space=pl.ANY), pl.BlockSpec(memory_space=pltpu.VMEM)
    shape, sems = jax.ShapeDtypeStruct, lambda n: pltpu.SemaphoreType.DMA((n,))
    return pl.pallas_call(
        functools.partial(front_kernel, HDIM ** (-0.5)),
        out_shape=[
            shape((length, width), BF),
            shape((8,) + units.shape[1:], BF),
            half_of(given),
            shape((length, width), BF),
            shape((length, width), BF),
            *[shape((length, HDIM), BF)] * 4,
            shape((length, HDIM), F32),
        ],
        in_specs=[hbm] * 4 + [vmem] * 4,
        out_specs=[hbm] * 5 + [vmem] * 5,
        scratch_shapes=[
            pltpu.VMEM((2, length // 4, width), BF),
            pltpu.VMEM((2, length // 4, width), BF),
            pltpu.VMEM((2, 256, width), BF),
            pltpu.SemaphoreType.DMA,
            sems(19),
            sems(15),
            sems(1),
            sems(7),
            sems(8),
            sems(1),
            sems(1),
            sems(2),
            sems(2),
            sems(2),
        ],
        compiler_params=pltpu.CompilerParams(
            collective_id=cid, has_side_effects=True, vmem_limit_bytes=60 * 1024 * 1024
        ),
    )(dy, tokens_all, units, given, gain, w_qkv, w_out, tables)


def by_four(matrix):
    rows, columns = matrix.shape
    return matrix.reshape(rows, 4, columns // 4).transpose(1, 0, 2)


def turn_tables(length):
    inverse = 10000.0 ** (-np.arange(HDIM // 2).astype(np.float64) * 2.0 / HDIM)
    angles = np.arange(length).astype(np.float64)[:, None] * inverse[None, :]
    return np.cos(angles).astype(np.float32), np.sin(angles).astype(np.float32)


def fast_body(
    tokens,
    routes,
    norm_attn,
    w_query,
    w_key,
    w_value,
    w_out,
    norm_mix,
    w_router,
    shared_gate,
    shared_up,
    shared_down,
    expert_gate,
    expert_up,
    expert_down,
    out_grad,
):
    dp, ctx, exp = lax.axis_index("dp"), lax.axis_index("ctx"), lax.axis_index("exp")
    rows_here, width = tokens.shape[1], tokens.shape[2]
    quarter = rows_here // 4
    length = rows_here * 4
    experts = w_router.shape[1]
    capacity = quarter * TOPK * 4 // (3 * experts)
    groups = length // quarter
    dense = w_query.shape[0]
    cut = shared_gate.shape[1] // 4
    wide = 256
    start = exp * quarter
    tokens_own = lax.dynamic_slice_in_dim(tokens[0], start, quarter, 0)
    dy_own = lax.dynamic_slice_in_dim(out_grad[0], start, quarter, 0)

    route_rows = routes[0].T
    theirs = jnp.arange(4, dtype=jnp.int32)[:, None, None] * 4 + exp
    named = jnp.any(route_rows[None] == theirs, axis=1).astype(BF).reshape(4, 2, dense)
    little = jnp.concatenate([w_router.T, norm_attn[None], norm_mix[None]], axis=0)
    little = jnp.concatenate([jnp.broadcast_to(little[None], (4,) + little.shape), named], axis=1)
    few = -(-little.shape[1] // 16) * 16
    little = jnp.pad(little, ((0, 0), (0, few - little.shape[1]), (0, 0)))
    sent_head = jnp.concatenate([by_four(w_query), by_four(w_key), by_four(w_value)], axis=2)
    sent_out = w_out.reshape(4, HDIM, dense)
    sent_units = jnp.stack([shared_gate.T, shared_up.T, shared_down], axis=0)
    sent_units = sent_units.reshape(3, 4, cut, dense).transpose(1, 0, 2, 3).reshape(4, 3 * cut, dense)
    own_gate, own_up, own_down = expert_gate[0].T, expert_up[0].T, expert_down[0]
    part = own_gate.shape[0] // 2
    tokens_all, early, early_out, early_little, gate_0 = all_rows(
        tokens[0], True, 1, (sent_head, sent_out, little), (own_gate,), (0,)
    )
    w_qkv = early.reshape(width, 3 * HDIM)
    early_little = early_little.transpose(1, 0, 2)
    router_rows = early_little[:experts].reshape(experts, width)
    attention_gain = early_little[experts].reshape(width).astype(F32)
    mixer_gain = early_little[experts + 1].reshape(width).astype(F32)
    hits = early_little[experts + 2 : experts + 4].transpose(1, 0, 2).reshape(2, length)
    hits = lax.dynamic_index_in_dim(hits, dp, 0, False).astype(F32).reshape(groups, quarter)
    w_out_head = early_out.transpose(1, 0, 2).reshape(HDIM, width)

    cosine, sine = turn_tables(length)
    tables = np.stack(
        [np.concatenate([cosine, cosine], axis=1), np.concatenate([sine, -sine], axis=1)]
    )
    dy_all, late, gate_1, normed, attn_part, query, key, value, heads_out, lse = front(
        out_grad[0],
        tokens_all,
        sent_units,
        own_gate,
        jnp.broadcast_to(attention_gain[None], (8, width)),
        w_qkv,
        w_out_head,
        tables,
        2,
    )
    late = late.transpose(1, 0, 2).reshape(3, cut, width)
    late = jnp.pad(late, ((0, 0), (0, wide - cut), (0, 0)))
    shared_in = late[:2].reshape(2 * wide, width)
    shared_out = late[2]
    attn, up_0, up_1 = own_rows(attn_part, 3, (own_up, own_up), (0, part))
    middle = tokens_own.astype(F32) + attn
    normed_own = rms_scale(middle, mixer_gain).astype(BF)

    mine = ctx * 4 + exp
    place = jnp.cumsum(hits, axis=1) - 1.0
    first = (jnp.arange(groups) % 4 * capacity).astype(F32)[:, None]
    place = jnp.where(hits > 0.5, place + first, -1.0).reshape(4, 1, 4 * quarter)
    blocks = place == jnp.arange(4 * capacity).astype(F32)[None, :, None]
    blocks = blocks.astype(BF)
    router_wide = jnp.pad(router_rows, ((0, HDIM - experts), (0, 0)))
    (
        mix_all,
        picked,
        picked_dy,
        scaled,
        g_back,
        u_back,
        gate_back,
        shared_act,
        shared_gu_back,
        down_0,
        down_1,
    ) = expert_rows(
        normed_own,
        dy_all,
        blocks,
        router_wide,
        experts,
        shared_in,
        shared_out,
        (own_gate, own_up, own_down, gate_0, gate_1, up_0, up_1),
        (own_down, own_down),
        4,
    )
    other_down = (down_0, down_1)

    mix_back, gate_0, gate_1, up_0, up_1, down_0, down_1 = expert_back(
        blocks,
        gate_back,
        shared_in,
        g_back,
        u_back,
        shared_gu_back,
        picked,
        picked_dy,
        scaled,
        (own_gate, own_up, gate_0, gate_1, up_0, up_1),
        5,
    )
    gate_back_own = mix_back[:, width : width + experts]
    mix_back = mix_back[:, :width]

    router_own = jax.nn.softmax(transposed_right(normed_own, router_rows), axis=-1)
    logit_back = (
        router_own * (gate_back_own - jnp.sum(router_own * gate_back_own, axis=-1, keepdims=True))
    ).astype(BF)
    router_part = transposed_left(logit_back, normed_own)

    mix_back = mix_back + product(logit_back, router_rows)
    _, norm_mix_back = jax.vjp(rms_scale, middle, mixer_gain)
    middle_norm_back, gain_mix_part = norm_mix_back(mix_back)
    middle_back = dy_own.astype(F32) + middle_norm_back
    attn_back = middle_back.astype(BF)
    attn_back_all, mixed_part, units_part, gate_1, up_0 = gather_back(
        attn_back,
        (gate_1, up_0),
        blocks,
        shared_out,
        scaled,
        shared_act,
        shared_gu_back,
        (own_down, *other_down),
        mix_all,
        dy_all,
        cut,
        7,
    )
    mixed_sum, normed_part, head_part, up_1, down_0 = mixed_rows(
        w_out_head,
        w_qkv.T,
        tables,
        query,
        key,
        value,
        lse,
        heads_out,
        mixed_part,
        attn_back_all,
        normed,
        (up_1, down_0),
        9,
    )
    mixed_own = (middle + mixed_sum).astype(BF)
    small_part = jnp.concatenate([gain_mix_part[None], router_part], axis=0).astype(BF)
    small_rows = -(-(experts + 1) // 16) * 16
    small_part = jnp.pad(small_part, ((0, small_rows - experts - 1), (0, 0)))
    small_part = small_part.reshape(small_rows, 8, dense).transpose(1, 0, 2)
    normed_back, _, gate_grad, up_grad, down_grad, mixed, head_grad, units_grad, small = last_rows(
        normed_part,
        g_back,
        u_back,
        scaled,
        picked,
        picked_dy,
        (head_part, units_part, small_part),
        mixed_own,
        down_1,
        (gate_0, gate_1, up_0, up_1, down_0),
        8,
    )
    head_grad, units_grad = head_grad.astype(F32), units_grad.astype(F32)
    small_part = jnp.sum(small.astype(F32), axis=0)
    _, norm_attn_back = jax.vjp(rms_scale, tokens_own.astype(F32), attention_gain)
    input_norm_back, gain_attn_part = norm_attn_back(normed_back)
    tokens_back_own = (middle_back + input_norm_back).astype(BF)

    gain_part = jnp.pad(gain_attn_part.reshape(8, 1, dense), ((0, 0), (0, 7), (0, 0)))
    tokens_back, gain_attn, small = end(tokens_back_own, gain_part, small_part, 6)

    def columns_of(parts):
        return parts.transpose(2, 0, 1).reshape(dense, -1)

    def rows_of(parts):
        return parts.reshape(-1, dense)

    return (
        mixed[None],
        tokens_back[None],
        gain_attn[0],
        columns_of(head_grad[:, :HDIM]),
        columns_of(head_grad[:, HDIM : 2 * HDIM]),
        columns_of(head_grad[:, 2 * HDIM : 3 * HDIM]),
        rows_of(head_grad[:, 3 * HDIM :]),
        small[0],
        small[1 : experts + 1].T,
        rows_of(units_grad[:, :cut]).T,
        rows_of(units_grad[:, cut : 2 * cut]).T,
        rows_of(units_grad[:, 2 * cut :]),
        gate_grad.T[None],
        up_grad.T[None],
        down_grad[None],
    )


def solution(mesh):
    sizes = dict(mesh.shape)

    def chosen(*args):
        heads = args[3].shape[1] * sizes["exp"] // HDIM
        one_head_each = heads == sizes["ctx"] * sizes["exp"]
        built_for = (sizes["dp"], sizes["ctx"], sizes["exp"]) == (2, 4, 4)
        return fast_body(*args) if one_head_each and built_for else body(*args)

    in_specs = (
        P("dp", "ctx", None),
        P("dp", "ctx", None),
        P(("dp", "ctx")),
        P(("dp", "ctx"), "exp"),
        P(("dp", "ctx"), "exp"),
        P(("dp", "ctx"), "exp"),
        P("exp", ("dp", "ctx")),
        P(("dp", "ctx")),
        P(("dp", "ctx"), None),
        P(("dp", "ctx"), "exp"),
        P(("dp", "ctx"), "exp"),
        P("exp", ("dp", "ctx")),
        P(("ctx", "exp"), None, "dp"),
        P(("ctx", "exp"), None, "dp"),
        P(("ctx", "exp"), "dp", None),
        P("dp", "ctx", None),
    )
    out_specs = (
        P("dp", "ctx", None),
        P("dp", "ctx", None),
        P(("dp", "ctx")),
        P(("dp", "ctx"), "exp"),
        P(("dp", "ctx"), "exp"),
        P(("dp", "ctx"), "exp"),
        P("exp", ("dp", "ctx")),
        P(("dp", "ctx")),
        P(("dp", "ctx"), None),
        P(("dp", "ctx"), "exp"),
        P(("dp", "ctx"), "exp"),
        P("exp", ("dp", "ctx")),
        P(("ctx", "exp"), None, "dp"),
        P(("ctx", "exp"), None, "dp"),
        P(("ctx", "exp"), "dp", None),
    )
    return jax.shard_map(chosen, mesh=mesh, in_specs=in_specs, out_specs=out_specs, check_vma=False)
```

```python
import functools

import jax
import jax.numpy as jnp
import numpy as np
from jax import lax
from jax.experimental import pallas as pl
from jax.experimental.pallas import tpu as pltpu
from jax.sharding import PartitionSpec as P

HDIM = 128
TOPK = 6


EPSILON = 1e-06
MASKED = -1e30
HIGHEST = lax.Precision.HIGHEST


def rms_scale(values, gain_row):
    return (
        values * lax.rsqrt(jnp.mean(values * values, axis=-1, keepdims=True) + EPSILON) * gain_row
    )


def rope_tables(positions, rope_width):
    inverse = 10000.0 ** (-jnp.arange(rope_width // 2).astype(jnp.float32) * 2.0 / rope_width)
    angles = positions.astype(jnp.float32)[:, None] * inverse[None, :]
    return (jnp.cos(angles), jnp.sin(angles))


def rotate(values, cosine, sine_table):
    half_size = values.shape[-1] // 2
    first_half = values[..., :half_size]
    second = values[..., half_size:]
    cosine = cosine[:, None, :]
    sine_table = sine_table[:, None, :]
    return jnp.concatenate(
        [first_half * cosine - second * sine_table, second * cosine + first_half * sine_table],
        axis=-1,
    )


def silu_mix(gate_rows, up_rows):
    return jax.nn.silu(gate_rows) * up_rows


def product(left_side, right_side):
    return jnp.dot(left_side, right_side, preferred_element_type=jnp.float32)


def transposed_left(left_side, right_side):
    return lax.dot_general(
        left_side, right_side, (((0,), (0,)), ((), ())), preferred_element_type=jnp.float32
    )


def transposed_right(left_side, right_side):
    return lax.dot_general(
        left_side, right_side, (((1,), (1,)), ((), ())), preferred_element_type=jnp.float32
    )


def place_rows(part, start_row, total_rows):
    blank = jnp.zeros((total_rows, part.shape[1]), jnp.float32)
    return lax.dynamic_update_slice_in_dim(blank, part, start_row, 0)


def to_owners(buffer):
    copies = lax.axis_size("dp")
    widened = jnp.broadcast_to(buffer[None], (copies,) + buffer.shape)
    widened = widened.reshape((copies * buffer.shape[0],) + buffer.shape[1:])
    return lax.all_to_all(widened, ("dp", "ctx", "exp"), split_axis=0, concat_axis=0, tiled=True)


def values_home(partial_value):
    returned = lax.all_to_all(
        partial_value, ("dp", "ctx", "exp"), split_axis=0, concat_axis=0, tiled=True
    )
    grouped = returned.reshape((lax.axis_size("dp"), -1) + returned.shape[1:])
    return jnp.sum(grouped.astype(jnp.float32), axis=0).astype(jnp.bfloat16)


def grads_home(partial_value):
    returned = lax.all_to_all(
        partial_value.astype(jnp.bfloat16),
        ("dp", "ctx", "exp"),
        split_axis=0,
        concat_axis=0,
        tiled=True,
    ).astype(partial_value.dtype)
    grouped = returned.reshape((lax.axis_size("dp"), -1) + returned.shape[1:])
    return jnp.sum(grouped, axis=0)


def body(
    tokens,
    routes,
    norm_attn,
    w_query,
    w_key,
    w_value,
    w_out,
    norm_mix,
    w_router,
    shared_gate,
    shared_up,
    shared_down,
    expert_gate,
    expert_up,
    expert_down,
    out_grad,
):
    gathered = (
        lax.all_gather(norm_attn, ("dp", "ctx"), axis=0, tiled=True),
        lax.all_gather(w_query, ("dp", "ctx"), axis=0, tiled=True),
        lax.all_gather(w_key, ("dp", "ctx"), axis=0, tiled=True),
        lax.all_gather(w_value, ("dp", "ctx"), axis=0, tiled=True),
        lax.all_gather(w_out, ("dp", "ctx"), axis=1, tiled=True),
        lax.all_gather(norm_mix, ("dp", "ctx"), axis=0, tiled=True),
        lax.all_gather(w_router, ("dp", "ctx"), axis=0, tiled=True),
        lax.all_gather(shared_gate, ("dp", "ctx"), axis=0, tiled=True),
        lax.all_gather(shared_up, ("dp", "ctx"), axis=0, tiled=True),
        lax.all_gather(shared_down, ("dp", "ctx"), axis=1, tiled=True),
    )
    (
        attention_gain,
        query_matrix,
        key_matrix,
        value_matrix,
        output_matrix,
        mixer_gain,
        router_matrix,
        shared_gate_matrix,
        shared_up_matrix,
        shared_down_matrix,
    ) = gathered
    rows_here = tokens.shape[1]
    model_width = tokens.shape[2]
    heads_here = query_matrix.shape[1] // HDIM
    quarter = rows_here // lax.axis_size("exp")
    start_row = lax.axis_index("exp") * quarter
    layer_input = tokens[0].astype(jnp.float32)
    grad_rows = out_grad[0]
    grad_float = grad_rows.astype(jnp.float32)
    seq_length = rows_here * lax.axis_size("ctx")
    positions = lax.axis_index("ctx") * rows_here + jnp.arange(rows_here, dtype=jnp.int32)
    cosine, sine_table = rope_tables(positions, HDIM)
    visible = positions[:, None] >= jnp.arange(seq_length, dtype=jnp.int32)[None, :]
    scale = HDIM ** (-0.5)
    head_shape = (rows_here, heads_here, HDIM)
    normed = rms_scale(layer_input, attention_gain).astype(jnp.bfloat16)
    query_rot = rotate(
        product(normed, query_matrix).reshape(head_shape), cosine, sine_table
    ).astype(jnp.bfloat16)
    key_rot = (
        rotate(product(normed, key_matrix).reshape(head_shape), cosine, sine_table)
        .astype(jnp.bfloat16)
        .reshape(rows_here, -1)
    )
    value_low = product(normed, value_matrix).astype(jnp.bfloat16)
    key_all, value_all = (
        lax.all_gather(key_rot, "ctx", axis=0, tiled=True),
        lax.all_gather(value_low, "ctx", axis=0, tiled=True),
    )
    key_heads = key_all.reshape(seq_length, heads_here, HDIM)
    value_heads = value_all.reshape(seq_length, heads_here, HDIM)

    def attention_scores():
        scores = (
            jnp.einsum("qhd,khd->hqk", query_rot, key_heads, preferred_element_type=jnp.float32)
            * scale
        )
        return jnp.where(visible[None], scores, MASKED)

    scores = attention_scores()
    largest = jnp.max(scores, axis=-1, keepdims=True)
    log_total = largest + jnp.log(jnp.sum(jnp.exp(scores - largest), axis=-1, keepdims=True))
    weights_low = jnp.exp(scores - log_total).astype(jnp.bfloat16)
    heads_out = (
        jnp.einsum("hqk,khd->qhd", weights_low, value_heads, preferred_element_type=jnp.float32)
        .reshape(rows_here, -1)
        .astype(jnp.bfloat16)
    )
    attn_total = lax.psum(product(heads_out, output_matrix), "exp")
    middle = layer_input + attn_total
    normed_mix = rms_scale(middle, mixer_gain).astype(jnp.bfloat16)
    normed_quarter = lax.dynamic_slice_in_dim(normed_mix, start_row, quarter, 0)
    route_quarter = lax.dynamic_slice_in_dim(routes[0], start_row, quarter, 0)
    grad_quarter = lax.dynamic_slice_in_dim(grad_rows, start_row, quarter, 0)
    logits = product(normed_quarter, router_matrix)
    probabilities = jax.nn.softmax(logits, axis=-1)
    owners = lax.axis_size(("ctx", "exp"))
    local_experts = expert_gate.shape[0]
    experts = local_experts * owners
    capacity = max(quarter * TOPK * 4 // (3 * experts), 2)
    expert_choice_index = jnp.arange(experts, dtype=jnp.int32)
    chosen = (route_quarter[:, :, None] == expert_choice_index[None, None, :]).astype(jnp.float32)
    gates = jnp.sum(chosen * probabilities[:, None, :], axis=-1)
    route_flat = route_quarter.reshape(-1)
    expert_hits = (route_flat[:, None] == expert_choice_index[None, :]).astype(jnp.int32)
    slot_index = jnp.sum(jnp.cumsum(expert_hits, axis=0) * expert_hits, axis=1) - 1
    slot_place = route_flat * capacity + slot_index
    matches = (
        jnp.arange(experts * capacity, dtype=jnp.int32)[:, None] == slot_place[None, :]
    ).astype(jnp.float32)
    dispatch = jnp.sum(matches.reshape(experts * capacity, quarter, TOPK), axis=2).astype(
        jnp.bfloat16
    )
    slot_gates = jnp.dot(matches, gates.reshape(-1), precision=HIGHEST)
    buffer_shape = (owners, local_experts, capacity, model_width)
    outgoing = product(dispatch, normed_quarter).astype(jnp.bfloat16).reshape(buffer_shape)
    arrived = to_owners(outgoing)
    gate_hidden = jnp.einsum(
        "sicd,idf->sicf", arrived, expert_gate, preferred_element_type=jnp.float32
    )
    up_hidden = jnp.einsum("sicd,idf->sicf", arrived, expert_up, preferred_element_type=jnp.float32)
    expert_act = silu_mix(gate_hidden, up_hidden).astype(jnp.bfloat16)
    partial_value = jnp.einsum(
        "sicf,ifd->sicd", expert_act, expert_down, preferred_element_type=jnp.float32
    ).astype(jnp.bfloat16)
    expert_values = values_home(partial_value).reshape(experts * capacity, model_width)
    route_values = expert_values[slot_place].astype(jnp.float32).reshape(quarter, TOPK, model_width)
    combined = jnp.sum(route_values * gates[:, :, None], axis=1)
    shared_gate_rows = product(normed_mix, shared_gate_matrix)
    shared_up_rows = product(normed_mix, shared_up_matrix)
    shared_act = silu_mix(shared_gate_rows, shared_up_rows).astype(jnp.bfloat16)
    branch_part = product(shared_act, shared_down_matrix) + place_rows(
        combined, start_row, rows_here
    )
    result = middle + lax.psum(branch_part.astype(jnp.bfloat16), "exp").astype(jnp.float32)
    grad_slots = (
        (product(dispatch, grad_quarter) * slot_gates[:, None])
        .astype(jnp.bfloat16)
        .reshape(buffer_shape)
    )
    grad_arrived = to_owners(grad_slots)
    act_grad = jnp.einsum(
        "sicd,ifd->sicf", grad_arrived, expert_down, preferred_element_type=jnp.float32
    )
    down_grad = jnp.einsum(
        "sicf,sicd->ifd", expert_act, grad_arrived, preferred_element_type=jnp.float32
    )
    _, mix_back = jax.vjp(silu_mix, gate_hidden, up_hidden)
    gate_back, up_back = mix_back(act_grad)
    gate_back = gate_back.astype(jnp.bfloat16)
    up_back = up_back.astype(jnp.bfloat16)
    gate_grad = jnp.einsum("sicd,sicf->idf", arrived, gate_back, preferred_element_type=jnp.float32)
    up_grad = jnp.einsum("sicd,sicf->idf", arrived, up_back, preferred_element_type=jnp.float32)
    input_back = jnp.einsum(
        "sicf,idf->sicd", gate_back, expert_gate, preferred_element_type=jnp.float32
    ) + jnp.einsum("sicf,idf->sicd", up_back, expert_up, preferred_element_type=jnp.float32)
    rows_back = grads_home(input_back).reshape(experts * capacity, model_width)
    moe_back = jnp.sum(rows_back[slot_place].reshape(quarter, TOPK, model_width), axis=1)
    gate_route_back = jnp.sum(route_values * grad_quarter.astype(jnp.float32)[:, None, :], axis=-1)
    prob_back = jnp.sum(chosen * gate_route_back[:, :, None], axis=1)
    _, soft_back = jax.vjp(lambda values: jax.nn.softmax(values, axis=-1), logits)
    logit_back = soft_back(prob_back)[0].astype(jnp.bfloat16)
    router_term = transposed_left(normed_quarter, logit_back)
    shared_back = transposed_right(grad_rows, shared_down_matrix)
    _, shared_mix_back = jax.vjp(silu_mix, shared_gate_rows, shared_up_rows)
    sgate_back, sup_back = shared_mix_back(shared_back)
    sgate_back = sgate_back.astype(jnp.bfloat16)
    sup_back = sup_back.astype(jnp.bfloat16)
    quarter_back = transposed_right(logit_back, router_matrix) + moe_back
    mix_part = (
        transposed_right(sgate_back, shared_gate_matrix)
        + transposed_right(sup_back, shared_up_matrix)
        + place_rows(quarter_back, start_row, rows_here)
    )
    mix_total, router_grad = (
        lax.psum(mix_part.astype(jnp.bfloat16), "exp").astype(jnp.float32),
        lax.psum(router_term.astype(jnp.bfloat16), "exp").astype(jnp.float32),
    )
    _, norm_mix_back = jax.vjp(rms_scale, middle, mixer_gain.astype(jnp.float32))
    middle_norm_back, gain_mix_grad = norm_mix_back(mix_total)
    middle_grad = grad_float + middle_norm_back
    sdown_grad = transposed_left(shared_act, grad_rows)
    sgate_grad = transposed_left(normed_mix, sgate_back)
    sup_grad = transposed_left(normed_mix, sup_back)
    attn_back = middle_grad.astype(jnp.bfloat16)
    heads_back = transposed_right(attn_back, output_matrix).astype(jnp.bfloat16).reshape(head_shape)
    weights_full = jnp.exp(attention_scores() - log_total)
    weights_again = weights_full.astype(jnp.bfloat16)
    weight_back = jnp.einsum(
        "qhd,khd->hqk", heads_back, value_heads, preferred_element_type=jnp.float32
    )
    value_term = jnp.einsum(
        "hqk,qhd->khd", weights_again, heads_back, preferred_element_type=jnp.float32
    ).reshape(seq_length, -1)
    score_back = (
        weights_full * (weight_back - jnp.sum(weights_full * weight_back, axis=-1, keepdims=True))
    ).astype(jnp.bfloat16)
    query_rot_back = (
        jnp.einsum("hqk,khd->qhd", score_back, key_heads, preferred_element_type=jnp.float32)
        * scale
    )
    key_term = (
        jnp.einsum("hqk,qhd->khd", score_back, query_rot, preferred_element_type=jnp.float32)
        * scale
    ).reshape(seq_length, -1)
    key_sum, value_sum = (
        lax.psum_scatter(
            key_term.astype(jnp.bfloat16), "ctx", scatter_dimension=0, tiled=True
        ).astype(jnp.float32),
        lax.psum_scatter(
            value_term.astype(jnp.bfloat16), "ctx", scatter_dimension=0, tiled=True
        ).astype(jnp.float32),
    )
    _, rotate_back = jax.vjp(
        lambda values: rotate(values, cosine, sine_table), jnp.zeros(head_shape, jnp.float32)
    )
    query_low = rotate_back(query_rot_back)[0].reshape(rows_here, -1).astype(jnp.bfloat16)
    key_low = (
        rotate_back(key_sum.reshape(head_shape))[0].reshape(rows_here, -1).astype(jnp.bfloat16)
    )
    value_back_low = value_sum.astype(jnp.bfloat16)
    normed_part = (
        transposed_right(query_low, query_matrix)
        + transposed_right(key_low, key_matrix)
        + transposed_right(value_back_low, value_matrix)
    )
    normed_back = lax.psum(normed_part.astype(jnp.bfloat16), "exp").astype(jnp.float32)
    _, norm_attn_back = jax.vjp(rms_scale, layer_input, attention_gain.astype(jnp.float32))
    input_norm_back, gain_attn_grad = norm_attn_back(normed_back)
    tokens_back = (middle_grad + input_norm_back).astype(jnp.bfloat16)
    out_weight_grad = transposed_left(heads_out, attn_back)
    query_grad = transposed_left(normed, query_low)
    key_grad = transposed_left(normed, key_low)
    value_grad = transposed_left(normed, value_back_low)
    all_sums = (
        lax.psum_scatter(
            gain_attn_grad.astype(jnp.bfloat16), ("dp", "ctx"), scatter_dimension=0, tiled=True
        ).astype(jnp.float32),
        lax.psum_scatter(
            query_grad.astype(jnp.bfloat16), ("dp", "ctx"), scatter_dimension=0, tiled=True
        ).astype(jnp.float32),
        lax.psum_scatter(
            key_grad.astype(jnp.bfloat16), ("dp", "ctx"), scatter_dimension=0, tiled=True
        ).astype(jnp.float32),
        lax.psum_scatter(
            value_grad.astype(jnp.bfloat16), ("dp", "ctx"), scatter_dimension=0, tiled=True
        ).astype(jnp.float32),
        lax.psum_scatter(
            out_weight_grad.astype(jnp.bfloat16), ("dp", "ctx"), scatter_dimension=1, tiled=True
        ).astype(jnp.float32),
        lax.psum_scatter(
            gain_mix_grad.astype(jnp.bfloat16), ("dp", "ctx"), scatter_dimension=0, tiled=True
        ).astype(jnp.float32),
        lax.psum_scatter(
            router_grad.astype(jnp.bfloat16), ("dp", "ctx"), scatter_dimension=0, tiled=True
        ).astype(jnp.float32),
        lax.psum_scatter(
            sgate_grad.astype(jnp.bfloat16), ("dp", "ctx"), scatter_dimension=0, tiled=True
        ).astype(jnp.float32),
        lax.psum_scatter(
            sup_grad.astype(jnp.bfloat16), ("dp", "ctx"), scatter_dimension=0, tiled=True
        ).astype(jnp.float32),
        lax.psum_scatter(
            sdown_grad.astype(jnp.bfloat16), ("dp", "ctx"), scatter_dimension=1, tiled=True
        ).astype(jnp.float32),
    )
    (
        gain_attn_sum,
        query_sum,
        key_sum_out,
        value_sum_out,
        out_sum,
        gain_mix_sum,
        router_sum,
        sgate_sum,
        sup_sum,
        sdown_sum,
    ) = all_sums
    return (
        result.astype(jnp.bfloat16)[None],
        tokens_back[None],
        gain_attn_sum,
        query_sum,
        key_sum_out,
        value_sum_out,
        out_sum,
        gain_mix_sum,
        router_sum,
        sgate_sum,
        sup_sum,
        sdown_sum,
        gate_grad,
        up_grad,
        down_grad,
    )


MESH = pl.DeviceIdType.MESH
BF = jnp.bfloat16
F32 = jnp.float32


class Place:
    def __init__(self):
        self.x = lax.axis_index("dp")
        self.z = lax.axis_index("ctx")
        self.e = lax.axis_index("exp")
        z = self.z
        high = lax.div(z, 2)
        self.zs = [z, z + 1 - 2 * lax.rem(z, 2), 2 - high, 3 - 3 * high]
        self.inner = 3 - z
        self.inside = lax.div(z * (3 - z), 2)
        self.middle = self.inside == 1
        self.dx = 1 - 2 * self.x
        self.dy = 2 - 4 * lax.div(self.e, 2)
        self.dc = 1 - 2 * lax.rem(self.e, 2)

    def device(self, ox=0, oe=0, zi=0):
        return (self.x + ox, self.zs[zi], self.e + oe)

    def inward(self):
        return (self.x, self.inner, self.e)

    def shard(self, oe, zi):
        return self.zs[zi] * 4 + self.e + oe


def greet(at, everyone, pair=False):
    barrier = pltpu.get_barrier_semaphore()
    peers = [at.device(zi=1), at.device(oe=at.dy), at.device(oe=at.dc)]
    if everyone or pair:
        peers.append(at.device(ox=at.dx))
    if everyone:
        peers += [at.device(zi=2), at.device(zi=3)]
    for peer in peers:
        pl.semaphore_signal(barrier, inc=1, device_id=peer, device_id_type=MESH)
    if everyone:
        pl.semaphore_wait(barrier, len(peers))
        return

    @pl.when(at.middle)
    def _():
        pl.semaphore_signal(barrier, inc=1, device_id=at.inward(), device_id_type=MESH)

    pl.semaphore_wait(barrier, len(peers) + at.inside)


def remote(src, dst, send, recv, device):
    return pltpu.make_async_remote_copy(
        src_ref=src, dst_ref=dst, send_sem=send, recv_sem=recv, device_id=device, device_id_type=MESH
    )


def keep(src, dst):
    def run(held, sems):
        for j, (a, b) in enumerate(((src, held), (held, dst))):
            copy = pltpu.make_async_copy(a, b, sems.at[j])
            copy.start()
            copy.wait()

    pl.run_scoped(run, pltpu.VMEM(src.shape, src.dtype), pltpu.SemaphoreType.DMA((2,)))


def half_of(array):
    return jax.ShapeDtypeStruct((array.shape[0] // 2,) + array.shape[1:], array.dtype)


def cross(at, sent, got, send_sem, recv_sem, starts=None):
    starts = starts or (0,) * len(sent)
    return [
        remote(
            a.at[pl.ds(start, b.shape[0])],
            b,
            send_sem.at[m],
            recv_sem.at[m],
            at.device(ox=at.dx),
        )
        for m, (a, b, start) in enumerate(zip(sent, got, starts))
    ]


class Exchange:
    def __init__(self, at, sent, got, send_sem, recv_sem):
        self.at, self.sent, self.got = at, sent, got
        self.send_sem, self.recv_sem = send_sem, recv_sem
        self.waits = []

    def push(self, src, m, z_from, slot, device):
        at = self.at
        spot = self.got[m].at[at.x * 4 + z_from]
        copy = remote(
            src, spot, self.send_sem.at[m * 7 + slot], self.recv_sem.at[m * 8 + (0 if slot < 3 else 4) + z_from], device
        )
        copy.start()
        self.waits.append(copy)

    def start(self):
        at = self.at
        for m, sent in enumerate(self.sent):
            self.push(sent.at[at.z], m, at.z, 3, at.device(ox=at.dx))
        for m, sent in enumerate(self.sent):
            keep(sent.at[at.z], self.got[m].at[at.x * 4 + at.z])

    def along(self, zi):
        at = self.at
        for m, sent in enumerate(self.sent):
            self.push(sent.at[at.zs[zi]], m, at.z, zi - 1, at.device(zi=zi))

    def arrive(self, m, slot):
        src = self.sent[m].at[0]
        remote(
            src, self.got[m].at[0], self.send_sem.at[0], self.recv_sem.at[slot], self.at.device(ox=self.at.dx)
        ).wait_recv()

    def forward(self, zi):
        at = self.at
        for m in range(len(self.sent)):
            self.arrive(m, m * 8 + at.zs[zi])
            self.push(self.got[m].at[at.x * 4 + at.zs[zi]], m, at.zs[zi], 3 + zi, at.device(ox=at.dx))

    def finish(self):
        at = self.at
        for m, sent in enumerate(self.sent):
            for z in range(4):
                self.arrive(m, m * 8 + 4 + z)
        for copy in self.waits:
            copy.wait_send()


def gather_kernel(block, rows, parts, extras, starts, *refs):
    swaps = len(starts)
    refs = list(refs)

    def take(count):
        taken = refs[:count]
        del refs[:count]
        return taken

    (x_ref,), sent, given = take(1), take(extras), take(swaps)
    (out_ref,), got, taken = take(1), take(extras), take(swaps)
    send_sem, recv_sem = take(2)
    extra_sems = take(2 if extras else 0)
    at = Place()
    greet(at, extras > 0, swaps > 0)
    crossing = cross(at, given, taken, *refs, starts) if swaps else []
    piece = rows // parts
    slot_z, slot_f, slot_s = 0, 3, 7
    started, inside = [], []
    firsts = 1 if block else 0
    shift = at.e * rows if block else 0

    def where(f, zi, p):
        return pl.ds(
            pl.multiple_of(at.shard(f * at.dy, zi) * rows + p * piece, piece), piece
        )

    def push(src, dst, slot, p, device, sends=None, record=None):
        k = slot * parts + p
        j = k if sends is None else sends * parts + p
        remote(src, out_ref.at[dst], send_sem.at[j], recv_sem.at[k], device).start()
        (started if record is None else record).append(j)

    f_dev, s_dev, z_dev = at.device(oe=at.dy), at.device(oe=at.dc), at.device(zi=1)

    def gone(j):
        remote(
            x_ref.at[pl.ds(0, piece)], out_ref.at[pl.ds(0, piece)], send_sem.at[j], recv_sem.at[0], s_dev
        ).wait_send()

    def arrive(slot, p):
        k = slot * parts + p
        remote(
            x_ref.at[pl.ds(0, piece)], out_ref.at[pl.ds(0, piece)], send_sem.at[k], recv_sem.at[k], s_dev
        ).wait_recv()

    if block:
        spot = pl.ds(pl.multiple_of(at.z * 4 * rows, 4 * rows), 4 * rows)
    else:
        spot = pl.ds(pl.multiple_of(at.shard(0, 0) * rows, rows), rows)

    def source(f, zi, p):
        if f == 0 and zi == 0:
            return x_ref.at[pl.ds(pl.multiple_of(shift + p * piece, piece), piece)]
        return out_ref.at[where(f, zi, p)]

    def along(zi, p):
        src, dst = source(0, zi, p), where(0, zi, p)
        if zi == 0:
            push(src, dst, slot_z, p, z_dev)
        if zi < 2:
            pl.when(at.middle)(
                lambda: push(src, dst, slot_z + 1 + zi, p, at.inward(), 15 + zi, inside)
            )
        else:
            pl.when(at.middle)(lambda: push(src, dst, slot_z + zi - 1, p, z_dev, 15 + zi, inside))

    def forward(f, zi, p):
        src, dst = source(f, zi, p), where(f, zi, p)
        if f == 0:
            along(zi, p)
        if zi >= firsts:
            if f == 0:
                push(src, dst, slot_f + zi, p, f_dev)
            push(src, dst, slot_s + f * 4 + zi, p, s_dev)

    for p in range(parts):
        forward(0, 0, p)
    if extras:
        swap_in = Exchange(at, sent, got, *extra_sems)
        for zi in (1, 2, 3):
            swap_in.along(zi)
        swap_in.start()
    for copy in crossing:
        copy.start()
    keep(x_ref, out_ref.at[spot])
    for zi in range(1, 5):
        for p in range(parts):
            if zi < 4:
                arrive(slot_z + zi - 1, p)
                forward(0, zi, p)
            if zi - 1 >= firsts:
                arrive(slot_f + zi - 1, p)
                forward(1, zi - 1, p)
        if extras and zi > 1:
            swap_in.forward(zi - 1)
    for f in range(2):
        for zi in range(firsts, 4):
            for p in range(parts):
                arrive(slot_s + f * 4 + zi, p)
    if extras:
        swap_in.finish()
    for copy in crossing:
        copy.wait()
    for j in started:
        gone(j)

    @pl.when(at.middle)
    def _():
        for j in inside:
            gone(j)


def all_rows(x, block, cid, sent=(), given=(), starts=(), parts=2):
    rows, width = x.shape
    total = rows * (4 if block else 16)
    rows = rows // 4 if block else rows
    extras, swaps = len(sent), len(given)
    hbm = pl.BlockSpec(memory_space=pl.ANY)
    outs = [jax.ShapeDtypeStruct((total, width), x.dtype)]
    outs += [jax.ShapeDtypeStruct((8,) + a.shape[1:], a.dtype) for a in sent]
    outs += [half_of(a) for a in given]
    scratch = [
        pltpu.SemaphoreType.DMA((19 * parts,)),
        pltpu.SemaphoreType.DMA((15 * parts,)),
    ]
    if extras:
        scratch += [
            pltpu.SemaphoreType.DMA((7 * extras,)),
            pltpu.SemaphoreType.DMA((8 * extras,)),
        ]
    if swaps:
        scratch += [pltpu.SemaphoreType.DMA((swaps,)), pltpu.SemaphoreType.DMA((swaps,))]
    got = pl.pallas_call(
        functools.partial(gather_kernel, block, rows, parts, extras, starts),
        out_shape=outs,
        in_specs=[hbm] * len(outs),
        out_specs=[hbm] * len(outs),
        scratch_shapes=scratch,
        compiler_params=pltpu.CompilerParams(collective_id=cid, has_side_effects=True),
    )(x, *sent, *given)
    return got if extras or swaps else got[0]


class Scatter:
    def __init__(self, at, acc, got_s, got_f, got_z, send_sem, recv_sem, out_ref, by_block=False):
        self.by_block = by_block
        self.at, self.acc, self.got_s, self.got_f, self.got_z = at, acc, got_s, got_f, got_z
        self.send_sem, self.recv_sem, self.out_ref = send_sem, recv_sem, out_ref
        self.rows = acc.shape[1]
        self.f_dev, self.s_dev, self.z_dev = (
            at.device(oe=at.dy),
            at.device(oe=at.dc),
            at.device(zi=1),
        )
        self.twins = [[], [], [], []]
        self.started, self.in_middle, self.at_end = [], [], []

    def held(self, f, zi, twin=0):
        at = self.at
        return zi * 4 + at.e + f * at.dy + twin * at.dc if self.by_block else f * 4 + zi

    def push(self, src, dst, slot, device, sends=None, record=None):
        j = slot if sends is None else sends
        remote(src, dst, self.send_sem.at[j], self.recv_sem.at[slot], device).start()
        (self.started if record is None else record).append(j)

    def gone(self, j):
        spot = self.acc.at[0]
        remote(spot, spot, self.send_sem.at[j], self.recv_sem.at[0], self.s_dev).wait_send()

    def arrive(self, dst, slot):
        remote(
            self.acc.at[0], dst, self.send_sem.at[slot], self.recv_sem.at[slot], self.s_dev
        ).wait_recv()

    def to_twin(self, src, f, zi):
        k = f * 4 + zi
        self.push(src, self.got_s.at[k], 9 + k, self.s_dev, None, self.twins[zi])

    def twin_gone(self, zi):
        for j in self.twins[zi]:
            self.gone(j)
        self.twins[zi] = []

    def add(self, k, *others, into=None):
        acc = self.acc

        @pl.loop(0, self.rows // 16)
        def _(i):
            span = pl.ds(pl.multiple_of(i * 16, 16), 16)
            total = acc[k, span, :].astype(F32)
            for ref, j in others:
                total = total + ref[j, span, :].astype(F32)
            if into is None:
                acc[k, span, :] = total.astype(BF)
            else:
                into[span, :] = total

    def first(self, zi):
        k = self.held(1, zi)
        self.arrive(self.got_s.at[4 + zi], 13 + zi)
        self.add(k, (self.got_s, 4 + zi))
        self.push(self.acc.at[k], self.got_f.at[zi], 5 + zi, self.f_dev)

    def second(self, zi, who="all"):
        if who != "middle":
            pl.when(jnp.logical_not(self.at.middle))(lambda: self.from_end(zi))
        if who != "end":
            pl.when(self.at.middle)(lambda: self.from_middle(zi))

    def terms(self, zi):
        self.arrive(self.got_s.at[zi], 9 + zi)
        self.arrive(self.got_f.at[zi], 5 + zi)
        return self.held(0, zi), [(self.got_s, zi), (self.got_f, zi)]

    def from_end(self, zi):
        k, others = self.terms(zi)
        acc, got_z = self.acc, self.got_z
        if zi == 0:
            self.arrive(got_z.at[4], 4)
            self.add(k, *others, (got_z, 4), into=self.out_ref)
            return
        self.add(k, *others)
        self.push(acc.at[k], got_z.at[3 - zi], 3 - zi, self.z_dev, zi, self.at_end)

    def from_middle(self, zi):
        k, others = self.terms(zi)
        acc, got_z = self.acc, self.got_z
        if zi == 0:
            self.arrive(got_z.at[2], 2)
            self.arrive(got_z.at[4], 4)
            self.add(k, *others, (got_z, 2), (got_z, 4), into=self.out_ref)
            return
        came = 3 if zi == 1 else 3 - zi
        self.arrive(got_z.at[came], came)
        self.add(k, *others, (got_z, came))
        there = 3 if zi == 3 else 4
        device = self.z_dev if zi == 1 else self.at.inward()
        self.push(acc.at[k], got_z.at[there], there, device, zi, self.in_middle)

    def finish(self):
        for zi in range(4):
            self.twin_gone(zi)
        for j in self.started:
            self.gone(j)

        @pl.when(self.at.middle)
        def _():
            for j in self.in_middle:
                self.gone(j)

        @pl.when(jnp.logical_not(self.at.middle))
        def _():
            for j in self.at_end:
                self.gone(j)


def scatter_buffers(rows, width, held=8):
    return [
        pltpu.VMEM((held, rows, width), BF),
        pltpu.VMEM((8, rows, width), BF),
        pltpu.VMEM((4, rows, width), BF),
        pltpu.VMEM((5, rows, width), BF),
        pltpu.SemaphoreType.DMA((17,)),
        pltpu.SemaphoreType.DMA((17,)),
    ]


def scatter_kernel(rows, starts, in_ref, *refs):
    swaps = len(starts)
    given, out_ref, taken = refs[:swaps], refs[swaps], refs[swaps + 1 : 2 * swaps + 1]
    buffers, load_sem = refs[2 * swaps + 1 : 2 * swaps + 7], refs[2 * swaps + 7]
    acc = buffers[0]
    at = Place()
    greet(at, False, swaps > 0)
    crossing = cross(at, given, taken, *refs[2 * swaps + 8 :], starts) if swaps else []
    total = Scatter(at, *buffers, out_ref)

    def rows_of(rank):
        return in_ref.at[pl.ds(pl.multiple_of(rank * rows, rows), rows)]

    order = [(f, zi) for f in (1, 0) for zi in (3, 2, 1, 0)]
    loads = {}
    for f, zi in order:
        k = f * 4 + zi
        total.to_twin(rows_of(at.shard(f * at.dy + at.dc, zi)), f, zi)
        loads[k] = pltpu.make_async_copy(
            rows_of(at.shard(f * at.dy, zi)), acc.at[k], load_sem.at[k]
        )
        loads[k].start()
    for copy in crossing:
        copy.start()
    for f, zi in order:
        loads[f * 4 + zi].wait()
        (total.first if f else total.second)(zi)
    for copy in crossing:
        copy.wait()
    total.finish()


def own_rows(x, cid, given=(), starts=()):
    rows, width = x.shape[0] // 16, x.shape[1]
    swaps = len(given)
    hbm = pl.BlockSpec(memory_space=pl.ANY)
    crossing = [pltpu.SemaphoreType.DMA((swaps,))] * 2 if swaps else []
    got = pl.pallas_call(
        functools.partial(scatter_kernel, rows, starts),
        out_shape=[jax.ShapeDtypeStruct((rows, width), F32)]
        + [half_of(a) for a in given],
        in_specs=[hbm] * (1 + swaps),
        out_specs=[pl.BlockSpec(memory_space=pltpu.VMEM)] + [hbm] * swaps,
        scratch_shapes=[
            *scatter_buffers(rows, width),
            pltpu.SemaphoreType.DMA((8,)),
            *crossing,
        ],
        compiler_params=pltpu.CompilerParams(
            collective_id=cid, has_side_effects=True, vmem_limit_bytes=40 * 1024 * 1024
        ),
    )(x, *given)
    return got if swaps else got[0]


class Gather:
    parts = 2

    def __init__(self, at, x_ref, out_ref, send_sem, recv_sem, block=False):
        self.at, self.x_ref, self.out_ref, self.block = at, x_ref, out_ref, block
        self.send_sem, self.recv_sem = send_sem, recv_sem
        rows = x_ref.shape[0] // (4 if block else 1)
        self.rows, self.piece = rows, rows // self.parts
        self.f_dev, self.s_dev, self.z_dev = (
            at.device(oe=at.dy),
            at.device(oe=at.dc),
            at.device(zi=1),
        )
        self.started, self.inside = [], []
        if block:
            spot = pl.ds(pl.multiple_of(at.z * 4 * rows, 4 * rows), 4 * rows)
        else:
            spot = pl.ds(pl.multiple_of(at.shard(0, 0) * rows, rows), rows)
        self.place = spot

    def push(self, f, zi, p, slot, device, sends=None, record=None):
        at, piece = self.at, self.piece
        spot = at.shard(f * at.dy, zi) * self.rows + p * piece
        dst = self.out_ref.at[pl.ds(pl.multiple_of(spot, piece), piece)]
        src = dst
        if f == 0 and zi == 0:
            spot = (at.e * self.rows if self.block else 0) + p * piece
            src = self.x_ref.at[pl.ds(pl.multiple_of(spot, piece), piece)]
        j = (slot if sends is None else sends) * self.parts + p
        k = slot * self.parts + p
        remote(src, dst, self.send_sem.at[j], self.recv_sem.at[k], device).start()
        (self.started if record is None else record).append(j)

    def spot(self):
        span = pl.ds(0, self.piece)
        return self.x_ref.at[span], self.out_ref.at[span]

    def arrive(self, slot, p):
        k = slot * self.parts + p
        remote(*self.spot(), self.send_sem.at[k], self.recv_sem.at[k], self.s_dev).wait_recv()

    def forward(self, f, zi, p):
        if f == 0:
            if zi == 0:
                self.push(0, 0, p, 0, self.z_dev)
            if zi < 2:
                pl.when(self.at.middle)(
                    lambda: self.push(0, zi, p, 1 + zi, self.at.inward(), 15 + zi, self.inside)
                )
            else:
                pl.when(self.at.middle)(
                    lambda: self.push(0, zi, p, zi - 1, self.z_dev, 15 + zi, self.inside)
                )
        if self.block and zi == 0:
            return
        if f == 0:
            self.push(0, zi, p, 3 + zi, self.f_dev)
        self.push(f, zi, p, 7 + f * 4 + zi, self.s_dev)

    def begin(self):
        for p in range(self.parts):
            self.forward(0, 0, p)
        keep(self.x_ref, self.out_ref.at[self.place])

    def step(self, zi):
        for p in range(self.parts):
            if zi < 4:
                self.arrive(zi - 1, p)
                self.forward(0, zi, p)
            if zi > 1 or not self.block:
                self.arrive(2 + zi, p)
                self.forward(1, zi - 1, p)

    def twin(self, zi):
        for p in range(self.parts):
            self.arrive(7 + zi, p)
            self.arrive(11 + zi, p)

    def finish(self, arrived=False):
        for zi in range(4):
            if not arrived and not (self.block and zi == 0):
                self.twin(zi)

        def gone(j):
            remote(*self.spot(), self.send_sem.at[j], self.recv_sem.at[0], self.s_dev).wait_send()

        for j in self.started:
            gone(j)

        @pl.when(self.at.middle)
        def _():
            for j in self.inside:
                gone(j)


def columns_loop(width, parts):
    size = width // parts

    def over(run):
        @pl.loop(0, parts)
        def _(n):
            run(pl.ds(pl.multiple_of(n * size, size), size))

    return over


def expert_gather_kernel(experts, *refs):
    refs = list(refs)

    def take(count):
        taken = refs[:count]
        del refs[:count]
        return taken

    x_ref, dy_ref, disp, w_router, units = take(5)
    weights, given = take(7), take(2)
    out_ref, picked, picked_dy, scaled_out, g_out, u_out, gb_out, sa_out, sg_out = take(9)
    taken, units_out = take(2), take(2)
    shared_in, shared_out = take(2)
    wg, wu, wd, xb, dyd, sb, pk, pdy, sc, gg, uu, hid, gb, sa, sg = take(15)
    send_sem, recv_sem, load_sem, block_sem, store_sem, cross_send, cross_recv, unit_sem = take(8)
    at = Place()
    greet(at, False, True)
    gather = Gather(at, x_ref, out_ref, send_sem, recv_sem)
    crossing = cross(at, given, taken, cross_send, cross_recv, (0, taken[0].shape[0]))
    block = xb.shape[1]
    slots = pk.shape[0] // 4
    part = wd.shape[1] // 2
    mine = at.z * 4 + at.e

    def span(zi, size):
        return pl.ds(pl.multiple_of(at.zs[zi] * size, size), size)

    def dy_load(zi):
        return pltpu.make_async_copy(
            dy_ref.at[span(zi, block)], xb.at[zi % 2], block_sem.at[2 + zi % 2]
        )

    def x_load(zi):
        return pltpu.make_async_copy(
            out_ref.at[span(zi, block)], xb.at[zi % 2], block_sem.at[zi % 2]
        )

    def stores(zi):
        b = zi % 2
        pairs = [(sa.at[b], sa_out.at[span(zi, block)]), (sg.at[b], sg_out.at[span(zi, block)])]
        return [
            pltpu.make_async_copy(src, dst, store_sem.at[b * 2 + j])
            for j, (src, dst) in enumerate(pairs)
        ]

    def parts_of(gate, up):
        s = 1.0 / (1.0 + jnp.exp(-gate))
        act = gate * s
        return act * up, s * (1.0 + gate * (1.0 - s)) * up, act

    cut, size = units.shape[1] // 3, units.shape[2]
    wide = shared_out.shape[0]
    unit_loads = []
    for d in range(8):
        for m in range(3):
            ref, first = (shared_out, 0) if m == 2 else (shared_in, m * wide)
            unit_loads.append(
                pltpu.make_async_copy(
                    units.at[d, pl.ds(m * cut, cut)],
                    ref.at[pl.ds(first, cut), pl.ds(d * size, size)],
                    unit_sem.at[d * 3 + m],
                )
            )

    def ahead(zi):
        b = zi % 2
        some = span(zi, slots)
        dy_load(zi).wait()
        pdy[some, :] = product(disp[at.zs[zi]], xb[b]).astype(BF)
        sb[span(zi, block), :] = transposed_right(xb[b], shared_out[...])
        if zi < 2:
            dy_load(zi + 2).start()
        dyd[some, :] = transposed_right(pdy[some, :], wd[0])

    def work(zi):
        b = zi % 2
        some = span(zi, slots)
        x_load(zi).wait()
        if zi >= 2:
            for copy in stores(zi - 2):
                copy.wait()
        pk[some, :] = product(disp[at.zs[zi]], xb[b]).astype(BF)
        logits = transposed_right(pk[some, :], w_router[...])
        lane = lax.broadcasted_iota(jnp.int32, logits.shape, 1)
        logits = jnp.where(lane < experts, logits, MASKED)
        powers = jnp.exp(logits - jnp.max(logits, axis=1, keepdims=True))
        own_power = jnp.sum(jnp.where(lane == mine, powers, 0.0), axis=1, keepdims=True)
        gate_of = own_power / jnp.sum(powers, axis=1, keepdims=True)
        for h in range(2):
            hidden, by_gate, by_up = parts_of(
                transposed_right(pk[some, :], wg[h]), transposed_right(pk[some, :], wu[h])
            )
            sc[h, some, :] = (hidden * gate_of).astype(BF)
            if h == 0:
                dy_down = dyd[some, :]
                act_back = gate_of * dy_down
                gg[0, some, :] = (act_back * by_gate).astype(BF)
                uu[0, some, :] = (act_back * by_up).astype(BF)
                gb[some, :] = jnp.broadcast_to(
                    jnp.sum(hidden * dy_down, axis=1, keepdims=True), (slots, gb.shape[1])
                )
            else:
                hid[some, :] = hidden.astype(BF)
                gg[1, some, :] = (gate_of * by_gate).astype(BF)
                uu[1, some, :] = (gate_of * by_up).astype(BF)
        both = transposed_right(xb[b], shared_in[...])
        wide = both.shape[1] // 2
        hidden, by_gate, by_up = parts_of(both[:, :wide], both[:, wide:])
        back = sb[span(zi, block), :]
        sa[b] = hidden.astype(BF)
        sg[b, :, :wide] = (back * by_gate).astype(BF)
        sg[b, :, wide:] = (back * by_up).astype(BF)
        for copy in stores(zi):
            copy.start()

    def other_half(zi):
        some = span(zi, slots)
        dy_down = transposed_right(pdy[some, :], wd[1])
        gg[1, some, :] = (dy_down * gg[1, some, :].astype(F32)).astype(BF)
        uu[1, some, :] = (dy_down * uu[1, some, :].astype(F32)).astype(BF)
        gb[some, :] += jnp.broadcast_to(
            jnp.sum(hid[some, :].astype(F32) * dy_down, axis=1, keepdims=True), (slots, gb.shape[1])
        )

    gather.begin()
    places = [
        wg.at[0],
        wu.at[0],
        wd.at[0],
        wg.at[1, pl.ds(0, part)],
        wg.at[1, pl.ds(part, part)],
        wu.at[1, pl.ds(0, part)],
        wu.at[1, pl.ds(part, part)],
        wd.at[1, pl.ds(0, part)],
        wd.at[1, pl.ds(part, part)],
    ]
    loads = [
        pltpu.make_async_copy(a, b, load_sem.at[j]) for j, (a, b) in enumerate(zip(weights + taken, places))
    ]
    dy_load(0).start()
    dy_load(1).start()
    for j in (2, 0, 1, 3, 4, 5, 6):
        loads[j].start()
    for copy in crossing:
        copy.start()
    shared_in[...] = jnp.zeros_like(shared_in)
    shared_out[...] = jnp.zeros_like(shared_out)
    for copy in unit_loads:
        copy.start()
    for copy in unit_loads:
        copy.wait()
    loads[2].wait()
    for zi in range(3):
        ahead(zi)
    for zi in range(4):
        gather.step(zi + 1)
        if zi == 0:
            ahead(3)
        gather.twin(zi)
        x_load(zi).start()
        if zi == 0:
            for j in (0, 1, 3, 4, 5, 6):
                loads[j].wait()
        work(zi)
    results = [(pk, picked), (pdy, picked_dy), (sc, scaled_out)]
    results += [(shared_in, units_out[0]), (shared_out, units_out[1])]
    results += [(gg, g_out), (uu, u_out), (gb, gb_out)]
    results = [
        pltpu.make_async_copy(a, b, store_sem.at[4 + j]) for j, (a, b) in enumerate(results)
    ]
    for copy in results[:5]:
        copy.start()
    for m in range(2):
        crossing[m].wait_recv()
        loads[7 + m].start()
    for m in range(2):
        loads[7 + m].wait()
    for zi in range(4):
        other_half(zi)
    for copy in results[5:]:
        copy.start()
    for copy in results:
        copy.wait()
    for zi in (2, 3):
        for copy in stores(zi):
            copy.wait()
    for copy in crossing:
        copy.wait_send()
    gather.finish(True)


def expert_rows(x, dy_all, dispatch, w_router, experts, units, wide, weights, given, cid):
    rows, width = x.shape
    total, block = 16 * rows, 4 * rows
    slots = 4 * dispatch.shape[1]
    hidden = weights[0].shape[0]
    halves = [half_of(a) for a in given]
    hbm, vmem = pl.BlockSpec(memory_space=pl.ANY), pl.BlockSpec(memory_space=pltpu.VMEM)
    shape, sems = jax.ShapeDtypeStruct, lambda n: pltpu.SemaphoreType.DMA((n,))
    return pl.pallas_call(
        functools.partial(expert_gather_kernel, experts),
        out_shape=[
            shape((total, width), BF),
            shape((slots, width), BF),
            shape((slots, width), BF),
            shape((2, slots, hidden), BF),
            shape((2, slots, hidden), BF),
            shape((2, slots, hidden), BF),
            shape((slots, 128), F32),
            shape((total, wide), BF),
            shape((total, 2 * wide), BF),
            *halves,
            shape((2 * wide, width), BF),
            shape((wide, width), BF),
        ],
        in_specs=[hbm, hbm, vmem, vmem] + [hbm] * 10,
        out_specs=[hbm] * 13,
        scratch_shapes=[
            pltpu.VMEM((2 * wide, width), BF),
            pltpu.VMEM((wide, width), BF),
            pltpu.VMEM((2, hidden, width), BF),
            pltpu.VMEM((2, hidden, width), BF),
            pltpu.VMEM((2, hidden, width), BF),
            pltpu.VMEM((2, block, width), BF),
            pltpu.VMEM((slots, hidden), F32),
            pltpu.VMEM((total, wide), F32),
            pltpu.VMEM((slots, width), BF),
            pltpu.VMEM((slots, width), BF),
            pltpu.VMEM((2, slots, hidden), BF),
            pltpu.VMEM((2, slots, hidden), BF),
            pltpu.VMEM((2, slots, hidden), BF),
            pltpu.VMEM((slots, hidden), BF),
            pltpu.VMEM((slots, 128), F32),
            pltpu.VMEM((2, block, wide), BF),
            pltpu.VMEM((2, block, 2 * wide), BF),
            sems(38),
            sems(30),
            sems(9),
            sems(4),
            sems(12),
            sems(2),
            sems(2),
            sems(24),
        ],
        compiler_params=pltpu.CompilerParams(
            collective_id=cid, has_side_effects=True, vmem_limit_bytes=62 * 1024 * 1024
        ),
    )(x, dy_all, dispatch, w_router, units, *weights, *given)


def expert_scatter_kernel(*refs):
    refs = list(refs)

    def take(count):
        taken = refs[:count]
        del refs[:count]
        return taken

    disp, gate_back, shared_in, g_ref, u_ref, sg_ref, picked_ref, dy_ref, scaled_ref = take(9)
    weights = take(6)
    out_ref, taken, *grads = take(7)
    wg, wu, gs, us, sg, picked, picked_dy, scaled, ib, grad, turned = take(11)
    acc, got_s, got_f, got_z, send_sem, recv_sem = take(6)
    load_sem, store_sem, cross_send, cross_recv = take(4)
    at = Place()
    greet(at, False, True)
    rows, full = acc.shape[1:]
    width = shared_in.shape[1]
    slots = ib.shape[0]
    block = 4 * rows
    over = columns_loop(width, 4)
    mine = at.z * 4 + at.e
    total = Scatter(at, acc, got_s, got_f, got_z, send_sem, recv_sem, out_ref, True)

    part = wg.shape[1] // 2
    pairs = [
        (weights[0], wg.at[0]),
        (weights[1], wu.at[0]),
        (weights[2], wg.at[1, pl.ds(0, part)]),
        (weights[3], wg.at[1, pl.ds(part, part)]),
        (weights[4], wu.at[1, pl.ds(0, part)]),
        (weights[5], wu.at[1, pl.ds(part, part)]),
        (g_ref, gs),
        (u_ref, us),
        (sg_ref, sg),
        (picked_ref, picked),
        (dy_ref, picked_dy),
        (scaled_ref.at[1], scaled),
    ]
    loads = [pltpu.make_async_copy(a, b, load_sem.at[j]) for j, (a, b) in enumerate(pairs)]
    for copy in loads:
        copy.start()

    def work(zi):
        place = at.zs[zi]
        some = pl.ds(pl.multiple_of(place * slots, slots), slots)

        hot = disp[place]
        tokens = pl.ds(pl.multiple_of(place * block, block), block)

        @over
        def _(columns):
            terms = product(gs[0, some, :], wg[0, :, columns])
            terms += product(us[0, some, :], wu[0, :, columns])
            terms += product(gs[1, some, :], wg[1, :, columns])
            terms += product(us[1, some, :], wu[1, :, columns])
            ib[:, columns] = terms.astype(BF)

        @over
        def _(columns):
            terms = transposed_left(hot, ib[:, columns])
            terms += product(sg[tokens, :], shared_in[:, columns])
            for e in range(4):
                acc[zi * 4 + e, :, columns] = terms[e * rows : (e + 1) * rows].astype(BF)

        from_gates = gate_back[some, :]
        lane = lax.broadcasted_iota(jnp.int32, from_gates.shape, 1)
        terms = transposed_left(hot, jnp.where(lane == mine, from_gates, 0.0).astype(BF))
        for e in range(4):
            acc[zi * 4 + e, :, width:] = terms[e * rows : (e + 1) * rows].astype(BF)

    def gradient(m):
        step = 256
        right = picked_dy if m == 2 else picked
        turned[...] = (scaled[...] if m == 2 else gs[1] if m == 0 else us[1]).T

        @pl.loop(0, width // step)
        def _(n):
            columns = pl.ds(pl.multiple_of(n * step, step), step)
            grad[min(m, 1), :, columns] = product(turned[...], right[:, columns]).astype(BF)

    crossing = cross(at, [grad.at[0, pl.ds(0, part)]], [taken], cross_send, cross_recv)[0]
    stores = [
        pltpu.make_async_copy(
            grad.at[min(j // 2, 1), pl.ds(j % 2 * part, part)], grads[j - 1], store_sem.at[j]
        )
        for j in range(1, 6)
    ]
    for copy in loads[:9]:
        copy.wait()
    for zi in (3, 2, 1, 0):
        work(zi)
        for f in range(2):
            total.to_twin(acc.at[total.held(f, zi, 1)], f, zi)
        total.first(zi)
        if zi == 1:
            total.second(3, "end")
    for copy in loads[9:]:
        copy.wait()
    for m, zi in ((0, 2), (1, 1), (2, 0)):
        if m == 2:
            stores[1].wait()
            stores[2].wait()
        gradient(m)
        if m == 0:
            total.second(3, "middle")
        if m == 0:
            crossing.start()
        for j in (2 * m, 2 * m + 1):
            if j > 0:
                stores[j - 1].start()
        total.second(zi)
    for j in (0, 3, 4):
        stores[j].wait()
    crossing.wait()
    total.finish()


def expert_back(dispatch, gate_back, shared_in, g, u, sg, picked, picked_dy, scaled, weights, cid):
    total, wide = sg.shape
    width = shared_in.shape[1]
    rows, full = total // 16, width + 128
    slots = picked.shape[0]
    hidden = g.shape[2]
    hbm, vmem = pl.BlockSpec(memory_space=pl.ANY), pl.BlockSpec(memory_space=pltpu.VMEM)
    shape = jax.ShapeDtypeStruct
    return pl.pallas_call(
        expert_scatter_kernel,
        out_shape=[
            shape((rows, full), F32),
            *[shape((hidden // 2, width), BF)] * 6,
        ],
        in_specs=[vmem] * 3 + [hbm] * 12,
        out_specs=[vmem] + [hbm] * 6,
        scratch_shapes=[
            pltpu.VMEM((2, hidden, width), BF),
            pltpu.VMEM((2, hidden, width), BF),
            pltpu.VMEM((2, slots, hidden), BF),
            pltpu.VMEM((2, slots, hidden), BF),
            pltpu.VMEM((total, wide), BF),
            pltpu.VMEM((slots, width), BF),
            pltpu.VMEM((slots, width), BF),
            pltpu.VMEM((slots, hidden), BF),
            pltpu.VMEM((slots // 4, width), BF),
            pltpu.VMEM((2, hidden, width), BF),
            pltpu.VMEM((hidden, slots), BF),
            *scatter_buffers(rows, full, 16),
            pltpu.SemaphoreType.DMA((12,)),
            pltpu.SemaphoreType.DMA((6,)),
            pltpu.SemaphoreType.DMA((1,)),
            pltpu.SemaphoreType.DMA((1,)),
        ],
        compiler_params=pltpu.CompilerParams(
            collective_id=cid, has_side_effects=True, vmem_limit_bytes=63 * 1024 * 1024
        ),
    )(dispatch, gate_back, shared_in, g, u, sg, picked, picked_dy, scaled, *weights)


def mixed_kernel(*refs):
    refs = list(refs)

    def take(count):
        taken = refs[:count]
        del refs[:count]
        return taken

    w_out, w_qkv, tables, q_ref, k_ref, v_ref, lse_ref, heads_out = take(8)
    in_ref, back_ref, normed_ref, *given = take(5)
    out_ref, normed_back, home_out, *taken = take(5)
    rows_in, do, dk, dv, qkv, out_sum, qkv_sum, staged = take(8)
    buffers = take(6)
    first_sem, in_sem, store_sem, cross_send, cross_recv = take(5)
    at = Place()
    greet(at, False, True)
    total = Scatter(at, *buffers, out_ref)
    acc = buffers[0]
    rows, width = acc.shape[1:]
    length = q_ref.shape[0]
    block = length // 4
    crossing = cross(at, given, taken, cross_send, cross_recv)

    def rows_of(rank):
        return in_ref.at[pl.ds(pl.multiple_of(rank * rows, rows), rows)]

    order = [(f, zi) for f in (1, 0) for zi in (3, 2, 1, 0)]
    firsts = {}
    for f, zi in order:
        m = f * 4 + zi
        total.to_twin(rows_of(at.shard(f * at.dy + at.dc, zi)), f, zi)
        firsts[m] = pltpu.make_async_copy(
            rows_of(at.shard(f * at.dy, zi)), acc.at[m], first_sem.at[m]
        )
        firsts[m].start()
    for copy in crossing:
        copy.start()

    def rows_load(j):
        ref = back_ref if j < 4 else normed_ref
        return pltpu.make_async_copy(
            ref.at[pl.ds(j % 4 * block, block)], rows_in.at[j % 2], in_sem.at[j % 2]
        )

    rows_load(0).start()
    rows_load(1).start()

    def heads_back(j):
        rows_load(j).wait()
        here = pl.ds(j * block, block)
        do[here, :] = transposed_right(rows_in[j % 2], w_out[...]).astype(BF)
        turned = heads_out[here, :].T

        @pl.loop(0, 4)
        def _(n):
            columns = pl.ds(pl.multiple_of(n * (width // 4), width // 4), width // 4)
            terms = product(turned, rows_in[j % 2, :, columns])
            out_sum[:, columns] = terms if j == 0 else out_sum[:, columns] + terms

        rows_load(j + 2).start()

    scale = HDIM ** (-0.5)
    step = 256

    def attend_rows(i):
        seen = (i + 1) * step
        here = pl.ds(i * step, step)
        q, go = q_ref[here, :], do[here, :]
        scores = transposed_right(q, k_ref[0:seen, :]) * scale
        row_at = lax.broadcasted_iota(jnp.int32, scores.shape, 0) + i * step
        col_at = lax.broadcasted_iota(jnp.int32, scores.shape, 1)
        scores = jnp.where(row_at >= col_at, scores, MASKED)
        probs = jnp.exp(scores - lse_ref[here, 0:1])
        weight_back = transposed_right(go, v_ref[0:seen, :])
        inner = jnp.sum(probs * weight_back, axis=-1, keepdims=True)
        score_back = (probs * (weight_back - inner)).astype(BF)
        dv[0:seen, :] += transposed_left(probs.astype(BF), go)
        dk[0:seen, :] += transposed_left(score_back, q) * scale
        qkv[here, 0:HDIM] = turn_rows(product(score_back, k_ref[0:seen, :]) * scale, here)

    def turn_rows(values, here):
        other = pltpu.roll(values, HDIM // 2, 1)
        return (values * tables[0, here, :] + other * tables[1, here, :]).astype(BF)

    def finish_heads():
        for j in range(8):
            here = pl.ds(j * step, step)
            qkv[here, HDIM : 2 * HDIM] = turn_rows(dk[here, :], here)
            qkv[here, 2 * HDIM :] = dv[here, :].astype(BF)

    def normed_store(j):
        return pltpu.make_async_copy(
            staged.at[j % 2], normed_back.at[pl.ds(j * step, step)], store_sem.at[j % 2]
        )

    def normed_rows(j):
        if j >= 2:
            normed_store(j - 2).wait()

        @pl.loop(0, 4)
        def _(n):
            columns = pl.ds(pl.multiple_of(n * (width // 4), width // 4), width // 4)
            staged[j % 2, :, columns] = product(
                qkv[pl.ds(j * step, step), :], w_qkv[:, columns]
            ).astype(BF)

        normed_store(j).start()

    def qkv_rows(j):
        rows_load(4 + j).wait()
        turned = qkv[pl.ds(j * block, block), :].T

        @pl.loop(0, 4)
        def _(n):
            columns = pl.ds(pl.multiple_of(n * (width // 4), width // 4), width // 4)
            terms = product(turned, rows_in[j % 2, :, columns])
            qkv_sum[:, columns] = terms if j == 0 else qkv_sum[:, columns] + terms

        if j < 2:
            rows_load(6 + j).start()

    for zi in (3, 2, 1, 0):
        firsts[4 + zi].wait()
        total.first(zi)
    for j in range(4):
        heads_back(j)
    for m in (3, 2, 1, 0):
        firsts[m].wait()
    total.second(3, "end")
    dk[...] = jnp.zeros_like(dk)
    dv[...] = jnp.zeros_like(dv)
    for i in range(5):
        attend_rows(i)
    total.second(3, "middle")
    total.second(2, "end")
    for i in range(5, 8):
        attend_rows(i)
    finish_heads()
    for j in range(3):
        normed_rows(j)
    total.second(2, "middle")
    total.second(1, "end")
    for j in range(3, 8):
        normed_rows(j)
    total.second(1, "middle")
    for j in range(4):
        qkv_rows(j)
    size = home_out.shape[2]
    for j in range(8):
        columns = slice(j * size, (j + 1) * size)
        home_out[j, : 3 * HDIM, :] = qkv_sum[:, columns].astype(BF)
        home_out[j, 3 * HDIM :, :] = out_sum[:, columns].astype(BF)
    total.second(0)
    for j in (6, 7):
        normed_store(j).wait()
    for copy in crossing:
        copy.wait()
    total.finish()


def mixed_rows(
    w_out, w_qkv, tables, q, k, v, lse, heads_out, mixed_part, attn_back, normed, given, cid
):
    length, width = attn_back.shape
    rows = length // 16
    hbm, vmem = pl.BlockSpec(memory_space=pl.ANY), pl.BlockSpec(memory_space=pltpu.VMEM)
    shape = jax.ShapeDtypeStruct
    return pl.pallas_call(
        mixed_kernel,
        out_shape=[
            shape((rows, width), F32),
            shape((length, width), BF),
            shape((8, 4 * HDIM, width // 8), BF),
            *[shape(a.shape, BF) for a in given],
        ],
        in_specs=[vmem] * 8 + [hbm] * 5,
        out_specs=[vmem, hbm, vmem, hbm, hbm],
        scratch_shapes=[
            pltpu.VMEM((2, length // 4, width), BF),
            pltpu.VMEM((length, HDIM), BF),
            pltpu.VMEM((length, HDIM), F32),
            pltpu.VMEM((length, HDIM), F32),
            pltpu.VMEM((length, 3 * HDIM), BF),
            pltpu.VMEM((HDIM, width), F32),
            pltpu.VMEM((3 * HDIM, width), F32),
            pltpu.VMEM((2, 256, width), BF),
            *scatter_buffers(rows, width),
            pltpu.SemaphoreType.DMA((8,)),
            pltpu.SemaphoreType.DMA((2,)),
            pltpu.SemaphoreType.DMA((2,)),
            pltpu.SemaphoreType.DMA((2,)),
            pltpu.SemaphoreType.DMA((2,)),
        ],
        compiler_params=pltpu.CompilerParams(
            collective_id=cid, has_side_effects=True, vmem_limit_bytes=63 * 1024 * 1024
        ),
    )(w_out, w_qkv, tables, q, k, v, lse, heads_out, mixed_part, attn_back, normed, *given)


def gather_back_kernel(*refs):
    refs = list(refs)

    def take(count):
        taken = refs[:count]
        del refs[:count]
        return taken

    x_ref, disp, shared_out = take(3)
    scaled_ref, act_ref, sg_ref, wd_a, wd_0, wd_1, mix_ref, dy_ref, *given = take(10)
    out_ref, mixed_part, units_grad, *taken = take(5)
    scaled, acts, sg, wd, eb, mixes, dys, staged, turned, turned_acts = take(10)
    send_sem, recv_sem, cross_send, cross_recv, load_sem, store_sem = take(6)
    at = Place()
    greet(at, False, True)
    gather = Gather(at, x_ref, out_ref, send_sem, recv_sem)
    crossing = cross(at, given, taken, cross_send, cross_recv)
    rows, width = x_ref.shape
    slots = eb.shape[0]
    block = 4 * rows
    units = acts.shape[1]
    cut = units_grad.shape[1] // 3
    over = columns_loop(width, 4)

    gather.begin()
    for copy in crossing:
        copy.start()
    pairs = [
        (scaled_ref, scaled),
        (act_ref, acts),
        (wd_a, wd.at[0]),
        (wd_0, wd.at[1, pl.ds(0, wd_0.shape[0])]),
        (wd_1, wd.at[1, pl.ds(wd_0.shape[0], wd_0.shape[0])]),
        (sg_ref, sg),
        (mix_ref, mixes),
        (dy_ref, dys),
    ]
    loads = [pltpu.make_async_copy(a, b, load_sem.at[j]) for j, (a, b) in enumerate(pairs)]
    for copy in loads:
        copy.start()

    def mixed_store(j):
        return pltpu.make_async_copy(
            staged.at[j % 2], mixed_part.at[pl.ds(j * block, block)], store_sem.at[j % 2]
        )

    def mixed_rows_of(j):
        some = pl.ds(j * slots, slots)

        @over
        def _(columns):
            terms = product(scaled[0, some, :], wd[0, :, columns])
            terms += product(scaled[1, some, :], wd[1, :, columns])
            eb[:, columns] = terms.astype(BF)

        if j >= 2:
            mixed_store(j - 2).wait()
        tokens = pl.ds(j * block, block)

        @over
        def _(columns):
            terms = transposed_left(disp[j], eb[:, columns])
            terms += product(acts[tokens, :], shared_out[:, columns])
            staged[j % 2, :, columns] = terms.astype(BF)

        mixed_store(j).start()

    def units_of(first, count):
        size = units_grad.shape[2]

        @pl.loop(first, first + count)
        def _(n):
            columns = pl.ds(pl.multiple_of(n * size, size), size)
            terms = product(turned[...], mixes[:, columns]).astype(BF)
            units_grad[n, 0:cut, :] = terms[:cut]
            units_grad[n, cut : 2 * cut, :] = terms[units : units + cut]
            terms = product(turned_acts[...], dys[:, columns]).astype(BF)
            units_grad[n, 2 * cut :, :] = terms[:cut]

    for copy in loads[:5]:
        copy.wait()
    for zi in range(4):
        mixed_rows_of(zi)
        if zi == 0:
            for copy in loads[5:]:
                copy.wait()
            turned[...] = sg[...].T
            turned_acts[...] = acts[...].T
        units_of(2 * zi, 2)
        gather.step(zi + 1)
    for j in (2, 3):
        mixed_store(j).wait()
    for copy in crossing:
        copy.wait()
    gather.finish()


def gather_back(x, given, dispatch, shared_out, scaled, acts, sg, wd, mix_all, dy_all, cut, cid):
    rows, width = x.shape
    length, units = acts.shape
    slots, hidden = scaled.shape[1:]
    hbm, vmem = pl.BlockSpec(memory_space=pl.ANY), pl.BlockSpec(memory_space=pltpu.VMEM)
    shape = jax.ShapeDtypeStruct
    return pl.pallas_call(
        gather_back_kernel,
        out_shape=[
            shape((length, width), BF),
            shape((length, width), BF),
            shape((8, 3 * cut, width // 8), BF),
            *[shape(a.shape, BF) for a in given],
        ],
        in_specs=[hbm, vmem, vmem] + [hbm] * 10,
        out_specs=[hbm, hbm, vmem, hbm, hbm],
        scratch_shapes=[
            pltpu.VMEM((2, slots, hidden), BF),
            pltpu.VMEM(acts.shape, BF),
            pltpu.VMEM(sg.shape, BF),
            pltpu.VMEM((2, hidden, width), BF),
            pltpu.VMEM((slots // 4, width), BF),
            pltpu.VMEM((length, width), BF),
            pltpu.VMEM((length, width), BF),
            pltpu.VMEM((2, 4 * rows, width), BF),
            pltpu.VMEM((2 * units, length), BF),
            pltpu.VMEM((units, length), BF),
            pltpu.SemaphoreType.DMA((38,)),
            pltpu.SemaphoreType.DMA((30,)),
            pltpu.SemaphoreType.DMA((2,)),
            pltpu.SemaphoreType.DMA((2,)),
            pltpu.SemaphoreType.DMA((8,)),
            pltpu.SemaphoreType.DMA((2,)),
        ],
        compiler_params=pltpu.CompilerParams(
            collective_id=cid, has_side_effects=True, vmem_limit_bytes=60 * 1024 * 1024
        ),
    )(x, dispatch, shared_out, scaled, acts, sg, *wd, mix_all, dy_all, *given)


class Home:
    def __init__(self, at, arrays, outs, mine, got, load_sem, x_send, x_recv, z_send, z_recv):
        self.at, self.outs, self.mine, self.got = at, outs, mine, got
        self.z_send, self.z_recv = z_send, z_recv
        there = (1 - at.x) * 4
        self.loads, self.crossing, self.keep = {}, {}, []
        self.count = len(arrays)
        for m, array in enumerate(arrays):
            for k in range(4):
                spot, j = at.zs[k], m * 4 + k
                self.loads[m, k] = pltpu.make_async_copy(
                    array.at[at.x * 4 + spot], mine[m].at[spot], load_sem.at[m * 5 + k]
                )
                self.crossing[m, k] = remote(
                    array.at[there + spot],
                    got[m].at[spot],
                    x_send.at[j],
                    x_recv.at[j],
                    at.device(ox=at.dx),
                )
            self.keep.append(
                pltpu.make_async_copy(mine[m].at[at.z], outs[m].at[at.z], load_sem.at[m * 5 + 4])
            )

    def start(self):
        for k in (3, 2, 1, 0):
            for m in range(self.count):
                self.loads[m, k].start()
                self.crossing[m, k].start()

    def line(self, k):
        spot = self.at.zs[k]
        for m in range(self.count):
            mine, got = self.mine[m], self.got[m]
            self.loads[m, k].wait()
            self.crossing[m, k].wait_recv()

            @pl.loop(0, mine.shape[1] // 16)
            def _(i):
                span = pl.ds(pl.multiple_of(i * 16, 16), 16)
                both = mine[spot, span, :].astype(F32) + got[spot, span, :].astype(F32)
                mine[spot, span, :] = both.astype(BF)

            (self.copy(m, k) if k else self.keep[m]).start()

    def copy(self, m, k):
        at = self.at
        return remote(
            self.mine[m].at[at.zs[k]],
            self.outs[m].at[at.z],
            self.z_send.at[m * 3 + k - 1],
            self.z_recv.at[m * 4 + at.z],
            at.device(zi=k),
        )

    def finish(self):
        at = self.at
        for m in range(self.count):
            for k in (1, 2, 3):
                remote(
                    self.mine[m].at[at.z],
                    self.outs[m].at[at.zs[k]],
                    self.z_send.at[m * 3 + k - 1],
                    self.z_recv.at[m * 4 + at.zs[k]],
                    at.device(zi=k),
                ).wait_recv()
                self.copy(m, k).wait_send()
            self.keep[m].wait()
        for copy in self.crossing.values():
            copy.wait_send()


class Share:
    def __init__(self, at, ref, out, send_sem, recv_sem):
        self.at, rows = at, ref.shape[0]
        spot = lambda oe: out.at[pl.ds(pl.multiple_of((at.e + oe) * rows, rows), rows)]
        f_dev, s_dev = at.device(oe=at.dy), at.device(oe=at.dc)
        self.ref, self.place = ref, spot(0)
        self.far = remote(ref, spot(0), send_sem.at[0], recv_sem.at[0], f_dev)
        self.near = remote(ref, spot(0), send_sem.at[1], recv_sem.at[1], s_dev)
        self.over = remote(spot(at.dy), spot(at.dy), send_sem.at[2], recv_sem.at[2], s_dev)

    def start(self):
        for copy in (self.far, self.near):
            copy.start()
        keep(self.ref, self.place)

    def forward(self):
        self.far.wait_recv()
        self.over.start()

    def finish(self):
        self.far.wait_send()
        self.near.wait()
        self.over.wait()


def last_scatter_kernel(*refs):
    refs = list(refs)

    def take(count):
        taken = refs[:count]
        del refs[:count]
        return taken

    in_ref, g_ref, u_ref, scaled_ref, picked_ref, dy_ref, mixed_ref, given = take(8)
    halves, home_refs = take(5), take(3)
    out_ref, taken, grad_gate, grad_up, grad_down, mixed_out = take(6)
    home_outs = take(3)
    right, left, other, grad, turned = take(5)
    mine, got = take(3), take(3)
    buffers = take(6)
    first_sem, cross_send, cross_recv, load_sem, store_sem = take(5)
    home_sems, share_sems = take(5), take(2)
    at = Place()
    greet(at, True)
    total = Scatter(at, *buffers, out_ref)
    acc = buffers[0]
    rows, width = acc.shape[1:]
    part = given.shape[0]
    crossing = cross(at, [given], [taken], cross_send, cross_recv)[0]
    home = Home(at, home_refs, home_outs, mine, got, *home_sems)
    sharing = Share(at, mixed_ref, mixed_out, *share_sems)

    def rows_of(rank):
        return in_ref.at[pl.ds(pl.multiple_of(rank * rows, rows), rows)]

    order = [(f, zi) for f in (1, 0) for zi in (3, 2, 1, 0)]
    firsts = {}
    for f, zi in order:
        k = f * 4 + zi
        total.to_twin(rows_of(at.shard(f * at.dy + at.dc, zi)), f, zi)
        firsts[k] = pltpu.make_async_copy(
            rows_of(at.shard(f * at.dy, zi)), acc.at[k], first_sem.at[k]
        )
        firsts[k].start()
    home.start()
    crossing.start()
    pairs = [
        (picked_ref, right.at[0]),
        (dy_ref, right.at[1]),
        (g_ref.at[0], left.at[0]),
        (u_ref.at[0], left.at[1]),
        (scaled_ref.at[0], left.at[2]),
    ]
    pairs += [
        (ref, other.at[j // 2 % 2, pl.ds(j % 2 * part, part)])
        for j, ref in enumerate(halves + [taken])
    ]
    loads = [pltpu.make_async_copy(a, b, load_sem.at[j]) for j, (a, b) in enumerate(pairs)]
    for copy in loads[:9]:
        copy.start()

    def store(m):
        ref = (grad_gate, grad_up, grad_down)[m]
        return pltpu.make_async_copy(grad.at[m % 2], ref, store_sem.at[m])

    def gradient(m, half=None):
        turned[...] = left[m].T
        span = slice(None) if half is None else pl.ds(half * part, part)

        @columns_loop(width, 8)
        def _(columns):
            terms = product(turned[span, :], right[m // 2, :, columns])
            grad[m % 2, span, columns] = terms + other[m % 2, span, columns].astype(F32)

        if half != 0:
            store(m).start()

    for zi in (3, 2, 1, 0):
        firsts[4 + zi].wait()
        total.first(zi)
    sharing.start()
    for copy in loads[:9]:
        copy.wait()
    for m in (3, 2, 1, 0):
        firsts[m].wait()
    gradient(0)
    loads[9].start()
    total.second(3, "end")
    home.line(3)
    total.second(3, "middle")
    total.second(2, "end")
    home.line(2)
    gradient(1)
    total.second(2, "middle")
    total.second(1, "end")
    home.line(1)
    total.second(1, "middle")
    home.line(0)
    sharing.forward()
    loads[9].wait()
    store(0).wait()
    gradient(2, 0)
    total.second(0)
    crossing.wait_recv()
    loads[10].start()
    loads[10].wait()
    gradient(2, 1)
    home.finish()
    sharing.finish()
    store(1).wait()
    store(2).wait()
    crossing.wait_send()
    total.finish()


def last_rows(x, g, u, scaled, picked, picked_dy, home, mixed_own, given, halves, cid):
    rows, width = x.shape[0] // 16, x.shape[1]
    slots, hidden = g.shape[1:]
    hbm, vmem = pl.BlockSpec(memory_space=pl.ANY), pl.BlockSpec(memory_space=pltpu.VMEM)
    shape, sems = jax.ShapeDtypeStruct, lambda n: pltpu.SemaphoreType.DMA((n,))
    return pl.pallas_call(
        last_scatter_kernel,
        out_shape=[
            shape((rows, width), F32),
            shape(given.shape, BF),
            *[shape((hidden, width), F32)] * 3,
            shape((4 * rows, width), BF),
            *[shape((4,) + a.shape[1:], BF) for a in home],
        ],
        in_specs=[hbm] * 16,
        out_specs=[vmem] + [hbm] * 8,
        scratch_shapes=[
            pltpu.VMEM((2, slots, width), BF),
            pltpu.VMEM((3, slots, hidden), BF),
            pltpu.VMEM((2, hidden, width), BF),
            pltpu.VMEM((2, hidden, width), F32),
            pltpu.VMEM((hidden, slots), BF),
            *[pltpu.VMEM((4,) + a.shape[1:], BF) for a in home] * 2,
            *scatter_buffers(rows, width),
            sems(8),
            sems(1),
            sems(1),
            sems(11),
            sems(3),
            sems(15),
            sems(12),
            sems(12),
            sems(9),
            sems(12),
            sems(3),
            sems(3),
        ],
        compiler_params=pltpu.CompilerParams(
            collective_id=cid, has_side_effects=True, vmem_limit_bytes=62 * 1024 * 1024
        ),
    )(x, g, u, scaled, picked, picked_dy, mixed_own, given, *halves, *home)


def end_kernel(tokens_ref, gain_ref, small_ref, out_ref, gain_out, small_out, *scratch):
    gain_got, gain_sum, gain_all, small_all = scratch[:4]
    share_sems = scratch[4:6]
    gain_send, gain_recv, sum_send, sum_recv, small_send, small_recv = scratch[6:]
    at = Place()
    barrier = pltpu.get_barrier_semaphore()
    blocks = [(at.device(ox=ox, zi=k), m * 4 + k) for m, ox in enumerate((0, at.dx)) for k in range(4)]
    group = [at.device(oe=oe) for oe in (at.dy, at.dc, at.dy + at.dc)]
    for peer in [device for device, j in blocks[1:]] + group:
        pl.semaphore_signal(barrier, inc=1, device_id=peer, device_id_type=MESH)
    pl.semaphore_wait(barrier, 10)
    sharing = Share(at, tokens_ref, out_ref, *share_sems)
    own = at.x * 4 + at.z
    copies = []
    for device, j in blocks[1:]:
        copy = remote(
            gain_ref.at[device[0] * 4 + device[1]],
            gain_got.at[own],
            gain_send.at[j],
            gain_recv.at[own],
            device,
        )
        copy.start()
        copies.append(copy)
    for j, device in enumerate(group):
        copy = remote(small_ref, small_all.at[j], small_send.at[j], small_recv.at[j], device)
        copy.start()
        copies.append(copy)
    sharing.start()
    gain = gain_ref[own]
    for device, j in blocks[1:]:
        there = device[0] * 4 + device[1]
        remote(
            gain_ref.at[0], gain_got.at[there], gain_send.at[j], gain_recv.at[there], device
        ).wait_recv()
        gain = gain + gain_got[there]
    gain_sum[...] = gain
    for j, device in enumerate(group):
        copy = remote(gain_sum, gain_all.at[j], sum_send.at[j], sum_recv.at[j], device)
        copy.start()
        copies.append(copy)
    small = small_ref[...]
    for j in range(3):
        copies[7 + j].wait_recv()
        copies[10 + j].wait_recv()
        small = small + small_all[j]
        gain = gain + gain_all[j]
    gain_out[...] = gain
    small_out[...] = small
    sharing.forward()
    sharing.finish()
    for copy in copies:
        copy.wait_send()


def end(tokens_own, gain_part, small, cid):
    rows, width = tokens_own.shape
    vmem, hbm = pl.BlockSpec(memory_space=pltpu.VMEM), pl.BlockSpec(memory_space=pl.ANY)
    shape, sems = jax.ShapeDtypeStruct, lambda n: pltpu.SemaphoreType.DMA((n,))
    return pl.pallas_call(
        end_kernel,
        out_shape=[
            shape((4 * rows, width), tokens_own.dtype),
            shape(gain_part.shape[1:], F32),
            shape(small.shape, F32),
        ],
        in_specs=[hbm, vmem, vmem],
        out_specs=[hbm, vmem, vmem],
        scratch_shapes=[
            pltpu.VMEM(gain_part.shape, F32),
            pltpu.VMEM(gain_part.shape[1:], F32),
            pltpu.VMEM((3,) + gain_part.shape[1:], F32),
            pltpu.VMEM((3,) + small.shape, F32),
            sems(3),
            sems(3),
            sems(8),
            sems(8),
            sems(3),
            sems(3),
            sems(3),
            sems(3),
        ],
        compiler_params=pltpu.CompilerParams(collective_id=cid, has_side_effects=True),
    )(tokens_own, gain_part, small)


def front_kernel(scale, *refs):
    refs = list(refs)

    def take(count):
        taken = refs[:count]
        del refs[:count]
        return taken

    dy_ref, tokens_ref, units, given, gain, w_qkv, w_out_blocks, tables = take(8)
    dy_out, units_out, taken, normed_out, part_out, q_out, k_out, v_out, heads_out, lse_out = take(10)
    w_out, w_qkv_turned = take(2)
    rows_in, normed, staged = take(3)
    send_sem, recv_sem, swap_send, swap_recv = take(4)
    cross_send, cross_recv, in_sem, normed_sem, part_sem = take(5)
    at = Place()
    greet(at, True)
    gather = Gather(at, dy_ref, dy_out, send_sem, recv_sem, True)
    swap_in = Exchange(at, [units], [units_out], swap_send, swap_recv)
    crossing = cross(at, [given], [taken], cross_send, cross_recv, (taken.shape[0],))[0]
    length, width = tokens_ref.shape
    block = length // 4
    step = 256
    over = columns_loop(width, 4)

    def rows_load(j):
        return pltpu.make_async_copy(
            tokens_ref.at[pl.ds(j * block, block)], rows_in.at[j % 2], in_sem.at[j % 2]
        )

    def normed_store(j):
        return pltpu.make_async_copy(
            normed.at[j % 2], normed_out.at[pl.ds(j * block, block)], normed_sem.at[j % 2]
        )

    def part_store(i):
        return pltpu.make_async_copy(
            staged.at[i % 2], part_out.at[pl.ds(i * step, step)], part_sem.at[i % 2]
        )

    def turn_rows(values, here):
        other = pltpu.roll(values, HDIM // 2, 1)
        return (values * tables[0, here, :] - other * tables[1, here, :]).astype(BF)

    def project(j):
        rows_load(j).wait()
        if j >= 2:
            normed_store(j - 2).wait()

        @pl.loop(0, block // 64)
        def _(n):
            span = pl.ds(pl.multiple_of(n * 64, 64), 64)
            values = rows_in[j % 2, span, :].astype(F32)
            size = jnp.mean(values * values, axis=-1, keepdims=True)
            normed[j % 2, span, :] = (values * lax.rsqrt(size + EPSILON) * gain[0:1, :]).astype(BF)

        normed_store(j).start()
        if j < 2:
            rows_load(j + 2).start()
        here = pl.ds(j * block, block)
        qkv = product(normed[j % 2], w_qkv[...])
        q_out[here, :] = turn_rows(qkv[:, :HDIM], here)
        k_out[here, :] = turn_rows(qkv[:, HDIM : 2 * HDIM], here)
        v_out[here, :] = qkv[:, 2 * HDIM :].astype(BF)

    def attend_rows(i):
        seen = (i + 1) * step
        here = pl.ds(i * step, step)
        scores = transposed_right(q_out[here, :], k_out[0:seen, :]) * scale
        row_at = lax.broadcasted_iota(jnp.int32, scores.shape, 0) + i * step
        col_at = lax.broadcasted_iota(jnp.int32, scores.shape, 1)
        scores = jnp.where(row_at >= col_at, scores, MASKED)
        top = jnp.max(scores, axis=-1, keepdims=True)
        powers = jnp.exp(scores - top)
        lse = top + jnp.log(jnp.sum(powers, axis=-1, keepdims=True))
        probs = jnp.exp(scores - lse).astype(BF)
        heads_out[here, :] = product(probs, v_out[0:seen, :]).astype(BF)
        lse_out[here, :] = jnp.broadcast_to(lse, (step, HDIM))
        if i >= 2:
            part_store(i - 2).wait()

        @over
        def _(columns):
            staged[i % 2, :, columns] = product(heads_out[here, :], w_out[:, columns]).astype(BF)

        part_store(i).start()

    gather.begin()
    for zi in (1, 2, 3):
        swap_in.along(zi)
    swap_in.start()
    crossing.start()
    rows_load(0).start()
    rows_load(1).start()
    size = w_out_blocks.shape[2]
    for d in range(8):
        w_out[:, d * size : (d + 1) * size] = w_out_blocks[d]
    w_qkv_turned[...] = w_qkv[...].T
    project(0)
    project(1)
    attend_rows(0)
    gather.step(1)
    project(2)
    attend_rows(1)
    attend_rows(2)
    gather.step(2)
    swap_in.forward(1)
    project(3)
    attend_rows(3)
    attend_rows(4)
    gather.step(3)
    swap_in.forward(2)
    attend_rows(5)
    attend_rows(6)
    attend_rows(7)
    gather.step(4)
    swap_in.forward(3)
    for j in (2, 3):
        normed_store(j).wait()
    for i in (6, 7):
        part_store(i).wait()
    swap_in.finish()
    crossing.wait()
    gather.finish()


def front(dy, tokens_all, units, given, gain, w_qkv, w_out, tables, cid):
    length, width = tokens_all.shape
    hbm, vmem = pl.BlockSpec(memory_space=pl.ANY), pl.BlockSpec(memory_space=pltpu.VMEM)
    shape, sems = jax.ShapeDtypeStruct, lambda n: pltpu.SemaphoreType.DMA((n,))
    return pl.pallas_call(
        functools.partial(front_kernel, HDIM ** (-0.5)),
        out_shape=[
            shape((length, width), BF),
            shape((8,) + units.shape[1:], BF),
            half_of(given),
            shape((length, width), BF),
            shape((length, width), BF),
            *[shape((length, HDIM), BF)] * 4,
            shape((length, HDIM), F32),
            shape((HDIM, width), BF),
            shape((3 * HDIM, width), BF),
        ],
        in_specs=[hbm] * 4 + [vmem] * 4,
        out_specs=[hbm] * 5 + [vmem] * 7,
        scratch_shapes=[
            pltpu.VMEM((2, length // 4, width), BF),
            pltpu.VMEM((2, length // 4, width), BF),
            pltpu.VMEM((2, 256, width), BF),
            sems(38),
            sems(30),
            sems(7),
            sems(8),
            sems(1),
            sems(1),
            sems(2),
            sems(2),
            sems(2),
        ],
        compiler_params=pltpu.CompilerParams(
            collective_id=cid, has_side_effects=True, vmem_limit_bytes=60 * 1024 * 1024
        ),
    )(dy, tokens_all, units, given, gain, w_qkv, w_out, tables)


def by_four(matrix):
    rows, columns = matrix.shape
    return matrix.reshape(rows, 4, columns // 4).transpose(1, 0, 2)


def turn_tables(length):
    inverse = 10000.0 ** (-np.arange(HDIM // 2).astype(np.float64) * 2.0 / HDIM)
    angles = np.arange(length).astype(np.float64)[:, None] * inverse[None, :]
    return np.cos(angles).astype(np.float32), np.sin(angles).astype(np.float32)


def fast_body(
    tokens,
    routes,
    norm_attn,
    w_query,
    w_key,
    w_value,
    w_out,
    norm_mix,
    w_router,
    shared_gate,
    shared_up,
    shared_down,
    expert_gate,
    expert_up,
    expert_down,
    out_grad,
):
    dp, ctx, exp = lax.axis_index("dp"), lax.axis_index("ctx"), lax.axis_index("exp")
    rows_here, width = tokens.shape[1], tokens.shape[2]
    quarter = rows_here // 4
    length = rows_here * 4
    experts = w_router.shape[1]
    capacity = quarter * TOPK * 4 // (3 * experts)
    groups = length // quarter
    dense = w_query.shape[0]
    cut = shared_gate.shape[1] // 4
    wide = 256
    start = exp * quarter
    tokens_own = lax.dynamic_slice_in_dim(tokens[0], start, quarter, 0)
    dy_own = lax.dynamic_slice_in_dim(out_grad[0], start, quarter, 0)

    route_rows = routes[0].T
    theirs = jnp.arange(4, dtype=jnp.int32)[:, None, None] * 4 + exp
    named = jnp.any(route_rows[None] == theirs, axis=1).astype(BF).reshape(4, 2, dense)
    little = jnp.concatenate([w_router.T, norm_attn[None], norm_mix[None]], axis=0)
    little = jnp.concatenate([jnp.broadcast_to(little[None], (4,) + little.shape), named], axis=1)
    few = -(-little.shape[1] // 16) * 16
    little = jnp.pad(little, ((0, 0), (0, few - little.shape[1]), (0, 0)))
    sent_head = jnp.concatenate([by_four(w_query), by_four(w_key), by_four(w_value)], axis=2)
    sent_out = w_out.reshape(4, HDIM, dense)
    sent_units = jnp.stack([shared_gate.T, shared_up.T, shared_down], axis=0)
    sent_units = sent_units.reshape(3, 4, cut, dense).transpose(1, 0, 2, 3).reshape(4, 3 * cut, dense)
    own_gate, own_up, own_down = expert_gate[0].T, expert_up[0].T, expert_down[0]
    part = own_gate.shape[0] // 2
    tokens_all, early, early_out, early_little, gate_0 = all_rows(
        tokens[0], True, 1, (sent_head, sent_out, little), (own_gate,), (0,)
    )
    w_qkv = early.reshape(width, 3 * HDIM)
    early_little = early_little.transpose(1, 0, 2)
    router_rows = early_little[:experts].reshape(experts, width)
    attention_gain = early_little[experts].reshape(width).astype(F32)
    mixer_gain = early_little[experts + 1].reshape(width).astype(F32)
    hits = early_little[experts + 2 : experts + 4].transpose(1, 0, 2).reshape(2, length)
    hits = lax.dynamic_index_in_dim(hits, dp, 0, False).astype(F32).reshape(groups, quarter)

    cosine, sine = turn_tables(length)
    tables = np.stack(
        [np.concatenate([cosine, cosine], axis=1), np.concatenate([sine, -sine], axis=1)]
    )
    dy_all, late, gate_1, normed, attn_part, query, key, value, heads_out, lse, w_out_head, w_qkv_turned = front(
        out_grad[0],
        tokens_all,
        sent_units,
        own_gate,
        jnp.broadcast_to(attention_gain[None], (8, width)),
        w_qkv,
        early_out,
        tables,
        2,
    )
    attn, up_0, up_1 = own_rows(attn_part, 3, (own_up, own_up), (0, part))
    middle = tokens_own.astype(F32) + attn
    normed_own = rms_scale(middle, mixer_gain).astype(BF)

    mine = ctx * 4 + exp
    place = jnp.cumsum(hits, axis=1) - 1.0
    first = (jnp.arange(groups) % 4 * capacity).astype(F32)[:, None]
    place = jnp.where(hits > 0.5, place + first, -1.0).reshape(4, 1, 4 * quarter)
    blocks = place == jnp.arange(4 * capacity).astype(F32)[None, :, None]
    blocks = blocks.astype(BF)
    router_wide = jnp.pad(router_rows, ((0, HDIM - experts), (0, 0)))
    (
        mix_all,
        picked,
        picked_dy,
        scaled,
        g_back,
        u_back,
        gate_back,
        shared_act,
        shared_gu_back,
        down_0,
        down_1,
        shared_in,
        shared_out,
    ) = expert_rows(
        normed_own,
        dy_all,
        blocks,
        router_wide,
        experts,
        late,
        wide,
        (own_gate, own_up, own_down, gate_0, gate_1, up_0, up_1),
        (own_down, own_down),
        4,
    )
    other_down = (down_0, down_1)

    mix_back, gate_0, gate_1, up_0, up_1, down_0, down_1 = expert_back(
        blocks,
        gate_back,
        shared_in,
        g_back,
        u_back,
        shared_gu_back,
        picked,
        picked_dy,
        scaled,
        (own_gate, own_up, gate_0, gate_1, up_0, up_1),
        5,
    )
    gate_back_own = mix_back[:, width : width + experts]
    mix_back = mix_back[:, :width]

    router_own = jax.nn.softmax(transposed_right(normed_own, router_rows), axis=-1)
    logit_back = (
        router_own * (gate_back_own - jnp.sum(router_own * gate_back_own, axis=-1, keepdims=True))
    ).astype(BF)
    router_part = transposed_left(logit_back, normed_own)

    mix_back = mix_back + product(logit_back, router_rows)
    _, norm_mix_back = jax.vjp(rms_scale, middle, mixer_gain)
    middle_norm_back, gain_mix_part = norm_mix_back(mix_back)
    middle_back = dy_own.astype(F32) + middle_norm_back
    attn_back = middle_back.astype(BF)
    attn_back_all, mixed_part, units_part, gate_1, up_0 = gather_back(
        attn_back,
        (gate_1, up_0),
        blocks,
        shared_out,
        scaled,
        shared_act,
        shared_gu_back,
        (own_down, *other_down),
        mix_all,
        dy_all,
        cut,
        7,
    )
    mixed_sum, normed_part, head_part, up_1, down_0 = mixed_rows(
        w_out_head,
        w_qkv_turned,
        tables,
        query,
        key,
        value,
        lse,
        heads_out,
        mixed_part,
        attn_back_all,
        normed,
        (up_1, down_0),
        9,
    )
    mixed_own = (middle + mixed_sum).astype(BF)
    small_part = jnp.concatenate([gain_mix_part[None], router_part], axis=0).astype(BF)
    small_rows = -(-(experts + 1) // 16) * 16
    small_part = jnp.pad(small_part, ((0, small_rows - experts - 1), (0, 0)))
    small_part = small_part.reshape(small_rows, 8, dense).transpose(1, 0, 2)
    normed_back, _, gate_grad, up_grad, down_grad, mixed, head_grad, units_grad, small = last_rows(
        normed_part,
        g_back,
        u_back,
        scaled,
        picked,
        picked_dy,
        (head_part, units_part, small_part),
        mixed_own,
        down_1,
        (gate_0, gate_1, up_0, up_1, down_0),
        8,
    )
    head_grad, units_grad = head_grad.astype(F32), units_grad.astype(F32)
    small_part = jnp.sum(small.astype(F32), axis=0)
    _, norm_attn_back = jax.vjp(rms_scale, tokens_own.astype(F32), attention_gain)
    input_norm_back, gain_attn_part = norm_attn_back(normed_back)
    tokens_back_own = (middle_back + input_norm_back).astype(BF)

    gain_part = jnp.pad(gain_attn_part.reshape(8, 1, dense), ((0, 0), (0, 7), (0, 0)))
    tokens_back, gain_attn, small = end(tokens_back_own, gain_part, small_part, 6)

    def columns_of(parts):
        return parts.transpose(2, 0, 1).reshape(dense, -1)

    def rows_of(parts):
        return parts.reshape(-1, dense)

    return (
        mixed[None],
        tokens_back[None],
        gain_attn[0],
        columns_of(head_grad[:, :HDIM]),
        columns_of(head_grad[:, HDIM : 2 * HDIM]),
        columns_of(head_grad[:, 2 * HDIM : 3 * HDIM]),
        rows_of(head_grad[:, 3 * HDIM :]),
        small[0],
        small[1 : experts + 1].T,
        rows_of(units_grad[:, :cut]).T,
        rows_of(units_grad[:, cut : 2 * cut]).T,
        rows_of(units_grad[:, 2 * cut :]),
        gate_grad.T[None],
        up_grad.T[None],
        down_grad[None],
    )


def solution(mesh):
    sizes = dict(mesh.shape)

    def chosen(*args):
        heads = args[3].shape[1] * sizes["exp"] // HDIM
        one_head_each = heads == sizes["ctx"] * sizes["exp"]
        built_for = (sizes["dp"], sizes["ctx"], sizes["exp"]) == (2, 4, 4)
        return fast_body(*args) if one_head_each and built_for else body(*args)

    in_specs = (
        P("dp", "ctx", None),
        P("dp", "ctx", None),
        P(("dp", "ctx")),
        P(("dp", "ctx"), "exp"),
        P(("dp", "ctx"), "exp"),
        P(("dp", "ctx"), "exp"),
        P("exp", ("dp", "ctx")),
        P(("dp", "ctx")),
        P(("dp", "ctx"), None),
        P(("dp", "ctx"), "exp"),
        P(("dp", "ctx"), "exp"),
        P("exp", ("dp", "ctx")),
        P(("ctx", "exp"), None, "dp"),
        P(("ctx", "exp"), None, "dp"),
        P(("ctx", "exp"), "dp", None),
        P("dp", "ctx", None),
    )
    out_specs = (
        P("dp", "ctx", None),
        P("dp", "ctx", None),
        P(("dp", "ctx")),
        P(("dp", "ctx"), "exp"),
        P(("dp", "ctx"), "exp"),
        P(("dp", "ctx"), "exp"),
        P("exp", ("dp", "ctx")),
        P(("dp", "ctx")),
        P(("dp", "ctx"), None),
        P(("dp", "ctx"), "exp"),
        P(("dp", "ctx"), "exp"),
        P("exp", ("dp", "ctx")),
        P(("ctx", "exp"), None, "dp"),
        P(("ctx", "exp"), None, "dp"),
        P(("ctx", "exp"), "dp", None),
    )
    return jax.shard_map(chosen, mesh=mesh, in_specs=in_specs, out_specs=out_specs, check_vma=False)
```

```python
import functools

import jax
import jax.numpy as jnp
import numpy as np
from jax import lax
from jax.experimental import pallas as pl
from jax.experimental.pallas import tpu as pltpu
from jax.sharding import PartitionSpec as P

HDIM = 128
TOPK = 6


EPSILON = 1e-06
MASKED = -1e30
HIGHEST = lax.Precision.HIGHEST


def rms_scale(values, gain_row):
    return (
        values * lax.rsqrt(jnp.mean(values * values, axis=-1, keepdims=True) + EPSILON) * gain_row
    )


def rope_tables(positions, rope_width):
    inverse = 10000.0 ** (-jnp.arange(rope_width // 2).astype(jnp.float32) * 2.0 / rope_width)
    angles = positions.astype(jnp.float32)[:, None] * inverse[None, :]
    return (jnp.cos(angles), jnp.sin(angles))


def rotate(values, cosine, sine_table):
    half_size = values.shape[-1] // 2
    first_half = values[..., :half_size]
    second = values[..., half_size:]
    cosine = cosine[:, None, :]
    sine_table = sine_table[:, None, :]
    return jnp.concatenate(
        [first_half * cosine - second * sine_table, second * cosine + first_half * sine_table],
        axis=-1,
    )


def silu_mix(gate_rows, up_rows):
    return jax.nn.silu(gate_rows) * up_rows


def product(left_side, right_side):
    return jnp.dot(left_side, right_side, preferred_element_type=jnp.float32)


def transposed_left(left_side, right_side):
    return lax.dot_general(
        left_side, right_side, (((0,), (0,)), ((), ())), preferred_element_type=jnp.float32
    )


def transposed_right(left_side, right_side):
    return lax.dot_general(
        left_side, right_side, (((1,), (1,)), ((), ())), preferred_element_type=jnp.float32
    )


def place_rows(part, start_row, total_rows):
    blank = jnp.zeros((total_rows, part.shape[1]), jnp.float32)
    return lax.dynamic_update_slice_in_dim(blank, part, start_row, 0)


def to_owners(buffer):
    copies = lax.axis_size("dp")
    widened = jnp.broadcast_to(buffer[None], (copies,) + buffer.shape)
    widened = widened.reshape((copies * buffer.shape[0],) + buffer.shape[1:])
    return lax.all_to_all(widened, ("dp", "ctx", "exp"), split_axis=0, concat_axis=0, tiled=True)


def values_home(partial_value):
    returned = lax.all_to_all(
        partial_value, ("dp", "ctx", "exp"), split_axis=0, concat_axis=0, tiled=True
    )
    grouped = returned.reshape((lax.axis_size("dp"), -1) + returned.shape[1:])
    return jnp.sum(grouped.astype(jnp.float32), axis=0).astype(jnp.bfloat16)


def grads_home(partial_value):
    returned = lax.all_to_all(
        partial_value.astype(jnp.bfloat16),
        ("dp", "ctx", "exp"),
        split_axis=0,
        concat_axis=0,
        tiled=True,
    ).astype(partial_value.dtype)
    grouped = returned.reshape((lax.axis_size("dp"), -1) + returned.shape[1:])
    return jnp.sum(grouped, axis=0)


def body(
    tokens,
    routes,
    norm_attn,
    w_query,
    w_key,
    w_value,
    w_out,
    norm_mix,
    w_router,
    shared_gate,
    shared_up,
    shared_down,
    expert_gate,
    expert_up,
    expert_down,
    out_grad,
):
    gathered = (
        lax.all_gather(norm_attn, ("dp", "ctx"), axis=0, tiled=True),
        lax.all_gather(w_query, ("dp", "ctx"), axis=0, tiled=True),
        lax.all_gather(w_key, ("dp", "ctx"), axis=0, tiled=True),
        lax.all_gather(w_value, ("dp", "ctx"), axis=0, tiled=True),
        lax.all_gather(w_out, ("dp", "ctx"), axis=1, tiled=True),
        lax.all_gather(norm_mix, ("dp", "ctx"), axis=0, tiled=True),
        lax.all_gather(w_router, ("dp", "ctx"), axis=0, tiled=True),
        lax.all_gather(shared_gate, ("dp", "ctx"), axis=0, tiled=True),
        lax.all_gather(shared_up, ("dp", "ctx"), axis=0, tiled=True),
        lax.all_gather(shared_down, ("dp", "ctx"), axis=1, tiled=True),
    )
    (
        attention_gain,
        query_matrix,
        key_matrix,
        value_matrix,
        output_matrix,
        mixer_gain,
        router_matrix,
        shared_gate_matrix,
        shared_up_matrix,
        shared_down_matrix,
    ) = gathered
    rows_here = tokens.shape[1]
    model_width = tokens.shape[2]
    heads_here = query_matrix.shape[1] // HDIM
    quarter = rows_here // lax.axis_size("exp")
    start_row = lax.axis_index("exp") * quarter
    layer_input = tokens[0].astype(jnp.float32)
    grad_rows = out_grad[0]
    grad_float = grad_rows.astype(jnp.float32)
    seq_length = rows_here * lax.axis_size("ctx")
    positions = lax.axis_index("ctx") * rows_here + jnp.arange(rows_here, dtype=jnp.int32)
    cosine, sine_table = rope_tables(positions, HDIM)
    visible = positions[:, None] >= jnp.arange(seq_length, dtype=jnp.int32)[None, :]
    scale = HDIM ** (-0.5)
    head_shape = (rows_here, heads_here, HDIM)
    normed = rms_scale(layer_input, attention_gain).astype(jnp.bfloat16)
    query_rot = rotate(
        product(normed, query_matrix).reshape(head_shape), cosine, sine_table
    ).astype(jnp.bfloat16)
    key_rot = (
        rotate(product(normed, key_matrix).reshape(head_shape), cosine, sine_table)
        .astype(jnp.bfloat16)
        .reshape(rows_here, -1)
    )
    value_low = product(normed, value_matrix).astype(jnp.bfloat16)
    key_all, value_all = (
        lax.all_gather(key_rot, "ctx", axis=0, tiled=True),
        lax.all_gather(value_low, "ctx", axis=0, tiled=True),
    )
    key_heads = key_all.reshape(seq_length, heads_here, HDIM)
    value_heads = value_all.reshape(seq_length, heads_here, HDIM)

    def attention_scores():
        scores = (
            jnp.einsum("qhd,khd->hqk", query_rot, key_heads, preferred_element_type=jnp.float32)
            * scale
        )
        return jnp.where(visible[None], scores, MASKED)

    scores = attention_scores()
    largest = jnp.max(scores, axis=-1, keepdims=True)
    log_total = largest + jnp.log(jnp.sum(jnp.exp(scores - largest), axis=-1, keepdims=True))
    weights_low = jnp.exp(scores - log_total).astype(jnp.bfloat16)
    heads_out = (
        jnp.einsum("hqk,khd->qhd", weights_low, value_heads, preferred_element_type=jnp.float32)
        .reshape(rows_here, -1)
        .astype(jnp.bfloat16)
    )
    attn_total = lax.psum(product(heads_out, output_matrix), "exp")
    middle = layer_input + attn_total
    normed_mix = rms_scale(middle, mixer_gain).astype(jnp.bfloat16)
    normed_quarter = lax.dynamic_slice_in_dim(normed_mix, start_row, quarter, 0)
    route_quarter = lax.dynamic_slice_in_dim(routes[0], start_row, quarter, 0)
    grad_quarter = lax.dynamic_slice_in_dim(grad_rows, start_row, quarter, 0)
    logits = product(normed_quarter, router_matrix)
    probabilities = jax.nn.softmax(logits, axis=-1)
    owners = lax.axis_size(("ctx", "exp"))
    local_experts = expert_gate.shape[0]
    experts = local_experts * owners
    capacity = max(quarter * TOPK * 4 // (3 * experts), 2)
    expert_choice_index = jnp.arange(experts, dtype=jnp.int32)
    chosen = (route_quarter[:, :, None] == expert_choice_index[None, None, :]).astype(jnp.float32)
    gates = jnp.sum(chosen * probabilities[:, None, :], axis=-1)
    route_flat = route_quarter.reshape(-1)
    expert_hits = (route_flat[:, None] == expert_choice_index[None, :]).astype(jnp.int32)
    slot_index = jnp.sum(jnp.cumsum(expert_hits, axis=0) * expert_hits, axis=1) - 1
    slot_place = route_flat * capacity + slot_index
    matches = (
        jnp.arange(experts * capacity, dtype=jnp.int32)[:, None] == slot_place[None, :]
    ).astype(jnp.float32)
    dispatch = jnp.sum(matches.reshape(experts * capacity, quarter, TOPK), axis=2).astype(
        jnp.bfloat16
    )
    slot_gates = jnp.dot(matches, gates.reshape(-1), precision=HIGHEST)
    buffer_shape = (owners, local_experts, capacity, model_width)
    outgoing = product(dispatch, normed_quarter).astype(jnp.bfloat16).reshape(buffer_shape)
    arrived = to_owners(outgoing)
    gate_hidden = jnp.einsum(
        "sicd,idf->sicf", arrived, expert_gate, preferred_element_type=jnp.float32
    )
    up_hidden = jnp.einsum("sicd,idf->sicf", arrived, expert_up, preferred_element_type=jnp.float32)
    expert_act = silu_mix(gate_hidden, up_hidden).astype(jnp.bfloat16)
    partial_value = jnp.einsum(
        "sicf,ifd->sicd", expert_act, expert_down, preferred_element_type=jnp.float32
    ).astype(jnp.bfloat16)
    expert_values = values_home(partial_value).reshape(experts * capacity, model_width)
    route_values = expert_values[slot_place].astype(jnp.float32).reshape(quarter, TOPK, model_width)
    combined = jnp.sum(route_values * gates[:, :, None], axis=1)
    shared_gate_rows = product(normed_mix, shared_gate_matrix)
    shared_up_rows = product(normed_mix, shared_up_matrix)
    shared_act = silu_mix(shared_gate_rows, shared_up_rows).astype(jnp.bfloat16)
    branch_part = product(shared_act, shared_down_matrix) + place_rows(
        combined, start_row, rows_here
    )
    result = middle + lax.psum(branch_part.astype(jnp.bfloat16), "exp").astype(jnp.float32)
    grad_slots = (
        (product(dispatch, grad_quarter) * slot_gates[:, None])
        .astype(jnp.bfloat16)
        .reshape(buffer_shape)
    )
    grad_arrived = to_owners(grad_slots)
    act_grad = jnp.einsum(
        "sicd,ifd->sicf", grad_arrived, expert_down, preferred_element_type=jnp.float32
    )
    down_grad = jnp.einsum(
        "sicf,sicd->ifd", expert_act, grad_arrived, preferred_element_type=jnp.float32
    )
    _, mix_back = jax.vjp(silu_mix, gate_hidden, up_hidden)
    gate_back, up_back = mix_back(act_grad)
    gate_back = gate_back.astype(jnp.bfloat16)
    up_back = up_back.astype(jnp.bfloat16)
    gate_grad = jnp.einsum("sicd,sicf->idf", arrived, gate_back, preferred_element_type=jnp.float32)
    up_grad = jnp.einsum("sicd,sicf->idf", arrived, up_back, preferred_element_type=jnp.float32)
    input_back = jnp.einsum(
        "sicf,idf->sicd", gate_back, expert_gate, preferred_element_type=jnp.float32
    ) + jnp.einsum("sicf,idf->sicd", up_back, expert_up, preferred_element_type=jnp.float32)
    rows_back = grads_home(input_back).reshape(experts * capacity, model_width)
    moe_back = jnp.sum(rows_back[slot_place].reshape(quarter, TOPK, model_width), axis=1)
    gate_route_back = jnp.sum(route_values * grad_quarter.astype(jnp.float32)[:, None, :], axis=-1)
    prob_back = jnp.sum(chosen * gate_route_back[:, :, None], axis=1)
    _, soft_back = jax.vjp(lambda values: jax.nn.softmax(values, axis=-1), logits)
    logit_back = soft_back(prob_back)[0].astype(jnp.bfloat16)
    router_term = transposed_left(normed_quarter, logit_back)
    shared_back = transposed_right(grad_rows, shared_down_matrix)
    _, shared_mix_back = jax.vjp(silu_mix, shared_gate_rows, shared_up_rows)
    sgate_back, sup_back = shared_mix_back(shared_back)
    sgate_back = sgate_back.astype(jnp.bfloat16)
    sup_back = sup_back.astype(jnp.bfloat16)
    quarter_back = transposed_right(logit_back, router_matrix) + moe_back
    mix_part = (
        transposed_right(sgate_back, shared_gate_matrix)
        + transposed_right(sup_back, shared_up_matrix)
        + place_rows(quarter_back, start_row, rows_here)
    )
    mix_total, router_grad = (
        lax.psum(mix_part.astype(jnp.bfloat16), "exp").astype(jnp.float32),
        lax.psum(router_term.astype(jnp.bfloat16), "exp").astype(jnp.float32),
    )
    _, norm_mix_back = jax.vjp(rms_scale, middle, mixer_gain.astype(jnp.float32))
    middle_norm_back, gain_mix_grad = norm_mix_back(mix_total)
    middle_grad = grad_float + middle_norm_back
    sdown_grad = transposed_left(shared_act, grad_rows)
    sgate_grad = transposed_left(normed_mix, sgate_back)
    sup_grad = transposed_left(normed_mix, sup_back)
    attn_back = middle_grad.astype(jnp.bfloat16)
    heads_back = transposed_right(attn_back, output_matrix).astype(jnp.bfloat16).reshape(head_shape)
    weights_full = jnp.exp(attention_scores() - log_total)
    weights_again = weights_full.astype(jnp.bfloat16)
    weight_back = jnp.einsum(
        "qhd,khd->hqk", heads_back, value_heads, preferred_element_type=jnp.float32
    )
    value_term = jnp.einsum(
        "hqk,qhd->khd", weights_again, heads_back, preferred_element_type=jnp.float32
    ).reshape(seq_length, -1)
    score_back = (
        weights_full * (weight_back - jnp.sum(weights_full * weight_back, axis=-1, keepdims=True))
    ).astype(jnp.bfloat16)
    query_rot_back = (
        jnp.einsum("hqk,khd->qhd", score_back, key_heads, preferred_element_type=jnp.float32)
        * scale
    )
    key_term = (
        jnp.einsum("hqk,qhd->khd", score_back, query_rot, preferred_element_type=jnp.float32)
        * scale
    ).reshape(seq_length, -1)
    key_sum, value_sum = (
        lax.psum_scatter(
            key_term.astype(jnp.bfloat16), "ctx", scatter_dimension=0, tiled=True
        ).astype(jnp.float32),
        lax.psum_scatter(
            value_term.astype(jnp.bfloat16), "ctx", scatter_dimension=0, tiled=True
        ).astype(jnp.float32),
    )
    _, rotate_back = jax.vjp(
        lambda values: rotate(values, cosine, sine_table), jnp.zeros(head_shape, jnp.float32)
    )
    query_low = rotate_back(query_rot_back)[0].reshape(rows_here, -1).astype(jnp.bfloat16)
    key_low = (
        rotate_back(key_sum.reshape(head_shape))[0].reshape(rows_here, -1).astype(jnp.bfloat16)
    )
    value_back_low = value_sum.astype(jnp.bfloat16)
    normed_part = (
        transposed_right(query_low, query_matrix)
        + transposed_right(key_low, key_matrix)
        + transposed_right(value_back_low, value_matrix)
    )
    normed_back = lax.psum(normed_part.astype(jnp.bfloat16), "exp").astype(jnp.float32)
    _, norm_attn_back = jax.vjp(rms_scale, layer_input, attention_gain.astype(jnp.float32))
    input_norm_back, gain_attn_grad = norm_attn_back(normed_back)
    tokens_back = (middle_grad + input_norm_back).astype(jnp.bfloat16)
    out_weight_grad = transposed_left(heads_out, attn_back)
    query_grad = transposed_left(normed, query_low)
    key_grad = transposed_left(normed, key_low)
    value_grad = transposed_left(normed, value_back_low)
    all_sums = (
        lax.psum_scatter(
            gain_attn_grad.astype(jnp.bfloat16), ("dp", "ctx"), scatter_dimension=0, tiled=True
        ).astype(jnp.float32),
        lax.psum_scatter(
            query_grad.astype(jnp.bfloat16), ("dp", "ctx"), scatter_dimension=0, tiled=True
        ).astype(jnp.float32),
        lax.psum_scatter(
            key_grad.astype(jnp.bfloat16), ("dp", "ctx"), scatter_dimension=0, tiled=True
        ).astype(jnp.float32),
        lax.psum_scatter(
            value_grad.astype(jnp.bfloat16), ("dp", "ctx"), scatter_dimension=0, tiled=True
        ).astype(jnp.float32),
        lax.psum_scatter(
            out_weight_grad.astype(jnp.bfloat16), ("dp", "ctx"), scatter_dimension=1, tiled=True
        ).astype(jnp.float32),
        lax.psum_scatter(
            gain_mix_grad.astype(jnp.bfloat16), ("dp", "ctx"), scatter_dimension=0, tiled=True
        ).astype(jnp.float32),
        lax.psum_scatter(
            router_grad.astype(jnp.bfloat16), ("dp", "ctx"), scatter_dimension=0, tiled=True
        ).astype(jnp.float32),
        lax.psum_scatter(
            sgate_grad.astype(jnp.bfloat16), ("dp", "ctx"), scatter_dimension=0, tiled=True
        ).astype(jnp.float32),
        lax.psum_scatter(
            sup_grad.astype(jnp.bfloat16), ("dp", "ctx"), scatter_dimension=0, tiled=True
        ).astype(jnp.float32),
        lax.psum_scatter(
            sdown_grad.astype(jnp.bfloat16), ("dp", "ctx"), scatter_dimension=1, tiled=True
        ).astype(jnp.float32),
    )
    (
        gain_attn_sum,
        query_sum,
        key_sum_out,
        value_sum_out,
        out_sum,
        gain_mix_sum,
        router_sum,
        sgate_sum,
        sup_sum,
        sdown_sum,
    ) = all_sums
    return (
        result.astype(jnp.bfloat16)[None],
        tokens_back[None],
        gain_attn_sum,
        query_sum,
        key_sum_out,
        value_sum_out,
        out_sum,
        gain_mix_sum,
        router_sum,
        sgate_sum,
        sup_sum,
        sdown_sum,
        gate_grad,
        up_grad,
        down_grad,
    )


MESH = pl.DeviceIdType.MESH
BF = jnp.bfloat16
F32 = jnp.float32


class Place:
    def __init__(self):
        self.x = lax.axis_index("dp")
        self.z = lax.axis_index("ctx")
        self.e = lax.axis_index("exp")
        z = self.z
        high = lax.div(z, 2)
        self.zs = [z, z + 1 - 2 * lax.rem(z, 2), 2 - high, 3 - 3 * high]
        self.inner = 3 - z
        self.inside = lax.div(z * (3 - z), 2)
        self.middle = self.inside == 1
        self.dx = 1 - 2 * self.x
        self.dy = 2 - 4 * lax.div(self.e, 2)
        self.dc = 1 - 2 * lax.rem(self.e, 2)

    def device(self, ox=0, oe=0, zi=0):
        return (self.x + ox, self.zs[zi], self.e + oe)

    def inward(self):
        return (self.x, self.inner, self.e)

    def shard(self, oe, zi):
        return self.zs[zi] * 4 + self.e + oe


def greet(at, everyone, pair=False):
    barrier = pltpu.get_barrier_semaphore()
    peers = [at.device(zi=1), at.device(oe=at.dy), at.device(oe=at.dc)]
    if everyone or pair:
        peers.append(at.device(ox=at.dx))
    if everyone:
        peers += [at.device(zi=2), at.device(zi=3)]
    for peer in peers:
        pl.semaphore_signal(barrier, inc=1, device_id=peer, device_id_type=MESH)
    if everyone:
        pl.semaphore_wait(barrier, len(peers))
        return

    @pl.when(at.middle)
    def _():
        pl.semaphore_signal(barrier, inc=1, device_id=at.inward(), device_id_type=MESH)

    pl.semaphore_wait(barrier, len(peers) + at.inside)


def remote(src, dst, send, recv, device):
    return pltpu.make_async_remote_copy(
        src_ref=src, dst_ref=dst, send_sem=send, recv_sem=recv, device_id=device, device_id_type=MESH
    )


def keep(src, dst):
    def run(held, sems):
        for j, (a, b) in enumerate(((src, held), (held, dst))):
            copy = pltpu.make_async_copy(a, b, sems.at[j])
            copy.start()
            copy.wait()

    pl.run_scoped(run, pltpu.VMEM(src.shape, src.dtype), pltpu.SemaphoreType.DMA((2,)))


def half_of(array):
    return jax.ShapeDtypeStruct((array.shape[0] // 2,) + array.shape[1:], array.dtype)


def cross(at, sent, got, send_sem, recv_sem, starts=None):
    starts = starts or (0,) * len(sent)
    return [
        remote(
            a.at[pl.ds(start, b.shape[0])],
            b,
            send_sem.at[m],
            recv_sem.at[m],
            at.device(ox=at.dx),
        )
        for m, (a, b, start) in enumerate(zip(sent, got, starts))
    ]


class Exchange:
    def __init__(self, at, sent, got, send_sem, recv_sem):
        self.at, self.sent, self.got = at, sent, got
        self.send_sem, self.recv_sem = send_sem, recv_sem
        self.waits = []

    def push(self, src, m, z_from, slot, device):
        at = self.at
        spot = self.got[m].at[at.x * 4 + z_from]
        copy = remote(
            src, spot, self.send_sem.at[m * 7 + slot], self.recv_sem.at[m * 8 + (0 if slot < 3 else 4) + z_from], device
        )
        copy.start()
        self.waits.append(copy)

    def start(self):
        at = self.at
        for m, sent in enumerate(self.sent):
            self.push(sent.at[at.z], m, at.z, 3, at.device(ox=at.dx))
        for m, sent in enumerate(self.sent):
            keep(sent.at[at.z], self.got[m].at[at.x * 4 + at.z])

    def along(self, zi):
        at = self.at
        for m, sent in enumerate(self.sent):
            self.push(sent.at[at.zs[zi]], m, at.z, zi - 1, at.device(zi=zi))

    def arrive(self, m, slot):
        src = self.sent[m].at[0]
        remote(
            src, self.got[m].at[0], self.send_sem.at[0], self.recv_sem.at[slot], self.at.device(ox=self.at.dx)
        ).wait_recv()

    def forward(self, zi):
        at = self.at
        for m in range(len(self.sent)):
            self.arrive(m, m * 8 + at.zs[zi])
            self.push(self.got[m].at[at.x * 4 + at.zs[zi]], m, at.zs[zi], 3 + zi, at.device(ox=at.dx))

    def finish(self):
        at = self.at
        for m, sent in enumerate(self.sent):
            for z in range(4):
                self.arrive(m, m * 8 + 4 + z)
        for copy in self.waits:
            copy.wait_send()


def gather_kernel(block, rows, parts, extras, starts, *refs):
    swaps = len(starts)
    refs = list(refs)

    def take(count):
        taken = refs[:count]
        del refs[:count]
        return taken

    (x_ref,), sent, given = take(1), take(extras), take(swaps)
    (out_ref,), got, taken = take(1), take(extras), take(swaps)
    send_sem, recv_sem = take(2)
    extra_sems = take(2 if extras else 0)
    at = Place()
    greet(at, extras > 0, swaps > 0)
    crossing = cross(at, given, taken, *refs, starts) if swaps else []
    piece = rows // parts
    slot_z, slot_f, slot_s = 0, 3, 7
    started, inside = [], []
    firsts = 1 if block else 0
    shift = at.e * rows if block else 0

    def where(f, zi, p):
        return pl.ds(
            pl.multiple_of(at.shard(f * at.dy, zi) * rows + p * piece, piece), piece
        )

    def push(src, dst, slot, p, device, sends=None, record=None):
        k = slot * parts + p
        j = k if sends is None else sends * parts + p
        remote(src, out_ref.at[dst], send_sem.at[j], recv_sem.at[k], device).start()
        (started if record is None else record).append(j)

    f_dev, s_dev, z_dev = at.device(oe=at.dy), at.device(oe=at.dc), at.device(zi=1)

    def gone(j):
        remote(
            x_ref.at[pl.ds(0, piece)], out_ref.at[pl.ds(0, piece)], send_sem.at[j], recv_sem.at[0], s_dev
        ).wait_send()

    def arrive(slot, p):
        k = slot * parts + p
        remote(
            x_ref.at[pl.ds(0, piece)], out_ref.at[pl.ds(0, piece)], send_sem.at[k], recv_sem.at[k], s_dev
        ).wait_recv()

    if block:
        spot = pl.ds(pl.multiple_of(at.z * 4 * rows, 4 * rows), 4 * rows)
    else:
        spot = pl.ds(pl.multiple_of(at.shard(0, 0) * rows, rows), rows)

    def source(f, zi, p):
        if f == 0 and zi == 0:
            return x_ref.at[pl.ds(pl.multiple_of(shift + p * piece, piece), piece)]
        return out_ref.at[where(f, zi, p)]

    def along(zi, p):
        src, dst = source(0, zi, p), where(0, zi, p)
        if zi == 0:
            push(src, dst, slot_z, p, z_dev)
        if zi < 2:
            pl.when(at.middle)(
                lambda: push(src, dst, slot_z + 1 + zi, p, at.inward(), 15 + zi, inside)
            )
        else:
            pl.when(at.middle)(lambda: push(src, dst, slot_z + zi - 1, p, z_dev, 15 + zi, inside))

    def forward(f, zi, p):
        src, dst = source(f, zi, p), where(f, zi, p)
        if f == 0:
            along(zi, p)
        if zi >= firsts:
            if f == 0:
                push(src, dst, slot_f + zi, p, f_dev)
            push(src, dst, slot_s + f * 4 + zi, p, s_dev)

    for p in range(parts):
        forward(0, 0, p)
    if extras:
        swap_in = Exchange(at, sent, got, *extra_sems)
        for zi in (1, 2, 3):
            swap_in.along(zi)
        swap_in.start()
    for copy in crossing:
        copy.start()
    keep(x_ref, out_ref.at[spot])
    for zi in range(1, 5):
        for p in range(parts):
            if zi < 4:
                arrive(slot_z + zi - 1, p)
                forward(0, zi, p)
            if zi - 1 >= firsts:
                arrive(slot_f + zi - 1, p)
                forward(1, zi - 1, p)
        if extras and zi > 1:
            swap_in.forward(zi - 1)
    for f in range(2):
        for zi in range(firsts, 4):
            for p in range(parts):
                arrive(slot_s + f * 4 + zi, p)
    if extras:
        swap_in.finish()
    for copy in crossing:
        copy.wait()
    for j in started:
        gone(j)

    @pl.when(at.middle)
    def _():
        for j in inside:
            gone(j)


def all_rows(x, block, cid, sent=(), given=(), starts=(), parts=2):
    rows, width = x.shape
    total = rows * (4 if block else 16)
    rows = rows // 4 if block else rows
    extras, swaps = len(sent), len(given)
    hbm = pl.BlockSpec(memory_space=pl.ANY)
    outs = [jax.ShapeDtypeStruct((total, width), x.dtype)]
    outs += [jax.ShapeDtypeStruct((8,) + a.shape[1:], a.dtype) for a in sent]
    outs += [half_of(a) for a in given]
    scratch = [
        pltpu.SemaphoreType.DMA((19 * parts,)),
        pltpu.SemaphoreType.DMA((15 * parts,)),
    ]
    if extras:
        scratch += [
            pltpu.SemaphoreType.DMA((7 * extras,)),
            pltpu.SemaphoreType.DMA((8 * extras,)),
        ]
    if swaps:
        scratch += [pltpu.SemaphoreType.DMA((swaps,)), pltpu.SemaphoreType.DMA((swaps,))]
    got = pl.pallas_call(
        functools.partial(gather_kernel, block, rows, parts, extras, starts),
        out_shape=outs,
        in_specs=[hbm] * len(outs),
        out_specs=[hbm] * len(outs),
        scratch_shapes=scratch,
        compiler_params=pltpu.CompilerParams(collective_id=cid, has_side_effects=True),
    )(x, *sent, *given)
    return got if extras or swaps else got[0]


class Scatter:
    def __init__(self, at, acc, got_s, got_f, got_z, send_sem, recv_sem, out_ref, by_block=False):
        self.by_block = by_block
        self.at, self.acc, self.got_s, self.got_f, self.got_z = at, acc, got_s, got_f, got_z
        self.send_sem, self.recv_sem, self.out_ref = send_sem, recv_sem, out_ref
        self.rows = acc.shape[1]
        self.f_dev, self.s_dev, self.z_dev = (
            at.device(oe=at.dy),
            at.device(oe=at.dc),
            at.device(zi=1),
        )
        self.started, self.in_middle, self.at_end = [], [], []

    def held(self, f, zi, twin=0):
        at = self.at
        return zi * 4 + at.e + f * at.dy + twin * at.dc if self.by_block else f * 4 + zi

    def span(self, p):
        size = self.rows // 2
        return pl.ds(p * size, size)

    def push(self, src, dst, slot, p, device, sends=None, record=None):
        j = (slot if sends is None else sends) * 2 + p
        src, dst = src.at[self.span(p)], dst.at[self.span(p)]
        remote(src, dst, self.send_sem.at[j], self.recv_sem.at[slot * 2 + p], device).start()
        (self.started if record is None else record).append(j)

    def gone(self, j):
        spot = self.acc.at[0, self.span(0)]
        remote(spot, spot, self.send_sem.at[j], self.recv_sem.at[0], self.s_dev).wait_send()

    def arrive(self, dst, slot, p):
        j, dst = slot * 2 + p, dst.at[self.span(p)]
        src = self.acc.at[0, self.span(p)]
        remote(src, dst, self.send_sem.at[j], self.recv_sem.at[j], self.s_dev).wait_recv()

    def to_twin(self, src, f, zi):
        k = f * 4 + zi
        for p in range(2):
            self.push(src, self.got_s.at[k], 9 + k, p, self.s_dev)

    def add(self, k, p, *others, into=None):
        acc = self.acc
        size = self.rows // 2

        @pl.loop(0, size // 16)
        def _(i):
            span = pl.ds(pl.multiple_of(p * size + i * 16, 16), 16)
            total = acc[k, span, :].astype(F32)
            for ref, j in others:
                total = total + ref[j, span, :].astype(F32)
            if into is None:
                acc[k, span, :] = total.astype(BF)
            else:
                into[span, :] = total

    def first(self, zi):
        k = self.held(1, zi)
        for p in range(2):
            self.arrive(self.got_s.at[4 + zi], 13 + zi, p)
            self.add(k, p, (self.got_s, 4 + zi))
            self.push(self.acc.at[k], self.got_f.at[zi], 5 + zi, p, self.f_dev)

    def second(self, zi, who="all"):
        if who != "middle":
            pl.when(jnp.logical_not(self.at.middle))(lambda: self.from_end(zi))
        if who != "end":
            pl.when(self.at.middle)(lambda: self.from_middle(zi))

    def terms(self, zi, p):
        self.arrive(self.got_s.at[zi], 9 + zi, p)
        self.arrive(self.got_f.at[zi], 5 + zi, p)
        return self.held(0, zi), [(self.got_s, zi), (self.got_f, zi)]

    def from_end(self, zi):
        acc, got_z = self.acc, self.got_z
        for p in range(2):
            k, others = self.terms(zi, p)
            if zi == 0:
                self.arrive(got_z.at[4], 4, p)
                self.add(k, p, *others, (got_z, 4), into=self.out_ref)
                continue
            self.add(k, p, *others)
            self.push(acc.at[k], got_z.at[3 - zi], 3 - zi, p, self.z_dev, zi, self.at_end)

    def from_middle(self, zi):
        acc, got_z = self.acc, self.got_z
        for p in range(2):
            k, others = self.terms(zi, p)
            if zi == 0:
                self.arrive(got_z.at[2], 2, p)
                self.arrive(got_z.at[4], 4, p)
                self.add(k, p, *others, (got_z, 2), (got_z, 4), into=self.out_ref)
                continue
            came = 3 if zi == 1 else 3 - zi
            self.arrive(got_z.at[came], came, p)
            self.add(k, p, *others, (got_z, came))
            there = 3 if zi == 3 else 4
            device = self.z_dev if zi == 1 else self.at.inward()
            self.push(acc.at[k], got_z.at[there], there, p, device, zi, self.in_middle)

    def finish(self):
        for j in self.started:
            self.gone(j)

        @pl.when(self.at.middle)
        def _():
            for j in self.in_middle:
                self.gone(j)

        @pl.when(jnp.logical_not(self.at.middle))
        def _():
            for j in self.at_end:
                self.gone(j)


def scatter_buffers(rows, width, held=8):
    return [
        pltpu.VMEM((held, rows, width), BF),
        pltpu.VMEM((8, rows, width), BF),
        pltpu.VMEM((4, rows, width), BF),
        pltpu.VMEM((5, rows, width), BF),
        pltpu.SemaphoreType.DMA((34,)),
        pltpu.SemaphoreType.DMA((34,)),
    ]


def scatter_kernel(rows, starts, in_ref, *refs):
    swaps = len(starts)
    given, out_ref, taken = refs[:swaps], refs[swaps], refs[swaps + 1 : 2 * swaps + 1]
    buffers, load_sem = refs[2 * swaps + 1 : 2 * swaps + 7], refs[2 * swaps + 7]
    acc = buffers[0]
    at = Place()
    greet(at, False, swaps > 0)
    crossing = cross(at, given, taken, *refs[2 * swaps + 8 :], starts) if swaps else []
    total = Scatter(at, *buffers, out_ref)

    def rows_of(rank):
        return in_ref.at[pl.ds(pl.multiple_of(rank * rows, rows), rows)]

    for copy in crossing:
        copy.start()
    order = [(f, zi) for f in (1, 0) for zi in (3, 2, 1, 0)]
    loads = {}
    for f, zi in order:
        k = f * 4 + zi
        total.to_twin(rows_of(at.shard(f * at.dy + at.dc, zi)), f, zi)
        loads[k] = pltpu.make_async_copy(
            rows_of(at.shard(f * at.dy, zi)), acc.at[k], load_sem.at[k]
        )
        loads[k].start()
    for f, zi in order:
        loads[f * 4 + zi].wait()
        (total.first if f else total.second)(zi)
    for copy in crossing:
        copy.wait()
    total.finish()


def own_rows(x, cid, given=(), starts=()):
    rows, width = x.shape[0] // 16, x.shape[1]
    swaps = len(given)
    hbm = pl.BlockSpec(memory_space=pl.ANY)
    crossing = [pltpu.SemaphoreType.DMA((swaps,))] * 2 if swaps else []
    got = pl.pallas_call(
        functools.partial(scatter_kernel, rows, starts),
        out_shape=[jax.ShapeDtypeStruct((rows, width), F32)]
        + [half_of(a) for a in given],
        in_specs=[hbm] * (1 + swaps),
        out_specs=[pl.BlockSpec(memory_space=pltpu.VMEM)] + [hbm] * swaps,
        scratch_shapes=[
            *scatter_buffers(rows, width),
            pltpu.SemaphoreType.DMA((8,)),
            *crossing,
        ],
        compiler_params=pltpu.CompilerParams(
            collective_id=cid, has_side_effects=True, vmem_limit_bytes=40 * 1024 * 1024
        ),
    )(x, *given)
    return got if swaps else got[0]


class Gather:
    parts = 2

    def __init__(self, at, x_ref, out_ref, send_sem, recv_sem, block=False):
        self.at, self.x_ref, self.out_ref, self.block = at, x_ref, out_ref, block
        self.send_sem, self.recv_sem = send_sem, recv_sem
        rows = x_ref.shape[0] // (4 if block else 1)
        self.rows, self.piece = rows, rows // self.parts
        self.f_dev, self.s_dev, self.z_dev = (
            at.device(oe=at.dy),
            at.device(oe=at.dc),
            at.device(zi=1),
        )
        self.started, self.inside = [], []
        if block:
            spot = pl.ds(pl.multiple_of(at.z * 4 * rows, 4 * rows), 4 * rows)
        else:
            spot = pl.ds(pl.multiple_of(at.shard(0, 0) * rows, rows), rows)
        self.place = spot

    def push(self, f, zi, p, slot, device, sends=None, record=None):
        at, piece = self.at, self.piece
        spot = at.shard(f * at.dy, zi) * self.rows + p * piece
        dst = self.out_ref.at[pl.ds(pl.multiple_of(spot, piece), piece)]
        src = dst
        if f == 0 and zi == 0:
            spot = (at.e * self.rows if self.block else 0) + p * piece
            src = self.x_ref.at[pl.ds(pl.multiple_of(spot, piece), piece)]
        j = (slot if sends is None else sends) * self.parts + p
        k = slot * self.parts + p
        remote(src, dst, self.send_sem.at[j], self.recv_sem.at[k], device).start()
        (self.started if record is None else record).append(j)

    def spot(self):
        span = pl.ds(0, self.piece)
        return self.x_ref.at[span], self.out_ref.at[span]

    def arrive(self, slot, p):
        k = slot * self.parts + p
        remote(*self.spot(), self.send_sem.at[k], self.recv_sem.at[k], self.s_dev).wait_recv()

    def forward(self, f, zi, p):
        if f == 0:
            if zi == 0:
                self.push(0, 0, p, 0, self.z_dev)
            if zi < 2:
                pl.when(self.at.middle)(
                    lambda: self.push(0, zi, p, 1 + zi, self.at.inward(), 15 + zi, self.inside)
                )
            else:
                pl.when(self.at.middle)(
                    lambda: self.push(0, zi, p, zi - 1, self.z_dev, 15 + zi, self.inside)
                )
        if self.block and zi == 0:
            return
        if f == 0:
            self.push(0, zi, p, 3 + zi, self.f_dev)
        self.push(f, zi, p, 7 + f * 4 + zi, self.s_dev)

    def begin(self):
        for p in range(self.parts):
            self.forward(0, 0, p)
        keep(self.x_ref, self.out_ref.at[self.place])

    def step(self, zi):
        for p in range(self.parts):
            if zi < 4:
                self.arrive(zi - 1, p)
                self.forward(0, zi, p)
            if zi > 1 or not self.block:
                self.arrive(2 + zi, p)
                self.forward(1, zi - 1, p)

    def twin(self, zi):
        for p in range(self.parts):
            self.arrive(7 + zi, p)
            self.arrive(11 + zi, p)

    def finish(self, arrived=False):
        for zi in range(4):
            if not arrived and not (self.block and zi == 0):
                self.twin(zi)

        def gone(j):
            remote(*self.spot(), self.send_sem.at[j], self.recv_sem.at[0], self.s_dev).wait_send()

        for j in self.started:
            gone(j)

        @pl.when(self.at.middle)
        def _():
            for j in self.inside:
                gone(j)


def columns_loop(width, parts):
    size = width // parts

    def over(run):
        @pl.loop(0, parts)
        def _(n):
            run(pl.ds(pl.multiple_of(n * size, size), size))

    return over


def expert_gather_kernel(experts, *refs):
    refs = list(refs)

    def take(count):
        taken = refs[:count]
        del refs[:count]
        return taken

    x_ref, dy_ref, disp, w_router, units = take(5)
    weights, given = take(7), take(2)
    out_ref, picked, picked_dy, scaled_out, g_out, u_out, gb_out, sa_out, sg_out = take(9)
    taken, units_out = take(2), take(2)
    shared_in, shared_out = take(2)
    wg, wu, wd, xb, dyd, sb, pk, pdy, sc, gg, uu, hid, gb, sa, sg = take(15)
    send_sem, recv_sem, load_sem, block_sem, store_sem, cross_send, cross_recv, unit_sem = take(8)
    at = Place()
    gather = Gather(at, x_ref, out_ref, send_sem, recv_sem)
    crossing = cross(at, given, taken, cross_send, cross_recv, (0, taken[0].shape[0]))
    block = xb.shape[1]
    slots = pk.shape[0] // 4
    part = wd.shape[1] // 2
    mine = at.z * 4 + at.e

    def span(zi, size):
        return pl.ds(pl.multiple_of(at.zs[zi] * size, size), size)

    def dy_load(zi):
        return pltpu.make_async_copy(
            dy_ref.at[span(zi, block)], xb.at[zi % 2], block_sem.at[2 + zi % 2]
        )

    def x_load(zi):
        return pltpu.make_async_copy(
            out_ref.at[span(zi, block)], xb.at[zi % 2], block_sem.at[zi % 2]
        )

    def stores(zi):
        b = zi % 2
        pairs = [(sa.at[b], sa_out.at[span(zi, block)]), (sg.at[b], sg_out.at[span(zi, block)])]
        return [
            pltpu.make_async_copy(src, dst, store_sem.at[b * 2 + j])
            for j, (src, dst) in enumerate(pairs)
        ]

    def parts_of(gate, up):
        s = 1.0 / (1.0 + jnp.exp(-gate))
        act = gate * s
        return act * up, s * (1.0 + gate * (1.0 - s)) * up, act

    cut, size = units.shape[1] // 3, units.shape[2]
    wide = shared_out.shape[0]
    unit_loads = []
    for d in range(8):
        for m in range(3):
            ref, first = (shared_out, 0) if m == 2 else (shared_in, m * wide)
            unit_loads.append(
                pltpu.make_async_copy(
                    units.at[d, pl.ds(m * cut, cut)],
                    ref.at[pl.ds(first, cut), pl.ds(d * size, size)],
                    unit_sem.at[d * 3 + m],
                )
            )

    def ahead(zi):
        b = zi % 2
        some = span(zi, slots)
        dy_load(zi).wait()
        pdy[some, :] = product(disp[at.zs[zi]], xb[b]).astype(BF)
        sb[span(zi, block), :] = transposed_right(xb[b], shared_out[...])
        if zi < 2:
            dy_load(zi + 2).start()
        dyd[some, :] = transposed_right(pdy[some, :], wd[0])

    def work(zi):
        b = zi % 2
        some = span(zi, slots)
        x_load(zi).wait()
        if zi >= 2:
            for copy in stores(zi - 2):
                copy.wait()
        pk[some, :] = product(disp[at.zs[zi]], xb[b]).astype(BF)
        logits = transposed_right(pk[some, :], w_router[...])
        lane = lax.broadcasted_iota(jnp.int32, logits.shape, 1)
        logits = jnp.where(lane < experts, logits, MASKED)
        powers = jnp.exp(logits - jnp.max(logits, axis=1, keepdims=True))
        own_power = jnp.sum(jnp.where(lane == mine, powers, 0.0), axis=1, keepdims=True)
        gate_of = own_power / jnp.sum(powers, axis=1, keepdims=True)
        for h in range(2):
            hidden, by_gate, by_up = parts_of(
                transposed_right(pk[some, :], wg[h]), transposed_right(pk[some, :], wu[h])
            )
            sc[h, some, :] = (hidden * gate_of).astype(BF)
            if h == 0:
                dy_down = dyd[some, :]
                act_back = gate_of * dy_down
                gg[0, some, :] = (act_back * by_gate).astype(BF)
                uu[0, some, :] = (act_back * by_up).astype(BF)
                gb[some, :] = jnp.broadcast_to(
                    jnp.sum(hidden * dy_down, axis=1, keepdims=True), (slots, gb.shape[1])
                )
            else:
                hid[some, :] = hidden.astype(BF)
                gg[1, some, :] = (gate_of * by_gate).astype(BF)
                uu[1, some, :] = (gate_of * by_up).astype(BF)
        both = transposed_right(xb[b], shared_in[...])
        wide = both.shape[1] // 2
        hidden, by_gate, by_up = parts_of(both[:, :wide], both[:, wide:])
        back = sb[span(zi, block), :]
        sa[b] = hidden.astype(BF)
        sg[b, :, :wide] = (back * by_gate).astype(BF)
        sg[b, :, wide:] = (back * by_up).astype(BF)
        for copy in stores(zi):
            copy.start()

    def other_half(zi):
        some = span(zi, slots)
        dy_down = transposed_right(pdy[some, :], wd[1])
        gg[1, some, :] = (dy_down * gg[1, some, :].astype(F32)).astype(BF)
        uu[1, some, :] = (dy_down * uu[1, some, :].astype(F32)).astype(BF)
        gb[some, :] += jnp.broadcast_to(
            jnp.sum(hid[some, :].astype(F32) * dy_down, axis=1, keepdims=True), (slots, gb.shape[1])
        )

    places = [
        wg.at[0],
        wu.at[0],
        wd.at[0],
        wg.at[1, pl.ds(0, part)],
        wg.at[1, pl.ds(part, part)],
        wu.at[1, pl.ds(0, part)],
        wu.at[1, pl.ds(part, part)],
        wd.at[1, pl.ds(0, part)],
        wd.at[1, pl.ds(part, part)],
    ]
    loads = [
        pltpu.make_async_copy(a, b, load_sem.at[j]) for j, (a, b) in enumerate(zip(weights + taken, places))
    ]
    dy_load(0).start()
    dy_load(1).start()
    for j in (2, 0, 1, 3, 4, 5, 6):
        loads[j].start()
    shared_in[...] = jnp.zeros_like(shared_in)
    shared_out[...] = jnp.zeros_like(shared_out)
    for copy in unit_loads:
        copy.start()
    greet(at, False, True)
    for copy in crossing:
        copy.start()
    gather.begin()
    for copy in unit_loads:
        copy.wait()
    loads[2].wait()
    for zi in range(3):
        ahead(zi)
    for zi in range(4):
        gather.step(zi + 1)
        if zi == 0:
            ahead(3)
        gather.twin(zi)
        x_load(zi).start()
        if zi == 0:
            for j in (0, 1, 3, 4, 5, 6):
                loads[j].wait()
        work(zi)
    results = [(pk, picked), (pdy, picked_dy), (sc, scaled_out)]
    results += [(shared_in, units_out[0]), (shared_out, units_out[1])]
    results += [(gg, g_out), (uu, u_out), (gb, gb_out)]
    results = [
        pltpu.make_async_copy(a, b, store_sem.at[4 + j]) for j, (a, b) in enumerate(results)
    ]
    for copy in results[:5]:
        copy.start()
    for m in range(2):
        crossing[m].wait_recv()
        loads[7 + m].start()
    for m in range(2):
        loads[7 + m].wait()
    for zi in range(4):
        other_half(zi)
    for copy in results[5:]:
        copy.start()
    for copy in results:
        copy.wait()
    for zi in (2, 3):
        for copy in stores(zi):
            copy.wait()
    for copy in crossing:
        copy.wait_send()
    gather.finish(True)


def expert_rows(x, dy_all, dispatch, w_router, experts, units, wide, weights, given, cid):
    rows, width = x.shape
    total, block = 16 * rows, 4 * rows
    slots = 4 * dispatch.shape[1]
    hidden = weights[0].shape[0]
    halves = [half_of(a) for a in given]
    hbm, vmem = pl.BlockSpec(memory_space=pl.ANY), pl.BlockSpec(memory_space=pltpu.VMEM)
    shape, sems = jax.ShapeDtypeStruct, lambda n: pltpu.SemaphoreType.DMA((n,))
    return pl.pallas_call(
        functools.partial(expert_gather_kernel, experts),
        out_shape=[
            shape((total, width), BF),
            shape((slots, width), BF),
            shape((slots, width), BF),
            shape((2, slots, hidden), BF),
            shape((2, slots, hidden), BF),
            shape((2, slots, hidden), BF),
            shape((slots, 128), F32),
            shape((total, wide), BF),
            shape((total, 2 * wide), BF),
            *halves,
            shape((2 * wide, width), BF),
            shape((wide, width), BF),
        ],
        in_specs=[hbm, hbm, vmem, vmem] + [hbm] * 10,
        out_specs=[hbm] * 13,
        scratch_shapes=[
            pltpu.VMEM((2 * wide, width), BF),
            pltpu.VMEM((wide, width), BF),
            pltpu.VMEM((2, hidden, width), BF),
            pltpu.VMEM((2, hidden, width), BF),
            pltpu.VMEM((2, hidden, width), BF),
            pltpu.VMEM((2, block, width), BF),
            pltpu.VMEM((slots, hidden), F32),
            pltpu.VMEM((total, wide), F32),
            pltpu.VMEM((slots, width), BF),
            pltpu.VMEM((slots, width), BF),
            pltpu.VMEM((2, slots, hidden), BF),
            pltpu.VMEM((2, slots, hidden), BF),
            pltpu.VMEM((2, slots, hidden), BF),
            pltpu.VMEM((slots, hidden), BF),
            pltpu.VMEM((slots, 128), F32),
            pltpu.VMEM((2, block, wide), BF),
            pltpu.VMEM((2, block, 2 * wide), BF),
            sems(38),
            sems(30),
            sems(9),
            sems(4),
            sems(12),
            sems(2),
            sems(2),
            sems(24),
        ],
        compiler_params=pltpu.CompilerParams(
            collective_id=cid, has_side_effects=True, vmem_limit_bytes=62 * 1024 * 1024
        ),
    )(x, dy_all, dispatch, w_router, units, *weights, *given)


def expert_scatter_kernel(*refs):
    refs = list(refs)

    def take(count):
        taken = refs[:count]
        del refs[:count]
        return taken

    disp, gate_back, shared_in, g_ref, u_ref, sg_ref, picked_ref, dy_ref, scaled_ref = take(9)
    weights = take(6)
    out_ref, taken, *grads = take(7)
    wg, wu, gs, us, sg, picked, picked_dy, scaled, ib, grad, turned = take(11)
    acc, got_s, got_f, got_z, send_sem, recv_sem = take(6)
    load_sem, store_sem, cross_send, cross_recv = take(4)
    at = Place()
    rows, full = acc.shape[1:]
    width = shared_in.shape[1]
    slots = ib.shape[0]
    block = 4 * rows
    over = columns_loop(width, 4)
    mine = at.z * 4 + at.e
    total = Scatter(at, acc, got_s, got_f, got_z, send_sem, recv_sem, out_ref, True)

    part = wg.shape[1] // 2
    pairs = [
        (weights[0], wg.at[0]),
        (weights[1], wu.at[0]),
        (weights[2], wg.at[1, pl.ds(0, part)]),
        (weights[3], wg.at[1, pl.ds(part, part)]),
        (weights[4], wu.at[1, pl.ds(0, part)]),
        (weights[5], wu.at[1, pl.ds(part, part)]),
        (g_ref, gs),
        (u_ref, us),
        (sg_ref, sg),
        (picked_ref, picked),
        (dy_ref, picked_dy),
        (scaled_ref.at[1], scaled),
    ]
    loads = [pltpu.make_async_copy(a, b, load_sem.at[j]) for j, (a, b) in enumerate(pairs)]
    for copy in loads:
        copy.start()
    greet(at, False, True)

    def work(zi):
        place = at.zs[zi]
        some = pl.ds(pl.multiple_of(place * slots, slots), slots)

        hot = disp[place]
        tokens = pl.ds(pl.multiple_of(place * block, block), block)

        @over
        def _(columns):
            terms = product(gs[0, some, :], wg[0, :, columns])
            terms += product(us[0, some, :], wu[0, :, columns])
            terms += product(gs[1, some, :], wg[1, :, columns])
            terms += product(us[1, some, :], wu[1, :, columns])
            ib[:, columns] = terms.astype(BF)

        @over
        def _(columns):
            terms = transposed_left(hot, ib[:, columns])
            terms += product(sg[tokens, :], shared_in[:, columns])
            for e in range(4):
                acc[zi * 4 + e, :, columns] = terms[e * rows : (e + 1) * rows].astype(BF)

        from_gates = gate_back[some, :]
        lane = lax.broadcasted_iota(jnp.int32, from_gates.shape, 1)
        terms = transposed_left(hot, jnp.where(lane == mine, from_gates, 0.0).astype(BF))
        for e in range(4):
            acc[zi * 4 + e, :, width:] = terms[e * rows : (e + 1) * rows].astype(BF)

    def gradient(m):
        step = 256
        right = picked_dy if m == 2 else picked
        turned[...] = (scaled[...] if m == 2 else gs[1] if m == 0 else us[1]).T

        @pl.loop(0, width // step)
        def _(n):
            columns = pl.ds(pl.multiple_of(n * step, step), step)
            grad[min(m, 1), :, columns] = product(turned[...], right[:, columns]).astype(BF)

    crossing = cross(at, [grad.at[0, pl.ds(0, part)]], [taken], cross_send, cross_recv)[0]
    stores = [
        pltpu.make_async_copy(
            grad.at[min(j // 2, 1), pl.ds(j % 2 * part, part)], grads[j - 1], store_sem.at[j]
        )
        for j in range(1, 6)
    ]
    for copy in loads[:9]:
        copy.wait()
    for zi in (3, 2, 1, 0):
        work(zi)
        for f in range(2):
            total.to_twin(acc.at[total.held(f, zi, 1)], f, zi)
        total.first(zi)
        if zi == 1:
            total.second(3, "end")
    for copy in loads[9:]:
        copy.wait()
    for m, zi in ((0, 2), (1, 1), (2, 0)):
        if m == 2:
            stores[1].wait()
            stores[2].wait()
        gradient(m)
        if m == 0:
            total.second(3, "middle")
        if m == 0:
            crossing.start()
        for j in (2 * m, 2 * m + 1):
            if j > 0:
                stores[j - 1].start()
        total.second(zi)
    for j in (0, 3, 4):
        stores[j].wait()
    crossing.wait()
    total.finish()


def expert_back(dispatch, gate_back, shared_in, g, u, sg, picked, picked_dy, scaled, weights, cid):
    total, wide = sg.shape
    width = shared_in.shape[1]
    rows, full = total // 16, width + 128
    slots = picked.shape[0]
    hidden = g.shape[2]
    hbm, vmem = pl.BlockSpec(memory_space=pl.ANY), pl.BlockSpec(memory_space=pltpu.VMEM)
    shape = jax.ShapeDtypeStruct
    return pl.pallas_call(
        expert_scatter_kernel,
        out_shape=[
            shape((rows, full), F32),
            *[shape((hidden // 2, width), BF)] * 6,
        ],
        in_specs=[vmem] * 3 + [hbm] * 12,
        out_specs=[vmem] + [hbm] * 6,
        scratch_shapes=[
            pltpu.VMEM((2, hidden, width), BF),
            pltpu.VMEM((2, hidden, width), BF),
            pltpu.VMEM((2, slots, hidden), BF),
            pltpu.VMEM((2, slots, hidden), BF),
            pltpu.VMEM((total, wide), BF),
            pltpu.VMEM((slots, width), BF),
            pltpu.VMEM((slots, width), BF),
            pltpu.VMEM((slots, hidden), BF),
            pltpu.VMEM((slots // 4, width), BF),
            pltpu.VMEM((2, hidden, width), BF),
            pltpu.VMEM((hidden, slots), BF),
            *scatter_buffers(rows, full, 16),
            pltpu.SemaphoreType.DMA((12,)),
            pltpu.SemaphoreType.DMA((6,)),
            pltpu.SemaphoreType.DMA((1,)),
            pltpu.SemaphoreType.DMA((1,)),
        ],
        compiler_params=pltpu.CompilerParams(
            collective_id=cid, has_side_effects=True, vmem_limit_bytes=63 * 1024 * 1024
        ),
    )(dispatch, gate_back, shared_in, g, u, sg, picked, picked_dy, scaled, *weights)


def mixed_kernel(*refs):
    refs = list(refs)

    def take(count):
        taken = refs[:count]
        del refs[:count]
        return taken

    w_out, w_qkv, tables, q_ref, k_ref, v_ref, lse_ref, heads_out = take(8)
    in_ref, back_ref, normed_ref, *given = take(5)
    out_ref, normed_back, home_out, *taken = take(5)
    rows_in, do, dk, dv, qkv, out_sum, qkv_sum, staged = take(8)
    buffers = take(6)
    first_sem, in_sem, store_sem, cross_send, cross_recv = take(5)
    at = Place()
    total = Scatter(at, *buffers, out_ref)
    acc = buffers[0]
    rows, width = acc.shape[1:]
    length = q_ref.shape[0]
    block = length // 4
    crossing = cross(at, given, taken, cross_send, cross_recv)

    def rows_of(rank):
        return in_ref.at[pl.ds(pl.multiple_of(rank * rows, rows), rows)]

    def rows_load(j):
        ref = back_ref if j < 4 else normed_ref
        return pltpu.make_async_copy(
            ref.at[pl.ds(j % 4 * block, block)], rows_in.at[j % 2], in_sem.at[j % 2]
        )

    rows_load(0).start()
    rows_load(1).start()
    greet(at, False, True)
    for copy in crossing:
        copy.start()
    order = [(f, zi) for f in (1, 0) for zi in (3, 2, 1, 0)]
    firsts = {}
    for f, zi in order:
        m = f * 4 + zi
        total.to_twin(rows_of(at.shard(f * at.dy + at.dc, zi)), f, zi)
        firsts[m] = pltpu.make_async_copy(
            rows_of(at.shard(f * at.dy, zi)), acc.at[m], first_sem.at[m]
        )
        firsts[m].start()

    def heads_back(j):
        rows_load(j).wait()
        here = pl.ds(j * block, block)
        do[here, :] = transposed_right(rows_in[j % 2], w_out[...]).astype(BF)
        turned = heads_out[here, :].T

        @pl.loop(0, 4)
        def _(n):
            columns = pl.ds(pl.multiple_of(n * (width // 4), width // 4), width // 4)
            terms = product(turned, rows_in[j % 2, :, columns])
            out_sum[:, columns] = terms if j == 0 else out_sum[:, columns] + terms

        rows_load(j + 2).start()

    scale = HDIM ** (-0.5)
    step = 256

    def attend_rows(i):
        seen = (i + 1) * step
        here = pl.ds(i * step, step)
        q, go = q_ref[here, :], do[here, :]
        scores = transposed_right(q, k_ref[0:seen, :]) * scale
        row_at = lax.broadcasted_iota(jnp.int32, scores.shape, 0) + i * step
        col_at = lax.broadcasted_iota(jnp.int32, scores.shape, 1)
        scores = jnp.where(row_at >= col_at, scores, MASKED)
        probs = jnp.exp(scores - lse_ref[here, 0:1])
        weight_back = transposed_right(go, v_ref[0:seen, :])
        inner = jnp.sum(probs * weight_back, axis=-1, keepdims=True)
        score_back = (probs * (weight_back - inner)).astype(BF)
        dv[0:seen, :] += transposed_left(probs.astype(BF), go)
        dk[0:seen, :] += transposed_left(score_back, q) * scale
        qkv[here, 0:HDIM] = turn_rows(product(score_back, k_ref[0:seen, :]) * scale, here)

    def turn_rows(values, here):
        other = pltpu.roll(values, HDIM // 2, 1)
        return (values * tables[0, here, :] + other * tables[1, here, :]).astype(BF)

    def finish_heads():
        for j in range(8):
            here = pl.ds(j * step, step)
            qkv[here, HDIM : 2 * HDIM] = turn_rows(dk[here, :], here)
            qkv[here, 2 * HDIM :] = dv[here, :].astype(BF)

    def normed_store(j):
        return pltpu.make_async_copy(
            staged.at[j % 2], normed_back.at[pl.ds(j * step, step)], store_sem.at[j % 2]
        )

    def normed_rows(j):
        if j >= 2:
            normed_store(j - 2).wait()

        @pl.loop(0, 4)
        def _(n):
            columns = pl.ds(pl.multiple_of(n * (width // 4), width // 4), width // 4)
            staged[j % 2, :, columns] = product(
                qkv[pl.ds(j * step, step), :], w_qkv[:, columns]
            ).astype(BF)

        normed_store(j).start()

    def qkv_rows(j):
        rows_load(4 + j).wait()
        turned = qkv[pl.ds(j * block, block), :].T

        @pl.loop(0, 4)
        def _(n):
            columns = pl.ds(pl.multiple_of(n * (width // 4), width // 4), width // 4)
            terms = product(turned, rows_in[j % 2, :, columns])
            qkv_sum[:, columns] = terms if j == 0 else qkv_sum[:, columns] + terms

        if j < 2:
            rows_load(6 + j).start()

    for zi in (3, 2, 1, 0):
        firsts[4 + zi].wait()
        total.first(zi)
    for j in range(4):
        heads_back(j)
    for m in (3, 2, 1, 0):
        firsts[m].wait()
    total.second(3, "end")
    dk[...] = jnp.zeros_like(dk)
    dv[...] = jnp.zeros_like(dv)
    for i in range(5):
        attend_rows(i)
    total.second(3, "middle")
    total.second(2, "end")
    for i in range(5, 8):
        attend_rows(i)
    finish_heads()
    for j in range(3):
        normed_rows(j)
    total.second(2, "middle")
    total.second(1, "end")
    for j in range(3, 8):
        normed_rows(j)
    total.second(1, "middle")
    for j in range(4):
        qkv_rows(j)
    size = home_out.shape[2]
    for j in range(8):
        columns = slice(j * size, (j + 1) * size)
        home_out[j, : 3 * HDIM, :] = qkv_sum[:, columns].astype(BF)
        home_out[j, 3 * HDIM :, :] = out_sum[:, columns].astype(BF)
    total.second(0)
    for j in (6, 7):
        normed_store(j).wait()
    for copy in crossing:
        copy.wait()
    total.finish()


def mixed_rows(
    w_out, w_qkv, tables, q, k, v, lse, heads_out, mixed_part, attn_back, normed, given, cid
):
    length, width = attn_back.shape
    rows = length // 16
    hbm, vmem = pl.BlockSpec(memory_space=pl.ANY), pl.BlockSpec(memory_space=pltpu.VMEM)
    shape = jax.ShapeDtypeStruct
    return pl.pallas_call(
        mixed_kernel,
        out_shape=[
            shape((rows, width), F32),
            shape((length, width), BF),
            shape((8, 4 * HDIM, width // 8), BF),
            *[shape(a.shape, BF) for a in given],
        ],
        in_specs=[vmem] * 8 + [hbm] * 5,
        out_specs=[vmem, hbm, vmem, hbm, hbm],
        scratch_shapes=[
            pltpu.VMEM((2, length // 4, width), BF),
            pltpu.VMEM((length, HDIM), BF),
            pltpu.VMEM((length, HDIM), F32),
            pltpu.VMEM((length, HDIM), F32),
            pltpu.VMEM((length, 3 * HDIM), BF),
            pltpu.VMEM((HDIM, width), F32),
            pltpu.VMEM((3 * HDIM, width), F32),
            pltpu.VMEM((2, 256, width), BF),
            *scatter_buffers(rows, width),
            pltpu.SemaphoreType.DMA((8,)),
            pltpu.SemaphoreType.DMA((2,)),
            pltpu.SemaphoreType.DMA((2,)),
            pltpu.SemaphoreType.DMA((2,)),
            pltpu.SemaphoreType.DMA((2,)),
        ],
        compiler_params=pltpu.CompilerParams(
            collective_id=cid, has_side_effects=True, vmem_limit_bytes=63 * 1024 * 1024
        ),
    )(w_out, w_qkv, tables, q, k, v, lse, heads_out, mixed_part, attn_back, normed, *given)


def gather_back_kernel(*refs):
    refs = list(refs)

    def take(count):
        taken = refs[:count]
        del refs[:count]
        return taken

    x_ref, disp, shared_out = take(3)
    scaled_ref, act_ref, sg_ref, wd_a, wd_0, wd_1, mix_ref, dy_ref, *given = take(10)
    out_ref, mixed_part, units_grad, *taken = take(5)
    scaled, acts, sg, wd, eb, mixes, dys, staged, turned, turned_acts = take(10)
    send_sem, recv_sem, cross_send, cross_recv, load_sem, store_sem = take(6)
    at = Place()
    gather = Gather(at, x_ref, out_ref, send_sem, recv_sem)
    crossing = cross(at, given, taken, cross_send, cross_recv)
    rows, width = x_ref.shape
    slots = eb.shape[0]
    block = 4 * rows
    units = acts.shape[1]
    cut = units_grad.shape[1] // 3
    over = columns_loop(width, 4)

    pairs = [
        (scaled_ref, scaled),
        (act_ref, acts),
        (wd_a, wd.at[0]),
        (wd_0, wd.at[1, pl.ds(0, wd_0.shape[0])]),
        (wd_1, wd.at[1, pl.ds(wd_0.shape[0], wd_0.shape[0])]),
        (sg_ref, sg),
        (mix_ref, mixes),
        (dy_ref, dys),
    ]
    loads = [pltpu.make_async_copy(a, b, load_sem.at[j]) for j, (a, b) in enumerate(pairs)]
    for copy in loads:
        copy.start()
    greet(at, False, True)
    for copy in crossing:
        copy.start()
    gather.begin()

    def mixed_store(j):
        return pltpu.make_async_copy(
            staged.at[j % 2], mixed_part.at[pl.ds(j * block, block)], store_sem.at[j % 2]
        )

    def mixed_rows_of(j):
        some = pl.ds(j * slots, slots)

        @over
        def _(columns):
            terms = product(scaled[0, some, :], wd[0, :, columns])
            terms += product(scaled[1, some, :], wd[1, :, columns])
            eb[:, columns] = terms.astype(BF)

        if j >= 2:
            mixed_store(j - 2).wait()
        tokens = pl.ds(j * block, block)

        @over
        def _(columns):
            terms = transposed_left(disp[j], eb[:, columns])
            terms += product(acts[tokens, :], shared_out[:, columns])
            staged[j % 2, :, columns] = terms.astype(BF)

        mixed_store(j).start()

    def units_of(first, count):
        size = units_grad.shape[2]

        @pl.loop(first, first + count)
        def _(n):
            columns = pl.ds(pl.multiple_of(n * size, size), size)
            terms = product(turned[...], mixes[:, columns]).astype(BF)
            units_grad[n, 0:cut, :] = terms[:cut]
            units_grad[n, cut : 2 * cut, :] = terms[units : units + cut]
            terms = product(turned_acts[...], dys[:, columns]).astype(BF)
            units_grad[n, 2 * cut :, :] = terms[:cut]

    for copy in loads[:5]:
        copy.wait()
    for zi in range(4):
        mixed_rows_of(zi)
        if zi == 0:
            for copy in loads[5:]:
                copy.wait()
            turned[...] = sg[...].T
            turned_acts[...] = acts[...].T
        units_of(2 * zi, 2)
        gather.step(zi + 1)
    for j in (2, 3):
        mixed_store(j).wait()
    for copy in crossing:
        copy.wait()
    gather.finish()


def gather_back(x, given, dispatch, shared_out, scaled, acts, sg, wd, mix_all, dy_all, cut, cid):
    rows, width = x.shape
    length, units = acts.shape
    slots, hidden = scaled.shape[1:]
    hbm, vmem = pl.BlockSpec(memory_space=pl.ANY), pl.BlockSpec(memory_space=pltpu.VMEM)
    shape = jax.ShapeDtypeStruct
    return pl.pallas_call(
        gather_back_kernel,
        out_shape=[
            shape((length, width), BF),
            shape((length, width), BF),
            shape((8, 3 * cut, width // 8), BF),
            *[shape(a.shape, BF) for a in given],
        ],
        in_specs=[hbm, vmem, vmem] + [hbm] * 10,
        out_specs=[hbm, hbm, vmem, hbm, hbm],
        scratch_shapes=[
            pltpu.VMEM((2, slots, hidden), BF),
            pltpu.VMEM(acts.shape, BF),
            pltpu.VMEM(sg.shape, BF),
            pltpu.VMEM((2, hidden, width), BF),
            pltpu.VMEM((slots // 4, width), BF),
            pltpu.VMEM((length, width), BF),
            pltpu.VMEM((length, width), BF),
            pltpu.VMEM((2, 4 * rows, width), BF),
            pltpu.VMEM((2 * units, length), BF),
            pltpu.VMEM((units, length), BF),
            pltpu.SemaphoreType.DMA((38,)),
            pltpu.SemaphoreType.DMA((30,)),
            pltpu.SemaphoreType.DMA((2,)),
            pltpu.SemaphoreType.DMA((2,)),
            pltpu.SemaphoreType.DMA((8,)),
            pltpu.SemaphoreType.DMA((2,)),
        ],
        compiler_params=pltpu.CompilerParams(
            collective_id=cid, has_side_effects=True, vmem_limit_bytes=60 * 1024 * 1024
        ),
    )(x, dispatch, shared_out, scaled, acts, sg, *wd, mix_all, dy_all, *given)


class Home:
    def __init__(self, at, arrays, outs, mine, got, load_sem, x_send, x_recv, z_send, z_recv):
        self.at, self.outs, self.mine, self.got = at, outs, mine, got
        self.z_send, self.z_recv = z_send, z_recv
        there = (1 - at.x) * 4
        self.loads, self.crossing, self.keep = {}, {}, []
        self.count = len(arrays)
        for m, array in enumerate(arrays):
            for k in range(4):
                spot, j = at.zs[k], m * 4 + k
                self.loads[m, k] = pltpu.make_async_copy(
                    array.at[at.x * 4 + spot], mine[m].at[spot], load_sem.at[m * 5 + k]
                )
                self.crossing[m, k] = remote(
                    array.at[there + spot],
                    got[m].at[spot],
                    x_send.at[j],
                    x_recv.at[j],
                    at.device(ox=at.dx),
                )
            self.keep.append(
                pltpu.make_async_copy(mine[m].at[at.z], outs[m].at[at.z], load_sem.at[m * 5 + 4])
            )

    def start(self):
        for k in (3, 2, 1, 0):
            for m in range(self.count):
                self.loads[m, k].start()
                self.crossing[m, k].start()

    def line(self, k):
        spot = self.at.zs[k]
        for m in range(self.count):
            mine, got = self.mine[m], self.got[m]
            self.loads[m, k].wait()
            self.crossing[m, k].wait_recv()

            @pl.loop(0, mine.shape[1] // 16)
            def _(i):
                span = pl.ds(pl.multiple_of(i * 16, 16), 16)
                both = mine[spot, span, :].astype(F32) + got[spot, span, :].astype(F32)
                mine[spot, span, :] = both.astype(BF)

            (self.copy(m, k) if k else self.keep[m]).start()

    def copy(self, m, k):
        at = self.at
        return remote(
            self.mine[m].at[at.zs[k]],
            self.outs[m].at[at.z],
            self.z_send.at[m * 3 + k - 1],
            self.z_recv.at[m * 4 + at.z],
            at.device(zi=k),
        )

    def finish(self):
        at = self.at
        for m in range(self.count):
            for k in (1, 2, 3):
                remote(
                    self.mine[m].at[at.z],
                    self.outs[m].at[at.zs[k]],
                    self.z_send.at[m * 3 + k - 1],
                    self.z_recv.at[m * 4 + at.zs[k]],
                    at.device(zi=k),
                ).wait_recv()
                self.copy(m, k).wait_send()
            self.keep[m].wait()
        for copy in self.crossing.values():
            copy.wait_send()


class Share:
    def __init__(self, at, ref, out, send_sem, recv_sem):
        self.at, rows = at, ref.shape[0]
        spot = lambda oe: out.at[pl.ds(pl.multiple_of((at.e + oe) * rows, rows), rows)]
        f_dev, s_dev = at.device(oe=at.dy), at.device(oe=at.dc)
        self.ref, self.place = ref, spot(0)
        self.far = remote(ref, spot(0), send_sem.at[0], recv_sem.at[0], f_dev)
        self.near = remote(ref, spot(0), send_sem.at[1], recv_sem.at[1], s_dev)
        self.over = remote(spot(at.dy), spot(at.dy), send_sem.at[2], recv_sem.at[2], s_dev)

    def start(self):
        for copy in (self.far, self.near):
            copy.start()
        keep(self.ref, self.place)

    def forward(self):
        self.far.wait_recv()
        self.over.start()

    def finish(self):
        self.far.wait_send()
        self.near.wait()
        self.over.wait()


def last_scatter_kernel(*refs):
    refs = list(refs)

    def take(count):
        taken = refs[:count]
        del refs[:count]
        return taken

    in_ref, g_ref, u_ref, scaled_ref, picked_ref, dy_ref, mixed_ref, given = take(8)
    halves, home_refs = take(5), take(3)
    out_ref, taken, grad_gate, grad_up, grad_down, mixed_out = take(6)
    home_outs = take(3)
    right, left, other, grad, turned = take(5)
    mine, got = take(3), take(3)
    buffers = take(6)
    first_sem, cross_send, cross_recv, load_sem, store_sem = take(5)
    home_sems, share_sems = take(5), take(2)
    at = Place()
    greet(at, True)
    total = Scatter(at, *buffers, out_ref)
    acc = buffers[0]
    rows, width = acc.shape[1:]
    part = given.shape[0]
    crossing = cross(at, [given], [taken], cross_send, cross_recv)[0]
    home = Home(at, home_refs, home_outs, mine, got, *home_sems)
    sharing = Share(at, mixed_ref, mixed_out, *share_sems)

    def rows_of(rank):
        return in_ref.at[pl.ds(pl.multiple_of(rank * rows, rows), rows)]

    order = [(f, zi) for f in (1, 0) for zi in (3, 2, 1, 0)]
    firsts = {}
    for f, zi in order:
        k = f * 4 + zi
        total.to_twin(rows_of(at.shard(f * at.dy + at.dc, zi)), f, zi)
        firsts[k] = pltpu.make_async_copy(
            rows_of(at.shard(f * at.dy, zi)), acc.at[k], first_sem.at[k]
        )
        firsts[k].start()
    home.start()
    crossing.start()
    pairs = [
        (picked_ref, right.at[0]),
        (dy_ref, right.at[1]),
        (g_ref.at[0], left.at[0]),
        (u_ref.at[0], left.at[1]),
        (scaled_ref.at[0], left.at[2]),
    ]
    pairs += [
        (ref, other.at[j // 2 % 2, pl.ds(j % 2 * part, part)])
        for j, ref in enumerate(halves + [taken])
    ]
    loads = [pltpu.make_async_copy(a, b, load_sem.at[j]) for j, (a, b) in enumerate(pairs)]
    for copy in loads[:9]:
        copy.start()

    def store(m):
        ref = (grad_gate, grad_up, grad_down)[m]
        return pltpu.make_async_copy(grad.at[m % 2], ref, store_sem.at[m])

    def gradient(m, half=None):
        turned[...] = left[m].T
        span = slice(None) if half is None else pl.ds(half * part, part)

        @columns_loop(width, 8)
        def _(columns):
            terms = product(turned[span, :], right[m // 2, :, columns])
            grad[m % 2, span, columns] = terms + other[m % 2, span, columns].astype(F32)

        if half != 0:
            store(m).start()

    for zi in (3, 2, 1, 0):
        firsts[4 + zi].wait()
        total.first(zi)
    sharing.start()
    for copy in loads[:9]:
        copy.wait()
    for m in (3, 2, 1, 0):
        firsts[m].wait()
    gradient(0)
    loads[9].start()
    total.second(3, "end")
    home.line(3)
    total.second(3, "middle")
    total.second(2, "end")
    home.line(2)
    gradient(1)
    total.second(2, "middle")
    total.second(1, "end")
    home.line(1)
    total.second(1, "middle")
    home.line(0)
    sharing.forward()
    loads[9].wait()
    store(0).wait()
    gradient(2, 0)
    total.second(0)
    crossing.wait_recv()
    loads[10].start()
    loads[10].wait()
    gradient(2, 1)
    home.finish()
    sharing.finish()
    store(1).wait()
    store(2).wait()
    crossing.wait_send()
    total.finish()


def last_rows(x, g, u, scaled, picked, picked_dy, home, mixed_own, given, halves, cid):
    rows, width = x.shape[0] // 16, x.shape[1]
    slots, hidden = g.shape[1:]
    hbm, vmem = pl.BlockSpec(memory_space=pl.ANY), pl.BlockSpec(memory_space=pltpu.VMEM)
    shape, sems = jax.ShapeDtypeStruct, lambda n: pltpu.SemaphoreType.DMA((n,))
    return pl.pallas_call(
        last_scatter_kernel,
        out_shape=[
            shape((rows, width), F32),
            shape(given.shape, BF),
            *[shape((hidden, width), F32)] * 3,
            shape((4 * rows, width), BF),
            *[shape((4,) + a.shape[1:], BF) for a in home],
        ],
        in_specs=[hbm] * 16,
        out_specs=[vmem] + [hbm] * 8,
        scratch_shapes=[
            pltpu.VMEM((2, slots, width), BF),
            pltpu.VMEM((3, slots, hidden), BF),
            pltpu.VMEM((2, hidden, width), BF),
            pltpu.VMEM((2, hidden, width), F32),
            pltpu.VMEM((hidden, slots), BF),
            *[pltpu.VMEM((4,) + a.shape[1:], BF) for a in home] * 2,
            *scatter_buffers(rows, width),
            sems(8),
            sems(1),
            sems(1),
            sems(11),
            sems(3),
            sems(15),
            sems(12),
            sems(12),
            sems(9),
            sems(12),
            sems(3),
            sems(3),
        ],
        compiler_params=pltpu.CompilerParams(
            collective_id=cid, has_side_effects=True, vmem_limit_bytes=62 * 1024 * 1024
        ),
    )(x, g, u, scaled, picked, picked_dy, mixed_own, given, *halves, *home)


def end_kernel(tokens_ref, gain_ref, small_ref, out_ref, gain_out, small_out, *scratch):
    gain_got, gain_sum, gain_all, small_all = scratch[:4]
    share_sems = scratch[4:6]
    gain_send, gain_recv, sum_send, sum_recv, small_send, small_recv = scratch[6:]
    at = Place()
    barrier = pltpu.get_barrier_semaphore()
    blocks = [(at.device(ox=ox, zi=k), m * 4 + k) for m, ox in enumerate((0, at.dx)) for k in range(4)]
    group = [at.device(oe=oe) for oe in (at.dy, at.dc, at.dy + at.dc)]
    for peer in [device for device, j in blocks[1:]] + group:
        pl.semaphore_signal(barrier, inc=1, device_id=peer, device_id_type=MESH)
    pl.semaphore_wait(barrier, 10)
    sharing = Share(at, tokens_ref, out_ref, *share_sems)
    own = at.x * 4 + at.z
    copies = []
    for device, j in blocks[1:]:
        copy = remote(
            gain_ref.at[device[0] * 4 + device[1]],
            gain_got.at[own],
            gain_send.at[j],
            gain_recv.at[own],
            device,
        )
        copy.start()
        copies.append(copy)
    for j, device in enumerate(group):
        copy = remote(small_ref, small_all.at[j], small_send.at[j], small_recv.at[j], device)
        copy.start()
        copies.append(copy)
    sharing.start()
    gain = gain_ref[own]
    for device, j in blocks[1:]:
        there = device[0] * 4 + device[1]
        remote(
            gain_ref.at[0], gain_got.at[there], gain_send.at[j], gain_recv.at[there], device
        ).wait_recv()
        gain = gain + gain_got[there]
    gain_sum[...] = gain
    for j, device in enumerate(group):
        copy = remote(gain_sum, gain_all.at[j], sum_send.at[j], sum_recv.at[j], device)
        copy.start()
        copies.append(copy)
    small = small_ref[...]
    for j in range(3):
        copies[7 + j].wait_recv()
        copies[10 + j].wait_recv()
        small = small + small_all[j]
        gain = gain + gain_all[j]
    gain_out[...] = gain
    small_out[...] = small
    sharing.forward()
    sharing.finish()
    for copy in copies:
        copy.wait_send()


def end(tokens_own, gain_part, small, cid):
    rows, width = tokens_own.shape
    vmem, hbm = pl.BlockSpec(memory_space=pltpu.VMEM), pl.BlockSpec(memory_space=pl.ANY)
    shape, sems = jax.ShapeDtypeStruct, lambda n: pltpu.SemaphoreType.DMA((n,))
    return pl.pallas_call(
        end_kernel,
        out_shape=[
            shape((4 * rows, width), tokens_own.dtype),
            shape(gain_part.shape[1:], F32),
            shape(small.shape, F32),
        ],
        in_specs=[hbm, vmem, vmem],
        out_specs=[hbm, vmem, vmem],
        scratch_shapes=[
            pltpu.VMEM(gain_part.shape, F32),
            pltpu.VMEM(gain_part.shape[1:], F32),
            pltpu.VMEM((3,) + gain_part.shape[1:], F32),
            pltpu.VMEM((3,) + small.shape, F32),
            sems(3),
            sems(3),
            sems(8),
            sems(8),
            sems(3),
            sems(3),
            sems(3),
            sems(3),
        ],
        compiler_params=pltpu.CompilerParams(collective_id=cid, has_side_effects=True),
    )(tokens_own, gain_part, small)


def front_kernel(scale, *refs):
    refs = list(refs)

    def take(count):
        taken = refs[:count]
        del refs[:count]
        return taken

    dy_ref, tokens_ref, units, given, gain, w_qkv, w_out_blocks, tables = take(8)
    dy_out, units_out, taken, normed_out, part_out, q_out, k_out, v_out, heads_out, lse_out = take(10)
    w_out, w_qkv_turned = take(2)
    rows_in, normed, staged = take(3)
    send_sem, recv_sem, swap_send, swap_recv = take(4)
    cross_send, cross_recv, in_sem, normed_sem, part_sem = take(5)
    at = Place()
    greet(at, True)
    gather = Gather(at, dy_ref, dy_out, send_sem, recv_sem, True)
    swap_in = Exchange(at, [units], [units_out], swap_send, swap_recv)
    crossing = cross(at, [given], [taken], cross_send, cross_recv, (taken.shape[0],))[0]
    length, width = tokens_ref.shape
    block = length // 4
    step = 256
    over = columns_loop(width, 4)

    def rows_load(j):
        return pltpu.make_async_copy(
            tokens_ref.at[pl.ds(j * block, block)], rows_in.at[j % 2], in_sem.at[j % 2]
        )

    def normed_store(j):
        return pltpu.make_async_copy(
            normed.at[j % 2], normed_out.at[pl.ds(j * block, block)], normed_sem.at[j % 2]
        )

    def part_store(i):
        return pltpu.make_async_copy(
            staged.at[i % 2], part_out.at[pl.ds(i * step, step)], part_sem.at[i % 2]
        )

    def turn_rows(values, here):
        other = pltpu.roll(values, HDIM // 2, 1)
        return (values * tables[0, here, :] - other * tables[1, here, :]).astype(BF)

    def project(j):
        rows_load(j).wait()
        if j >= 2:
            normed_store(j - 2).wait()

        @pl.loop(0, block // 64)
        def _(n):
            span = pl.ds(pl.multiple_of(n * 64, 64), 64)
            values = rows_in[j % 2, span, :].astype(F32)
            size = jnp.mean(values * values, axis=-1, keepdims=True)
            normed[j % 2, span, :] = (values * lax.rsqrt(size + EPSILON) * gain[0:1, :]).astype(BF)

        normed_store(j).start()
        if j < 2:
            rows_load(j + 2).start()
        here = pl.ds(j * block, block)
        qkv = product(normed[j % 2], w_qkv[...])
        q_out[here, :] = turn_rows(qkv[:, :HDIM], here)
        k_out[here, :] = turn_rows(qkv[:, HDIM : 2 * HDIM], here)
        v_out[here, :] = qkv[:, 2 * HDIM :].astype(BF)

    def attend_rows(i):
        seen = (i + 1) * step
        here = pl.ds(i * step, step)
        scores = transposed_right(q_out[here, :], k_out[0:seen, :]) * scale
        row_at = lax.broadcasted_iota(jnp.int32, scores.shape, 0) + i * step
        col_at = lax.broadcasted_iota(jnp.int32, scores.shape, 1)
        scores = jnp.where(row_at >= col_at, scores, MASKED)
        top = jnp.max(scores, axis=-1, keepdims=True)
        powers = jnp.exp(scores - top)
        lse = top + jnp.log(jnp.sum(powers, axis=-1, keepdims=True))
        probs = jnp.exp(scores - lse).astype(BF)
        heads_out[here, :] = product(probs, v_out[0:seen, :]).astype(BF)
        lse_out[here, :] = jnp.broadcast_to(lse, (step, HDIM))
        if i >= 2:
            part_store(i - 2).wait()

        @over
        def _(columns):
            staged[i % 2, :, columns] = product(heads_out[here, :], w_out[:, columns]).astype(BF)

        part_store(i).start()

    gather.begin()
    for zi in (1, 2, 3):
        swap_in.along(zi)
    swap_in.start()
    crossing.start()
    rows_load(0).start()
    rows_load(1).start()
    size = w_out_blocks.shape[2]
    for d in range(8):
        w_out[:, d * size : (d + 1) * size] = w_out_blocks[d]
    w_qkv_turned[...] = w_qkv[...].T
    project(0)
    project(1)
    attend_rows(0)
    gather.step(1)
    project(2)
    attend_rows(1)
    attend_rows(2)
    gather.step(2)
    swap_in.forward(1)
    project(3)
    attend_rows(3)
    attend_rows(4)
    gather.step(3)
    swap_in.forward(2)
    attend_rows(5)
    attend_rows(6)
    attend_rows(7)
    gather.step(4)
    swap_in.forward(3)
    for j in (2, 3):
        normed_store(j).wait()
    for i in (6, 7):
        part_store(i).wait()
    swap_in.finish()
    crossing.wait()
    gather.finish()


def front(dy, tokens_all, units, given, gain, w_qkv, w_out, tables, cid):
    length, width = tokens_all.shape
    hbm, vmem = pl.BlockSpec(memory_space=pl.ANY), pl.BlockSpec(memory_space=pltpu.VMEM)
    shape, sems = jax.ShapeDtypeStruct, lambda n: pltpu.SemaphoreType.DMA((n,))
    return pl.pallas_call(
        functools.partial(front_kernel, HDIM ** (-0.5)),
        out_shape=[
            shape((length, width), BF),
            shape((8,) + units.shape[1:], BF),
            half_of(given),
            shape((length, width), BF),
            shape((length, width), BF),
            *[shape((length, HDIM), BF)] * 4,
            shape((length, HDIM), F32),
            shape((HDIM, width), BF),
            shape((3 * HDIM, width), BF),
        ],
        in_specs=[hbm] * 4 + [vmem] * 4,
        out_specs=[hbm] * 5 + [vmem] * 7,
        scratch_shapes=[
            pltpu.VMEM((2, length // 4, width), BF),
            pltpu.VMEM((2, length // 4, width), BF),
            pltpu.VMEM((2, 256, width), BF),
            sems(38),
            sems(30),
            sems(7),
            sems(8),
            sems(1),
            sems(1),
            sems(2),
            sems(2),
            sems(2),
        ],
        compiler_params=pltpu.CompilerParams(
            collective_id=cid, has_side_effects=True, vmem_limit_bytes=60 * 1024 * 1024
        ),
    )(dy, tokens_all, units, given, gain, w_qkv, w_out, tables)


def by_four(matrix):
    rows, columns = matrix.shape
    return matrix.reshape(rows, 4, columns // 4).transpose(1, 0, 2)


def turn_tables(length):
    inverse = 10000.0 ** (-np.arange(HDIM // 2).astype(np.float64) * 2.0 / HDIM)
    angles = np.arange(length).astype(np.float64)[:, None] * inverse[None, :]
    return np.cos(angles).astype(np.float32), np.sin(angles).astype(np.float32)


def fast_body(
    tokens,
    routes,
    norm_attn,
    w_query,
    w_key,
    w_value,
    w_out,
    norm_mix,
    w_router,
    shared_gate,
    shared_up,
    shared_down,
    expert_gate,
    expert_up,
    expert_down,
    out_grad,
):
    dp, ctx, exp = lax.axis_index("dp"), lax.axis_index("ctx"), lax.axis_index("exp")
    rows_here, width = tokens.shape[1], tokens.shape[2]
    quarter = rows_here // 4
    length = rows_here * 4
    experts = w_router.shape[1]
    capacity = quarter * TOPK * 4 // (3 * experts)
    groups = length // quarter
    dense = w_query.shape[0]
    cut = shared_gate.shape[1] // 4
    wide = 256
    start = exp * quarter
    tokens_own = lax.dynamic_slice_in_dim(tokens[0], start, quarter, 0)
    dy_own = lax.dynamic_slice_in_dim(out_grad[0], start, quarter, 0)

    route_rows = routes[0].T
    theirs = jnp.arange(4, dtype=jnp.int32)[:, None, None] * 4 + exp
    named = jnp.any(route_rows[None] == theirs, axis=1).astype(BF).reshape(4, 2, dense)
    little = jnp.concatenate([w_router.T, norm_attn[None], norm_mix[None]], axis=0)
    little = jnp.concatenate([jnp.broadcast_to(little[None], (4,) + little.shape), named], axis=1)
    few = -(-little.shape[1] // 16) * 16
    little = jnp.pad(little, ((0, 0), (0, few - little.shape[1]), (0, 0)))
    sent_head = jnp.concatenate([by_four(w_query), by_four(w_key), by_four(w_value)], axis=2)
    sent_out = w_out.reshape(4, HDIM, dense)
    sent_units = jnp.stack([shared_gate.T, shared_up.T, shared_down], axis=0)
    sent_units = sent_units.reshape(3, 4, cut, dense).transpose(1, 0, 2, 3).reshape(4, 3 * cut, dense)
    own_gate, own_up, own_down = expert_gate[0].T, expert_up[0].T, expert_down[0]
    part = own_gate.shape[0] // 2
    tokens_all, early, early_out, early_little, gate_0 = all_rows(
        tokens[0], True, 1, (sent_head, sent_out, little), (own_gate,), (0,)
    )
    w_qkv = early.reshape(width, 3 * HDIM)
    early_little = early_little.transpose(1, 0, 2)
    router_rows = early_little[:experts].reshape(experts, width)
    attention_gain = early_little[experts].reshape(width).astype(F32)
    mixer_gain = early_little[experts + 1].reshape(width).astype(F32)
    hits = early_little[experts + 2 : experts + 4].transpose(1, 0, 2).reshape(2, length)
    hits = lax.dynamic_index_in_dim(hits, dp, 0, False).astype(F32).reshape(groups, quarter)

    cosine, sine = turn_tables(length)
    tables = np.stack(
        [np.concatenate([cosine, cosine], axis=1), np.concatenate([sine, -sine], axis=1)]
    )
    dy_all, late, gate_1, normed, attn_part, query, key, value, heads_out, lse, w_out_head, w_qkv_turned = front(
        out_grad[0],
        tokens_all,
        sent_units,
        own_gate,
        jnp.broadcast_to(attention_gain[None], (8, width)),
        w_qkv,
        early_out,
        tables,
        2,
    )
    attn, up_0, up_1 = own_rows(attn_part, 3, (own_up, own_up), (0, part))
    middle = tokens_own.astype(F32) + attn
    normed_own = rms_scale(middle, mixer_gain).astype(BF)

    mine = ctx * 4 + exp
    place = jnp.cumsum(hits, axis=1) - 1.0
    first = (jnp.arange(groups) % 4 * capacity).astype(F32)[:, None]
    place = jnp.where(hits > 0.5, place + first, -1.0).reshape(4, 1, 4 * quarter)
    blocks = place == jnp.arange(4 * capacity).astype(F32)[None, :, None]
    blocks = blocks.astype(BF)
    router_wide = jnp.pad(router_rows, ((0, HDIM - experts), (0, 0)))
    (
        mix_all,
        picked,
        picked_dy,
        scaled,
        g_back,
        u_back,
        gate_back,
        shared_act,
        shared_gu_back,
        down_0,
        down_1,
        shared_in,
        shared_out,
    ) = expert_rows(
        normed_own,
        dy_all,
        blocks,
        router_wide,
        experts,
        late,
        wide,
        (own_gate, own_up, own_down, gate_0, gate_1, up_0, up_1),
        (own_down, own_down),
        4,
    )
    other_down = (down_0, down_1)

    mix_back, gate_0, gate_1, up_0, up_1, down_0, down_1 = expert_back(
        blocks,
        gate_back,
        shared_in,
        g_back,
        u_back,
        shared_gu_back,
        picked,
        picked_dy,
        scaled,
        (own_gate, own_up, gate_0, gate_1, up_0, up_1),
        5,
    )
    gate_back_own = mix_back[:, width : width + experts]
    mix_back = mix_back[:, :width]

    router_own = jax.nn.softmax(transposed_right(normed_own, router_rows), axis=-1)
    logit_back = (
        router_own * (gate_back_own - jnp.sum(router_own * gate_back_own, axis=-1, keepdims=True))
    ).astype(BF)
    router_part = transposed_left(logit_back, normed_own)

    mix_back = mix_back + product(logit_back, router_rows)
    _, norm_mix_back = jax.vjp(rms_scale, middle, mixer_gain)
    middle_norm_back, gain_mix_part = norm_mix_back(mix_back)
    middle_back = dy_own.astype(F32) + middle_norm_back
    attn_back = middle_back.astype(BF)
    attn_back_all, mixed_part, units_part, gate_1, up_0 = gather_back(
        attn_back,
        (gate_1, up_0),
        blocks,
        shared_out,
        scaled,
        shared_act,
        shared_gu_back,
        (own_down, *other_down),
        mix_all,
        dy_all,
        cut,
        7,
    )
    mixed_sum, normed_part, head_part, up_1, down_0 = mixed_rows(
        w_out_head,
        w_qkv_turned,
        tables,
        query,
        key,
        value,
        lse,
        heads_out,
        mixed_part,
        attn_back_all,
        normed,
        (up_1, down_0),
        9,
    )
    mixed_own = (middle + mixed_sum).astype(BF)
    small_part = jnp.concatenate([gain_mix_part[None], router_part], axis=0).astype(BF)
    small_rows = -(-(experts + 1) // 16) * 16
    small_part = jnp.pad(small_part, ((0, small_rows - experts - 1), (0, 0)))
    small_part = small_part.reshape(small_rows, 8, dense).transpose(1, 0, 2)
    normed_back, _, gate_grad, up_grad, down_grad, mixed, head_grad, units_grad, small = last_rows(
        normed_part,
        g_back,
        u_back,
        scaled,
        picked,
        picked_dy,
        (head_part, units_part, small_part),
        mixed_own,
        down_1,
        (gate_0, gate_1, up_0, up_1, down_0),
        8,
    )
    head_grad, units_grad = head_grad.astype(F32), units_grad.astype(F32)
    small_part = jnp.sum(small.astype(F32), axis=0)
    _, norm_attn_back = jax.vjp(rms_scale, tokens_own.astype(F32), attention_gain)
    input_norm_back, gain_attn_part = norm_attn_back(normed_back)
    tokens_back_own = (middle_back + input_norm_back).astype(BF)

    gain_part = jnp.pad(gain_attn_part.reshape(8, 1, dense), ((0, 0), (0, 7), (0, 0)))
    tokens_back, gain_attn, small = end(tokens_back_own, gain_part, small_part, 6)

    def columns_of(parts):
        return parts.transpose(2, 0, 1).reshape(dense, -1)

    def rows_of(parts):
        return parts.reshape(-1, dense)

    return (
        mixed[None],
        tokens_back[None],
        gain_attn[0],
        columns_of(head_grad[:, :HDIM]),
        columns_of(head_grad[:, HDIM : 2 * HDIM]),
        columns_of(head_grad[:, 2 * HDIM : 3 * HDIM]),
        rows_of(head_grad[:, 3 * HDIM :]),
        small[0],
        small[1 : experts + 1].T,
        rows_of(units_grad[:, :cut]).T,
        rows_of(units_grad[:, cut : 2 * cut]).T,
        rows_of(units_grad[:, 2 * cut :]),
        gate_grad.T[None],
        up_grad.T[None],
        down_grad[None],
    )


def solution(mesh):
    sizes = dict(mesh.shape)

    def chosen(*args):
        heads = args[3].shape[1] * sizes["exp"] // HDIM
        one_head_each = heads == sizes["ctx"] * sizes["exp"]
        built_for = (sizes["dp"], sizes["ctx"], sizes["exp"]) == (2, 4, 4)
        return fast_body(*args) if one_head_each and built_for else body(*args)

    in_specs = (
        P("dp", "ctx", None),
        P("dp", "ctx", None),
        P(("dp", "ctx")),
        P(("dp", "ctx"), "exp"),
        P(("dp", "ctx"), "exp"),
        P(("dp", "ctx"), "exp"),
        P("exp", ("dp", "ctx")),
        P(("dp", "ctx")),
        P(("dp", "ctx"), None),
        P(("dp", "ctx"), "exp"),
        P(("dp", "ctx"), "exp"),
        P("exp", ("dp", "ctx")),
        P(("ctx", "exp"), None, "dp"),
        P(("ctx", "exp"), None, "dp"),
        P(("ctx", "exp"), "dp", None),
        P("dp", "ctx", None),
    )
    out_specs = (
        P("dp", "ctx", None),
        P("dp", "ctx", None),
        P(("dp", "ctx")),
        P(("dp", "ctx"), "exp"),
        P(("dp", "ctx"), "exp"),
        P(("dp", "ctx"), "exp"),
        P("exp", ("dp", "ctx")),
        P(("dp", "ctx")),
        P(("dp", "ctx"), None),
        P(("dp", "ctx"), "exp"),
        P(("dp", "ctx"), "exp"),
        P("exp", ("dp", "ctx")),
        P(("ctx", "exp"), None, "dp"),
        P(("ctx", "exp"), None, "dp"),
        P(("ctx", "exp"), "dp", None),
    )
    return jax.shard_map(chosen, mesh=mesh, in_specs=in_specs, out_specs=out_specs, check_vma=False)
```

```python
import functools

import jax
import jax.numpy as jnp
import numpy as np
from jax import lax
from jax.experimental import pallas as pl
from jax.experimental.pallas import tpu as pltpu
from jax.sharding import PartitionSpec as P

HDIM = 128
TOPK = 6


EPSILON = 1e-06
MASKED = -1e30
HIGHEST = lax.Precision.HIGHEST


def rms_scale(values, gain_row):
    return (
        values * lax.rsqrt(jnp.mean(values * values, axis=-1, keepdims=True) + EPSILON) * gain_row
    )


def rope_tables(positions, rope_width):
    inverse = 10000.0 ** (-jnp.arange(rope_width // 2).astype(jnp.float32) * 2.0 / rope_width)
    angles = positions.astype(jnp.float32)[:, None] * inverse[None, :]
    return (jnp.cos(angles), jnp.sin(angles))


def rotate(values, cosine, sine_table):
    half_size = values.shape[-1] // 2
    first_half = values[..., :half_size]
    second = values[..., half_size:]
    cosine = cosine[:, None, :]
    sine_table = sine_table[:, None, :]
    return jnp.concatenate(
        [first_half * cosine - second * sine_table, second * cosine + first_half * sine_table],
        axis=-1,
    )


def silu_mix(gate_rows, up_rows):
    return jax.nn.silu(gate_rows) * up_rows


def product(left_side, right_side):
    return jnp.dot(left_side, right_side, preferred_element_type=jnp.float32)


def transposed_left(left_side, right_side):
    return lax.dot_general(
        left_side, right_side, (((0,), (0,)), ((), ())), preferred_element_type=jnp.float32
    )


def transposed_right(left_side, right_side):
    return lax.dot_general(
        left_side, right_side, (((1,), (1,)), ((), ())), preferred_element_type=jnp.float32
    )


def place_rows(part, start_row, total_rows):
    blank = jnp.zeros((total_rows, part.shape[1]), jnp.float32)
    return lax.dynamic_update_slice_in_dim(blank, part, start_row, 0)


def to_owners(buffer):
    copies = lax.axis_size("dp")
    widened = jnp.broadcast_to(buffer[None], (copies,) + buffer.shape)
    widened = widened.reshape((copies * buffer.shape[0],) + buffer.shape[1:])
    return lax.all_to_all(widened, ("dp", "ctx", "exp"), split_axis=0, concat_axis=0, tiled=True)


def values_home(partial_value):
    returned = lax.all_to_all(
        partial_value, ("dp", "ctx", "exp"), split_axis=0, concat_axis=0, tiled=True
    )
    grouped = returned.reshape((lax.axis_size("dp"), -1) + returned.shape[1:])
    return jnp.sum(grouped.astype(jnp.float32), axis=0).astype(jnp.bfloat16)


def grads_home(partial_value):
    returned = lax.all_to_all(
        partial_value.astype(jnp.bfloat16),
        ("dp", "ctx", "exp"),
        split_axis=0,
        concat_axis=0,
        tiled=True,
    ).astype(partial_value.dtype)
    grouped = returned.reshape((lax.axis_size("dp"), -1) + returned.shape[1:])
    return jnp.sum(grouped, axis=0)


def body(
    tokens,
    routes,
    norm_attn,
    w_query,
    w_key,
    w_value,
    w_out,
    norm_mix,
    w_router,
    shared_gate,
    shared_up,
    shared_down,
    expert_gate,
    expert_up,
    expert_down,
    out_grad,
):
    gathered = (
        lax.all_gather(norm_attn, ("dp", "ctx"), axis=0, tiled=True),
        lax.all_gather(w_query, ("dp", "ctx"), axis=0, tiled=True),
        lax.all_gather(w_key, ("dp", "ctx"), axis=0, tiled=True),
        lax.all_gather(w_value, ("dp", "ctx"), axis=0, tiled=True),
        lax.all_gather(w_out, ("dp", "ctx"), axis=1, tiled=True),
        lax.all_gather(norm_mix, ("dp", "ctx"), axis=0, tiled=True),
        lax.all_gather(w_router, ("dp", "ctx"), axis=0, tiled=True),
        lax.all_gather(shared_gate, ("dp", "ctx"), axis=0, tiled=True),
        lax.all_gather(shared_up, ("dp", "ctx"), axis=0, tiled=True),
        lax.all_gather(shared_down, ("dp", "ctx"), axis=1, tiled=True),
    )
    (
        attention_gain,
        query_matrix,
        key_matrix,
        value_matrix,
        output_matrix,
        mixer_gain,
        router_matrix,
        shared_gate_matrix,
        shared_up_matrix,
        shared_down_matrix,
    ) = gathered
    rows_here = tokens.shape[1]
    model_width = tokens.shape[2]
    heads_here = query_matrix.shape[1] // HDIM
    quarter = rows_here // lax.axis_size("exp")
    start_row = lax.axis_index("exp") * quarter
    layer_input = tokens[0].astype(jnp.float32)
    grad_rows = out_grad[0]
    grad_float = grad_rows.astype(jnp.float32)
    seq_length = rows_here * lax.axis_size("ctx")
    positions = lax.axis_index("ctx") * rows_here + jnp.arange(rows_here, dtype=jnp.int32)
    cosine, sine_table = rope_tables(positions, HDIM)
    visible = positions[:, None] >= jnp.arange(seq_length, dtype=jnp.int32)[None, :]
    scale = HDIM ** (-0.5)
    head_shape = (rows_here, heads_here, HDIM)
    normed = rms_scale(layer_input, attention_gain).astype(jnp.bfloat16)
    query_rot = rotate(
        product(normed, query_matrix).reshape(head_shape), cosine, sine_table
    ).astype(jnp.bfloat16)
    key_rot = (
        rotate(product(normed, key_matrix).reshape(head_shape), cosine, sine_table)
        .astype(jnp.bfloat16)
        .reshape(rows_here, -1)
    )
    value_low = product(normed, value_matrix).astype(jnp.bfloat16)
    key_all, value_all = (
        lax.all_gather(key_rot, "ctx", axis=0, tiled=True),
        lax.all_gather(value_low, "ctx", axis=0, tiled=True),
    )
    key_heads = key_all.reshape(seq_length, heads_here, HDIM)
    value_heads = value_all.reshape(seq_length, heads_here, HDIM)

    def attention_scores():
        scores = (
            jnp.einsum("qhd,khd->hqk", query_rot, key_heads, preferred_element_type=jnp.float32)
            * scale
        )
        return jnp.where(visible[None], scores, MASKED)

    scores = attention_scores()
    largest = jnp.max(scores, axis=-1, keepdims=True)
    log_total = largest + jnp.log(jnp.sum(jnp.exp(scores - largest), axis=-1, keepdims=True))
    weights_low = jnp.exp(scores - log_total).astype(jnp.bfloat16)
    heads_out = (
        jnp.einsum("hqk,khd->qhd", weights_low, value_heads, preferred_element_type=jnp.float32)
        .reshape(rows_here, -1)
        .astype(jnp.bfloat16)
    )
    attn_total = lax.psum(product(heads_out, output_matrix), "exp")
    middle = layer_input + attn_total
    normed_mix = rms_scale(middle, mixer_gain).astype(jnp.bfloat16)
    normed_quarter = lax.dynamic_slice_in_dim(normed_mix, start_row, quarter, 0)
    route_quarter = lax.dynamic_slice_in_dim(routes[0], start_row, quarter, 0)
    grad_quarter = lax.dynamic_slice_in_dim(grad_rows, start_row, quarter, 0)
    logits = product(normed_quarter, router_matrix)
    probabilities = jax.nn.softmax(logits, axis=-1)
    owners = lax.axis_size(("ctx", "exp"))
    local_experts = expert_gate.shape[0]
    experts = local_experts * owners
    capacity = max(quarter * TOPK * 4 // (3 * experts), 2)
    expert_choice_index = jnp.arange(experts, dtype=jnp.int32)
    chosen = (route_quarter[:, :, None] == expert_choice_index[None, None, :]).astype(jnp.float32)
    gates = jnp.sum(chosen * probabilities[:, None, :], axis=-1)
    route_flat = route_quarter.reshape(-1)
    expert_hits = (route_flat[:, None] == expert_choice_index[None, :]).astype(jnp.int32)
    slot_index = jnp.sum(jnp.cumsum(expert_hits, axis=0) * expert_hits, axis=1) - 1
    slot_place = route_flat * capacity + slot_index
    matches = (
        jnp.arange(experts * capacity, dtype=jnp.int32)[:, None] == slot_place[None, :]
    ).astype(jnp.float32)
    dispatch = jnp.sum(matches.reshape(experts * capacity, quarter, TOPK), axis=2).astype(
        jnp.bfloat16
    )
    slot_gates = jnp.dot(matches, gates.reshape(-1), precision=HIGHEST)
    buffer_shape = (owners, local_experts, capacity, model_width)
    outgoing = product(dispatch, normed_quarter).astype(jnp.bfloat16).reshape(buffer_shape)
    arrived = to_owners(outgoing)
    gate_hidden = jnp.einsum(
        "sicd,idf->sicf", arrived, expert_gate, preferred_element_type=jnp.float32
    )
    up_hidden = jnp.einsum("sicd,idf->sicf", arrived, expert_up, preferred_element_type=jnp.float32)
    expert_act = silu_mix(gate_hidden, up_hidden).astype(jnp.bfloat16)
    partial_value = jnp.einsum(
        "sicf,ifd->sicd", expert_act, expert_down, preferred_element_type=jnp.float32
    ).astype(jnp.bfloat16)
    expert_values = values_home(partial_value).reshape(experts * capacity, model_width)
    route_values = expert_values[slot_place].astype(jnp.float32).reshape(quarter, TOPK, model_width)
    combined = jnp.sum(route_values * gates[:, :, None], axis=1)
    shared_gate_rows = product(normed_mix, shared_gate_matrix)
    shared_up_rows = product(normed_mix, shared_up_matrix)
    shared_act = silu_mix(shared_gate_rows, shared_up_rows).astype(jnp.bfloat16)
    branch_part = product(shared_act, shared_down_matrix) + place_rows(
        combined, start_row, rows_here
    )
    result = middle + lax.psum(branch_part.astype(jnp.bfloat16), "exp").astype(jnp.float32)
    grad_slots = (
        (product(dispatch, grad_quarter) * slot_gates[:, None])
        .astype(jnp.bfloat16)
        .reshape(buffer_shape)
    )
    grad_arrived = to_owners(grad_slots)
    act_grad = jnp.einsum(
        "sicd,ifd->sicf", grad_arrived, expert_down, preferred_element_type=jnp.float32
    )
    down_grad = jnp.einsum(
        "sicf,sicd->ifd", expert_act, grad_arrived, preferred_element_type=jnp.float32
    )
    _, mix_back = jax.vjp(silu_mix, gate_hidden, up_hidden)
    gate_back, up_back = mix_back(act_grad)
    gate_back = gate_back.astype(jnp.bfloat16)
    up_back = up_back.astype(jnp.bfloat16)
    gate_grad = jnp.einsum("sicd,sicf->idf", arrived, gate_back, preferred_element_type=jnp.float32)
    up_grad = jnp.einsum("sicd,sicf->idf", arrived, up_back, preferred_element_type=jnp.float32)
    input_back = jnp.einsum(
        "sicf,idf->sicd", gate_back, expert_gate, preferred_element_type=jnp.float32
    ) + jnp.einsum("sicf,idf->sicd", up_back, expert_up, preferred_element_type=jnp.float32)
    rows_back = grads_home(input_back).reshape(experts * capacity, model_width)
    moe_back = jnp.sum(rows_back[slot_place].reshape(quarter, TOPK, model_width), axis=1)
    gate_route_back = jnp.sum(route_values * grad_quarter.astype(jnp.float32)[:, None, :], axis=-1)
    prob_back = jnp.sum(chosen * gate_route_back[:, :, None], axis=1)
    _, soft_back = jax.vjp(lambda values: jax.nn.softmax(values, axis=-1), logits)
    logit_back = soft_back(prob_back)[0].astype(jnp.bfloat16)
    router_term = transposed_left(normed_quarter, logit_back)
    shared_back = transposed_right(grad_rows, shared_down_matrix)
    _, shared_mix_back = jax.vjp(silu_mix, shared_gate_rows, shared_up_rows)
    sgate_back, sup_back = shared_mix_back(shared_back)
    sgate_back = sgate_back.astype(jnp.bfloat16)
    sup_back = sup_back.astype(jnp.bfloat16)
    quarter_back = transposed_right(logit_back, router_matrix) + moe_back
    mix_part = (
        transposed_right(sgate_back, shared_gate_matrix)
        + transposed_right(sup_back, shared_up_matrix)
        + place_rows(quarter_back, start_row, rows_here)
    )
    mix_total, router_grad = (
        lax.psum(mix_part.astype(jnp.bfloat16), "exp").astype(jnp.float32),
        lax.psum(router_term.astype(jnp.bfloat16), "exp").astype(jnp.float32),
    )
    _, norm_mix_back = jax.vjp(rms_scale, middle, mixer_gain.astype(jnp.float32))
    middle_norm_back, gain_mix_grad = norm_mix_back(mix_total)
    middle_grad = grad_float + middle_norm_back
    sdown_grad = transposed_left(shared_act, grad_rows)
    sgate_grad = transposed_left(normed_mix, sgate_back)
    sup_grad = transposed_left(normed_mix, sup_back)
    attn_back = middle_grad.astype(jnp.bfloat16)
    heads_back = transposed_right(attn_back, output_matrix).astype(jnp.bfloat16).reshape(head_shape)
    weights_full = jnp.exp(attention_scores() - log_total)
    weights_again = weights_full.astype(jnp.bfloat16)
    weight_back = jnp.einsum(
        "qhd,khd->hqk", heads_back, value_heads, preferred_element_type=jnp.float32
    )
    value_term = jnp.einsum(
        "hqk,qhd->khd", weights_again, heads_back, preferred_element_type=jnp.float32
    ).reshape(seq_length, -1)
    score_back = (
        weights_full * (weight_back - jnp.sum(weights_full * weight_back, axis=-1, keepdims=True))
    ).astype(jnp.bfloat16)
    query_rot_back = (
        jnp.einsum("hqk,khd->qhd", score_back, key_heads, preferred_element_type=jnp.float32)
        * scale
    )
    key_term = (
        jnp.einsum("hqk,qhd->khd", score_back, query_rot, preferred_element_type=jnp.float32)
        * scale
    ).reshape(seq_length, -1)
    key_sum, value_sum = (
        lax.psum_scatter(
            key_term.astype(jnp.bfloat16), "ctx", scatter_dimension=0, tiled=True
        ).astype(jnp.float32),
        lax.psum_scatter(
            value_term.astype(jnp.bfloat16), "ctx", scatter_dimension=0, tiled=True
        ).astype(jnp.float32),
    )
    _, rotate_back = jax.vjp(
        lambda values: rotate(values, cosine, sine_table), jnp.zeros(head_shape, jnp.float32)
    )
    query_low = rotate_back(query_rot_back)[0].reshape(rows_here, -1).astype(jnp.bfloat16)
    key_low = (
        rotate_back(key_sum.reshape(head_shape))[0].reshape(rows_here, -1).astype(jnp.bfloat16)
    )
    value_back_low = value_sum.astype(jnp.bfloat16)
    normed_part = (
        transposed_right(query_low, query_matrix)
        + transposed_right(key_low, key_matrix)
        + transposed_right(value_back_low, value_matrix)
    )
    normed_back = lax.psum(normed_part.astype(jnp.bfloat16), "exp").astype(jnp.float32)
    _, norm_attn_back = jax.vjp(rms_scale, layer_input, attention_gain.astype(jnp.float32))
    input_norm_back, gain_attn_grad = norm_attn_back(normed_back)
    tokens_back = (middle_grad + input_norm_back).astype(jnp.bfloat16)
    out_weight_grad = transposed_left(heads_out, attn_back)
    query_grad = transposed_left(normed, query_low)
    key_grad = transposed_left(normed, key_low)
    value_grad = transposed_left(normed, value_back_low)
    all_sums = (
        lax.psum_scatter(
            gain_attn_grad.astype(jnp.bfloat16), ("dp", "ctx"), scatter_dimension=0, tiled=True
        ).astype(jnp.float32),
        lax.psum_scatter(
            query_grad.astype(jnp.bfloat16), ("dp", "ctx"), scatter_dimension=0, tiled=True
        ).astype(jnp.float32),
        lax.psum_scatter(
            key_grad.astype(jnp.bfloat16), ("dp", "ctx"), scatter_dimension=0, tiled=True
        ).astype(jnp.float32),
        lax.psum_scatter(
            value_grad.astype(jnp.bfloat16), ("dp", "ctx"), scatter_dimension=0, tiled=True
        ).astype(jnp.float32),
        lax.psum_scatter(
            out_weight_grad.astype(jnp.bfloat16), ("dp", "ctx"), scatter_dimension=1, tiled=True
        ).astype(jnp.float32),
        lax.psum_scatter(
            gain_mix_grad.astype(jnp.bfloat16), ("dp", "ctx"), scatter_dimension=0, tiled=True
        ).astype(jnp.float32),
        lax.psum_scatter(
            router_grad.astype(jnp.bfloat16), ("dp", "ctx"), scatter_dimension=0, tiled=True
        ).astype(jnp.float32),
        lax.psum_scatter(
            sgate_grad.astype(jnp.bfloat16), ("dp", "ctx"), scatter_dimension=0, tiled=True
        ).astype(jnp.float32),
        lax.psum_scatter(
            sup_grad.astype(jnp.bfloat16), ("dp", "ctx"), scatter_dimension=0, tiled=True
        ).astype(jnp.float32),
        lax.psum_scatter(
            sdown_grad.astype(jnp.bfloat16), ("dp", "ctx"), scatter_dimension=1, tiled=True
        ).astype(jnp.float32),
    )
    (
        gain_attn_sum,
        query_sum,
        key_sum_out,
        value_sum_out,
        out_sum,
        gain_mix_sum,
        router_sum,
        sgate_sum,
        sup_sum,
        sdown_sum,
    ) = all_sums
    return (
        result.astype(jnp.bfloat16)[None],
        tokens_back[None],
        gain_attn_sum,
        query_sum,
        key_sum_out,
        value_sum_out,
        out_sum,
        gain_mix_sum,
        router_sum,
        sgate_sum,
        sup_sum,
        sdown_sum,
        gate_grad,
        up_grad,
        down_grad,
    )


MESH = pl.DeviceIdType.MESH
BF = jnp.bfloat16
F32 = jnp.float32


class Place:
    def __init__(self):
        self.x = lax.axis_index("dp")
        self.z = lax.axis_index("ctx")
        self.e = lax.axis_index("exp")
        z = self.z
        high = lax.div(z, 2)
        self.zs = [z, z + 1 - 2 * lax.rem(z, 2), 2 - high, 3 - 3 * high]
        self.inner = 3 - z
        self.inside = lax.div(z * (3 - z), 2)
        self.middle = self.inside == 1
        self.dx = 1 - 2 * self.x
        self.dy = 2 - 4 * lax.div(self.e, 2)
        self.dc = 1 - 2 * lax.rem(self.e, 2)

    def device(self, ox=0, oe=0, zi=0):
        return (self.x + ox, self.zs[zi], self.e + oe)

    def inward(self):
        return (self.x, self.inner, self.e)

    def shard(self, oe, zi):
        return self.zs[zi] * 4 + self.e + oe


def greet(at, everyone, pair=False):
    barrier = pltpu.get_barrier_semaphore()
    peers = [at.device(zi=1), at.device(oe=at.dy), at.device(oe=at.dc)]
    if everyone or pair:
        peers.append(at.device(ox=at.dx))
    if everyone:
        peers += [at.device(zi=2), at.device(zi=3)]
    for peer in peers:
        pl.semaphore_signal(barrier, inc=1, device_id=peer, device_id_type=MESH)
    if everyone:
        pl.semaphore_wait(barrier, len(peers))
        return

    @pl.when(at.middle)
    def _():
        pl.semaphore_signal(barrier, inc=1, device_id=at.inward(), device_id_type=MESH)

    pl.semaphore_wait(barrier, len(peers) + at.inside)


def remote(src, dst, send, recv, device):
    return pltpu.make_async_remote_copy(
        src_ref=src, dst_ref=dst, send_sem=send, recv_sem=recv, device_id=device, device_id_type=MESH
    )


def keep(src, dst):
    def run(held, sems):
        for j, (a, b) in enumerate(((src, held), (held, dst))):
            copy = pltpu.make_async_copy(a, b, sems.at[j])
            copy.start()
            copy.wait()

    pl.run_scoped(run, pltpu.VMEM(src.shape, src.dtype), pltpu.SemaphoreType.DMA((2,)))


def half_of(array):
    return jax.ShapeDtypeStruct((array.shape[0] // 2,) + array.shape[1:], array.dtype)


def cross(at, sent, got, send_sem, recv_sem, starts=None):
    starts = starts or (0,) * len(sent)
    return [
        remote(
            a.at[pl.ds(start, b.shape[0])],
            b,
            send_sem.at[m],
            recv_sem.at[m],
            at.device(ox=at.dx),
        )
        for m, (a, b, start) in enumerate(zip(sent, got, starts))
    ]


class Exchange:
    def __init__(self, at, sent, got, send_sem, recv_sem):
        self.at, self.sent, self.got = at, sent, got
        self.send_sem, self.recv_sem = send_sem, recv_sem
        self.waits = []

    def push(self, src, m, z_from, slot, device):
        at = self.at
        spot = self.got[m].at[at.x * 4 + z_from]
        copy = remote(
            src, spot, self.send_sem.at[m * 7 + slot], self.recv_sem.at[m * 8 + (0 if slot < 3 else 4) + z_from], device
        )
        copy.start()
        self.waits.append(copy)

    def start(self):
        at = self.at
        for m, sent in enumerate(self.sent):
            self.push(sent.at[at.z], m, at.z, 3, at.device(ox=at.dx))
        for m, sent in enumerate(self.sent):
            keep(sent.at[at.z], self.got[m].at[at.x * 4 + at.z])

    def along(self, zi):
        at = self.at
        for m, sent in enumerate(self.sent):
            self.push(sent.at[at.zs[zi]], m, at.z, zi - 1, at.device(zi=zi))

    def arrive(self, m, slot):
        src = self.sent[m].at[0]
        remote(
            src, self.got[m].at[0], self.send_sem.at[0], self.recv_sem.at[slot], self.at.device(ox=self.at.dx)
        ).wait_recv()

    def forward(self, zi):
        at = self.at
        for m in range(len(self.sent)):
            self.arrive(m, m * 8 + at.zs[zi])
            self.push(self.got[m].at[at.x * 4 + at.zs[zi]], m, at.zs[zi], 3 + zi, at.device(ox=at.dx))

    def finish(self):
        at = self.at
        for m, sent in enumerate(self.sent):
            for z in range(4):
                self.arrive(m, m * 8 + 4 + z)
        for copy in self.waits:
            copy.wait_send()


def gather_kernel(block, rows, parts, extras, starts, *refs):
    swaps = len(starts)
    refs = list(refs)

    def take(count):
        taken = refs[:count]
        del refs[:count]
        return taken

    (x_ref,), sent, given = take(1), take(extras), take(swaps)
    (out_ref,), got, taken = take(1), take(extras), take(swaps)
    send_sem, recv_sem = take(2)
    extra_sems = take(2 if extras else 0)
    at = Place()
    greet(at, extras > 0, swaps > 0)
    crossing = cross(at, given, taken, *refs, starts) if swaps else []
    piece = rows // parts
    slot_z, slot_f, slot_s = 0, 3, 7
    started, inside = [], []
    firsts = 1 if block else 0
    shift = at.e * rows if block else 0

    def where(f, zi, p):
        return pl.ds(
            pl.multiple_of(at.shard(f * at.dy, zi) * rows + p * piece, piece), piece
        )

    def push(src, dst, slot, p, device, sends=None, record=None):
        k = slot * parts + p
        j = k if sends is None else sends * parts + p
        remote(src, out_ref.at[dst], send_sem.at[j], recv_sem.at[k], device).start()
        (started if record is None else record).append(j)

    f_dev, s_dev, z_dev = at.device(oe=at.dy), at.device(oe=at.dc), at.device(zi=1)

    def gone(j):
        remote(
            x_ref.at[pl.ds(0, piece)], out_ref.at[pl.ds(0, piece)], send_sem.at[j], recv_sem.at[0], s_dev
        ).wait_send()

    def arrive(slot, p):
        k = slot * parts + p
        remote(
            x_ref.at[pl.ds(0, piece)], out_ref.at[pl.ds(0, piece)], send_sem.at[k], recv_sem.at[k], s_dev
        ).wait_recv()

    if block:
        spot = pl.ds(pl.multiple_of(at.z * 4 * rows, 4 * rows), 4 * rows)
    else:
        spot = pl.ds(pl.multiple_of(at.shard(0, 0) * rows, rows), rows)

    def source(f, zi, p):
        if f == 0 and zi == 0:
            return x_ref.at[pl.ds(pl.multiple_of(shift + p * piece, piece), piece)]
        return out_ref.at[where(f, zi, p)]

    def along(zi, p):
        src, dst = source(0, zi, p), where(0, zi, p)
        if zi == 0:
            push(src, dst, slot_z, p, z_dev)
        if zi < 2:
            pl.when(at.middle)(
                lambda: push(src, dst, slot_z + 1 + zi, p, at.inward(), 15 + zi, inside)
            )
        else:
            pl.when(at.middle)(lambda: push(src, dst, slot_z + zi - 1, p, z_dev, 15 + zi, inside))

    def forward(f, zi, p):
        src, dst = source(f, zi, p), where(f, zi, p)
        if f == 0:
            along(zi, p)
        if zi >= firsts:
            if f == 0:
                push(src, dst, slot_f + zi, p, f_dev)
            push(src, dst, slot_s + f * 4 + zi, p, s_dev)

    for p in range(parts):
        forward(0, 0, p)
    if extras:
        swap_in = Exchange(at, sent, got, *extra_sems)
        for zi in (1, 2, 3):
            swap_in.along(zi)
        swap_in.start()
    for copy in crossing:
        copy.start()
    keep(x_ref, out_ref.at[spot])
    for zi in range(1, 5):
        for p in range(parts):
            if zi < 4:
                arrive(slot_z + zi - 1, p)
                forward(0, zi, p)
            if zi - 1 >= firsts:
                arrive(slot_f + zi - 1, p)
                forward(1, zi - 1, p)
        if extras and zi > 1:
            swap_in.forward(zi - 1)
    for f in range(2):
        for zi in range(firsts, 4):
            for p in range(parts):
                arrive(slot_s + f * 4 + zi, p)
    if extras:
        swap_in.finish()
    for copy in crossing:
        copy.wait()
    for j in started:
        gone(j)

    @pl.when(at.middle)
    def _():
        for j in inside:
            gone(j)


def all_rows(x, block, cid, sent=(), given=(), starts=(), parts=2):
    rows, width = x.shape
    total = rows * (4 if block else 16)
    rows = rows // 4 if block else rows
    extras, swaps = len(sent), len(given)
    hbm = pl.BlockSpec(memory_space=pl.ANY)
    outs = [jax.ShapeDtypeStruct((total, width), x.dtype)]
    outs += [jax.ShapeDtypeStruct((8,) + a.shape[1:], a.dtype) for a in sent]
    outs += [half_of(a) for a in given]
    scratch = [
        pltpu.SemaphoreType.DMA((19 * parts,)),
        pltpu.SemaphoreType.DMA((15 * parts,)),
    ]
    if extras:
        scratch += [
            pltpu.SemaphoreType.DMA((7 * extras,)),
            pltpu.SemaphoreType.DMA((8 * extras,)),
        ]
    if swaps:
        scratch += [pltpu.SemaphoreType.DMA((swaps,)), pltpu.SemaphoreType.DMA((swaps,))]
    got = pl.pallas_call(
        functools.partial(gather_kernel, block, rows, parts, extras, starts),
        out_shape=outs,
        in_specs=[hbm] * len(outs),
        out_specs=[hbm] * len(outs),
        scratch_shapes=scratch,
        compiler_params=pltpu.CompilerParams(collective_id=cid, has_side_effects=True),
    )(x, *sent, *given)
    return got if extras or swaps else got[0]


class Scatter:
    def __init__(self, at, acc, got_s, got_f, got_z, send_sem, recv_sem, out_ref, by_block=False):
        self.by_block = by_block
        self.at, self.acc, self.got_s, self.got_f, self.got_z = at, acc, got_s, got_f, got_z
        self.send_sem, self.recv_sem, self.out_ref = send_sem, recv_sem, out_ref
        self.rows = acc.shape[1]
        self.f_dev, self.s_dev, self.z_dev = (
            at.device(oe=at.dy),
            at.device(oe=at.dc),
            at.device(zi=1),
        )
        self.started, self.in_middle, self.at_end = [], [], []

    def held(self, f, zi, twin=0):
        at = self.at
        return zi * 4 + at.e + f * at.dy + twin * at.dc if self.by_block else f * 4 + zi

    def span(self, p):
        size = self.rows // 2
        return pl.ds(p * size, size)

    def push(self, src, dst, slot, p, device, sends=None, record=None):
        j = (slot if sends is None else sends) * 2 + p
        src, dst = src.at[self.span(p)], dst.at[self.span(p)]
        remote(src, dst, self.send_sem.at[j], self.recv_sem.at[slot * 2 + p], device).start()
        (self.started if record is None else record).append(j)

    def gone(self, j):
        spot = self.acc.at[0, self.span(0)]
        remote(spot, spot, self.send_sem.at[j], self.recv_sem.at[0], self.s_dev).wait_send()

    def arrive(self, dst, slot, p):
        j, dst = slot * 2 + p, dst.at[self.span(p)]
        src = self.acc.at[0, self.span(p)]
        remote(src, dst, self.send_sem.at[j], self.recv_sem.at[j], self.s_dev).wait_recv()

    def to_twin(self, src, f, zi):
        k = f * 4 + zi
        for p in range(2):
            self.push(src, self.got_s.at[k], 9 + k, p, self.s_dev)

    def add(self, k, p, *others, into=None):
        acc = self.acc
        size = self.rows // 2

        @pl.loop(0, size // 16)
        def _(i):
            span = pl.ds(pl.multiple_of(p * size + i * 16, 16), 16)
            total = acc[k, span, :].astype(F32)
            for ref, j in others:
                total = total + ref[j, span, :].astype(F32)
            if into is None:
                acc[k, span, :] = total.astype(BF)
            else:
                into[span, :] = total

    def first(self, zi):
        k = self.held(1, zi)
        for p in range(2):
            self.arrive(self.got_s.at[4 + zi], 13 + zi, p)
            self.add(k, p, (self.got_s, 4 + zi))
            self.push(self.acc.at[k], self.got_f.at[zi], 5 + zi, p, self.f_dev)

    def second(self, zi, who="all"):
        if who != "middle":
            pl.when(jnp.logical_not(self.at.middle))(lambda: self.from_end(zi))
        if who != "end":
            pl.when(self.at.middle)(lambda: self.from_middle(zi))

    def terms(self, zi, p):
        self.arrive(self.got_s.at[zi], 9 + zi, p)
        self.arrive(self.got_f.at[zi], 5 + zi, p)
        return self.held(0, zi), [(self.got_s, zi), (self.got_f, zi)]

    def from_end(self, zi):
        acc, got_z = self.acc, self.got_z
        for p in range(2):
            k, others = self.terms(zi, p)
            if zi == 0:
                self.arrive(got_z.at[4], 4, p)
                self.add(k, p, *others, (got_z, 4), into=self.out_ref)
                continue
            self.add(k, p, *others)
            self.push(acc.at[k], got_z.at[3 - zi], 3 - zi, p, self.z_dev, zi, self.at_end)

    def from_middle(self, zi):
        acc, got_z = self.acc, self.got_z
        for p in range(2):
            k, others = self.terms(zi, p)
            if zi == 0:
                self.arrive(got_z.at[2], 2, p)
                self.arrive(got_z.at[4], 4, p)
                self.add(k, p, *others, (got_z, 2), (got_z, 4), into=self.out_ref)
                continue
            came = 3 if zi == 1 else 3 - zi
            self.arrive(got_z.at[came], came, p)
            self.add(k, p, *others, (got_z, came))
            there = 3 if zi == 3 else 4
            device = self.z_dev if zi == 1 else self.at.inward()
            self.push(acc.at[k], got_z.at[there], there, p, device, zi, self.in_middle)

    def finish(self):
        for j in self.started:
            self.gone(j)

        @pl.when(self.at.middle)
        def _():
            for j in self.in_middle:
                self.gone(j)

        @pl.when(jnp.logical_not(self.at.middle))
        def _():
            for j in self.at_end:
                self.gone(j)


def scatter_buffers(rows, width, held=8):
    return [
        pltpu.VMEM((held, rows, width), BF),
        pltpu.VMEM((8, rows, width), BF),
        pltpu.VMEM((4, rows, width), BF),
        pltpu.VMEM((5, rows, width), BF),
        pltpu.SemaphoreType.DMA((34,)),
        pltpu.SemaphoreType.DMA((34,)),
    ]


def scatter_kernel(rows, starts, in_ref, *refs):
    swaps = len(starts)
    given, out_ref, taken = refs[:swaps], refs[swaps], refs[swaps + 1 : 2 * swaps + 1]
    buffers, load_sem = refs[2 * swaps + 1 : 2 * swaps + 7], refs[2 * swaps + 7]
    acc = buffers[0]
    at = Place()
    greet(at, False, swaps > 0)
    crossing = cross(at, given, taken, *refs[2 * swaps + 8 :], starts) if swaps else []
    total = Scatter(at, *buffers, out_ref)

    def rows_of(rank):
        return in_ref.at[pl.ds(pl.multiple_of(rank * rows, rows), rows)]

    for copy in crossing:
        copy.start()
    order = [(f, zi) for f in (1, 0) for zi in (3, 2, 1, 0)]
    loads = {}
    for f, zi in order:
        k = f * 4 + zi
        total.to_twin(rows_of(at.shard(f * at.dy + at.dc, zi)), f, zi)
        loads[k] = pltpu.make_async_copy(
            rows_of(at.shard(f * at.dy, zi)), acc.at[k], load_sem.at[k]
        )
        loads[k].start()
    for f, zi in order:
        loads[f * 4 + zi].wait()
        (total.first if f else total.second)(zi)
    for copy in crossing:
        copy.wait()
    total.finish()


def own_rows(x, cid, given=(), starts=()):
    rows, width = x.shape[0] // 16, x.shape[1]
    swaps = len(given)
    hbm = pl.BlockSpec(memory_space=pl.ANY)
    crossing = [pltpu.SemaphoreType.DMA((swaps,))] * 2 if swaps else []
    got = pl.pallas_call(
        functools.partial(scatter_kernel, rows, starts),
        out_shape=[jax.ShapeDtypeStruct((rows, width), F32)]
        + [half_of(a) for a in given],
        in_specs=[hbm] * (1 + swaps),
        out_specs=[pl.BlockSpec(memory_space=pltpu.VMEM)] + [hbm] * swaps,
        scratch_shapes=[
            *scatter_buffers(rows, width),
            pltpu.SemaphoreType.DMA((8,)),
            *crossing,
        ],
        compiler_params=pltpu.CompilerParams(
            collective_id=cid, has_side_effects=True, vmem_limit_bytes=40 * 1024 * 1024
        ),
    )(x, *given)
    return got if swaps else got[0]


class Gather:
    parts = 2

    def __init__(self, at, x_ref, out_ref, send_sem, recv_sem, block=False):
        self.at, self.x_ref, self.out_ref, self.block = at, x_ref, out_ref, block
        self.send_sem, self.recv_sem = send_sem, recv_sem
        rows = x_ref.shape[0] // (4 if block else 1)
        self.rows, self.piece = rows, rows // self.parts
        self.f_dev, self.s_dev, self.z_dev = (
            at.device(oe=at.dy),
            at.device(oe=at.dc),
            at.device(zi=1),
        )
        self.started, self.inside = [], []
        if block:
            spot = pl.ds(pl.multiple_of(at.z * 4 * rows, 4 * rows), 4 * rows)
        else:
            spot = pl.ds(pl.multiple_of(at.shard(0, 0) * rows, rows), rows)
        self.place = spot

    def push(self, f, zi, p, slot, device, sends=None, record=None):
        at, piece = self.at, self.piece
        spot = at.shard(f * at.dy, zi) * self.rows + p * piece
        dst = self.out_ref.at[pl.ds(pl.multiple_of(spot, piece), piece)]
        src = dst
        if f == 0 and zi == 0:
            spot = (at.e * self.rows if self.block else 0) + p * piece
            src = self.x_ref.at[pl.ds(pl.multiple_of(spot, piece), piece)]
        j = (slot if sends is None else sends) * self.parts + p
        k = slot * self.parts + p
        remote(src, dst, self.send_sem.at[j], self.recv_sem.at[k], device).start()
        (self.started if record is None else record).append(j)

    def spot(self):
        span = pl.ds(0, self.piece)
        return self.x_ref.at[span], self.out_ref.at[span]

    def arrive(self, slot, p):
        k = slot * self.parts + p
        remote(*self.spot(), self.send_sem.at[k], self.recv_sem.at[k], self.s_dev).wait_recv()

    def forward(self, f, zi, p):
        if f == 0:
            if zi == 0:
                self.push(0, 0, p, 0, self.z_dev)
            if zi < 2:
                pl.when(self.at.middle)(
                    lambda: self.push(0, zi, p, 1 + zi, self.at.inward(), 15 + zi, self.inside)
                )
            else:
                pl.when(self.at.middle)(
                    lambda: self.push(0, zi, p, zi - 1, self.z_dev, 15 + zi, self.inside)
                )
        if self.block and zi == 0:
            return
        if f == 0:
            self.push(0, zi, p, 3 + zi, self.f_dev)
        self.push(f, zi, p, 7 + f * 4 + zi, self.s_dev)

    def begin(self):
        for p in range(self.parts):
            self.forward(0, 0, p)
        keep(self.x_ref, self.out_ref.at[self.place])

    def step(self, zi):
        for p in range(self.parts):
            if zi < 4:
                self.arrive(zi - 1, p)
                self.forward(0, zi, p)
            if zi > 1 or not self.block:
                self.arrive(2 + zi, p)
                self.forward(1, zi - 1, p)

    def twin(self, zi):
        for p in range(self.parts):
            self.arrive(7 + zi, p)
            self.arrive(11 + zi, p)

    def finish(self, arrived=False):
        for zi in range(4):
            if not arrived and not (self.block and zi == 0):
                self.twin(zi)

        def gone(j):
            remote(*self.spot(), self.send_sem.at[j], self.recv_sem.at[0], self.s_dev).wait_send()

        for j in self.started:
            gone(j)

        @pl.when(self.at.middle)
        def _():
            for j in self.inside:
                gone(j)


def columns_loop(width, parts):
    size = width // parts

    def over(run):
        @pl.loop(0, parts)
        def _(n):
            run(pl.ds(pl.multiple_of(n * size, size), size))

    return over


def expert_gather_kernel(experts, *refs):
    refs = list(refs)

    def take(count):
        taken = refs[:count]
        del refs[:count]
        return taken

    x_ref, dy_ref, disp, w_router, units = take(5)
    weights, given = take(7), take(2)
    out_ref, picked, picked_dy, scaled_out, g_out, u_out, gb_out, sa_out, sg_out = take(9)
    taken, units_out = take(2), take(2)
    shared_in, shared_out = take(2)
    wg, wu, wd, xb, dyd, sb, pk, pdy, sc, gg, uu, hid, gb, sa, sg = take(15)
    send_sem, recv_sem, load_sem, block_sem, store_sem, cross_send, cross_recv, unit_sem = take(8)
    at = Place()
    gather = Gather(at, x_ref, out_ref, send_sem, recv_sem)
    crossing = cross(at, given, taken, cross_send, cross_recv, (0, taken[0].shape[0]))
    block = xb.shape[1]
    slots = pk.shape[0] // 4
    part = wd.shape[1] // 2
    mine = at.z * 4 + at.e

    def span(zi, size):
        return pl.ds(pl.multiple_of(at.zs[zi] * size, size), size)

    def dy_load(zi):
        return pltpu.make_async_copy(
            dy_ref.at[span(zi, block)], xb.at[zi % 2], block_sem.at[2 + zi % 2]
        )

    def x_load(zi):
        return pltpu.make_async_copy(
            out_ref.at[span(zi, block)], xb.at[zi % 2], block_sem.at[zi % 2]
        )

    def stores(zi):
        b = zi % 2
        pairs = [(sa.at[b], sa_out.at[span(zi, block)]), (sg.at[b], sg_out.at[span(zi, block)])]
        return [
            pltpu.make_async_copy(src, dst, store_sem.at[b * 2 + j])
            for j, (src, dst) in enumerate(pairs)
        ]

    def parts_of(gate, up):
        s = 1.0 / (1.0 + jnp.exp(-gate))
        act = gate * s
        return act * up, s * (1.0 + gate * (1.0 - s)) * up, act

    cut, size = units.shape[1] // 3, units.shape[2]
    wide = shared_out.shape[0]
    unit_loads = []
    for d in range(8):
        for m in range(3):
            ref, first = (shared_out, 0) if m == 2 else (shared_in, m * wide)
            unit_loads.append(
                pltpu.make_async_copy(
                    units.at[d, pl.ds(m * cut, cut)],
                    ref.at[pl.ds(first, cut), pl.ds(d * size, size)],
                    unit_sem.at[d * 3 + m],
                )
            )

    def ahead(zi):
        b = zi % 2
        some = span(zi, slots)
        dy_load(zi).wait()
        pdy[some, :] = product(disp[at.zs[zi]], xb[b]).astype(BF)
        sb[span(zi, block), :] = transposed_right(xb[b], shared_out[...])
        if zi < 2:
            dy_load(zi + 2).start()
        dyd[some, :] = transposed_right(pdy[some, :], wd[0])

    def work(zi):
        b = zi % 2
        some = span(zi, slots)
        x_load(zi).wait()
        if zi >= 2:
            for copy in stores(zi - 2):
                copy.wait()
        pk[some, :] = product(disp[at.zs[zi]], xb[b]).astype(BF)
        logits = transposed_right(pk[some, :], w_router[...])
        lane = lax.broadcasted_iota(jnp.int32, logits.shape, 1)
        logits = jnp.where(lane < experts, logits, MASKED)
        powers = jnp.exp(logits - jnp.max(logits, axis=1, keepdims=True))
        own_power = jnp.sum(jnp.where(lane == mine, powers, 0.0), axis=1, keepdims=True)
        gate_of = own_power / jnp.sum(powers, axis=1, keepdims=True)
        for h in range(2):
            hidden, by_gate, by_up = parts_of(
                transposed_right(pk[some, :], wg[h]), transposed_right(pk[some, :], wu[h])
            )
            sc[h, some, :] = (hidden * gate_of).astype(BF)
            if h == 0:
                dy_down = dyd[some, :]
                act_back = gate_of * dy_down
                gg[0, some, :] = (act_back * by_gate).astype(BF)
                uu[0, some, :] = (act_back * by_up).astype(BF)
                gb[some, :] = jnp.broadcast_to(
                    jnp.sum(hidden * dy_down, axis=1, keepdims=True), (slots, gb.shape[1])
                )
            else:
                hid[some, :] = hidden.astype(BF)
                gg[1, some, :] = (gate_of * by_gate).astype(BF)
                uu[1, some, :] = (gate_of * by_up).astype(BF)
        both = transposed_right(xb[b], shared_in[...])
        wide = both.shape[1] // 2
        hidden, by_gate, by_up = parts_of(both[:, :wide], both[:, wide:])
        back = sb[span(zi, block), :]
        sa[b] = hidden.astype(BF)
        sg[b, :, :wide] = (back * by_gate).astype(BF)
        sg[b, :, wide:] = (back * by_up).astype(BF)
        for copy in stores(zi):
            copy.start()

    def other_half(zi):
        some = span(zi, slots)
        dy_down = transposed_right(pdy[some, :], wd[1])
        gg[1, some, :] = (dy_down * gg[1, some, :].astype(F32)).astype(BF)
        uu[1, some, :] = (dy_down * uu[1, some, :].astype(F32)).astype(BF)
        gb[some, :] += jnp.broadcast_to(
            jnp.sum(hid[some, :].astype(F32) * dy_down, axis=1, keepdims=True), (slots, gb.shape[1])
        )

    places = [
        wg.at[0],
        wu.at[0],
        wd.at[0],
        wg.at[1, pl.ds(0, part)],
        wg.at[1, pl.ds(part, part)],
        wu.at[1, pl.ds(0, part)],
        wu.at[1, pl.ds(part, part)],
        wd.at[1, pl.ds(0, part)],
        wd.at[1, pl.ds(part, part)],
    ]
    loads = [
        pltpu.make_async_copy(a, b, load_sem.at[j]) for j, (a, b) in enumerate(zip(weights + taken, places))
    ]
    dy_load(0).start()
    dy_load(1).start()
    for j in (2, 0, 1, 3, 4, 5, 6):
        loads[j].start()
    shared_in[...] = jnp.zeros_like(shared_in)
    shared_out[...] = jnp.zeros_like(shared_out)
    for copy in unit_loads:
        copy.start()
    greet(at, False, True)
    for copy in crossing:
        copy.start()
    gather.begin()
    for copy in unit_loads:
        copy.wait()
    loads[2].wait()
    for zi in range(3):
        ahead(zi)
    for zi in range(4):
        gather.step(zi + 1)
        if zi == 0:
            ahead(3)
        gather.twin(zi)
        x_load(zi).start()
        if zi == 0:
            for j in (0, 1, 3, 4, 5, 6):
                loads[j].wait()
        work(zi)
    results = [(pk, picked), (pdy, picked_dy), (sc, scaled_out)]
    results += [(shared_in, units_out[0]), (shared_out, units_out[1])]
    results += [(gg, g_out), (uu, u_out), (gb, gb_out)]
    results = [
        pltpu.make_async_copy(a, b, store_sem.at[4 + j]) for j, (a, b) in enumerate(results)
    ]
    for copy in results[:5]:
        copy.start()
    for m in range(2):
        crossing[m].wait_recv()
        loads[7 + m].start()
    for m in range(2):
        loads[7 + m].wait()
    for zi in range(4):
        other_half(zi)
    for copy in results[5:]:
        copy.start()
    for copy in results:
        copy.wait()
    for zi in (2, 3):
        for copy in stores(zi):
            copy.wait()
    for copy in crossing:
        copy.wait_send()
    gather.finish(True)


def expert_rows(x, dy_all, dispatch, w_router, experts, units, wide, weights, given, cid):
    rows, width = x.shape
    total, block = 16 * rows, 4 * rows
    slots = 4 * dispatch.shape[1]
    hidden = weights[0].shape[0]
    halves = [half_of(a) for a in given]
    hbm, vmem = pl.BlockSpec(memory_space=pl.ANY), pl.BlockSpec(memory_space=pltpu.VMEM)
    shape, sems = jax.ShapeDtypeStruct, lambda n: pltpu.SemaphoreType.DMA((n,))
    return pl.pallas_call(
        functools.partial(expert_gather_kernel, experts),
        out_shape=[
            shape((total, width), BF),
            shape((slots, width), BF),
            shape((slots, width), BF),
            shape((2, slots, hidden), BF),
            shape((2, slots, hidden), BF),
            shape((2, slots, hidden), BF),
            shape((slots, 128), F32),
            shape((total, wide), BF),
            shape((total, 2 * wide), BF),
            *halves,
            shape((2 * wide, width), BF),
            shape((wide, width), BF),
        ],
        in_specs=[hbm, hbm, vmem, vmem] + [hbm] * 10,
        out_specs=[hbm] * 13,
        scratch_shapes=[
            pltpu.VMEM((2 * wide, width), BF),
            pltpu.VMEM((wide, width), BF),
            pltpu.VMEM((2, hidden, width), BF),
            pltpu.VMEM((2, hidden, width), BF),
            pltpu.VMEM((2, hidden, width), BF),
            pltpu.VMEM((2, block, width), BF),
            pltpu.VMEM((slots, hidden), F32),
            pltpu.VMEM((total, wide), F32),
            pltpu.VMEM((slots, width), BF),
            pltpu.VMEM((slots, width), BF),
            pltpu.VMEM((2, slots, hidden), BF),
            pltpu.VMEM((2, slots, hidden), BF),
            pltpu.VMEM((2, slots, hidden), BF),
            pltpu.VMEM((slots, hidden), BF),
            pltpu.VMEM((slots, 128), F32),
            pltpu.VMEM((2, block, wide), BF),
            pltpu.VMEM((2, block, 2 * wide), BF),
            sems(38),
            sems(30),
            sems(9),
            sems(4),
            sems(12),
            sems(2),
            sems(2),
            sems(24),
        ],
        compiler_params=pltpu.CompilerParams(
            collective_id=cid, has_side_effects=True, vmem_limit_bytes=62 * 1024 * 1024
        ),
    )(x, dy_all, dispatch, w_router, units, *weights, *given)


def expert_scatter_kernel(*refs):
    refs = list(refs)

    def take(count):
        taken = refs[:count]
        del refs[:count]
        return taken

    disp, gate_back, shared_in, g_ref, u_ref, sg_ref, picked_ref, dy_ref, scaled_ref = take(9)
    weights = take(6)
    out_ref, taken, *grads = take(7)
    wg, wu, gs, us, sg, picked, picked_dy, scaled, ib, grad, turned = take(11)
    acc, got_s, got_f, got_z, send_sem, recv_sem = take(6)
    load_sem, store_sem, cross_send, cross_recv = take(4)
    at = Place()
    rows, full = acc.shape[1:]
    width = shared_in.shape[1]
    slots = ib.shape[0]
    block = 4 * rows
    over = columns_loop(width, 4)
    mine = at.z * 4 + at.e
    total = Scatter(at, acc, got_s, got_f, got_z, send_sem, recv_sem, out_ref, True)

    part = wg.shape[1] // 2
    pairs = [
        (weights[0], wg.at[0]),
        (weights[1], wu.at[0]),
        (weights[2], wg.at[1, pl.ds(0, part)]),
        (weights[3], wg.at[1, pl.ds(part, part)]),
        (weights[4], wu.at[1, pl.ds(0, part)]),
        (weights[5], wu.at[1, pl.ds(part, part)]),
        (g_ref, gs),
        (u_ref, us),
        (sg_ref, sg),
        (picked_ref, picked),
        (dy_ref, picked_dy),
        (scaled_ref.at[1], scaled),
    ]
    loads = [pltpu.make_async_copy(a, b, load_sem.at[j]) for j, (a, b) in enumerate(pairs)]
    for copy in loads:
        copy.start()
    greet(at, False, True)

    def work(zi):
        place = at.zs[zi]
        some = pl.ds(pl.multiple_of(place * slots, slots), slots)

        hot = disp[place]
        tokens = pl.ds(pl.multiple_of(place * block, block), block)

        @over
        def _(columns):
            terms = product(gs[0, some, :], wg[0, :, columns])
            terms += product(us[0, some, :], wu[0, :, columns])
            terms += product(gs[1, some, :], wg[1, :, columns])
            terms += product(us[1, some, :], wu[1, :, columns])
            ib[:, columns] = terms.astype(BF)

        @over
        def _(columns):
            terms = transposed_left(hot, ib[:, columns])
            terms += product(sg[tokens, :], shared_in[:, columns])
            for e in range(4):
                acc[zi * 4 + e, :, columns] = terms[e * rows : (e + 1) * rows].astype(BF)

        from_gates = gate_back[some, :]
        lane = lax.broadcasted_iota(jnp.int32, from_gates.shape, 1)
        terms = transposed_left(hot, jnp.where(lane == mine, from_gates, 0.0).astype(BF))
        for e in range(4):
            acc[zi * 4 + e, :, width:] = terms[e * rows : (e + 1) * rows].astype(BF)

    def gradient(m):
        step = 256
        right = picked_dy if m == 2 else picked
        turned[...] = (scaled[...] if m == 2 else gs[1] if m == 0 else us[1]).T

        @pl.loop(0, width // step)
        def _(n):
            columns = pl.ds(pl.multiple_of(n * step, step), step)
            grad[min(m, 1), :, columns] = product(turned[...], right[:, columns]).astype(BF)

    crossing = cross(at, [grad.at[0, pl.ds(0, part)]], [taken], cross_send, cross_recv)[0]
    stores = [
        pltpu.make_async_copy(
            grad.at[min(j // 2, 1), pl.ds(j % 2 * part, part)], grads[j - 1], store_sem.at[j]
        )
        for j in range(1, 6)
    ]
    for copy in loads[:9]:
        copy.wait()
    for zi in (3, 2, 1, 0):
        work(zi)
        for f in range(2):
            total.to_twin(acc.at[total.held(f, zi, 1)], f, zi)
        total.first(zi)
        if zi == 1:
            total.second(3, "end")
    for copy in loads[9:]:
        copy.wait()
    for m, zi in ((0, 2), (1, 1), (2, 0)):
        if m == 2:
            stores[1].wait()
            stores[2].wait()
        gradient(m)
        if m == 0:
            total.second(3, "middle")
        if m == 0:
            crossing.start()
        for j in (2 * m, 2 * m + 1):
            if j > 0:
                stores[j - 1].start()
        total.second(zi)
    for j in (0, 3, 4):
        stores[j].wait()
    crossing.wait()
    total.finish()


def expert_back(dispatch, gate_back, shared_in, g, u, sg, picked, picked_dy, scaled, weights, cid):
    total, wide = sg.shape
    width = shared_in.shape[1]
    rows, full = total // 16, width + 128
    slots = picked.shape[0]
    hidden = g.shape[2]
    hbm, vmem = pl.BlockSpec(memory_space=pl.ANY), pl.BlockSpec(memory_space=pltpu.VMEM)
    shape = jax.ShapeDtypeStruct
    return pl.pallas_call(
        expert_scatter_kernel,
        out_shape=[
            shape((rows, full), F32),
            *[shape((hidden // 2, width), BF)] * 6,
        ],
        in_specs=[vmem] * 3 + [hbm] * 12,
        out_specs=[vmem] + [hbm] * 6,
        scratch_shapes=[
            pltpu.VMEM((2, hidden, width), BF),
            pltpu.VMEM((2, hidden, width), BF),
            pltpu.VMEM((2, slots, hidden), BF),
            pltpu.VMEM((2, slots, hidden), BF),
            pltpu.VMEM((total, wide), BF),
            pltpu.VMEM((slots, width), BF),
            pltpu.VMEM((slots, width), BF),
            pltpu.VMEM((slots, hidden), BF),
            pltpu.VMEM((slots // 4, width), BF),
            pltpu.VMEM((2, hidden, width), BF),
            pltpu.VMEM((hidden, slots), BF),
            *scatter_buffers(rows, full, 16),
            pltpu.SemaphoreType.DMA((12,)),
            pltpu.SemaphoreType.DMA((6,)),
            pltpu.SemaphoreType.DMA((1,)),
            pltpu.SemaphoreType.DMA((1,)),
        ],
        compiler_params=pltpu.CompilerParams(
            collective_id=cid, has_side_effects=True, vmem_limit_bytes=63 * 1024 * 1024
        ),
    )(dispatch, gate_back, shared_in, g, u, sg, picked, picked_dy, scaled, *weights)


def mixed_kernel(*refs):
    refs = list(refs)

    def take(count):
        taken = refs[:count]
        del refs[:count]
        return taken

    w_out, w_qkv, tables, q_ref, k_ref, v_ref, lse_ref, heads_out = take(8)
    in_ref, back_ref, normed_ref, *given = take(5)
    out_ref, normed_back, home_out, *taken = take(5)
    rows_in, do, dk, dv, qkv, out_sum, qkv_sum, staged = take(8)
    buffers = take(6)
    first_sem, in_sem, store_sem, cross_send, cross_recv = take(5)
    at = Place()
    total = Scatter(at, *buffers, out_ref)
    acc = buffers[0]
    rows, width = acc.shape[1:]
    length = q_ref.shape[0]
    block = length // 4
    crossing = cross(at, given, taken, cross_send, cross_recv)

    def rows_of(rank):
        return in_ref.at[pl.ds(pl.multiple_of(rank * rows, rows), rows)]

    def rows_load(j):
        ref = back_ref if j < 4 else normed_ref
        return pltpu.make_async_copy(
            ref.at[pl.ds(j % 4 * block, block)], rows_in.at[j % 2], in_sem.at[j % 2]
        )

    rows_load(0).start()
    rows_load(1).start()
    greet(at, False, True)
    for copy in crossing:
        copy.start()
    order = [(f, zi) for f in (1, 0) for zi in (3, 2, 1, 0)]
    firsts = {}
    for f, zi in order:
        m = f * 4 + zi
        total.to_twin(rows_of(at.shard(f * at.dy + at.dc, zi)), f, zi)
        firsts[m] = pltpu.make_async_copy(
            rows_of(at.shard(f * at.dy, zi)), acc.at[m], first_sem.at[m]
        )
        firsts[m].start()

    def heads_back(j):
        rows_load(j).wait()
        here = pl.ds(j * block, block)
        do[here, :] = transposed_right(rows_in[j % 2], w_out[...]).astype(BF)
        turned = heads_out[here, :].T

        @pl.loop(0, 4)
        def _(n):
            columns = pl.ds(pl.multiple_of(n * (width // 4), width // 4), width // 4)
            terms = product(turned, rows_in[j % 2, :, columns])
            out_sum[:, columns] = terms if j == 0 else out_sum[:, columns] + terms

        rows_load(j + 2).start()

    scale = HDIM ** (-0.5)
    step = 256

    def attend_rows(i):
        seen = (i + 1) * step
        here = pl.ds(i * step, step)
        q, go = q_ref[here, :], do[here, :]
        scores = transposed_right(q, k_ref[0:seen, :]) * scale
        row_at = lax.broadcasted_iota(jnp.int32, scores.shape, 0) + i * step
        col_at = lax.broadcasted_iota(jnp.int32, scores.shape, 1)
        scores = jnp.where(row_at >= col_at, scores, MASKED)
        probs = jnp.exp(scores - lse_ref[here, 0:1])
        weight_back = transposed_right(go, v_ref[0:seen, :])
        inner = jnp.sum(probs * weight_back, axis=-1, keepdims=True)
        score_back = (probs * (weight_back - inner)).astype(BF)
        dv[0:seen, :] += transposed_left(probs.astype(BF), go)
        dk[0:seen, :] += transposed_left(score_back, q) * scale
        qkv[here, 0:HDIM] = turn_rows(product(score_back, k_ref[0:seen, :]) * scale, here)

    def turn_rows(values, here):
        other = pltpu.roll(values, HDIM // 2, 1)
        return (values * tables[0, here, :] + other * tables[1, here, :]).astype(BF)

    def finish_heads():
        for j in range(8):
            here = pl.ds(j * step, step)
            qkv[here, HDIM : 2 * HDIM] = turn_rows(dk[here, :], here)
            qkv[here, 2 * HDIM :] = dv[here, :].astype(BF)

    def normed_store(j):
        return pltpu.make_async_copy(
            staged.at[j % 2], normed_back.at[pl.ds(j * step, step)], store_sem.at[j % 2]
        )

    def normed_rows(j):
        if j >= 2:
            normed_store(j - 2).wait()

        @pl.loop(0, 4)
        def _(n):
            columns = pl.ds(pl.multiple_of(n * (width // 4), width // 4), width // 4)
            staged[j % 2, :, columns] = product(
                qkv[pl.ds(j * step, step), :], w_qkv[:, columns]
            ).astype(BF)

        normed_store(j).start()

    def qkv_rows(j):
        rows_load(4 + j).wait()
        turned = qkv[pl.ds(j * block, block), :].T

        @pl.loop(0, 4)
        def _(n):
            columns = pl.ds(pl.multiple_of(n * (width // 4), width // 4), width // 4)
            terms = product(turned, rows_in[j % 2, :, columns])
            qkv_sum[:, columns] = terms if j == 0 else qkv_sum[:, columns] + terms

        if j < 2:
            rows_load(6 + j).start()

    for zi in (3, 2, 1, 0):
        firsts[4 + zi].wait()
        total.first(zi)
    for j in range(4):
        heads_back(j)
    for m in (3, 2, 1, 0):
        firsts[m].wait()
    total.second(3, "end")
    dk[...] = jnp.zeros_like(dk)
    dv[...] = jnp.zeros_like(dv)
    for i in range(5):
        attend_rows(i)
    total.second(3, "middle")
    total.second(2, "end")
    for i in range(5, 8):
        attend_rows(i)
    finish_heads()
    for j in range(3):
        normed_rows(j)
    total.second(2, "middle")
    total.second(1, "end")
    for j in range(3, 8):
        normed_rows(j)
    total.second(1, "middle")
    for j in range(4):
        qkv_rows(j)
    size = home_out.shape[2]
    for j in range(8):
        columns = slice(j * size, (j + 1) * size)
        home_out[j, : 3 * HDIM, :] = qkv_sum[:, columns].astype(BF)
        home_out[j, 3 * HDIM :, :] = out_sum[:, columns].astype(BF)
    total.second(0)
    for j in (6, 7):
        normed_store(j).wait()
    for copy in crossing:
        copy.wait()
    total.finish()


def mixed_rows(
    w_out, w_qkv, tables, q, k, v, lse, heads_out, mixed_part, attn_back, normed, given, cid
):
    length, width = attn_back.shape
    rows = length // 16
    hbm, vmem = pl.BlockSpec(memory_space=pl.ANY), pl.BlockSpec(memory_space=pltpu.VMEM)
    shape = jax.ShapeDtypeStruct
    return pl.pallas_call(
        mixed_kernel,
        out_shape=[
            shape((rows, width), F32),
            shape((length, width), BF),
            shape((8, 4 * HDIM, width // 8), BF),
            *[shape(a.shape, BF) for a in given],
        ],
        in_specs=[vmem] * 8 + [hbm] * 5,
        out_specs=[vmem, hbm, vmem, hbm, hbm],
        scratch_shapes=[
            pltpu.VMEM((2, length // 4, width), BF),
            pltpu.VMEM((length, HDIM), BF),
            pltpu.VMEM((length, HDIM), F32),
            pltpu.VMEM((length, HDIM), F32),
            pltpu.VMEM((length, 3 * HDIM), BF),
            pltpu.VMEM((HDIM, width), F32),
            pltpu.VMEM((3 * HDIM, width), F32),
            pltpu.VMEM((2, 256, width), BF),
            *scatter_buffers(rows, width),
            pltpu.SemaphoreType.DMA((8,)),
            pltpu.SemaphoreType.DMA((2,)),
            pltpu.SemaphoreType.DMA((2,)),
            pltpu.SemaphoreType.DMA((2,)),
            pltpu.SemaphoreType.DMA((2,)),
        ],
        compiler_params=pltpu.CompilerParams(
            collective_id=cid, has_side_effects=True, vmem_limit_bytes=63 * 1024 * 1024
        ),
    )(w_out, w_qkv, tables, q, k, v, lse, heads_out, mixed_part, attn_back, normed, *given)


def gather_back_kernel(*refs):
    refs = list(refs)

    def take(count):
        taken = refs[:count]
        del refs[:count]
        return taken

    x_ref, disp, shared_out = take(3)
    scaled_ref, act_ref, sg_ref, wd_a, wd_0, wd_1, mix_ref, dy_ref, *given = take(10)
    out_ref, mixed_part, units_grad, *taken = take(5)
    scaled, acts, sg, wd, eb, mixes, dys, staged, turned, turned_acts = take(10)
    send_sem, recv_sem, cross_send, cross_recv, load_sem, store_sem = take(6)
    at = Place()
    gather = Gather(at, x_ref, out_ref, send_sem, recv_sem)
    crossing = cross(at, given, taken, cross_send, cross_recv)
    rows, width = x_ref.shape
    slots = eb.shape[0]
    block = 4 * rows
    units = acts.shape[1]
    cut = units_grad.shape[1] // 3
    over = columns_loop(width, 4)

    pairs = [
        (scaled_ref, scaled),
        (act_ref, acts),
        (wd_a, wd.at[0]),
        (wd_0, wd.at[1, pl.ds(0, wd_0.shape[0])]),
        (wd_1, wd.at[1, pl.ds(wd_0.shape[0], wd_0.shape[0])]),
        (sg_ref, sg),
        (mix_ref, mixes),
        (dy_ref, dys),
    ]
    loads = [pltpu.make_async_copy(a, b, load_sem.at[j]) for j, (a, b) in enumerate(pairs)]
    for copy in loads:
        copy.start()
    greet(at, False, True)
    for copy in crossing:
        copy.start()
    gather.begin()

    def mixed_store(j):
        return pltpu.make_async_copy(
            staged.at[j % 2], mixed_part.at[pl.ds(j * block, block)], store_sem.at[j % 2]
        )

    def mixed_rows_of(j):
        some = pl.ds(j * slots, slots)

        @over
        def _(columns):
            terms = product(scaled[0, some, :], wd[0, :, columns])
            terms += product(scaled[1, some, :], wd[1, :, columns])
            eb[:, columns] = terms.astype(BF)

        if j >= 2:
            mixed_store(j - 2).wait()
        tokens = pl.ds(j * block, block)

        @over
        def _(columns):
            terms = transposed_left(disp[j], eb[:, columns])
            terms += product(acts[tokens, :], shared_out[:, columns])
            staged[j % 2, :, columns] = terms.astype(BF)

        mixed_store(j).start()

    def units_of(first, count):
        size = units_grad.shape[2]

        @pl.loop(first, first + count)
        def _(n):
            columns = pl.ds(pl.multiple_of(n * size, size), size)
            terms = product(turned[...], mixes[:, columns]).astype(BF)
            units_grad[n, 0:cut, :] = terms[:cut]
            units_grad[n, cut : 2 * cut, :] = terms[units : units + cut]
            terms = product(turned_acts[...], dys[:, columns]).astype(BF)
            units_grad[n, 2 * cut :, :] = terms[:cut]

    for copy in loads[:5]:
        copy.wait()
    for zi in range(4):
        mixed_rows_of(zi)
        if zi == 0:
            for copy in loads[5:]:
                copy.wait()
            turned[...] = sg[...].T
            turned_acts[...] = acts[...].T
        units_of(2 * zi, 2)
        gather.step(zi + 1)
    for j in (2, 3):
        mixed_store(j).wait()
    for copy in crossing:
        copy.wait()
    gather.finish()


def gather_back(x, given, dispatch, shared_out, scaled, acts, sg, wd, mix_all, dy_all, cut, cid):
    rows, width = x.shape
    length, units = acts.shape
    slots, hidden = scaled.shape[1:]
    hbm, vmem = pl.BlockSpec(memory_space=pl.ANY), pl.BlockSpec(memory_space=pltpu.VMEM)
    shape = jax.ShapeDtypeStruct
    return pl.pallas_call(
        gather_back_kernel,
        out_shape=[
            shape((length, width), BF),
            shape((length, width), BF),
            shape((8, 3 * cut, width // 8), BF),
            *[shape(a.shape, BF) for a in given],
        ],
        in_specs=[hbm, vmem, vmem] + [hbm] * 10,
        out_specs=[hbm, hbm, vmem, hbm, hbm],
        scratch_shapes=[
            pltpu.VMEM((2, slots, hidden), BF),
            pltpu.VMEM(acts.shape, BF),
            pltpu.VMEM(sg.shape, BF),
            pltpu.VMEM((2, hidden, width), BF),
            pltpu.VMEM((slots // 4, width), BF),
            pltpu.VMEM((length, width), BF),
            pltpu.VMEM((length, width), BF),
            pltpu.VMEM((2, 4 * rows, width), BF),
            pltpu.VMEM((2 * units, length), BF),
            pltpu.VMEM((units, length), BF),
            pltpu.SemaphoreType.DMA((38,)),
            pltpu.SemaphoreType.DMA((30,)),
            pltpu.SemaphoreType.DMA((2,)),
            pltpu.SemaphoreType.DMA((2,)),
            pltpu.SemaphoreType.DMA((8,)),
            pltpu.SemaphoreType.DMA((2,)),
        ],
        compiler_params=pltpu.CompilerParams(
            collective_id=cid, has_side_effects=True, vmem_limit_bytes=60 * 1024 * 1024
        ),
    )(x, dispatch, shared_out, scaled, acts, sg, *wd, mix_all, dy_all, *given)


class Home:
    def __init__(self, at, arrays, outs, mine, got, load_sem, x_send, x_recv, z_send, z_recv):
        self.at, self.outs, self.mine, self.got = at, outs, mine, got
        self.z_send, self.z_recv = z_send, z_recv
        there = (1 - at.x) * 4
        self.loads, self.crossing, self.keep = {}, {}, []
        self.count = len(arrays)
        for m, array in enumerate(arrays):
            for k in range(4):
                spot, j = at.zs[k], m * 4 + k
                self.loads[m, k] = pltpu.make_async_copy(
                    array.at[at.x * 4 + spot], mine[m].at[spot], load_sem.at[m * 5 + k]
                )
                self.crossing[m, k] = remote(
                    array.at[there + spot],
                    got[m].at[spot],
                    x_send.at[j],
                    x_recv.at[j],
                    at.device(ox=at.dx),
                )
            self.keep.append(
                pltpu.make_async_copy(mine[m].at[at.z], outs[m].at[at.z], load_sem.at[m * 5 + 4])
            )

    def start(self):
        for k in (3, 2, 1, 0):
            for m in range(self.count):
                self.loads[m, k].start()
                self.crossing[m, k].start()

    def line(self, k):
        spot = self.at.zs[k]
        for m in range(self.count):
            mine, got = self.mine[m], self.got[m]
            self.loads[m, k].wait()
            self.crossing[m, k].wait_recv()

            @pl.loop(0, mine.shape[1] // 16)
            def _(i):
                span = pl.ds(pl.multiple_of(i * 16, 16), 16)
                both = mine[spot, span, :].astype(F32) + got[spot, span, :].astype(F32)
                mine[spot, span, :] = both.astype(BF)

            (self.copy(m, k) if k else self.keep[m]).start()

    def copy(self, m, k):
        at = self.at
        return remote(
            self.mine[m].at[at.zs[k]],
            self.outs[m].at[at.z],
            self.z_send.at[m * 3 + k - 1],
            self.z_recv.at[m * 4 + at.z],
            at.device(zi=k),
        )

    def finish(self):
        at = self.at
        for m in range(self.count):
            for k in (1, 2, 3):
                remote(
                    self.mine[m].at[at.z],
                    self.outs[m].at[at.zs[k]],
                    self.z_send.at[m * 3 + k - 1],
                    self.z_recv.at[m * 4 + at.zs[k]],
                    at.device(zi=k),
                ).wait_recv()
                self.copy(m, k).wait_send()
            self.keep[m].wait()
        for copy in self.crossing.values():
            copy.wait_send()


class Share:
    def __init__(self, at, ref, out, send_sem, recv_sem):
        self.at, rows = at, ref.shape[0]
        spot = lambda oe: out.at[pl.ds(pl.multiple_of((at.e + oe) * rows, rows), rows)]
        f_dev, s_dev = at.device(oe=at.dy), at.device(oe=at.dc)
        self.ref, self.place = ref, spot(0)
        self.far = remote(ref, spot(0), send_sem.at[0], recv_sem.at[0], f_dev)
        self.near = remote(ref, spot(0), send_sem.at[1], recv_sem.at[1], s_dev)
        self.over = remote(spot(at.dy), spot(at.dy), send_sem.at[2], recv_sem.at[2], s_dev)

    def start(self):
        for copy in (self.far, self.near):
            copy.start()
        keep(self.ref, self.place)

    def forward(self):
        self.far.wait_recv()
        self.over.start()

    def finish(self):
        self.far.wait_send()
        self.near.wait()
        self.over.wait()


def last_scatter_kernel(*refs):
    refs = list(refs)

    def take(count):
        taken = refs[:count]
        del refs[:count]
        return taken

    in_ref, g_ref, u_ref, scaled_ref, picked_ref, dy_ref, mixed_ref, given = take(8)
    halves, home_refs = take(5), take(3)
    out_ref, taken, grad_gate, grad_up, grad_down, mixed_out = take(6)
    home_outs = take(3)
    right, left, other, grad, turned = take(5)
    mine, got = take(3), take(3)
    buffers = take(6)
    first_sem, cross_send, cross_recv, load_sem, store_sem = take(5)
    home_sems, share_sems = take(5), take(2)
    at = Place()
    greet(at, True)
    total = Scatter(at, *buffers, out_ref)
    acc = buffers[0]
    rows, width = acc.shape[1:]
    part = given.shape[0]
    crossing = cross(at, [given], [taken], cross_send, cross_recv)[0]
    home = Home(at, home_refs, home_outs, mine, got, *home_sems)
    sharing = Share(at, mixed_ref, mixed_out, *share_sems)

    def rows_of(rank):
        return in_ref.at[pl.ds(pl.multiple_of(rank * rows, rows), rows)]

    order = [(f, zi) for f in (1, 0) for zi in (3, 2, 1, 0)]
    firsts = {}
    for f, zi in order:
        k = f * 4 + zi
        total.to_twin(rows_of(at.shard(f * at.dy + at.dc, zi)), f, zi)
        firsts[k] = pltpu.make_async_copy(
            rows_of(at.shard(f * at.dy, zi)), acc.at[k], first_sem.at[k]
        )
        firsts[k].start()
    home.start()
    crossing.start()
    pairs = [
        (picked_ref, right.at[0]),
        (dy_ref, right.at[1]),
        (g_ref.at[0], left.at[0]),
        (u_ref.at[0], left.at[1]),
        (scaled_ref.at[0], left.at[2]),
    ]
    pairs += [
        (ref, other.at[j // 2 % 2, pl.ds(j % 2 * part, part)])
        for j, ref in enumerate(halves + [taken])
    ]
    loads = [pltpu.make_async_copy(a, b, load_sem.at[j]) for j, (a, b) in enumerate(pairs)]
    for copy in loads[:9]:
        copy.start()

    def store(m):
        ref = (grad_gate, grad_up, grad_down)[m]
        return pltpu.make_async_copy(grad.at[m % 2], ref, store_sem.at[m])

    def gradient(m, half=None):
        turned[...] = left[m].T
        span = slice(None) if half is None else pl.ds(half * part, part)

        @columns_loop(width, 8)
        def _(columns):
            terms = product(turned[span, :], right[m // 2, :, columns])
            grad[m % 2, span, columns] = terms + other[m % 2, span, columns].astype(F32)

        if half != 0:
            store(m).start()

    for zi in (3, 2, 1, 0):
        firsts[4 + zi].wait()
        total.first(zi)
    sharing.start()
    for copy in loads[:9]:
        copy.wait()
    for m in (3, 2, 1, 0):
        firsts[m].wait()
    gradient(0)
    loads[9].start()
    total.second(3, "end")
    home.line(3)
    total.second(3, "middle")
    total.second(2, "end")
    gradient(1)
    total.second(2, "middle")
    home.line(2)
    total.second(1)
    home.line(1)
    home.line(0)
    sharing.forward()
    loads[9].wait()
    store(0).wait()
    gradient(2, 0)
    total.second(0)
    crossing.wait_recv()
    loads[10].start()
    loads[10].wait()
    gradient(2, 1)
    home.finish()
    sharing.finish()
    store(1).wait()
    store(2).wait()
    crossing.wait_send()
    total.finish()


def last_rows(x, g, u, scaled, picked, picked_dy, home, mixed_own, given, halves, cid):
    rows, width = x.shape[0] // 16, x.shape[1]
    slots, hidden = g.shape[1:]
    hbm, vmem = pl.BlockSpec(memory_space=pl.ANY), pl.BlockSpec(memory_space=pltpu.VMEM)
    shape, sems = jax.ShapeDtypeStruct, lambda n: pltpu.SemaphoreType.DMA((n,))
    return pl.pallas_call(
        last_scatter_kernel,
        out_shape=[
            shape((rows, width), F32),
            shape(given.shape, BF),
            *[shape((hidden, width), F32)] * 3,
            shape((4 * rows, width), BF),
            *[shape((4,) + a.shape[1:], BF) for a in home],
        ],
        in_specs=[hbm] * 16,
        out_specs=[vmem] + [hbm] * 8,
        scratch_shapes=[
            pltpu.VMEM((2, slots, width), BF),
            pltpu.VMEM((3, slots, hidden), BF),
            pltpu.VMEM((2, hidden, width), BF),
            pltpu.VMEM((2, hidden, width), F32),
            pltpu.VMEM((hidden, slots), BF),
            *[pltpu.VMEM((4,) + a.shape[1:], BF) for a in home] * 2,
            *scatter_buffers(rows, width),
            sems(8),
            sems(1),
            sems(1),
            sems(11),
            sems(3),
            sems(15),
            sems(12),
            sems(12),
            sems(9),
            sems(12),
            sems(3),
            sems(3),
        ],
        compiler_params=pltpu.CompilerParams(
            collective_id=cid, has_side_effects=True, vmem_limit_bytes=62 * 1024 * 1024
        ),
    )(x, g, u, scaled, picked, picked_dy, mixed_own, given, *halves, *home)


def end_kernel(tokens_ref, gain_ref, small_ref, out_ref, gain_out, small_out, *scratch):
    gain_got, gain_sum, gain_all, small_all = scratch[:4]
    share_sems = scratch[4:6]
    gain_send, gain_recv, sum_send, sum_recv, small_send, small_recv = scratch[6:]
    at = Place()
    barrier = pltpu.get_barrier_semaphore()
    blocks = [(at.device(ox=ox, zi=k), m * 4 + k) for m, ox in enumerate((0, at.dx)) for k in range(4)]
    group = [at.device(oe=oe) for oe in (at.dy, at.dc, at.dy + at.dc)]
    for peer in [device for device, j in blocks[1:]] + group:
        pl.semaphore_signal(barrier, inc=1, device_id=peer, device_id_type=MESH)
    pl.semaphore_wait(barrier, 10)
    sharing = Share(at, tokens_ref, out_ref, *share_sems)
    own = at.x * 4 + at.z
    copies = []
    for device, j in blocks[1:]:
        copy = remote(
            gain_ref.at[device[0] * 4 + device[1]],
            gain_got.at[own],
            gain_send.at[j],
            gain_recv.at[own],
            device,
        )
        copy.start()
        copies.append(copy)
    for j, device in enumerate(group):
        copy = remote(small_ref, small_all.at[j], small_send.at[j], small_recv.at[j], device)
        copy.start()
        copies.append(copy)
    sharing.start()
    gain = gain_ref[own]
    for device, j in blocks[1:]:
        there = device[0] * 4 + device[1]
        remote(
            gain_ref.at[0], gain_got.at[there], gain_send.at[j], gain_recv.at[there], device
        ).wait_recv()
        gain = gain + gain_got[there]
    gain_sum[...] = gain
    for j, device in enumerate(group):
        copy = remote(gain_sum, gain_all.at[j], sum_send.at[j], sum_recv.at[j], device)
        copy.start()
        copies.append(copy)
    small = small_ref[...]
    for j in range(3):
        copies[7 + j].wait_recv()
        copies[10 + j].wait_recv()
        small = small + small_all[j]
        gain = gain + gain_all[j]
    gain_out[...] = gain
    small_out[...] = small
    sharing.forward()
    sharing.finish()
    for copy in copies:
        copy.wait_send()


def end(tokens_own, gain_part, small, cid):
    rows, width = tokens_own.shape
    vmem, hbm = pl.BlockSpec(memory_space=pltpu.VMEM), pl.BlockSpec(memory_space=pl.ANY)
    shape, sems = jax.ShapeDtypeStruct, lambda n: pltpu.SemaphoreType.DMA((n,))
    return pl.pallas_call(
        end_kernel,
        out_shape=[
            shape((4 * rows, width), tokens_own.dtype),
            shape(gain_part.shape[1:], F32),
            shape(small.shape, F32),
        ],
        in_specs=[hbm, vmem, vmem],
        out_specs=[hbm, vmem, vmem],
        scratch_shapes=[
            pltpu.VMEM(gain_part.shape, F32),
            pltpu.VMEM(gain_part.shape[1:], F32),
            pltpu.VMEM((3,) + gain_part.shape[1:], F32),
            pltpu.VMEM((3,) + small.shape, F32),
            sems(3),
            sems(3),
            sems(8),
            sems(8),
            sems(3),
            sems(3),
            sems(3),
            sems(3),
        ],
        compiler_params=pltpu.CompilerParams(collective_id=cid, has_side_effects=True),
    )(tokens_own, gain_part, small)


def front_kernel(scale, *refs):
    refs = list(refs)

    def take(count):
        taken = refs[:count]
        del refs[:count]
        return taken

    dy_ref, tokens_ref, units, given, gain, w_qkv, w_out_blocks, tables = take(8)
    dy_out, units_out, taken, normed_out, part_out, q_out, k_out, v_out, heads_out, lse_out = take(10)
    w_out, w_qkv_turned = take(2)
    rows_in, normed, staged = take(3)
    send_sem, recv_sem, swap_send, swap_recv = take(4)
    cross_send, cross_recv, in_sem, normed_sem, part_sem = take(5)
    at = Place()
    greet(at, True)
    gather = Gather(at, dy_ref, dy_out, send_sem, recv_sem, True)
    swap_in = Exchange(at, [units], [units_out], swap_send, swap_recv)
    crossing = cross(at, [given], [taken], cross_send, cross_recv, (taken.shape[0],))[0]
    length, width = tokens_ref.shape
    block = length // 4
    step = 256
    over = columns_loop(width, 4)

    def rows_load(j):
        return pltpu.make_async_copy(
            tokens_ref.at[pl.ds(j * block, block)], rows_in.at[j % 2], in_sem.at[j % 2]
        )

    def normed_store(j):
        return pltpu.make_async_copy(
            normed.at[j % 2], normed_out.at[pl.ds(j * block, block)], normed_sem.at[j % 2]
        )

    def part_store(i):
        return pltpu.make_async_copy(
            staged.at[i % 2], part_out.at[pl.ds(i * step, step)], part_sem.at[i % 2]
        )

    def turn_rows(values, here):
        other = pltpu.roll(values, HDIM // 2, 1)
        return (values * tables[0, here, :] - other * tables[1, here, :]).astype(BF)

    def project(j):
        rows_load(j).wait()
        if j >= 2:
            normed_store(j - 2).wait()

        @pl.loop(0, block // 64)
        def _(n):
            span = pl.ds(pl.multiple_of(n * 64, 64), 64)
            values = rows_in[j % 2, span, :].astype(F32)
            size = jnp.mean(values * values, axis=-1, keepdims=True)
            normed[j % 2, span, :] = (values * lax.rsqrt(size + EPSILON) * gain[0:1, :]).astype(BF)

        normed_store(j).start()
        if j < 2:
            rows_load(j + 2).start()
        here = pl.ds(j * block, block)
        qkv = product(normed[j % 2], w_qkv[...])
        q_out[here, :] = turn_rows(qkv[:, :HDIM], here)
        k_out[here, :] = turn_rows(qkv[:, HDIM : 2 * HDIM], here)
        v_out[here, :] = qkv[:, 2 * HDIM :].astype(BF)

    def attend_rows(i):
        seen = (i + 1) * step
        here = pl.ds(i * step, step)
        scores = transposed_right(q_out[here, :], k_out[0:seen, :]) * scale
        row_at = lax.broadcasted_iota(jnp.int32, scores.shape, 0) + i * step
        col_at = lax.broadcasted_iota(jnp.int32, scores.shape, 1)
        scores = jnp.where(row_at >= col_at, scores, MASKED)
        top = jnp.max(scores, axis=-1, keepdims=True)
        powers = jnp.exp(scores - top)
        lse = top + jnp.log(jnp.sum(powers, axis=-1, keepdims=True))
        probs = jnp.exp(scores - lse).astype(BF)
        heads_out[here, :] = product(probs, v_out[0:seen, :]).astype(BF)
        lse_out[here, :] = jnp.broadcast_to(lse, (step, HDIM))
        if i >= 2:
            part_store(i - 2).wait()

        @over
        def _(columns):
            staged[i % 2, :, columns] = product(heads_out[here, :], w_out[:, columns]).astype(BF)

        part_store(i).start()

    gather.begin()
    for zi in (1, 2, 3):
        swap_in.along(zi)
    swap_in.start()
    crossing.start()
    rows_load(0).start()
    rows_load(1).start()
    size = w_out_blocks.shape[2]
    for d in range(8):
        w_out[:, d * size : (d + 1) * size] = w_out_blocks[d]
    w_qkv_turned[...] = w_qkv[...].T
    project(0)
    project(1)
    attend_rows(0)
    gather.step(1)
    project(2)
    attend_rows(1)
    attend_rows(2)
    gather.step(2)
    swap_in.forward(1)
    project(3)
    attend_rows(3)
    attend_rows(4)
    gather.step(3)
    swap_in.forward(2)
    attend_rows(5)
    attend_rows(6)
    attend_rows(7)
    gather.step(4)
    swap_in.forward(3)
    for j in (2, 3):
        normed_store(j).wait()
    for i in (6, 7):
        part_store(i).wait()
    swap_in.finish()
    crossing.wait()
    gather.finish()


def front(dy, tokens_all, units, given, gain, w_qkv, w_out, tables, cid):
    length, width = tokens_all.shape
    hbm, vmem = pl.BlockSpec(memory_space=pl.ANY), pl.BlockSpec(memory_space=pltpu.VMEM)
    shape, sems = jax.ShapeDtypeStruct, lambda n: pltpu.SemaphoreType.DMA((n,))
    return pl.pallas_call(
        functools.partial(front_kernel, HDIM ** (-0.5)),
        out_shape=[
            shape((length, width), BF),
            shape((8,) + units.shape[1:], BF),
            half_of(given),
            shape((length, width), BF),
            shape((length, width), BF),
            *[shape((length, HDIM), BF)] * 4,
            shape((length, HDIM), F32),
            shape((HDIM, width), BF),
            shape((3 * HDIM, width), BF),
        ],
        in_specs=[hbm] * 4 + [vmem] * 4,
        out_specs=[hbm] * 5 + [vmem] * 7,
        scratch_shapes=[
            pltpu.VMEM((2, length // 4, width), BF),
            pltpu.VMEM((2, length // 4, width), BF),
            pltpu.VMEM((2, 256, width), BF),
            sems(38),
            sems(30),
            sems(7),
            sems(8),
            sems(1),
            sems(1),
            sems(2),
            sems(2),
            sems(2),
        ],
        compiler_params=pltpu.CompilerParams(
            collective_id=cid, has_side_effects=True, vmem_limit_bytes=60 * 1024 * 1024
        ),
    )(dy, tokens_all, units, given, gain, w_qkv, w_out, tables)


def by_four(matrix):
    rows, columns = matrix.shape
    return matrix.reshape(rows, 4, columns // 4).transpose(1, 0, 2)


def turn_tables(length):
    inverse = 10000.0 ** (-np.arange(HDIM // 2).astype(np.float64) * 2.0 / HDIM)
    angles = np.arange(length).astype(np.float64)[:, None] * inverse[None, :]
    return np.cos(angles).astype(np.float32), np.sin(angles).astype(np.float32)


def fast_body(
    tokens,
    routes,
    norm_attn,
    w_query,
    w_key,
    w_value,
    w_out,
    norm_mix,
    w_router,
    shared_gate,
    shared_up,
    shared_down,
    expert_gate,
    expert_up,
    expert_down,
    out_grad,
):
    dp, ctx, exp = lax.axis_index("dp"), lax.axis_index("ctx"), lax.axis_index("exp")
    rows_here, width = tokens.shape[1], tokens.shape[2]
    quarter = rows_here // 4
    length = rows_here * 4
    experts = w_router.shape[1]
    capacity = quarter * TOPK * 4 // (3 * experts)
    groups = length // quarter
    dense = w_query.shape[0]
    cut = shared_gate.shape[1] // 4
    wide = 256
    start = exp * quarter
    tokens_own = lax.dynamic_slice_in_dim(tokens[0], start, quarter, 0)
    dy_own = lax.dynamic_slice_in_dim(out_grad[0], start, quarter, 0)

    route_rows = routes[0].T
    theirs = jnp.arange(4, dtype=jnp.int32)[:, None, None] * 4 + exp
    named = jnp.any(route_rows[None] == theirs, axis=1).astype(BF).reshape(4, 2, dense)
    little = jnp.concatenate([w_router.T, norm_attn[None], norm_mix[None]], axis=0)
    little = jnp.concatenate([jnp.broadcast_to(little[None], (4,) + little.shape), named], axis=1)
    few = -(-little.shape[1] // 16) * 16
    little = jnp.pad(little, ((0, 0), (0, few - little.shape[1]), (0, 0)))
    sent_head = jnp.concatenate([by_four(w_query), by_four(w_key), by_four(w_value)], axis=2)
    sent_out = w_out.reshape(4, HDIM, dense)
    sent_units = jnp.stack([shared_gate.T, shared_up.T, shared_down], axis=0)
    sent_units = sent_units.reshape(3, 4, cut, dense).transpose(1, 0, 2, 3).reshape(4, 3 * cut, dense)
    own_gate, own_up, own_down = expert_gate[0].T, expert_up[0].T, expert_down[0]
    part = own_gate.shape[0] // 2
    tokens_all, early, early_out, early_little, gate_0 = all_rows(
        tokens[0], True, 1, (sent_head, sent_out, little), (own_gate,), (0,)
    )
    w_qkv = early.reshape(width, 3 * HDIM)
    early_little = early_little.transpose(1, 0, 2)
    router_rows = early_little[:experts].reshape(experts, width)
    attention_gain = early_little[experts].reshape(width).astype(F32)
    mixer_gain = early_little[experts + 1].reshape(width).astype(F32)
    hits = early_little[experts + 2 : experts + 4].transpose(1, 0, 2).reshape(2, length)
    hits = lax.dynamic_index_in_dim(hits, dp, 0, False).astype(F32).reshape(groups, quarter)

    cosine, sine = turn_tables(length)
    tables = np.stack(
        [np.concatenate([cosine, cosine], axis=1), np.concatenate([sine, -sine], axis=1)]
    )
    dy_all, late, gate_1, normed, attn_part, query, key, value, heads_out, lse, w_out_head, w_qkv_turned = front(
        out_grad[0],
        tokens_all,
        sent_units,
        own_gate,
        jnp.broadcast_to(attention_gain[None], (8, width)),
        w_qkv,
        early_out,
        tables,
        2,
    )
    attn, up_0, up_1 = own_rows(attn_part, 3, (own_up, own_up), (0, part))
    middle = tokens_own.astype(F32) + attn
    normed_own = rms_scale(middle, mixer_gain).astype(BF)

    mine = ctx * 4 + exp
    place = jnp.cumsum(hits, axis=1) - 1.0
    first = (jnp.arange(groups) % 4 * capacity).astype(F32)[:, None]
    place = jnp.where(hits > 0.5, place + first, -1.0).reshape(4, 1, 4 * quarter)
    blocks = place == jnp.arange(4 * capacity).astype(F32)[None, :, None]
    blocks = blocks.astype(BF)
    router_wide = jnp.pad(router_rows, ((0, HDIM - experts), (0, 0)))
    (
        mix_all,
        picked,
        picked_dy,
        scaled,
        g_back,
        u_back,
        gate_back,
        shared_act,
        shared_gu_back,
        down_0,
        down_1,
        shared_in,
        shared_out,
    ) = expert_rows(
        normed_own,
        dy_all,
        blocks,
        router_wide,
        experts,
        late,
        wide,
        (own_gate, own_up, own_down, gate_0, gate_1, up_0, up_1),
        (own_down, own_down),
        4,
    )
    other_down = (down_0, down_1)

    mix_back, gate_0, gate_1, up_0, up_1, down_0, down_1 = expert_back(
        blocks,
        gate_back,
        shared_in,
        g_back,
        u_back,
        shared_gu_back,
        picked,
        picked_dy,
        scaled,
        (own_gate, own_up, gate_0, gate_1, up_0, up_1),
        5,
    )
    gate_back_own = mix_back[:, width : width + experts]
    mix_back = mix_back[:, :width]

    router_own = jax.nn.softmax(transposed_right(normed_own, router_rows), axis=-1)
    logit_back = (
        router_own * (gate_back_own - jnp.sum(router_own * gate_back_own, axis=-1, keepdims=True))
    ).astype(BF)
    router_part = transposed_left(logit_back, normed_own)

    mix_back = mix_back + product(logit_back, router_rows)
    _, norm_mix_back = jax.vjp(rms_scale, middle, mixer_gain)
    middle_norm_back, gain_mix_part = norm_mix_back(mix_back)
    middle_back = dy_own.astype(F32) + middle_norm_back
    attn_back = middle_back.astype(BF)
    attn_back_all, mixed_part, units_part, gate_1, up_0 = gather_back(
        attn_back,
        (gate_1, up_0),
        blocks,
        shared_out,
        scaled,
        shared_act,
        shared_gu_back,
        (own_down, *other_down),
        mix_all,
        dy_all,
        cut,
        7,
    )
    mixed_sum, normed_part, head_part, up_1, down_0 = mixed_rows(
        w_out_head,
        w_qkv_turned,
        tables,
        query,
        key,
        value,
        lse,
        heads_out,
        mixed_part,
        attn_back_all,
        normed,
        (up_1, down_0),
        9,
    )
    mixed_own = (middle + mixed_sum).astype(BF)
    small_part = jnp.concatenate([gain_mix_part[None], router_part], axis=0).astype(BF)
    small_rows = -(-(experts + 1) // 16) * 16
    small_part = jnp.pad(small_part, ((0, small_rows - experts - 1), (0, 0)))
    small_part = small_part.reshape(small_rows, 8, dense).transpose(1, 0, 2)
    normed_back, _, gate_grad, up_grad, down_grad, mixed, head_grad, units_grad, small = last_rows(
        normed_part,
        g_back,
        u_back,
        scaled,
        picked,
        picked_dy,
        (head_part, units_part, small_part),
        mixed_own,
        down_1,
        (gate_0, gate_1, up_0, up_1, down_0),
        8,
    )
    head_grad, units_grad = head_grad.astype(F32), units_grad.astype(F32)
    small_part = jnp.sum(small.astype(F32), axis=0)
    _, norm_attn_back = jax.vjp(rms_scale, tokens_own.astype(F32), attention_gain)
    input_norm_back, gain_attn_part = norm_attn_back(normed_back)
    tokens_back_own = (middle_back + input_norm_back).astype(BF)

    gain_part = jnp.pad(gain_attn_part.reshape(8, 1, dense), ((0, 0), (0, 7), (0, 0)))
    tokens_back, gain_attn, small = end(tokens_back_own, gain_part, small_part, 6)

    def columns_of(parts):
        return parts.transpose(2, 0, 1).reshape(dense, -1)

    def rows_of(parts):
        return parts.reshape(-1, dense)

    return (
        mixed[None],
        tokens_back[None],
        gain_attn[0],
        columns_of(head_grad[:, :HDIM]),
        columns_of(head_grad[:, HDIM : 2 * HDIM]),
        columns_of(head_grad[:, 2 * HDIM : 3 * HDIM]),
        rows_of(head_grad[:, 3 * HDIM :]),
        small[0],
        small[1 : experts + 1].T,
        rows_of(units_grad[:, :cut]).T,
        rows_of(units_grad[:, cut : 2 * cut]).T,
        rows_of(units_grad[:, 2 * cut :]),
        gate_grad.T[None],
        up_grad.T[None],
        down_grad[None],
    )


def solution(mesh):
    sizes = dict(mesh.shape)

    def chosen(*args):
        heads = args[3].shape[1] * sizes["exp"] // HDIM
        one_head_each = heads == sizes["ctx"] * sizes["exp"]
        built_for = (sizes["dp"], sizes["ctx"], sizes["exp"]) == (2, 4, 4)
        return fast_body(*args) if one_head_each and built_for else body(*args)

    in_specs = (
        P("dp", "ctx", None),
        P("dp", "ctx", None),
        P(("dp", "ctx")),
        P(("dp", "ctx"), "exp"),
        P(("dp", "ctx"), "exp"),
        P(("dp", "ctx"), "exp"),
        P("exp", ("dp", "ctx")),
        P(("dp", "ctx")),
        P(("dp", "ctx"), None),
        P(("dp", "ctx"), "exp"),
        P(("dp", "ctx"), "exp"),
        P("exp", ("dp", "ctx")),
        P(("ctx", "exp"), None, "dp"),
        P(("ctx", "exp"), None, "dp"),
        P(("ctx", "exp"), "dp", None),
        P("dp", "ctx", None),
    )
    out_specs = (
        P("dp", "ctx", None),
        P("dp", "ctx", None),
        P(("dp", "ctx")),
        P(("dp", "ctx"), "exp"),
        P(("dp", "ctx"), "exp"),
        P(("dp", "ctx"), "exp"),
        P("exp", ("dp", "ctx")),
        P(("dp", "ctx")),
        P(("dp", "ctx"), None),
        P(("dp", "ctx"), "exp"),
        P(("dp", "ctx"), "exp"),
        P("exp", ("dp", "ctx")),
        P(("ctx", "exp"), None, "dp"),
        P(("ctx", "exp"), None, "dp"),
        P(("ctx", "exp"), "dp", None),
    )
    return jax.shard_map(chosen, mesh=mesh, in_specs=in_specs, out_specs=out_specs, check_vma=False)
```
